32 devices in a mesh: dp: 8 (over y, x, core), mp: 4 (over z).
Axes of the slice: x: 2, y: 2, z: 4, core: 2. Of those that a mesh axis runs over, the one named last changes fastest.
Arguments:
- frames: bfloat16 [24576, 512], P(('dp', 'mp')), may hold values from -6 to 6
- cotangent: bfloat16 [24576, 512], P(('dp', 'mp')), may hold values from -6 to 6
- lengths: int32 [32], P('dp'), may hold values from 256 to 768, as said below
- norm_gains: float32 [2, 5, 512], replicated, may hold values from 0.1 to 1.9
- ffn_in: float32 [2, 2, 512, 2048], P(None, None, 'dp', 'mp'), may hold values from -0.25 to 0.25
- ffn_out: float32 [2, 2, 2048, 512], P(None, None, 'mp', 'dp'), may hold values from -0.125 to 0.125
- attn_in: float32 [2, 3, 512, 512], P(None, None, 'dp', 'mp'), may hold values from -0.25 to 0.25
- attn_out: float32 [2, 512, 512], P(None, 'mp', 'dp'), may hold values from -1 to 1
- rel_bias: float32 [2, 8, 1536], P(None, 'mp'), may hold values from -4 to 4
- cg_in: float32 [2, 2, 512, 1536], P(None, None, 'dp', 'mp'), may hold values from -0.25 to 0.25
- csgu_gain: float32 [2, 1536], P(None, 'mp'), may hold values from 0.2 to 5
- csgu_conv: float32 [2, 31, 1536], P(None, None, 'mp'), may hold values from -2 to 2
- cg_out: float32 [2, 1536, 512], P(None, 'mp', 'dp'), may hold values from -1 to 1
- merge_conv: float32 [2, 31, 1024], replicated, may hold values from -1 to 1
- merge_out: float32 [2, 1024, 512], P(None, 'dp'), may hold values from -0.1875 to 0.1875
Outputs:
- output_frames: float32 [24576, 512], P(('dp', 'mp'))
- input_grad: float32 [24576, 512], P(('dp', 'mp'))
- grad_norm_gains: float32 [2, 5, 512], replicated
- grad_ffn_in: float32 [2, 2, 512, 2048], P(None, None, 'dp', 'mp')
- grad_ffn_out: float32 [2, 2, 2048, 512], P(None, None, 'mp', 'dp')
- grad_attn_in: float32 [2, 3, 512, 512], P(None, None, 'dp', 'mp')
- grad_attn_out: float32 [2, 512, 512], P(None, 'mp', 'dp')
- grad_rel_bias: float32 [2, 8, 1536], P(None, 'mp')
- grad_cg_in: float32 [2, 2, 512, 1536], P(None, None, 'dp', 'mp')
- grad_csgu_gain: float32 [2, 1536], P(None, 'mp')
- grad_csgu_conv: float32 [2, 31, 1536], P(None, None, 'mp')
- grad_cg_out: float32 [2, 1536, 512], P(None, 'mp', 'dp')
- grad_merge_conv: float32 [2, 31, 1024], replicated
- grad_merge_out: float32 [2, 1024, 512], P(None, 'dp')
The draws below stay inside these ranges and needn't reach their ends.
Inputs may be any that keep to these rules, and one draw needn't show every extreme that they name: `lengths`: in every draw all 4 utterances of one aligned block of 4 (those of one index of dp) are 768 frames long.
All inputs are finite; a program needn't handle non-finite values.
Results may differ from the reference program's by a relative error of at most 0.025.
Values may be sent and summed in bfloat16 or wider, within the bound.
A program may use at most 576 MiB of HBM per device.

```python
import jax
import jax.numpy as jnp
from jax import lax

D = 512
HEADS = 8
HEAD_DIM = 64
FF = 2048
CGH = 1536
KERNEL = 31
LEN = 768
LAYERS = 2
SEQ_DEV = 4
SEQS = 32
TOKENS = 24576
REL = 1536
N_DP = 8


def draw_lengths(key, part):
    first_key, second_key = jax.random.split(key)
    values = jax.random.randint(first_key, (SEQS,), LEN // 3, LEN + 1)
    chosen = jax.random.randint(second_key, (), 0, SEQS // SEQ_DEV)
    owners = jnp.arange(SEQS) // SEQ_DEV == chosen
    return jnp.where(owners, LEN, values).astype(jnp.int32)


def draw_csgu_gain(key, part):
    factor = jax.random.uniform(jax.random.fold_in(key, 11), (LAYERS, CGH), jnp.float32, 0.8, 1.2)
    place = jnp.arange(CGH, dtype=jnp.float32) / (CGH - 1)
    ramp = 0.3 + 2.7 * place
    return (factor * ramp[None, :]).astype(jnp.float32)


def draw_csgu_conv(key, part):
    taps = jnp.clip(jax.random.normal(jax.random.fold_in(key, 13), (LAYERS, KERNEL, CGH), jnp.float32), -4.0, 4.0)
    return (taps * KERNEL ** (-0.5) + 1.0 / KERNEL).astype(jnp.float32)


def draw_cg_out(key, part):
    own = jnp.clip(jax.random.normal(jax.random.fold_in(key, 17), (LAYERS, CGH, D), jnp.float32), -4.0, 4.0)
    common = jnp.clip(jax.random.normal(jax.random.fold_in(key, 19), (LAYERS, 1, D), jnp.float32), -4.0, 4.0)
    return ((own + common) * CGH ** (-0.5)).astype(jnp.float32)


def block_levels(rng, shape, shards, smallest, high):
    factor_of = 1.0
    for position, parts in shards:
        draws = jax.random.uniform(jax.random.fold_in(jax.random.fold_in(rng, 6), position), (parts,), jnp.float32, smallest / len(shards), high / len(shards))
        factor_of = factor_of * jnp.repeat(jnp.exp(draws), shape[position] // parts).reshape((-1,) + (1,) * (len(shape) - 1 - position))
    return factor_of


def gaussian(rng, shape, scale, most, cuts=(), kind=jnp.bfloat16):
    entries = jax.random.normal(rng, shape, jnp.float32) * scale
    if len(cuts) > 0:
        entries = block_levels(rng, shape, cuts, -0.22, 0.18) * entries
    return jnp.clip(entries, min=-most, max=most).astype(kind)


def setup_inputs(seed: int = 0) -> dict:
    key_of = jax.random.split(jax.random.key(seed), 16)
    return {
        "frames": gaussian(key_of[0], (TOKENS, D), 1.0, 6.0, ((0, 32),)),
        "cotangent": gaussian(key_of[1], (TOKENS, D), 1.0, 6.0, ((0, 32),)),
        "lengths": draw_lengths(jax.random.fold_in(key_of[15], 71), 0),
        "norm_gains": jnp.clip(1.0 + 0.18 * jax.random.normal(key_of[3], (LAYERS, 5, D), jnp.float32), 0.1, 1.9),
        "ffn_in": gaussian(key_of[4], (LAYERS, 2, D, FF), D ** -0.5, 0.25, ((2, 8), (3, 4)), jnp.float32),
        "ffn_out": gaussian(key_of[5], (LAYERS, 2, FF, D), FF ** -0.5, 0.125, ((2, 4), (3, 8)), jnp.float32),
        "attn_in": gaussian(key_of[6], (LAYERS, 3, D, D), D ** -0.5, 0.25, ((2, 8), (3, 4)), jnp.float32),
        "attn_out": gaussian(key_of[7], (LAYERS, D, D), (D // 16) ** -0.5, 1.0, ((1, 4), (2, 8)), jnp.float32),
        "rel_bias": gaussian(key_of[8], (LAYERS, HEADS, REL), 1.0, 4.0, ((1, 4),), jnp.float32),
        "cg_in": gaussian(key_of[9], (LAYERS, 2, D, CGH), D ** -0.5, 0.25, ((2, 8), (3, 4)), jnp.float32),
        "csgu_gain": draw_csgu_gain(jax.random.fold_in(key_of[15], 71), 0),
        "csgu_conv": draw_csgu_conv(jax.random.fold_in(key_of[15], 71), 0),
        "cg_out": draw_cg_out(jax.random.fold_in(key_of[15], 71), 0),
        "merge_conv": gaussian(key_of[13], (LAYERS, KERNEL, 2 * D), KERNEL ** -0.5, 1.0, (), jnp.float32),
        "merge_out": gaussian(key_of[14], (LAYERS, 2 * D, D), (2 * D) ** -0.5, 0.1875, ((1, 8),), jnp.float32),
    }


EPSILON = 1e-05
MASKED = -1000000000.0
HIGHEST = lax.Precision.HIGHEST

@jax.custom_vjp
def low(v):
    return lax.optimization_barrier(v.astype(jnp.bfloat16)).astype(jnp.float32)

@jax.custom_vjp
def low_back(v):
    return v

def low_keep(v):
    return (low(v), None)

def low_pass(kept, grad):
    return (grad,)

def back_keep(v):
    return (v, None)

def back_low(kept, grad):
    return (low(grad),)
low.defvjp(low_keep, low_pass)
low_back.defvjp(back_keep, back_low)

def matmul_full(left, right):
    return jnp.dot(left, right, precision=HIGHEST, preferred_element_type=jnp.float32)

def layer_norm(values, gain):
    centred = values - lax.optimization_barrier(jnp.mean(values, axis=-1, keepdims=True))
    spread = lax.optimization_barrier(jnp.mean(centred * centred, axis=-1, keepdims=True))
    return centred * lax.rsqrt(spread + EPSILON) * gain

def gelu_tanh(values):
    return 0.5 * values * (1.0 + jnp.tanh(0.7978845608028654 * (values + 0.044715 * values * values * values)))

def silu_plain(values):
    return values * jax.nn.sigmoid(values)

def depthwise(values, kernel, frame_count):
    kernel_width = kernel.shape[0]
    half_width = (kernel_width - 1) // 2
    blocks = values.reshape(-1, frame_count, values.shape[-1])
    padded = jnp.pad(blocks, ((0, 0), (half_width, half_width), (0, 0)))
    summed = jnp.zeros_like(blocks)
    for offset in range(kernel_width):
        summed = summed + padded[:, offset:offset + frame_count, :] * kernel[offset]
    return summed.reshape(values.shape)

def gate_norm(gated, first, second, gain, count):
    centre = first / count
    spread = second / count - centre * centre
    return (gated - centre[:, None]) * lax.rsqrt(spread + EPSILON)[:, None] * gain

def position_bias(table, frame_count):
    rows_index = lax.broadcasted_iota(jnp.int32, (frame_count, frame_count), 0)
    cols_index = lax.broadcasted_iota(jnp.int32, (frame_count, frame_count), 1)
    return jnp.take(table, cols_index - rows_index + frame_count, axis=1)

def attend(query, key, value, table, length):
    frame_count = query.shape[0]
    scores = jnp.einsum('qhe,khe->hqk', query, key, precision=HIGHEST) * query.shape[2] ** (-0.5)
    scores = low_back(scores + position_bias(table, frame_count))
    valid = lax.broadcasted_iota(jnp.int32, (1, 1, frame_count), 2) < length
    scores = jnp.where(valid, scores, MASKED)
    peak = lax.optimization_barrier(jnp.max(scores, axis=-1, keepdims=True))
    expos = jnp.exp(scores - peak)
    probs = low(expos / lax.optimization_barrier(jnp.sum(expos, axis=-1, keepdims=True)))
    return jnp.einsum('hqk,khe->qhe', probs, value, precision=HIGHEST)

def feed_forward(values, gain, weight_in, weight_out):
    normed = low(layer_norm(values, gain))
    hidden = low_back(matmul_full(normed, low(weight_in)))
    return low_back(matmul_full(low(silu_plain(hidden)), low(weight_out)))

def encoder_layer(values, group_lengths, frame_keep, params):
    gains = params['norm_gains']
    values = values + 0.5 * feed_forward(values, gains[0], params['ffn_in'][0], params['ffn_out'][0])
    normed_att = low(layer_norm(values, gains[1]))
    projected = [low(low_back(matmul_full(normed_att, low(params['attn_in'][member])))) for member in range(3)]
    shaped = [piece.reshape(SEQ_DEV, LEN, HEADS, HEAD_DIM) for piece in projected]
    table = params['rel_bias']

    def one_utterance(carried):
        return attend(carried[0], carried[1], carried[2], table, carried[3])
    attended = lax.map(jax.checkpoint(one_utterance), (shaped[0], shaped[1], shaped[2], group_lengths))
    attended = low(low_back(attended.reshape(-1, D)))
    att = low_back(matmul_full(attended, low(params['attn_out'])))
    normed_cg = low(layer_norm(values, gains[2]))
    rest = gelu_tanh(low_back(matmul_full(normed_cg, low(params['cg_in'][0]))))
    gated = gelu_tanh(low_back(matmul_full(normed_cg, low(params['cg_in'][1]))))
    first = lax.optimization_barrier(jnp.sum(gated, axis=-1))
    second = lax.optimization_barrier(jnp.sum(gated * gated, axis=-1))
    gate_normed = gate_norm(gated, first, second, params['csgu_gain'], CGH) * frame_keep[:, None]
    mixed = low(rest * depthwise(gate_normed, params['csgu_conv'], LEN))
    cg = low_back(matmul_full(mixed, low(params['cg_out'])))
    joined = jnp.concatenate([att, cg], axis=-1) * frame_keep[:, None]
    merged = low(joined + depthwise(joined, params['merge_conv'], LEN))
    values = values + low_back(matmul_full(merged, low(params['merge_out'])))
    values = values + 0.5 * feed_forward(values, gains[3], params['ffn_in'][1], params['ffn_out'][1])
    return layer_norm(values, gains[4])

def reference(frames, cotangent, lengths, norm_gains, ffn_in, ffn_out, attn_in, attn_out, rel_bias, cg_in, csgu_gain, csgu_conv, cg_out, merge_conv, merge_out):
    params = {'norm_gains': norm_gains, 'ffn_in': ffn_in, 'ffn_out': ffn_out, 'attn_in': attn_in, 'attn_out': attn_out, 'rel_bias': rel_bias, 'cg_in': cg_in, 'csgu_gain': csgu_gain, 'csgu_conv': csgu_conv, 'cg_out': cg_out, 'merge_conv': merge_conv, 'merge_out': merge_out}
    params = jax.tree.map(lambda array_leaf: array_leaf.astype(jnp.float32), params)
    group_rows = SEQ_DEV * LEN
    inputs_all = frames.astype(jnp.float32).reshape(N_DP, group_rows, D)
    cots_all = cotangent.astype(jnp.float32).reshape(N_DP, group_rows, D)
    length_rows = lengths.astype(jnp.int32).reshape(N_DP, SEQ_DEV)

    def group_step(summed, carried):
        values, incoming, group_lengths = carried
        positions = lax.broadcasted_iota(jnp.int32, (SEQ_DEV, LEN), 1)
        frame_keep = (positions < group_lengths[:, None]).astype(jnp.float32).reshape(-1)

        def forward(inputs, weights):
            state = inputs
            for layer_index in range(LAYERS):
                layer_params = {arg_name: array_leaf[layer_index] for arg_name, array_leaf in weights.items()}
                state = encoder_layer(state, group_lengths, frame_keep, layer_params)
            return state * frame_keep[:, None]
        result, pullback = jax.vjp(forward, values, params)
        grad_values, grad_params = pullback(incoming)
        summed = jax.tree.map(lambda first, second: first + second, summed, grad_params)
        return (summed, (result, grad_values))
    zeros_tree = jax.tree.map(jnp.zeros_like, params)
    summed, (results, grads) = lax.scan(group_step, zeros_tree, (inputs_all, cots_all, length_rows))
    return (results.reshape(TOKENS, D), grads.reshape(TOKENS, D), summed['norm_gains'], summed['ffn_in'], summed['ffn_out'], summed['attn_in'], summed['attn_out'], summed['rel_bias'], summed['cg_in'], summed['csgu_gain'], summed['csgu_conv'], summed['cg_out'], summed['merge_conv'], summed['merge_out'])
```

```python
import functools

import jax
import jax.numpy as jnp
from jax import lax
from jax.experimental import pallas as pl
from jax.experimental.pallas import tpu as pltpu
from jax.sharding import PartitionSpec as P

EPSILON = 1e-05
MASKED = -1000000000.0
F32 = jnp.float32
BF16 = jnp.bfloat16
SEG = 16
GELU_A = 0.7978845608028654
GELU_B = 0.044715


def dot(left, right):
    return lax.dot_general(left, right, (((1,), (0,)), ((), ())), preferred_element_type=F32)


def dot_nt(left, right):
    return lax.dot_general(left, right, (((1,), (1,)), ((), ())), preferred_element_type=F32)


def low(values):
    return values.astype(BF16)


def norm_parts(values):
    mean = jnp.mean(values, axis=-1, keepdims=True)
    centred = values - mean
    spread = jnp.mean(centred * centred, axis=-1, keepdims=True)
    rstd = lax.rsqrt(spread + EPSILON)
    return centred * rstd, rstd


def norm_back(normed, rstd, gain, grad):
    scaled = grad * gain
    first = jnp.mean(scaled, axis=-1, keepdims=True)
    second = jnp.mean(scaled * normed, axis=-1, keepdims=True)
    return rstd * (scaled - first - normed * second)


def gelu(values):
    half = 0.5 * values
    inner = values * (GELU_A + (GELU_A * GELU_B) * (values * values))
    return half + half * jnp.tanh(inner)


def gelu_and_slope(values):
    half = 0.5 * values
    square = values * values
    tanh = jnp.tanh(values * (GELU_A + (GELU_A * GELU_B) * square))
    value = half + half * tanh
    slope = 0.5 + 0.5 * tanh + (half - half * tanh * tanh) * (GELU_A + (3.0 * GELU_A * GELU_B) * square)
    return value, slope


def rows_keep(start, rows, frames, length):
    at = lax.broadcasted_iota(jnp.int32, (rows, 1), 0) + start
    frame = (at % SEG) * (frames // SEG) + at // SEG
    return (frame < length).astype(F32)


def fill_padded(padded, values, taps):
    rows, _, lanes = values.shape
    half = (taps - 1) // 2
    padded[pl.ds(half, rows)] = values
    place = lax.broadcasted_iota(jnp.int32, (half, SEG, lanes), 1)
    before = pltpu.roll(values[rows - half :].astype(F32), 1, axis=1)
    padded[pl.ds(0, half)] = low(jnp.where(place == 0, 0.0, before))
    after = pltpu.roll(values[:half].astype(F32), SEG - 1, axis=1)
    padded[pl.ds(half + rows, half)] = low(jnp.where(place == SEG - 1, 0.0, after))


def convolve(padded, taps_of, taps, rows, block, emit):
    weights = [taps_of(k) for k in range(taps)]

    def step(index, carry):
        start = index * block
        total = None
        for first in range(0, taps, 8):
            part = None
            for k in range(first, min(taps, first + 8)):
                term = weights[k] * padded[pl.ds(start + k, block)]
                part = term if part is None else part + term
            part = part.astype(F32)
            total = part if total is None else total + part
        emit(start, total)
        return carry

    lax.fori_loop(0, rows // block, step, 0)


def tap_grads(padded, grads, sums, taps, rows, block):
    sums[...] = jnp.zeros_like(sums)

    def step(index, carry):
        start = index * block
        here = grads[pl.ds(start, block)]
        for k in range(taps):
            term = here * padded[pl.ds(start + k, block)]
            count = block
            while count > 1:
                count //= 2
                term = term[:count] + term[count:]
            sums[k] += term[0].astype(F32)
        return carry

    lax.fori_loop(0, rows // block, step, 0)


def ffn_forward_kernel(final, blocks, x_ref, gain_ref, w_ref, *rest):
    if final:
        last_ref, out_ref, h_ref, y_ref = rest
    else:
        out_ref, h_ref = rest
    width = h_ref.shape[2]
    x = x_ref[...]
    normed, _ = norm_parts(x)
    a = low(normed * gain_ref[...])
    total = None
    for m in range(blocks):
        h = dot(a, w_ref[m, :, :width])
        h_ref[m] = low(h)
        half = 0.5 * h
        s = low(half + half * jnp.tanh(half))
        part = dot_nt(s, w_ref[m, :, width:])
        total = part if total is None else total + part
    out = x + 0.5 * total
    out_ref[...] = out
    if final:
        normed, _ = norm_parts(out)
        y_ref[...] = normed * last_ref[...]


def ffn_forward(x, gain, w, last=None):
    tokens, depth = x.shape
    blocks, _, width = w.shape
    width //= 2
    tile = min(256, tokens)
    row = pl.BlockSpec((tile, depth), lambda i: (i, 0))
    vec = pl.BlockSpec((1, depth), lambda i: (0, 0))
    out_shape = [jax.ShapeDtypeStruct(x.shape, F32), jax.ShapeDtypeStruct((blocks, tokens, width), BF16)]
    out_specs = [row, pl.BlockSpec((blocks, tile, width), lambda i: (0, i, 0))]
    in_specs = [row, vec, pl.BlockSpec(w.shape, lambda i: (0, 0, 0))]
    args = [x, gain, w]
    if last is not None:
        in_specs.append(vec)
        args.append(last)
        out_shape.append(jax.ShapeDtypeStruct(x.shape, F32))
        out_specs.append(row)
    return pl.pallas_call(
        functools.partial(ffn_forward_kernel, last is not None, blocks),
        grid=(tokens // tile,),
        in_specs=in_specs,
        out_specs=out_specs,
        out_shape=out_shape,
        compiler_params=pltpu.CompilerParams(vmem_limit_bytes=56 * 2**20),
    )(*args)


def ffn_backward_kernel(final, tile, g_ref, x_ref, gain_ref, h_ref, w_ref, *rest):
    if final:
        last_ref, y_ref, dx_ref, dw_ref, dgain_ref, dlast_ref, grad, at, gt, a_rows, g_rows, s_rows, d_rows, da = rest
    else:
        dx_ref, dw_ref, dgain_ref, grad, at, gt, a_rows, g_rows, s_rows, d_rows, da = rest
    m = pl.program_id(0)
    tokens = x_ref.shape[0]
    width = h_ref.shape[2]
    chunks = tokens // tile

    @pl.when(m == 0)
    def _():
        if final:
            dlast_ref[...] = jnp.zeros_like(dlast_ref)
        for c in range(chunks):
            here = pl.ds(c * tile, tile)
            g = g_ref[here, :]
            if final:
                normed, rstd = norm_parts(y_ref[here, :])
                dlast_ref[...] += jnp.sum(g * normed, axis=0, keepdims=True)
                g = norm_back(normed, rstd, last_ref[...], g)
                grad[here, :] = g
            g_low = low(0.5 * g)
            g_rows[here, :] = g_low
            normed, _ = norm_parts(x_ref[here, :])
            a_rows[here, :] = low(normed * gain_ref[...])
        at[...] = a_rows[...].T
        gt[...] = g_rows[...].T

    w_in = w_ref[0, :, :width]
    w_out = w_ref[0, :, width:]
    for c in range(chunks):
        here = pl.ds(c * tile, tile)
        ds = dot(g_rows[here, :], w_out)
        h = h_ref[0, here, :].astype(F32)
        half = 0.5 * h
        tanh = jnp.tanh(half)
        s = half + half * tanh
        s_rows[here, :] = low(s)
        sig = 0.5 + 0.5 * tanh
        dh = low(ds * (sig + s * (1.0 - sig)))
        d_rows[here, :] = dh
        part = dot_nt(dh, w_in)

        @pl.when(m == 0)
        def _():
            da[here, :] = part

        @pl.when(m != 0)
        def _():
            da[here, :] += part

    dw_ref[0, :, :width] = low(dot(at[...], d_rows[...]))
    dw_ref[0, :, width:] = low(dot(gt[...], s_rows[...]))

    @pl.when(m == pl.num_programs(0) - 1)
    def _():
        dgain_ref[...] = jnp.zeros_like(dgain_ref)
        for c in range(chunks):
            here = pl.ds(c * tile, tile)
            normed, rstd = norm_parts(x_ref[here, :])
            d = da[here, :]
            dgain_ref[...] += jnp.sum(d * normed, axis=0, keepdims=True)
            base = grad[here, :] if final else g_ref[here, :]
            dx_ref[here, :] = base + norm_back(normed, rstd, gain_ref[...], d)


def ffn_backward(g, x, gain, h, w, last=None, final_in=None):
    tokens, depth = x.shape
    blocks, _, width = w.shape
    width //= 2
    tile = min(256, tokens)
    full = pl.BlockSpec((tokens, depth), lambda i: (0, 0))
    vec = pl.BlockSpec((1, depth), lambda i: (0, 0))
    vec_shape = jax.ShapeDtypeStruct((1, depth), F32)
    in_specs = [full, full, vec, pl.BlockSpec((1, tokens, width), lambda i: (i, 0, 0)), pl.BlockSpec((1, depth, 2 * width), lambda i: (i, 0, 0))]
    args = [g, x, gain, h, w]
    out_specs = [full, pl.BlockSpec((1, depth, 2 * width), lambda i: (i, 0, 0)), vec]
    out_shape = [jax.ShapeDtypeStruct(x.shape, F32), jax.ShapeDtypeStruct(w.shape, BF16), vec_shape]
    if last is not None:
        in_specs += [vec, full]
        args += [last, final_in]
        out_specs.append(vec)
        out_shape.append(vec_shape)
    return pl.pallas_call(
        functools.partial(ffn_backward_kernel, last is not None, tile),
        grid=(blocks,),
        in_specs=in_specs,
        out_specs=out_specs,
        out_shape=out_shape,
        scratch_shapes=[
            pltpu.VMEM((tokens, depth) if last is not None else (8, 128), F32),
            pltpu.VMEM((depth, tokens), BF16),
            pltpu.VMEM((depth, tokens), BF16),
            pltpu.VMEM((tokens, depth), BF16),
            pltpu.VMEM((tokens, depth), BF16),
            pltpu.VMEM((tokens, width), BF16),
            pltpu.VMEM((tokens, width), BF16),
            pltpu.VMEM((tokens, depth), F32),
        ],
        compiler_params=pltpu.CompilerParams(vmem_limit_bytes=56 * 2**20),
    )(*args)


HEAD = 64
PAIR = 2
LANES = 128


def split_lanes(lanes_ref, here, values):
    for l in range(values.shape[1] // LANES):
        lanes_ref[l, here, :] = values[:, l * LANES : (l + 1) * LANES]


def reorder(lanes_ref, stride, emit):
    blocks, tokens, _ = lanes_ref.shape
    count = tokens // stride
    for start in range(stride):
        for l in range(blocks):
            emit(start * count, l, lanes_ref[l, pl.ds(start, count, stride=stride), :])


def attention_forward_kernel(len_ref, x_ref, gain_ref, w_ref, table_ref, att_ref, q_ref, k_ref, v_ref, o_ref, lse_ref, b_rows, total, bias, flat):
    m = pl.program_id(0)
    tokens = x_ref.shape[0]
    rows = tokens // SEG
    length = len_ref[0]
    tile = 256

    @pl.when(m == 0)
    def _():
        for c in range(tokens // tile):
            here = pl.ds(c * tile, tile)
            normed, _ = norm_parts(x_ref[here, :])
            split_lanes(flat, here, normed * gain_ref[...])

        def emit(start, l, piece):
            b_rows[pl.ds(start, rows), pl.ds(l * LANES, LANES)] = low(piece)

        reorder(flat, SEG, emit)

    wide = PAIR * HEAD
    qkv = dot(b_rows[...], w_ref[0, :, : 3 * wide])
    lane = lax.broadcasted_iota(jnp.int32, (tokens, LANES), 1)
    at = lax.broadcasted_iota(jnp.int32, (tokens, LANES), 0)
    hidden = jnp.where(at < length, 0.0, MASKED)
    for head in range(PAIR):
        cols = pl.ds(head * LANES, LANES)

        def mine(piece):
            return piece if head == 0 else pltpu.roll(piece, HEAD, axis=1)

        q = low(mine(qkv[:, :wide])).astype(F32) * (HEAD**-0.5)
        k = mine(qkv[:, wide : 2 * wide])
        v = mine(qkv[:, 2 * wide :])
        q_ref[0, :, cols] = low(jnp.where(lane < HEAD, q, jnp.where(lane == HEAD, 1.0, 0.0)))
        k_ref[0, :, cols] = low(jnp.where(lane < HEAD, k, jnp.where(lane == HEAD, hidden, jnp.where(lane <= HEAD + 2, -1.0, 0.0))))
        v_ref[0, :, cols] = low(jnp.where(lane < HEAD, v, jnp.where(lane <= HEAD + 1, 1.0, 0.0)))
        span = table_ref.shape[2]
        line = jnp.broadcast_to(table_ref[0, head : head + 1, :], (LANES, span))
        bias[...] = pltpu.roll(line, span - LANES, axis=1, stride=1, stride_axis=0)
        for t in range(tokens // tile):
            here = pl.ds(t * tile, tile)
            scores = dot_nt(q_ref[0, here, cols], k_ref[0, :, cols])
            parts = []
            for sub in range(tile // LANES):
                first = tokens - LANES - t * tile - sub * LANES
                parts.append(scores[sub * LANES : (sub + 1) * LANES] + bias[:, pl.ds(first, tokens)])
            scores = jnp.concatenate(parts, axis=0)
            peak = jnp.max(scores, axis=-1, keepdims=True)
            expos = low(jnp.exp(scores - peak))
            out = dot(expos, v_ref[0, :, cols])
            denom = out[:, HEAD : HEAD + 1]
            out = out * (1.0 / denom)
            lse = peak + jnp.log(denom)
            if head == 0:
                o_ref[0, here, :] = low(out)
            else:
                lane_t = lax.broadcasted_iota(jnp.int32, (tile, LANES), 1)
                o_ref[0, here, :] = low(jnp.where(lane_t < HEAD, o_ref[0, here, :].astype(F32), pltpu.roll(out, HEAD, axis=1)))
            lse_ref[here, :] = jnp.broadcast_to(lse, (tile, LANES))
        lse = lse_ref[...]
        lse_high = low(lse).astype(F32)
        q_now = q_ref[0, :, cols].astype(F32)
        q_ref[0, :, cols] = low(jnp.where(lane == HEAD + 1, lse_high, jnp.where(lane == HEAD + 2, lse - lse_high, q_now)))
    part = dot_nt(o_ref[0], w_ref[0, :, 3 * wide :])

    @pl.when(m == 0)
    def _():
        total[...] = part

    @pl.when(m != 0)
    def _():
        total[...] += part

    @pl.when(m == pl.num_programs(0) - 1)
    def _():
        split_lanes(flat, pl.ds(0, tokens), total[...])

        def emit(start, l, piece):
            att_ref[pl.ds(start, SEG), pl.ds(l * LANES, LANES)] = low(piece * rows_keep(start, SEG, tokens, length))

        reorder(flat, rows, emit)


def attention_forward(length, x, gain, w, table):
    tokens, depth = x.shape
    blocks = w.shape[0]
    full = pl.BlockSpec((tokens, depth), lambda i: (0, 0))
    heads = pl.BlockSpec((1, tokens, PAIR * LANES), lambda i: (i, 0, 0))
    pair = pl.BlockSpec((1, tokens, LANES), lambda i: (i, 0, 0))
    heads_shape = jax.ShapeDtypeStruct((blocks, tokens, PAIR * LANES), BF16)
    return pl.pallas_call(
        attention_forward_kernel,
        grid=(blocks,),
        in_specs=[
            pl.BlockSpec(memory_space=pltpu.SMEM),
            full,
            pl.BlockSpec((1, depth), lambda i: (0, 0)),
            pl.BlockSpec((1, depth, w.shape[2]), lambda i: (i, 0, 0)),
            pl.BlockSpec((1, PAIR, table.shape[2]), lambda i: (i, 0, 0)),
        ],
        out_specs=[full, heads, heads, heads, pair],
        out_shape=[
            jax.ShapeDtypeStruct((tokens, depth), BF16),
            heads_shape,
            heads_shape,
            heads_shape,
            jax.ShapeDtypeStruct((blocks, tokens, LANES), BF16),
        ],
        scratch_shapes=[
            pltpu.VMEM((tokens, LANES), F32),
            pltpu.VMEM((tokens, depth), BF16),
            pltpu.VMEM((tokens, depth), F32),
            pltpu.VMEM((LANES, table.shape[2]), F32),
            pltpu.VMEM((depth // LANES, tokens, LANES), F32),
        ],
        compiler_params=pltpu.CompilerParams(vmem_limit_bytes=56 * 2**20),
    )(length, x, gain, w, table)


def attention_backward_kernel(
    datt_ref, x_ref, gain_ref, res_ref, w_ref, table_ref, q_ref, k_ref, v_ref, o_ref,
    dx_ref, dw_ref, dgain_ref, dtable_ref,
    b_t, g_t, g_rows, flat, bias, dbias, do_aug, d_pair, dq_t, k_t, d_rows, db,
):
    m = pl.program_id(0)
    tokens = x_ref.shape[0]
    rows = tokens // SEG
    wide = PAIR * HEAD
    tile = 256
    span = table_ref.shape[2]
    stored = tokens // tile

    @pl.when(m == 0)
    def _():
        def emit(start, l, piece):
            g_rows[pl.ds(start, rows), pl.ds(l * LANES, LANES)] = low(piece)

        for c in range(tokens // tile):
            here = pl.ds(c * tile, tile)
            normed, _ = norm_parts(x_ref[here, :])
            split_lanes(flat, here, normed * gain_ref[...])
        reorder(flat, SEG, emit)
        b_t[...] = g_rows[...].T
        split_lanes(flat, pl.ds(0, tokens), datt_ref[...].astype(F32))
        reorder(flat, SEG, emit)
        g_t[...] = g_rows[...].T

    w_out = w_ref[0, :, 3 * wide :]
    do = low(dot(g_rows[...], w_out))
    dw_ref[0, :, 3 * wide :] = low(dot(g_t[...], o_ref[0]))
    lane = lax.broadcasted_iota(jnp.int32, (tokens, LANES), 1)
    do_full = do.astype(F32)
    product = do_full * o_ref[0].astype(F32)
    for head in range(PAIR):
        cols = pl.ds(head * LANES, LANES)
        inside = lane < HEAD if head == 0 else lane >= HEAD
        delta = jnp.sum(jnp.where(inside, product, 0.0), axis=-1, keepdims=True)
        delta_high = low(delta).astype(F32)
        mine = do_full if head == 0 else pltpu.roll(do_full, HEAD, axis=1)
        do_aug[...] = low(jnp.where(lane < HEAD, mine, jnp.where(lane == HEAD, -delta_high, jnp.where(lane == HEAD + 1, delta_high - delta, 0.0))))
        k_t[...] = k_ref[0, :, cols].T
        line = jnp.broadcast_to(table_ref[0, head : head + 1, :], (LANES, span))
        bias[...] = pltpu.roll(line, span - (LANES - 1), axis=1, stride=1, stride_axis=0)
        dbias[...] = jnp.zeros_like(dbias)
        for t in range(stored):
            here = pl.ds(t * tile, tile)
            scores = dot_nt(k_ref[0, here, cols], q_ref[0, :, cols])
            grads = dot_nt(v_ref[0, here, cols], do_aug[...])
            p_parts = []
            d_parts = []
            for sub in range(tile // LANES):
                first = tokens - LANES - t * tile - sub * LANES
                now = slice(sub * LANES, (sub + 1) * LANES)
                p = jnp.exp(scores[now] + bias[:, pl.ds(first, tokens)])
                ds = low(p * grads[now])
                dbias[:, pl.ds(first, tokens)] += ds.astype(F32)
                p_parts.append(low(p))
                d_parts.append(ds)
            p = jnp.concatenate(p_parts, axis=0)
            ds = jnp.concatenate(d_parts, axis=0)
            dv = dot(p, do_aug[...])
            dk = dot(ds, q_ref[0, :, cols])
            dq = dot(k_t[:, here], ds)
            if t == 0:
                dq_t[...] = dq
            else:
                dq_t[...] += dq
            if head == 0:
                d_pair[1, here, :] = dk
                d_pair[2, here, :] = dv
            else:
                lane_t = lax.broadcasted_iota(jnp.int32, (tile, LANES), 1)
                d_pair[1, here, :] = jnp.where(lane_t < HEAD, d_pair[1, here, :], pltpu.roll(dk, HEAD, axis=1))
                d_pair[2, here, :] = jnp.where(lane_t < HEAD, d_pair[2, here, :], pltpu.roll(dv, HEAD, axis=1))
        dq = dq_t[...].T * (HEAD**-0.5)
        if head == 0:
            d_pair[0] = dq
        else:
            d_pair[0] = jnp.where(lane < HEAD, d_pair[0], pltpu.roll(dq, HEAD, axis=1))
        folded = dbias[...]
        count = LANES
        while count > 1:
            count //= 2
            folded = folded[:count] + pltpu.roll(folded[count:], span - count, axis=1)
        dtable_ref[0, head : head + 1, :] = pltpu.roll(folded, LANES - 1, axis=1)
    for part in range(3):
        d_rows[:, pl.ds(part * wide, wide)] = low(d_pair[part])
    dw_ref[0, :, : 3 * wide] = low(dot(b_t[...], d_rows[...]))
    part = dot_nt(d_rows[...], w_ref[0, :, : 3 * wide])

    @pl.when(m == 0)
    def _():
        db[...] = part

    @pl.when(m != 0)
    def _():
        db[...] += part

    @pl.when(m == pl.num_programs(0) - 1)
    def _():
        dgain_ref[...] = jnp.zeros_like(dgain_ref)
        split_lanes(flat, pl.ds(0, tokens), db[...])

        def emit(start, l, piece):
            db[pl.ds(start, SEG), pl.ds(l * LANES, LANES)] = piece

        reorder(flat, rows, emit)
        for c in range(tokens // tile):
            here = pl.ds(c * tile, tile)
            normed, rstd = norm_parts(x_ref[here, :])
            d = db[here, :]
            dgain_ref[...] += jnp.sum(d * normed, axis=0, keepdims=True)
            dx_ref[here, :] = res_ref[here, :] + norm_back(normed, rstd, gain_ref[...], d)


def attention_backward(datt, x, gain, res, w, table_back, q, k, v, o):
    tokens, depth = x.shape
    blocks = w.shape[0]
    span = table_back.shape[2]
    full = pl.BlockSpec((tokens, depth), lambda i: (0, 0))
    heads = pl.BlockSpec((1, tokens, PAIR * LANES), lambda i: (i, 0, 0))
    pair = pl.BlockSpec((1, tokens, LANES), lambda i: (i, 0, 0))
    vec = pl.BlockSpec((1, depth), lambda i: (0, 0))
    w_spec = pl.BlockSpec((1, depth, w.shape[2]), lambda i: (i, 0, 0))
    t_spec = pl.BlockSpec((1, PAIR, span), lambda i: (i, 0, 0))
    wide = PAIR * HEAD
    return pl.pallas_call(
        attention_backward_kernel,
        grid=(blocks,),
        in_specs=[full, full, vec, full, w_spec, t_spec, heads, heads, heads, pair],
        out_specs=[full, w_spec, vec, t_spec],
        out_shape=[
            jax.ShapeDtypeStruct((tokens, depth), F32),
            jax.ShapeDtypeStruct(w.shape, BF16),
            jax.ShapeDtypeStruct((1, depth), F32),
            jax.ShapeDtypeStruct(table_back.shape, F32),
        ],
        scratch_shapes=[
            pltpu.VMEM((depth, tokens), BF16),
            pltpu.VMEM((depth, tokens), BF16),
            pltpu.VMEM((tokens, depth), BF16),
            pltpu.VMEM((depth // LANES, tokens, LANES), F32),
            pltpu.VMEM((LANES, span), F32),
            pltpu.VMEM((LANES, span), F32),
            pltpu.VMEM((tokens, LANES), BF16),
            pltpu.VMEM((3, tokens, LANES), F32),
            pltpu.VMEM((LANES, tokens), F32),
            pltpu.VMEM((LANES, tokens), BF16),
            pltpu.VMEM((tokens, 3 * wide), BF16),
            pltpu.VMEM((tokens, depth), F32),
        ],
        compiler_params=pltpu.CompilerParams(vmem_limit_bytes=56 * 2**20),
    )(datt, x, gain, res, w, table_back, q, k, v, o)


def gate_forward_kernel(
    taps, len_ref, x_ref, gain_ref, w_in_ref, w_out_ref, g_gain_ref, g_conv_ref,
    cg_ref, zr_ref, zg_ref, mean_ref, rstd_ref, conv_ref, gate_ref,
    c_rows, ur_all, ug_all, first, second, total, padded,
):
    i = pl.program_id(0)
    blocks = pl.num_programs(0) // 2
    tokens = x_ref.shape[0]
    rows = tokens // SEG
    width = zr_ref.shape[2]
    tile = 256
    channels = width * blocks
    length = len_ref[0]

    @pl.when(i == 0)
    def _():
        for c in range(tokens // tile):
            here = pl.ds(c * tile, tile)
            normed, _ = norm_parts(x_ref[here, :])
            c_rows[here, :] = low(normed * gain_ref[...])
        first[...] = jnp.zeros_like(first)
        second[...] = jnp.zeros_like(second)

    @pl.when(i < blocks)
    def _():
        for c in range(tokens // tile):
            here = pl.ds(c * tile, tile)
            z = dot(c_rows[here, :], w_in_ref[0])
            zr = z[:, :width]
            zg = z[:, width:]
            zr_ref[0, here, :] = low(zr)
            zg_ref[0, here, :] = low(zg)
            ur_all[i, here, :] = low(gelu(zr))
            ug = gelu(zg)
            ug_all[i, here, :] = low(ug)
            square = ug * ug
            one = ug[:, :LANES]
            two = square[:, :LANES]
            for l in range(1, width // LANES):
                one = one + ug[:, l * LANES : (l + 1) * LANES]
                two = two + square[:, l * LANES : (l + 1) * LANES]
            first[here, :] += one
            second[here, :] += two

    @pl.when(i == blocks - 1)
    def _():
        for c in range(tokens // tile):
            here = pl.ds(c * tile, tile)
            mean = jnp.sum(first[here, :], axis=-1, keepdims=True) / channels
            spread = jnp.sum(second[here, :], axis=-1, keepdims=True) / channels - mean * mean
            mean_ref[here, :] = jnp.broadcast_to(mean, (tile, LANES))
            rstd_ref[here, :] = jnp.broadcast_to(lax.rsqrt(spread + EPSILON), (tile, LANES))

    @pl.when(i >= blocks)
    def _():
        m = i - blocks
        keep = rows_keep(0, tokens, tokens, length)
        scale = rstd_ref[...] * keep
        shift = mean_ref[...] * scale
        for l in range(width // LANES):
            cols = pl.ds(l * LANES, LANES)
            ug = ug_all[m, :, cols].astype(F32)
            n = low((ug * scale - shift) * g_gain_ref[0, :, cols])
            fill_padded(padded, n.reshape(rows, SEG, LANES), taps)

            def taps_of(k):
                return low(jnp.broadcast_to(g_conv_ref[0, k : k + 1, cols], (SEG, LANES)))[None]

            def emit(start, value):
                block = value.shape[0]
                here = pl.ds(pl.multiple_of(start * SEG, block * SEG), block * SEG)
                flat = value.reshape(block * SEG, LANES)
                conv_ref[0, here, cols] = low(flat)
                gate_ref[0, here, cols] = low(ur_all[m, here, cols].astype(F32) * flat)

            convolve(padded, taps_of, taps, rows, 16, emit)
        part = dot_nt(gate_ref[0], w_out_ref[0])

        @pl.when(m == 0)
        def _():
            total[...] = part

        @pl.when(m != 0)
        def _():
            total[...] += part

        @pl.when(m == blocks - 1)
        def _():
            cg_ref[...] = low(total[...] * keep)


def gate_forward(length, x, gain, w, g_gain, g_conv, taps):
    tokens, depth = x.shape
    blocks = w.shape[0]
    width = w.shape[2] // 3
    full = pl.BlockSpec((tokens, depth), lambda i: (0, 0))
    lanes = pl.BlockSpec((tokens, LANES), lambda i: (0, 0))

    def early(i):
        return jnp.minimum(i, blocks - 1)

    def late(i):
        return jnp.maximum(i - blocks, 0)

    z_early = pl.BlockSpec((1, tokens, width), lambda i: (early(i), 0, 0))
    z_late = pl.BlockSpec((1, tokens, width), lambda i: (late(i), 0, 0))
    z_shape = jax.ShapeDtypeStruct((blocks, tokens, width), BF16)
    lane_shape = jax.ShapeDtypeStruct((tokens, LANES), F32)
    return pl.pallas_call(
        functools.partial(gate_forward_kernel, taps),
        grid=(2 * blocks,),
        in_specs=[
            pl.BlockSpec(memory_space=pltpu.SMEM),
            full,
            pl.BlockSpec((1, depth), lambda i: (0, 0)),
            pl.BlockSpec((1, depth, 2 * width), lambda i: (early(i), 0, 0)),
            pl.BlockSpec((1, depth, width), lambda i: (late(i), 0, 2)),
            pl.BlockSpec((1, 1, width), lambda i: (late(i), 0, 0)),
            pl.BlockSpec((1, taps, width), lambda i: (late(i), 0, 0)),
        ],
        out_specs=[full, z_early, z_early, lanes, lanes, z_late, z_late],
        out_shape=[jax.ShapeDtypeStruct((tokens, depth), BF16), z_shape, z_shape, lane_shape, lane_shape, z_shape, z_shape],
        scratch_shapes=[
            pltpu.VMEM((tokens, depth), BF16),
            pltpu.VMEM((blocks, tokens, width), BF16),
            pltpu.VMEM((blocks, tokens, width), BF16),
            pltpu.VMEM((tokens, LANES), F32),
            pltpu.VMEM((tokens, LANES), F32),
            pltpu.VMEM((tokens, depth), F32),
            pltpu.VMEM((tokens // SEG + taps - 1, SEG, LANES), BF16),
        ],
        compiler_params=pltpu.CompilerParams(vmem_limit_bytes=60 * 2**20),
    )(length, x, gain, w, w, g_gain, g_conv)


def gate_backward_kernel(
    taps, len_ref, dcg_ref, x_ref, gain_ref, res_ref, w_ref, zr_ref, zg_ref, conv_ref, gate_ref, mean_ref, rstd_ref, g_gain_ref, g_conv_ref,
    dx_ref, dwr_ref, dwg_ref, dwo_ref, dgain_ref, dg_gain_ref, dg_conv_ref,
    c_rows, c_t, g_t, ug_all, slope_all, dn_all, first, second, dc, padded, n_padded, d_rows, dconv, sums,
):
    i = pl.program_id(0)
    blocks = pl.num_programs(0) // 2
    tokens = x_ref.shape[0]
    rows = tokens // SEG
    width = zr_ref.shape[2]
    tile = 256
    channels = width * blocks
    length = len_ref[0]
    chunks = tokens // tile

    @pl.when(i == 0)
    def _():
        for c in range(chunks):
            here = pl.ds(c * tile, tile)
            normed, _ = norm_parts(x_ref[here, :])
            c_rows[here, :] = low(normed * gain_ref[...])
        c_t[...] = c_rows[...].T
        g_t[...] = dcg_ref[...].T
        first[...] = jnp.zeros_like(first)
        second[...] = jnp.zeros_like(second)
        dc[...] = jnp.zeros_like(dc)

    @pl.when(i < blocks)
    def _():
        m = i
        for c in range(chunks):
            here = pl.ds(c * tile, tile)
            dgate = dot(dcg_ref[here, :], w_ref[0, :, 2 * width :])
            ur, slope = gelu_and_slope(zr_ref[0, here, :].astype(F32))
            dzr = low(dgate * conv_ref[0, here, :].astype(F32) * slope)
            d_rows[here, :] = dzr
            dconv[here, :] = low(dgate * ur)
            dc[here, :] += dot_nt(dzr, w_ref[0, :, :width])
            ug, slope = gelu_and_slope(zg_ref[0, here, :].astype(F32))
            ug_all[m, here, :] = low(ug)
            slope_all[m, here, :] = low(slope)
        dwr_ref[0] = low(dot(c_t[...], d_rows[...]))
        dwo_ref[0] = low(dot(g_t[...], gate_ref[0]))
        keep = rows_keep(0, tokens, tokens, length)
        rstd = rstd_ref[...]
        shift = mean_ref[...] * rstd
        for l in range(width // LANES):
            cols = pl.ds(l * LANES, LANES)
            ug = ug_all[m, :, cols].astype(F32)
            n = low((ug * rstd - shift) * (g_gain_ref[0, :, cols] * keep))
            fill_padded(n_padded, n.reshape(rows, SEG, LANES), taps)
            d = dconv[:, cols].reshape(rows, SEG, LANES)
            fill_padded(padded, d, taps)
            tap_grads(n_padded, padded.at[pl.ds((taps - 1) // 2, rows)], sums, taps, rows, 8)
            dg_conv_ref[0, :, cols] = jnp.sum(sums[...], axis=1)
            dg_gain_ref[0, :, cols] = jnp.zeros((1, LANES), F32)

            def taps_of(k):
                return low(jnp.broadcast_to(g_conv_ref[0, taps - 1 - k : taps - k, cols], (SEG, LANES)))[None]

            def emit(start, value):
                block = value.shape[0]
                here = pl.ds(pl.multiple_of(start * SEG, block * SEG), block * SEG)
                dn = value.reshape(block * SEG, LANES) * rows_keep(start * SEG, block * SEG, tokens, length)
                normed = ug_all[m, here, cols].astype(F32) * rstd_ref[here, :] - mean_ref[here, :] * rstd_ref[here, :]
                product = dn * normed
                dg_gain_ref[0, :, cols] += jnp.sum(product, axis=0, keepdims=True)
                scaled = dn * g_gain_ref[0, :, cols]
                dn_all[m, here, cols] = low(scaled)
                first[here, :] += scaled
                second[here, :] += product * g_gain_ref[0, :, cols]

            convolve(padded, taps_of, taps, rows, 16, emit)

    @pl.when(i == blocks - 1)
    def _():
        for c in range(chunks):
            here = pl.ds(c * tile, tile)
            one = jnp.sum(first[here, :], axis=-1, keepdims=True) / channels
            two = jnp.sum(second[here, :], axis=-1, keepdims=True) / channels
            first[here, :] = jnp.broadcast_to(one, (tile, LANES))
            second[here, :] = jnp.broadcast_to(two, (tile, LANES))

    @pl.when(i >= blocks)
    def _():
        m = i - blocks
        for c in range(chunks):
            here = pl.ds(c * tile, tile)
            rstd = rstd_ref[here, :]
            shift = mean_ref[here, :] * rstd
            one = first[here, :]
            two = second[here, :]
            for l in range(width // LANES):
                cols = pl.ds(l * LANES, LANES)
                normed = ug_all[m, here, cols].astype(F32) * rstd - shift
                dug = rstd * (dn_all[m, here, cols].astype(F32) - one - normed * two)
                d_rows[here, cols] = low(dug * slope_all[m, here, cols].astype(F32))
            dc[here, :] += dot_nt(d_rows[here, :], w_ref[0, :, width : 2 * width])
        dwg_ref[0] = low(dot(c_t[...], d_rows[...]))

    @pl.when(i == 2 * blocks - 1)
    def _():
        dgain_ref[...] = jnp.zeros_like(dgain_ref)
        for c in range(chunks):
            here = pl.ds(c * tile, tile)
            normed, rstd = norm_parts(x_ref[here, :])
            d = dc[here, :]
            dgain_ref[...] += jnp.sum(d * normed, axis=0, keepdims=True)
            dx_ref[here, :] = res_ref[here, :] + norm_back(normed, rstd, gain_ref[...], d)


def gate_backward(length, dcg, x, gain, res, w, zr, zg, conv, gate, mean, rstd, g_gain, g_conv, taps):
    tokens, depth = x.shape
    blocks = w.shape[0]
    width = w.shape[2] // 3
    full = pl.BlockSpec((tokens, depth), lambda i: (0, 0))
    lanes = pl.BlockSpec((tokens, LANES), lambda i: (0, 0))
    vec = pl.BlockSpec((1, depth), lambda i: (0, 0))

    def early(i):
        return jnp.minimum(i, blocks - 1)

    def late(i):
        return jnp.maximum(i - blocks, 0)

    z_early = pl.BlockSpec((1, tokens, width), lambda i: (early(i), 0, 0))
    gain_spec = pl.BlockSpec((1, 1, width), lambda i: (early(i), 0, 0))
    conv_spec = pl.BlockSpec((1, taps, width), lambda i: (early(i), 0, 0))
    dw_shape = jax.ShapeDtypeStruct((blocks, depth, width), BF16)
    dw_early = pl.BlockSpec((1, depth, width), lambda i: (early(i), 0, 0))
    dw_late = pl.BlockSpec((1, depth, width), lambda i: (late(i), 0, 0))
    padded = (tokens // SEG + taps - 1, SEG, LANES)
    return pl.pallas_call(
        functools.partial(gate_backward_kernel, taps),
        grid=(2 * blocks,),
        in_specs=[
            pl.BlockSpec(memory_space=pltpu.SMEM),
            full,
            full,
            vec,
            full,
            pl.BlockSpec((1, depth, 3 * width), lambda i: (lax.rem(i, blocks), 0, 0)),
            z_early,
            z_early,
            z_early,
            z_early,
            lanes,
            lanes,
            gain_spec,
            conv_spec,
        ],
        out_specs=[full, dw_early, dw_late, dw_early, vec, gain_spec, conv_spec],
        out_shape=[
            jax.ShapeDtypeStruct((tokens, depth), F32),
            dw_shape,
            dw_shape,
            dw_shape,
            jax.ShapeDtypeStruct((1, depth), F32),
            jax.ShapeDtypeStruct(g_gain.shape, F32),
            jax.ShapeDtypeStruct(g_conv.shape, F32),
        ],
        scratch_shapes=[
            pltpu.VMEM((tokens, depth), BF16),
            pltpu.VMEM((depth, tokens), BF16),
            pltpu.VMEM((depth, tokens), BF16),
            pltpu.VMEM((blocks, tokens, width), BF16),
            pltpu.VMEM((blocks, tokens, width), BF16),
            pltpu.VMEM((blocks, tokens, width), BF16),
            pltpu.VMEM((tokens, LANES), F32),
            pltpu.VMEM((tokens, LANES), F32),
            pltpu.VMEM((tokens, depth), F32),
            pltpu.VMEM(padded, BF16),
            pltpu.VMEM(padded, BF16),
            pltpu.VMEM((tokens, width), BF16),
            pltpu.VMEM((tokens, width), BF16),
            pltpu.VMEM((taps, SEG, LANES), F32),
        ],
        compiler_params=pltpu.CompilerParams(vmem_limit_bytes=60 * 2**20),
    )(length, dcg, x, gain, res, w, zr, zg, conv, gate, mean, rstd, g_gain, g_conv)


def merge_forward_kernel(taps, x_ref, att_ref, cg_ref, w_ref, m_conv_ref, out_ref, merged_ref, padded):
    c = pl.program_id(0)
    tokens = x_ref.shape[0]
    rows = tokens // SEG
    half = pl.num_programs(0) // 2
    width = merged_ref.shape[1]
    for l in range(width // LANES):
        cols = pl.ds(l * LANES, LANES)

        @pl.when(c < half)
        def _():
            fill_padded(padded, att_ref[:, cols].reshape(rows, SEG, LANES), taps)

        @pl.when(c >= half)
        def _():
            fill_padded(padded, cg_ref[:, cols].reshape(rows, SEG, LANES), taps)

        def taps_of(k):
            return low(jnp.broadcast_to(m_conv_ref[k : k + 1, cols], (SEG, LANES)))[None]

        def emit(start, value):
            block = value.shape[0]
            here = pl.ds(pl.multiple_of(start * SEG, block * SEG), block * SEG)
            value = value + padded[pl.ds(start + (taps - 1) // 2, block)].astype(F32)
            merged_ref[here, cols] = low(value.reshape(block * SEG, LANES))

        convolve(padded, taps_of, taps, rows, 16, emit)
    w = jnp.concatenate([w_ref[m] for m in range(w_ref.shape[0])], axis=1)
    part = dot(merged_ref[...], w)

    @pl.when(c == 0)
    def _():
        out_ref[...] = x_ref[...] + part

    @pl.when(c != 0)
    def _():
        out_ref[...] += part


def merge_forward(x, att, cg, w, m_conv):
    tokens, depth = x.shape
    blocks, both, cols = w.shape
    taps = m_conv.shape[0]
    width = 256
    steps = both // width
    half = steps // 2
    full = pl.BlockSpec((tokens, depth), lambda i: (0, 0))
    return pl.pallas_call(
        functools.partial(merge_forward_kernel, taps),
        grid=(steps,),
        in_specs=[
            full,
            pl.BlockSpec((tokens, width), lambda i: (0, jnp.minimum(i, half - 1))),
            pl.BlockSpec((tokens, width), lambda i: (0, jnp.maximum(i - half, 0))),
            pl.BlockSpec((blocks, width, cols), lambda i: (0, i, 0)),
            pl.BlockSpec((taps, width), lambda i: (0, i)),
        ],
        out_specs=[full, pl.BlockSpec((tokens, width), lambda i: (0, i))],
        out_shape=[jax.ShapeDtypeStruct(x.shape, F32), jax.ShapeDtypeStruct((tokens, both), BF16)],
        scratch_shapes=[pltpu.VMEM((tokens // SEG + taps - 1, SEG, LANES), BF16)],
        compiler_params=pltpu.CompilerParams(vmem_limit_bytes=56 * 2**20),
    )(x, att, cg, w, m_conv)


def merge_backward_kernel(taps, len_ref, g_ref, att_ref, cg_ref, merged_ref, w_ref, m_conv_ref, datt_ref, dcg_ref, dw_ref, dconv_ref, g_rows, padded, j_padded, out, sums):
    c = pl.program_id(0)
    tokens = g_ref.shape[0]
    rows = tokens // SEG
    half = pl.num_programs(0) // 2
    blocks, width, narrow = w_ref.shape
    length = len_ref[0]

    @pl.when(c == 0)
    def _():
        g_rows[...] = low(g_ref[...])

    w = jnp.concatenate([w_ref[m] for m in range(blocks)], axis=1)
    dmerged = low(dot_nt(g_rows[...], w))
    dw = dot(merged_ref[...].T, g_rows[...])
    for m in range(blocks):
        dw_ref[m] = low(dw[:, m * narrow : (m + 1) * narrow])
    for l in range(width // LANES):
        cols = pl.ds(l * LANES, LANES)

        @pl.when(c < half)
        def _():
            fill_padded(j_padded, att_ref[:, cols].reshape(rows, SEG, LANES), taps)

        @pl.when(c >= half)
        def _():
            fill_padded(j_padded, cg_ref[:, cols].reshape(rows, SEG, LANES), taps)

        fill_padded(padded, dmerged[:, l * LANES : (l + 1) * LANES].reshape(rows, SEG, LANES), taps)
        tap_grads(j_padded, padded.at[pl.ds((taps - 1) // 2, rows)], sums, taps, rows, 8)
        dconv_ref[:, cols] = jnp.sum(sums[...], axis=1)

        def taps_of(k):
            return low(jnp.broadcast_to(m_conv_ref[taps - 1 - k : taps - k, cols], (SEG, LANES)))[None]

        def emit(start, value):
            block = value.shape[0]
            here = pl.ds(pl.multiple_of(start * SEG, block * SEG), block * SEG)
            value = value + padded[pl.ds(start + (taps - 1) // 2, block)].astype(F32)
            out[here, cols] = low(value.reshape(block * SEG, LANES) * rows_keep(start * SEG, block * SEG, tokens, length))

        convolve(padded, taps_of, taps, rows, 16, emit)

    @pl.when(c < half)
    def _():
        datt_ref[...] = out[...]

    @pl.when(c >= half)
    def _():
        dcg_ref[...] = out[...]


def merge_backward(length, g, att, cg, merged, w, m_conv):
    tokens, depth = g.shape
    blocks, both, cols = w.shape
    taps = m_conv.shape[0]
    width = 256
    steps = both // width
    half = steps // 2
    full = pl.BlockSpec((tokens, depth), lambda i: (0, 0))
    early = pl.BlockSpec((tokens, width), lambda i: (0, jnp.minimum(i, half - 1)))
    late = pl.BlockSpec((tokens, width), lambda i: (0, jnp.maximum(i - half, 0)))
    wide = pl.BlockSpec((tokens, width), lambda i: (0, i))
    w_spec = pl.BlockSpec((blocks, width, cols), lambda i: (0, i, 0))
    conv_spec = pl.BlockSpec((taps, width), lambda i: (0, i))
    padded = (tokens // SEG + taps - 1, SEG, LANES)
    return pl.pallas_call(
        functools.partial(merge_backward_kernel, taps),
        grid=(steps,),
        in_specs=[pl.BlockSpec(memory_space=pltpu.SMEM), full, early, late, wide, w_spec, conv_spec],
        out_specs=[early, late, w_spec, conv_spec],
        out_shape=[
            jax.ShapeDtypeStruct((tokens, depth), BF16),
            jax.ShapeDtypeStruct((tokens, depth), BF16),
            jax.ShapeDtypeStruct(w.shape, BF16),
            jax.ShapeDtypeStruct(m_conv.shape, F32),
        ],
        scratch_shapes=[
            pltpu.VMEM((tokens, depth), BF16),
            pltpu.VMEM(padded, BF16),
            pltpu.VMEM(padded, BF16),
            pltpu.VMEM((tokens, width), BF16),
            pltpu.VMEM((taps, SEG, LANES), F32),
        ],
        compiler_params=pltpu.CompilerParams(vmem_limit_bytes=56 * 2**20),
    )(length, g, att, cg, merged, w, m_conv)


def layer_forward(x, length, weights, small):
    g1, g2, g3, g4, g5 = weights
    gains, table, g_gain, g_conv, m_conv = small
    taps = m_conv.shape[0]
    x1, h1 = ffn_forward(x, gains[0:1], g1)
    att, q, k, v, o = attention_forward(length, x1, gains[1:2], g2, table)
    cg, zr, zg, mean, rstd, conv, gate = gate_forward(length, x1, gains[2:3], g3, g_gain, g_conv, taps)
    x2, merged = merge_forward(x1, att, cg, g4, m_conv)
    x3, h2, y = ffn_forward(x2, gains[3:4], g5, gains[4:5])
    saved = (x, x1, h1, att, q, k, v, o, cg, zr, zg, mean, rstd, conv, gate, x2, merged, x3, h2)
    return y, saved


def layer_backward(g, length, saved, weights, small):
    g1, g2, g3, g4, g5 = weights
    gains, table, g_gain, g_conv, m_conv = small
    taps = m_conv.shape[0]
    x, x1, h1, att, q, k, v, o, cg, zr, zg, mean, rstd, conv, gate, x2, merged, x3, h2 = saved
    dx2, dg5, dgain3, dgain4 = ffn_backward(g, x2, gains[3:4], h2, g5, gains[4:5], x3)
    datt, dcg, dg4, dm_conv = merge_backward(length, dx2, att, cg, merged, g4, m_conv)
    dx1, dwr, dwg, dwo, dgain2, dg_gain, dg_conv = gate_backward(
        length, dcg, x1, gains[2:3], dx2, g3, zr, zg, conv, gate, mean, rstd, g_gain, g_conv, taps
    )
    dx1, dg2, dgain1, dtable = attention_backward(datt, x1, gains[1:2], dx1, g2, table[:, :, ::-1], q, k, v, o)
    dx, dg1, dgain0 = ffn_backward(dx1, x, gains[0:1], h1, g1)
    dg3 = jnp.concatenate([dwr, dwg, dwo], axis=2)
    dgains = jnp.concatenate([dgain0, dgain1, dgain2, dgain3, dgain4], axis=0)
    return dx, (dg1, dg2, dg3, dg4, dg5), (dgains, dtable[:, :, ::-1], dg_gain, dg_conv, dm_conv)


def to_segments(values):
    tokens, depth = values.shape
    return values.reshape(SEG, tokens // SEG, depth).transpose(1, 0, 2).reshape(tokens, depth)


def from_segments(values):
    tokens, depth = values.shape
    return values.reshape(tokens // SEG, SEG, depth).transpose(1, 0, 2).reshape(tokens, depth)


def pack_layer(layer, ffn_in, ffn_out, attn_in, attn_out, cg_in, cg_out, merge_out, mp_index, mp_size):
    cols = merge_out.shape[2] // mp_size
    part = lax.dynamic_slice_in_dim(merge_out[layer], mp_index * cols, cols, axis=1)
    pieces = (
        jnp.concatenate([ffn_in[layer, 0], ffn_out[layer, 0].T], axis=1),
        jnp.concatenate([attn_in[layer, 0], attn_in[layer, 1], attn_in[layer, 2], attn_out[layer].T], axis=1),
        jnp.concatenate([cg_in[layer, 0], cg_in[layer, 1], cg_out[layer].T], axis=1),
        part,
        jnp.concatenate([ffn_in[layer, 1], ffn_out[layer, 1].T], axis=1),
    )
    return tuple(low(piece) for piece in pieces)


def body(frames, cotangent, lengths, norm_gains, ffn_in, ffn_out, attn_in, attn_out, rel_bias, cg_in, csgu_gain, csgu_conv, cg_out, merge_conv, merge_out):
    layers = norm_gains.shape[0]
    mp_size = lax.axis_size("mp")
    mp_index = lax.axis_index("mp")
    length = lax.dynamic_slice_in_dim(lengths, mp_index, 1)
    depth = frames.shape[1]
    tokens = frames.shape[0]
    taps = merge_conv.shape[1]

    table = lax.all_gather(rel_bias, "mp", axis=0)
    g_gain = lax.all_gather(csgu_gain, "mp", axis=0)
    g_conv = lax.all_gather(csgu_conv, "mp", axis=0)
    state = to_segments(frames).astype(F32)
    weights = []
    smalls = []
    saved = []
    for layer in range(layers):
        pieces = pack_layer(layer, ffn_in, ffn_out, attn_in, attn_out, cg_in, cg_out, merge_out, mp_index, mp_size)
        gathered = tuple(
            lax.all_gather(piece, ("mp", "dp"), axis=0, tiled=True).reshape(mp_size, -1, piece.shape[1]) for piece in pieces
        )
        weights.append(gathered)
        smalls.append((norm_gains[layer], table[:, layer], g_gain[:, layer][:, None], g_conv[:, layer], merge_conv[layer]))
        state, kept = layer_forward(state, length, gathered, smalls[layer])
        saved.append(kept)
    frame = lax.broadcasted_iota(jnp.int32, (tokens, 1), 0)
    keep = (frame < length).astype(F32)
    output_frames = from_segments(state) * keep
    incoming = to_segments(cotangent.astype(F32) * keep)
    big = [None] * layers
    tiny = [None] * layers
    for layer in reversed(range(layers)):
        incoming, grads, small = layer_backward(incoming, length, saved[layer], weights[layer], smalls[layer])
        big[layer] = tuple(
            lax.psum_scatter(grad.reshape(-1, grad.shape[2]), ("mp", "dp"), scatter_dimension=0, tiled=True).astype(F32) for grad in grads
        )
        tiny[layer] = small
    input_grad = from_segments(incoming)
    f = ffn_in.shape[3]
    h = attn_in.shape[3]
    c = cg_in.shape[3]
    one = [g[0] for g in big]
    two = [g[1] for g in big]
    three = [g[2] for g in big]
    four = [g[3] for g in big]
    five = [g[4] for g in big]
    grad_ffn_in = jnp.stack([jnp.stack([a[:, :f], b[:, :f]]) for a, b in zip(one, five)])
    grad_ffn_out = jnp.stack([jnp.stack([a[:, f:].T, b[:, f:].T]) for a, b in zip(one, five)])
    grad_attn_in = jnp.stack([jnp.stack([a[:, :h], a[:, h : 2 * h], a[:, 2 * h : 3 * h]]) for a in two])
    grad_attn_out = jnp.stack([a[:, 3 * h :].T for a in two])
    grad_cg_in = jnp.stack([jnp.stack([a[:, :c], a[:, c : 2 * c]]) for a in three])
    grad_cg_out = jnp.stack([a[:, 2 * c :].T for a in three])
    grad_merge = jnp.stack(four)
    grad_merge = lax.all_gather(grad_merge, "mp", axis=2, tiled=True)
    grad_gains = jnp.stack([t[0] for t in tiny])
    grad_m_conv = jnp.stack([t[4] for t in tiny])
    grad_table = jnp.stack([t[1] for t in tiny], axis=1)
    grad_g_gain = jnp.stack([t[2][:, 0] for t in tiny], axis=1)
    grad_g_conv = jnp.stack([t[3] for t in tiny], axis=1)
    grad_gains, grad_m_conv, grad_table, grad_g_gain, grad_g_conv = lax.psum(
        (grad_gains, grad_m_conv, grad_table, grad_g_gain, grad_g_conv), ("dp", "mp")
    )
    grad_table = lax.dynamic_index_in_dim(grad_table, mp_index, 0, keepdims=False)
    grad_g_gain = lax.dynamic_index_in_dim(grad_g_gain, mp_index, 0, keepdims=False)
    grad_g_conv = lax.dynamic_index_in_dim(grad_g_conv, mp_index, 0, keepdims=False)
    return (
        output_frames,
        input_grad,
        grad_gains,
        grad_ffn_in,
        grad_ffn_out,
        grad_attn_in,
        grad_attn_out,
        grad_table,
        grad_cg_in,
        grad_g_gain,
        grad_g_conv,
        grad_cg_out,
        grad_m_conv,
        grad_merge,
    )


def solution(mesh):
    tokens = P(("dp", "mp"), None)
    columns = P(None, None, "dp", "mp")
    rows = P(None, "mp", "dp")
    ffn_rows = P(None, None, "mp", "dp")
    heads = P(None, "mp", None)
    taps = P(None, None, "mp")
    return jax.shard_map(
        body,
        mesh=mesh,
        in_specs=(tokens, tokens, P("dp"), P(), columns, ffn_rows, columns, rows, heads, columns, P(None, "mp"), taps, rows, P(), P(None, "dp", None)),
        out_specs=(tokens, tokens, P(), columns, ffn_rows, columns, rows, heads, columns, P(None, "mp"), taps, rows, P(), P(None, "dp", None)),
        check_vma=False,
    )
```

```python
import functools

import jax
import jax.numpy as jnp
from jax import lax
from jax.experimental import pallas as pl
from jax.experimental.pallas import tpu as pltpu
from jax.sharding import PartitionSpec as P

EPSILON = 1e-05
MASKED = -1000000000.0
F32 = jnp.float32
BF16 = jnp.bfloat16
SEG = 16
GELU_A = 0.7978845608028654
GELU_B = 0.044715


def dot(left, right):
    return lax.dot_general(left, right, (((1,), (0,)), ((), ())), preferred_element_type=F32)


def dot_nt(left, right):
    return lax.dot_general(left, right, (((1,), (1,)), ((), ())), preferred_element_type=F32)


def low(values):
    return values.astype(BF16)


def norm_parts(values):
    mean = jnp.mean(values, axis=-1, keepdims=True)
    centred = values - mean
    spread = jnp.mean(centred * centred, axis=-1, keepdims=True)
    rstd = lax.rsqrt(spread + EPSILON)
    return centred * rstd, rstd


def norm_back(normed, rstd, gain, grad):
    scaled = grad * gain
    first = jnp.mean(scaled, axis=-1, keepdims=True)
    second = jnp.mean(scaled * normed, axis=-1, keepdims=True)
    return rstd * (scaled - first - normed * second)


def gelu(values):
    half = 0.5 * values
    inner = values * (GELU_A + (GELU_A * GELU_B) * (values * values))
    return half + half * jnp.tanh(inner)


def gelu_and_slope(values):
    half = 0.5 * values
    square = values * values
    tanh = jnp.tanh(values * (GELU_A + (GELU_A * GELU_B) * square))
    value = half + half * tanh
    slope = 0.5 + 0.5 * tanh + (half - half * tanh * tanh) * (GELU_A + (3.0 * GELU_A * GELU_B) * square)
    return value, slope


def rows_keep(start, rows, frames, length):
    at = lax.broadcasted_iota(jnp.int32, (rows, 1), 0) + start
    frame = (at % SEG) * (frames // SEG) + at // SEG
    return (frame < length).astype(F32)


def fill_padded(padded, values, taps):
    rows, _, lanes = values.shape
    half = (taps - 1) // 2
    padded[pl.ds(half, rows)] = values
    place = lax.broadcasted_iota(jnp.int32, (half, SEG, lanes), 1)
    before = pltpu.roll(values[rows - half :].astype(F32), 1, axis=1)
    padded[pl.ds(0, half)] = low(jnp.where(place == 0, 0.0, before))
    after = pltpu.roll(values[:half].astype(F32), SEG - 1, axis=1)
    padded[pl.ds(half + rows, half)] = low(jnp.where(place == SEG - 1, 0.0, after))


def convolve(padded, taps_of, taps, rows, block, emit):
    weights = [taps_of(k) for k in range(taps)]

    def step(index, carry):
        start = index * block
        total = None
        for first in range(0, taps, 8):
            part = None
            for k in range(first, min(taps, first + 8)):
                term = weights[k] * padded[pl.ds(start + k, block)]
                part = term if part is None else part + term
            part = part.astype(F32)
            total = part if total is None else total + part
        emit(start, total)
        return carry

    lax.fori_loop(0, rows // block, step, 0)


def tap_grads(padded, grads, sums, taps, rows, block):
    sums[...] = jnp.zeros_like(sums)

    def step(index, carry):
        start = index * block
        here = grads[pl.ds(start, block)]
        for k in range(taps):
            term = here * padded[pl.ds(start + k, block)]
            count = block
            while count > 1:
                count //= 2
                term = term[:count] + term[count:]
            sums[k] += term[0].astype(F32)
        return carry

    lax.fori_loop(0, rows // block, step, 0)


def ffn_forward_kernel(final, blocks, x_ref, gain_ref, w_ref, *rest):
    if final:
        last_ref, out_ref, h_ref, y_ref = rest
    else:
        out_ref, h_ref = rest
    width = h_ref.shape[2]
    x = x_ref[...]
    normed, _ = norm_parts(x)
    a = low(normed * gain_ref[...])
    total = None
    for m in range(blocks):
        h = dot(a, w_ref[m, :, :width])
        h_ref[m] = low(h)
        half = 0.5 * h
        s = low(half + half * jnp.tanh(half))
        part = dot_nt(s, w_ref[m, :, width:])
        total = part if total is None else total + part
    out = x + 0.5 * total
    out_ref[...] = out
    if final:
        normed, _ = norm_parts(out)
        y_ref[...] = normed * last_ref[...]


def ffn_forward(x, gain, w, last=None):
    tokens, depth = x.shape
    blocks, _, width = w.shape
    width //= 2
    tile = min(256, tokens)
    row = pl.BlockSpec((tile, depth), lambda i: (i, 0))
    vec = pl.BlockSpec((1, depth), lambda i: (0, 0))
    out_shape = [jax.ShapeDtypeStruct(x.shape, F32), jax.ShapeDtypeStruct((blocks, tokens, width), BF16)]
    out_specs = [row, pl.BlockSpec((blocks, tile, width), lambda i: (0, i, 0))]
    in_specs = [row, vec, pl.BlockSpec(w.shape, lambda i: (0, 0, 0))]
    args = [x, gain, w]
    if last is not None:
        in_specs.append(vec)
        args.append(last)
        out_shape.append(jax.ShapeDtypeStruct(x.shape, F32))
        out_specs.append(row)
    return pl.pallas_call(
        functools.partial(ffn_forward_kernel, last is not None, blocks),
        grid=(tokens // tile,),
        in_specs=in_specs,
        out_specs=out_specs,
        out_shape=out_shape,
        compiler_params=pltpu.CompilerParams(vmem_limit_bytes=56 * 2**20),
    )(*args)


def ffn_backward_kernel(final, tile, g_ref, x_ref, gain_ref, h_ref, w_ref, *rest):
    if final:
        last_ref, y_ref, dx_ref, dw_ref, dgain_ref, dlast_ref, grad, at, gt, a_rows, g_rows, s_rows, d_rows, da = rest
    else:
        dx_ref, dw_ref, dgain_ref, grad, at, gt, a_rows, g_rows, s_rows, d_rows, da = rest
    m = pl.program_id(0)
    tokens = x_ref.shape[0]
    width = h_ref.shape[2]
    chunks = tokens // tile

    @pl.when(m == 0)
    def _():
        if final:
            dlast_ref[...] = jnp.zeros_like(dlast_ref)
        for c in range(chunks):
            here = pl.ds(c * tile, tile)
            g = g_ref[here, :]
            if final:
                normed, rstd = norm_parts(y_ref[here, :])
                dlast_ref[...] += jnp.sum(g * normed, axis=0, keepdims=True)
                g = norm_back(normed, rstd, last_ref[...], g)
                grad[here, :] = g
            g_low = low(0.5 * g)
            g_rows[here, :] = g_low
            normed, _ = norm_parts(x_ref[here, :])
            a_rows[here, :] = low(normed * gain_ref[...])
        at[...] = a_rows[...].T
        gt[...] = g_rows[...].T

    w_in = w_ref[0, :, :width]
    w_out = w_ref[0, :, width:]
    for c in range(chunks):
        here = pl.ds(c * tile, tile)
        ds = dot(g_rows[here, :], w_out)
        h = h_ref[0, here, :].astype(F32)
        half = 0.5 * h
        tanh = jnp.tanh(half)
        s = half + half * tanh
        s_rows[here, :] = low(s)
        sig = 0.5 + 0.5 * tanh
        dh = low(ds * (sig + s * (1.0 - sig)))
        d_rows[here, :] = dh
        part = dot_nt(dh, w_in)

        @pl.when(m == 0)
        def _():
            da[here, :] = part

        @pl.when(m != 0)
        def _():
            da[here, :] += part

    dw_ref[0, :, :width] = low(dot(at[...], d_rows[...]))
    dw_ref[0, :, width:] = low(dot(gt[...], s_rows[...]))

    @pl.when(m == pl.num_programs(0) - 1)
    def _():
        dgain_ref[...] = jnp.zeros_like(dgain_ref)
        for c in range(chunks):
            here = pl.ds(c * tile, tile)
            normed, rstd = norm_parts(x_ref[here, :])
            d = da[here, :]
            dgain_ref[...] += jnp.sum(d * normed, axis=0, keepdims=True)
            base = grad[here, :] if final else g_ref[here, :]
            dx_ref[here, :] = base + norm_back(normed, rstd, gain_ref[...], d)


def ffn_backward(g, x, gain, h, w, last=None, final_in=None):
    tokens, depth = x.shape
    blocks, _, width = w.shape
    width //= 2
    tile = min(256, tokens)
    full = pl.BlockSpec((tokens, depth), lambda i: (0, 0))
    vec = pl.BlockSpec((1, depth), lambda i: (0, 0))
    vec_shape = jax.ShapeDtypeStruct((1, depth), F32)
    in_specs = [full, full, vec, pl.BlockSpec((1, tokens, width), lambda i: (i, 0, 0)), pl.BlockSpec((1, depth, 2 * width), lambda i: (i, 0, 0))]
    args = [g, x, gain, h, w]
    out_specs = [full, pl.BlockSpec((1, depth, 2 * width), lambda i: (i, 0, 0)), vec]
    out_shape = [jax.ShapeDtypeStruct(x.shape, F32), jax.ShapeDtypeStruct(w.shape, BF16), vec_shape]
    if last is not None:
        in_specs += [vec, full]
        args += [last, final_in]
        out_specs.append(vec)
        out_shape.append(vec_shape)
    return pl.pallas_call(
        functools.partial(ffn_backward_kernel, last is not None, tile),
        grid=(blocks,),
        in_specs=in_specs,
        out_specs=out_specs,
        out_shape=out_shape,
        scratch_shapes=[
            pltpu.VMEM((tokens, depth) if last is not None else (8, 128), F32),
            pltpu.VMEM((depth, tokens), BF16),
            pltpu.VMEM((depth, tokens), BF16),
            pltpu.VMEM((tokens, depth), BF16),
            pltpu.VMEM((tokens, depth), BF16),
            pltpu.VMEM((tokens, width), BF16),
            pltpu.VMEM((tokens, width), BF16),
            pltpu.VMEM((tokens, depth), F32),
        ],
        compiler_params=pltpu.CompilerParams(vmem_limit_bytes=56 * 2**20),
    )(*args)


HEAD = 64
PAIR = 2
LANES = 128


def split_lanes(lanes_ref, here, values):
    for l in range(values.shape[1] // LANES):
        lanes_ref[l, here, :] = values[:, l * LANES : (l + 1) * LANES]


def reorder(lanes_ref, stride, emit):
    blocks, tokens, _ = lanes_ref.shape
    count = tokens // stride
    for start in range(stride):
        for l in range(blocks):
            emit(start * count, l, lanes_ref[l, pl.ds(start, count, stride=stride), :])


def attention_forward_kernel(len_ref, x_ref, gain_ref, w_ref, table_ref, att_ref, q_ref, k_ref, v_ref, o_ref, lse_ref, b_rows, total, bias, flat):
    m = pl.program_id(0)
    tokens = x_ref.shape[0]
    rows = tokens // SEG
    length = len_ref[0]
    tile = 256

    @pl.when(m == 0)
    def _():
        for c in range(tokens // tile):
            here = pl.ds(c * tile, tile)
            normed, _ = norm_parts(x_ref[here, :])
            split_lanes(flat, here, normed * gain_ref[...])

        def emit(start, l, piece):
            b_rows[pl.ds(start, rows), pl.ds(l * LANES, LANES)] = low(piece)

        reorder(flat, SEG, emit)

    wide = PAIR * HEAD
    qkv = dot(b_rows[...], w_ref[0, :, : 3 * wide])
    lane = lax.broadcasted_iota(jnp.int32, (tokens, LANES), 1)
    at = lax.broadcasted_iota(jnp.int32, (tokens, LANES), 0)
    hidden = jnp.where(at < length, 0.0, MASKED)
    for head in range(PAIR):
        cols = pl.ds(head * LANES, LANES)

        def mine(piece):
            return piece if head == 0 else pltpu.roll(piece, HEAD, axis=1)

        q = low(mine(qkv[:, :wide])).astype(F32) * (HEAD**-0.5)
        k = mine(qkv[:, wide : 2 * wide])
        v = mine(qkv[:, 2 * wide :])
        q_ref[0, :, cols] = low(jnp.where(lane < HEAD, q, jnp.where(lane == HEAD, 1.0, 0.0)))
        k_ref[0, :, cols] = low(jnp.where(lane < HEAD, k, jnp.where(lane == HEAD, hidden, jnp.where(lane <= HEAD + 2, -1.0, 0.0))))
        v_ref[0, :, cols] = low(jnp.where(lane < HEAD, v, jnp.where(lane <= HEAD + 1, 1.0, 0.0)))
        span = table_ref.shape[2]
        line = jnp.broadcast_to(table_ref[0, head : head + 1, :], (LANES, span))
        bias[...] = pltpu.roll(line, span - LANES, axis=1, stride=1, stride_axis=0)
        for t in range(tokens // tile):
            here = pl.ds(t * tile, tile)
            scores = dot_nt(q_ref[0, here, cols], k_ref[0, :, cols])
            parts = []
            for sub in range(tile // LANES):
                first = tokens - LANES - t * tile - sub * LANES
                parts.append(scores[sub * LANES : (sub + 1) * LANES] + bias[:, pl.ds(first, tokens)])
            scores = jnp.concatenate(parts, axis=0)
            peak = jnp.max(scores, axis=-1, keepdims=True)
            expos = low(jnp.exp(scores - peak))
            out = dot(expos, v_ref[0, :, cols])
            denom = out[:, HEAD : HEAD + 1]
            out = out * (1.0 / denom)
            lse = peak + jnp.log(denom)
            if head == 0:
                o_ref[0, here, :] = low(out)
            else:
                lane_t = lax.broadcasted_iota(jnp.int32, (tile, LANES), 1)
                o_ref[0, here, :] = low(jnp.where(lane_t < HEAD, o_ref[0, here, :].astype(F32), pltpu.roll(out, HEAD, axis=1)))
            lse_ref[here, :] = jnp.broadcast_to(lse, (tile, LANES))
        lse = lse_ref[...]
        lse_high = low(lse).astype(F32)
        q_now = q_ref[0, :, cols].astype(F32)
        q_ref[0, :, cols] = low(jnp.where(lane == HEAD + 1, lse_high, jnp.where(lane == HEAD + 2, lse - lse_high, q_now)))
    part = dot_nt(o_ref[0], w_ref[0, :, 3 * wide :])

    @pl.when(m == 0)
    def _():
        total[...] = part

    @pl.when(m != 0)
    def _():
        total[...] += part

    @pl.when(m == pl.num_programs(0) - 1)
    def _():
        split_lanes(flat, pl.ds(0, tokens), total[...])

        def emit(start, l, piece):
            att_ref[pl.ds(start, SEG), pl.ds(l * LANES, LANES)] = low(piece * rows_keep(start, SEG, tokens, length))

        reorder(flat, rows, emit)


def attention_forward(length, x, gain, w, table):
    tokens, depth = x.shape
    blocks = w.shape[0]
    full = pl.BlockSpec((tokens, depth), lambda i: (0, 0))
    heads = pl.BlockSpec((1, tokens, PAIR * LANES), lambda i: (i, 0, 0))
    pair = pl.BlockSpec((1, tokens, LANES), lambda i: (i, 0, 0))
    heads_shape = jax.ShapeDtypeStruct((blocks, tokens, PAIR * LANES), BF16)
    return pl.pallas_call(
        attention_forward_kernel,
        grid=(blocks,),
        in_specs=[
            pl.BlockSpec(memory_space=pltpu.SMEM),
            full,
            pl.BlockSpec((1, depth), lambda i: (0, 0)),
            pl.BlockSpec((1, depth, w.shape[2]), lambda i: (i, 0, 0)),
            pl.BlockSpec((1, PAIR, table.shape[2]), lambda i: (i, 0, 0)),
        ],
        out_specs=[full, heads, heads, heads, pair],
        out_shape=[
            jax.ShapeDtypeStruct((tokens, depth), BF16),
            heads_shape,
            heads_shape,
            heads_shape,
            jax.ShapeDtypeStruct((blocks, tokens, LANES), BF16),
        ],
        scratch_shapes=[
            pltpu.VMEM((tokens, LANES), F32),
            pltpu.VMEM((tokens, depth), BF16),
            pltpu.VMEM((tokens, depth), F32),
            pltpu.VMEM((LANES, table.shape[2]), F32),
            pltpu.VMEM((depth // LANES, tokens, LANES), F32),
        ],
        compiler_params=pltpu.CompilerParams(vmem_limit_bytes=56 * 2**20),
    )(length, x, gain, w, table)


def attention_backward_kernel(
    datt_ref, x_ref, gain_ref, res_ref, w_ref, table_ref, q_ref, k_ref, v_ref, o_ref,
    dx_ref, dw_ref, dgain_ref, dtable_ref,
    b_t, g_t, g_rows, flat, bias, dbias, do_aug, d_pair, dq_t, k_t, d_rows, db,
):
    m = pl.program_id(0)
    tokens = x_ref.shape[0]
    rows = tokens // SEG
    wide = PAIR * HEAD
    tile = 256
    span = table_ref.shape[2]
    stored = tokens // tile

    @pl.when(m == 0)
    def _():
        def emit(start, l, piece):
            g_rows[pl.ds(start, rows), pl.ds(l * LANES, LANES)] = low(piece)

        for c in range(tokens // tile):
            here = pl.ds(c * tile, tile)
            normed, _ = norm_parts(x_ref[here, :])
            split_lanes(flat, here, normed * gain_ref[...])
        reorder(flat, SEG, emit)
        b_t[...] = g_rows[...].T
        split_lanes(flat, pl.ds(0, tokens), datt_ref[...].astype(F32))
        reorder(flat, SEG, emit)
        g_t[...] = g_rows[...].T

    w_out = w_ref[0, :, 3 * wide :]
    do = low(dot(g_rows[...], w_out))
    dw_ref[0, :, 3 * wide :] = low(dot(g_t[...], o_ref[0]))
    lane = lax.broadcasted_iota(jnp.int32, (tokens, LANES), 1)
    do_full = do.astype(F32)
    product = do_full * o_ref[0].astype(F32)
    for head in range(PAIR):
        cols = pl.ds(head * LANES, LANES)
        inside = lane < HEAD if head == 0 else lane >= HEAD
        delta = jnp.sum(jnp.where(inside, product, 0.0), axis=-1, keepdims=True)
        delta_high = low(delta).astype(F32)
        mine = do_full if head == 0 else pltpu.roll(do_full, HEAD, axis=1)
        do_aug[...] = low(jnp.where(lane < HEAD, mine, jnp.where(lane == HEAD, -delta_high, jnp.where(lane == HEAD + 1, delta_high - delta, 0.0))))
        k_t[...] = k_ref[0, :, cols].T
        line = jnp.broadcast_to(table_ref[0, head : head + 1, :], (LANES, span))
        bias[...] = pltpu.roll(line, span - (LANES - 1), axis=1, stride=1, stride_axis=0)
        dbias[...] = jnp.zeros_like(dbias)
        for t in range(stored):
            here = pl.ds(t * tile, tile)
            scores = dot_nt(k_ref[0, here, cols], q_ref[0, :, cols])
            grads = dot_nt(v_ref[0, here, cols], do_aug[...])
            p_parts = []
            d_parts = []
            for sub in range(tile // LANES):
                first = tokens - LANES - t * tile - sub * LANES
                now = slice(sub * LANES, (sub + 1) * LANES)
                p = jnp.exp(scores[now] + bias[:, pl.ds(first, tokens)])
                ds = low(p * grads[now])
                dbias[:, pl.ds(first, tokens)] += ds.astype(F32)
                p_parts.append(low(p))
                d_parts.append(ds)
            p = jnp.concatenate(p_parts, axis=0)
            ds = jnp.concatenate(d_parts, axis=0)
            dv = dot(p, do_aug[...])
            dk = dot(ds, q_ref[0, :, cols])
            dq = dot(k_t[:, here], ds)
            if t == 0:
                dq_t[...] = dq
            else:
                dq_t[...] += dq
            if head == 0:
                d_pair[1, here, :] = dk
                d_pair[2, here, :] = dv
            else:
                lane_t = lax.broadcasted_iota(jnp.int32, (tile, LANES), 1)
                d_pair[1, here, :] = jnp.where(lane_t < HEAD, d_pair[1, here, :], pltpu.roll(dk, HEAD, axis=1))
                d_pair[2, here, :] = jnp.where(lane_t < HEAD, d_pair[2, here, :], pltpu.roll(dv, HEAD, axis=1))
        dq = dq_t[...].T * (HEAD**-0.5)
        if head == 0:
            d_pair[0] = dq
        else:
            d_pair[0] = jnp.where(lane < HEAD, d_pair[0], pltpu.roll(dq, HEAD, axis=1))
        folded = dbias[...]
        count = LANES
        while count > 1:
            count //= 2
            folded = folded[:count] + pltpu.roll(folded[count:], span - count, axis=1)
        dtable_ref[0, head : head + 1, :] = pltpu.roll(folded, LANES - 1, axis=1)
    for part in range(3):
        d_rows[:, pl.ds(part * wide, wide)] = low(d_pair[part])
    dw_ref[0, :, : 3 * wide] = low(dot(b_t[...], d_rows[...]))
    part = dot_nt(d_rows[...], w_ref[0, :, : 3 * wide])

    @pl.when(m == 0)
    def _():
        db[...] = part

    @pl.when(m != 0)
    def _():
        db[...] += part

    @pl.when(m == pl.num_programs(0) - 1)
    def _():
        dgain_ref[...] = jnp.zeros_like(dgain_ref)
        split_lanes(flat, pl.ds(0, tokens), db[...])

        def emit(start, l, piece):
            db[pl.ds(start, SEG), pl.ds(l * LANES, LANES)] = piece

        reorder(flat, rows, emit)
        for c in range(tokens // tile):
            here = pl.ds(c * tile, tile)
            normed, rstd = norm_parts(x_ref[here, :])
            d = db[here, :]
            dgain_ref[...] += jnp.sum(d * normed, axis=0, keepdims=True)
            dx_ref[here, :] = res_ref[here, :] + norm_back(normed, rstd, gain_ref[...], d)


def attention_backward(datt, x, gain, res, w, table_back, q, k, v, o):
    tokens, depth = x.shape
    blocks = w.shape[0]
    span = table_back.shape[2]
    full = pl.BlockSpec((tokens, depth), lambda i: (0, 0))
    heads = pl.BlockSpec((1, tokens, PAIR * LANES), lambda i: (i, 0, 0))
    pair = pl.BlockSpec((1, tokens, LANES), lambda i: (i, 0, 0))
    vec = pl.BlockSpec((1, depth), lambda i: (0, 0))
    w_spec = pl.BlockSpec((1, depth, w.shape[2]), lambda i: (i, 0, 0))
    t_spec = pl.BlockSpec((1, PAIR, span), lambda i: (i, 0, 0))
    wide = PAIR * HEAD
    return pl.pallas_call(
        attention_backward_kernel,
        grid=(blocks,),
        in_specs=[full, full, vec, full, w_spec, t_spec, heads, heads, heads, pair],
        out_specs=[full, w_spec, vec, t_spec],
        out_shape=[
            jax.ShapeDtypeStruct((tokens, depth), F32),
            jax.ShapeDtypeStruct(w.shape, BF16),
            jax.ShapeDtypeStruct((1, depth), F32),
            jax.ShapeDtypeStruct(table_back.shape, F32),
        ],
        scratch_shapes=[
            pltpu.VMEM((depth, tokens), BF16),
            pltpu.VMEM((depth, tokens), BF16),
            pltpu.VMEM((tokens, depth), BF16),
            pltpu.VMEM((depth // LANES, tokens, LANES), F32),
            pltpu.VMEM((LANES, span), F32),
            pltpu.VMEM((LANES, span), F32),
            pltpu.VMEM((tokens, LANES), BF16),
            pltpu.VMEM((3, tokens, LANES), F32),
            pltpu.VMEM((LANES, tokens), F32),
            pltpu.VMEM((LANES, tokens), BF16),
            pltpu.VMEM((tokens, 3 * wide), BF16),
            pltpu.VMEM((tokens, depth), F32),
        ],
        compiler_params=pltpu.CompilerParams(vmem_limit_bytes=56 * 2**20),
    )(datt, x, gain, res, w, table_back, q, k, v, o)


def gate_forward_kernel(
    taps, len_ref, x_ref, gain_ref, w_in_ref, w_out_ref, g_gain_ref, g_conv_ref,
    cg_ref, zr_ref, zg_ref, mean_ref, rstd_ref, conv_ref, gate_ref,
    c_rows, ur_all, ug_all, first, second, total, padded,
):
    i = pl.program_id(0)
    blocks = pl.num_programs(0) // 2
    tokens = x_ref.shape[0]
    rows = tokens // SEG
    width = zr_ref.shape[2]
    tile = 256
    channels = width * blocks
    length = len_ref[0]

    @pl.when(i == 0)
    def _():
        for c in range(tokens // tile):
            here = pl.ds(c * tile, tile)
            normed, _ = norm_parts(x_ref[here, :])
            c_rows[here, :] = low(normed * gain_ref[...])
        first[...] = jnp.zeros_like(first)
        second[...] = jnp.zeros_like(second)

    @pl.when(i < blocks)
    def _():
        for c in range(tokens // tile):
            here = pl.ds(c * tile, tile)
            z = dot(c_rows[here, :], w_in_ref[0])
            zr = z[:, :width]
            zg = z[:, width:]
            zr_ref[0, here, :] = low(zr)
            zg_ref[0, here, :] = low(zg)
            ur_all[i, here, :] = low(gelu(zr))
            ug = gelu(zg)
            ug_all[i, here, :] = low(ug)
            square = ug * ug
            one = ug[:, :LANES]
            two = square[:, :LANES]
            for l in range(1, width // LANES):
                one = one + ug[:, l * LANES : (l + 1) * LANES]
                two = two + square[:, l * LANES : (l + 1) * LANES]
            first[here, :] += one
            second[here, :] += two

    @pl.when(i == blocks - 1)
    def _():
        for c in range(tokens // tile):
            here = pl.ds(c * tile, tile)
            mean = jnp.sum(first[here, :], axis=-1, keepdims=True) / channels
            spread = jnp.sum(second[here, :], axis=-1, keepdims=True) / channels - mean * mean
            mean_ref[here, :] = jnp.broadcast_to(mean, (tile, LANES))
            rstd_ref[here, :] = jnp.broadcast_to(lax.rsqrt(spread + EPSILON), (tile, LANES))

    @pl.when(i >= blocks)
    def _():
        m = i - blocks
        keep = rows_keep(0, tokens, tokens, length)
        scale = rstd_ref[...] * keep
        shift = mean_ref[...] * scale
        for l in range(width // LANES):
            cols = pl.ds(l * LANES, LANES)
            ug = ug_all[m, :, cols].astype(F32)
            n = low((ug * scale - shift) * g_gain_ref[0, :, cols])
            fill_padded(padded, n.reshape(rows, SEG, LANES), taps)

            def taps_of(k):
                return low(jnp.broadcast_to(g_conv_ref[0, k : k + 1, cols], (SEG, LANES)))[None]

            def emit(start, value):
                block = value.shape[0]
                here = pl.ds(pl.multiple_of(start * SEG, block * SEG), block * SEG)
                flat = value.reshape(block * SEG, LANES)
                conv_ref[0, here, cols] = low(flat)
                gate_ref[0, here, cols] = low(ur_all[m, here, cols].astype(F32) * flat)

            convolve(padded, taps_of, taps, rows, 16, emit)
        part = dot_nt(gate_ref[0], w_out_ref[0])

        @pl.when(m == 0)
        def _():
            total[...] = part

        @pl.when(m != 0)
        def _():
            total[...] += part

        @pl.when(m == blocks - 1)
        def _():
            cg_ref[...] = low(total[...] * keep)


def gate_forward(length, x, gain, w, g_gain, g_conv, taps):
    tokens, depth = x.shape
    blocks = w.shape[0]
    width = w.shape[2] // 3
    full = pl.BlockSpec((tokens, depth), lambda i: (0, 0))
    lanes = pl.BlockSpec((tokens, LANES), lambda i: (0, 0))

    def early(i):
        return jnp.minimum(i, blocks - 1)

    def late(i):
        return jnp.maximum(i - blocks, 0)

    z_early = pl.BlockSpec((1, tokens, width), lambda i: (early(i), 0, 0))
    z_late = pl.BlockSpec((1, tokens, width), lambda i: (late(i), 0, 0))
    z_shape = jax.ShapeDtypeStruct((blocks, tokens, width), BF16)
    lane_shape = jax.ShapeDtypeStruct((tokens, LANES), F32)
    return pl.pallas_call(
        functools.partial(gate_forward_kernel, taps),
        grid=(2 * blocks,),
        in_specs=[
            pl.BlockSpec(memory_space=pltpu.SMEM),
            full,
            pl.BlockSpec((1, depth), lambda i: (0, 0)),
            pl.BlockSpec((1, depth, 2 * width), lambda i: (early(i), 0, 0)),
            pl.BlockSpec((1, depth, width), lambda i: (late(i), 0, 2)),
            pl.BlockSpec((1, 1, width), lambda i: (late(i), 0, 0)),
            pl.BlockSpec((1, taps, width), lambda i: (late(i), 0, 0)),
        ],
        out_specs=[full, z_early, z_early, lanes, lanes, z_late, z_late],
        out_shape=[jax.ShapeDtypeStruct((tokens, depth), BF16), z_shape, z_shape, lane_shape, lane_shape, z_shape, z_shape],
        scratch_shapes=[
            pltpu.VMEM((tokens, depth), BF16),
            pltpu.VMEM((blocks, tokens, width), BF16),
            pltpu.VMEM((blocks, tokens, width), BF16),
            pltpu.VMEM((tokens, LANES), F32),
            pltpu.VMEM((tokens, LANES), F32),
            pltpu.VMEM((tokens, depth), F32),
            pltpu.VMEM((tokens // SEG + taps - 1, SEG, LANES), BF16),
        ],
        compiler_params=pltpu.CompilerParams(vmem_limit_bytes=60 * 2**20),
    )(length, x, gain, w, w, g_gain, g_conv)


def gate_backward_kernel(
    taps, len_ref, dcg_ref, x_ref, gain_ref, res_ref, w_ref, zr_ref, zg_ref, conv_ref, gate_ref, mean_ref, rstd_ref, g_gain_ref, g_conv_ref,
    dx_ref, dwr_ref, dwg_ref, dwo_ref, dgain_ref, dg_gain_ref, dg_conv_ref,
    c_rows, c_t, g_t, ug_all, slope_all, dn_all, first, second, dc, padded, n_padded, d_rows, dconv, sums,
):
    i = pl.program_id(0)
    blocks = pl.num_programs(0) // 2
    tokens = x_ref.shape[0]
    rows = tokens // SEG
    width = zr_ref.shape[2]
    tile = 256
    channels = width * blocks
    length = len_ref[0]
    chunks = tokens // tile

    @pl.when(i == 0)
    def _():
        for c in range(chunks):
            here = pl.ds(c * tile, tile)
            normed, _ = norm_parts(x_ref[here, :])
            c_rows[here, :] = low(normed * gain_ref[...])
        c_t[...] = c_rows[...].T
        g_t[...] = dcg_ref[...].T
        first[...] = jnp.zeros_like(first)
        second[...] = jnp.zeros_like(second)
        dc[...] = jnp.zeros_like(dc)

    @pl.when(i < blocks)
    def _():
        m = i
        for c in range(chunks):
            here = pl.ds(c * tile, tile)
            dgate = dot(dcg_ref[here, :], w_ref[0, :, 2 * width :])
            ur, slope = gelu_and_slope(zr_ref[0, here, :].astype(F32))
            dzr = low(dgate * conv_ref[0, here, :].astype(F32) * slope)
            d_rows[here, :] = dzr
            dconv[here, :] = low(dgate * ur)
            dc[here, :] += dot_nt(dzr, w_ref[0, :, :width])
            ug, slope = gelu_and_slope(zg_ref[0, here, :].astype(F32))
            ug_all[m, here, :] = low(ug)
            slope_all[m, here, :] = low(slope)
        dwr_ref[0] = low(dot(c_t[...], d_rows[...]))
        dwo_ref[0] = low(dot(g_t[...], gate_ref[0]))
        keep = rows_keep(0, tokens, tokens, length)
        rstd = rstd_ref[...]
        shift = mean_ref[...] * rstd
        for l in range(width // LANES):
            cols = pl.ds(l * LANES, LANES)
            ug = ug_all[m, :, cols].astype(F32)
            n = low((ug * rstd - shift) * (g_gain_ref[0, :, cols] * keep))
            fill_padded(n_padded, n.reshape(rows, SEG, LANES), taps)
            d = dconv[:, cols].reshape(rows, SEG, LANES)
            fill_padded(padded, d, taps)
            tap_grads(n_padded, padded.at[pl.ds((taps - 1) // 2, rows)], sums, taps, rows, 8)
            dg_conv_ref[0, :, cols] = jnp.sum(sums[...], axis=1)
            dg_gain_ref[0, :, cols] = jnp.zeros((1, LANES), F32)

            def taps_of(k):
                return low(jnp.broadcast_to(g_conv_ref[0, taps - 1 - k : taps - k, cols], (SEG, LANES)))[None]

            def emit(start, value):
                block = value.shape[0]
                here = pl.ds(pl.multiple_of(start * SEG, block * SEG), block * SEG)
                dn = value.reshape(block * SEG, LANES) * rows_keep(start * SEG, block * SEG, tokens, length)
                normed = ug_all[m, here, cols].astype(F32) * rstd_ref[here, :] - mean_ref[here, :] * rstd_ref[here, :]
                product = dn * normed
                dg_gain_ref[0, :, cols] += jnp.sum(product, axis=0, keepdims=True)
                scaled = dn * g_gain_ref[0, :, cols]
                dn_all[m, here, cols] = low(scaled)
                first[here, :] += scaled
                second[here, :] += product * g_gain_ref[0, :, cols]

            convolve(padded, taps_of, taps, rows, 16, emit)

    @pl.when(i == blocks - 1)
    def _():
        for c in range(chunks):
            here = pl.ds(c * tile, tile)
            one = jnp.sum(first[here, :], axis=-1, keepdims=True) / channels
            two = jnp.sum(second[here, :], axis=-1, keepdims=True) / channels
            first[here, :] = jnp.broadcast_to(one, (tile, LANES))
            second[here, :] = jnp.broadcast_to(two, (tile, LANES))

    @pl.when(i >= blocks)
    def _():
        m = i - blocks
        for c in range(chunks):
            here = pl.ds(c * tile, tile)
            rstd = rstd_ref[here, :]
            shift = mean_ref[here, :] * rstd
            one = first[here, :]
            two = second[here, :]
            for l in range(width // LANES):
                cols = pl.ds(l * LANES, LANES)
                normed = ug_all[m, here, cols].astype(F32) * rstd - shift
                dug = rstd * (dn_all[m, here, cols].astype(F32) - one - normed * two)
                d_rows[here, cols] = low(dug * slope_all[m, here, cols].astype(F32))
            dc[here, :] += dot_nt(d_rows[here, :], w_ref[0, :, width : 2 * width])
        dwg_ref[0] = low(dot(c_t[...], d_rows[...]))

    @pl.when(i == 2 * blocks - 1)
    def _():
        dgain_ref[...] = jnp.zeros_like(dgain_ref)
        for c in range(chunks):
            here = pl.ds(c * tile, tile)
            normed, rstd = norm_parts(x_ref[here, :])
            d = dc[here, :]
            dgain_ref[...] += jnp.sum(d * normed, axis=0, keepdims=True)
            dx_ref[here, :] = res_ref[here, :] + norm_back(normed, rstd, gain_ref[...], d)


def gate_backward(length, dcg, x, gain, res, w, zr, zg, conv, gate, mean, rstd, g_gain, g_conv, taps):
    tokens, depth = x.shape
    blocks = w.shape[0]
    width = w.shape[2] // 3
    full = pl.BlockSpec((tokens, depth), lambda i: (0, 0))
    lanes = pl.BlockSpec((tokens, LANES), lambda i: (0, 0))
    vec = pl.BlockSpec((1, depth), lambda i: (0, 0))

    def early(i):
        return jnp.minimum(i, blocks - 1)

    def late(i):
        return jnp.maximum(i - blocks, 0)

    z_early = pl.BlockSpec((1, tokens, width), lambda i: (early(i), 0, 0))
    gain_spec = pl.BlockSpec((1, 1, width), lambda i: (early(i), 0, 0))
    conv_spec = pl.BlockSpec((1, taps, width), lambda i: (early(i), 0, 0))
    dw_shape = jax.ShapeDtypeStruct((blocks, depth, width), BF16)
    dw_early = pl.BlockSpec((1, depth, width), lambda i: (early(i), 0, 0))
    dw_late = pl.BlockSpec((1, depth, width), lambda i: (late(i), 0, 0))
    padded = (tokens // SEG + taps - 1, SEG, LANES)
    return pl.pallas_call(
        functools.partial(gate_backward_kernel, taps),
        grid=(2 * blocks,),
        in_specs=[
            pl.BlockSpec(memory_space=pltpu.SMEM),
            full,
            full,
            vec,
            full,
            pl.BlockSpec((1, depth, 3 * width), lambda i: (lax.rem(i, blocks), 0, 0)),
            z_early,
            z_early,
            z_early,
            z_early,
            lanes,
            lanes,
            gain_spec,
            conv_spec,
        ],
        out_specs=[full, dw_early, dw_late, dw_early, vec, gain_spec, conv_spec],
        out_shape=[
            jax.ShapeDtypeStruct((tokens, depth), F32),
            dw_shape,
            dw_shape,
            dw_shape,
            jax.ShapeDtypeStruct((1, depth), F32),
            jax.ShapeDtypeStruct(g_gain.shape, F32),
            jax.ShapeDtypeStruct(g_conv.shape, F32),
        ],
        scratch_shapes=[
            pltpu.VMEM((tokens, depth), BF16),
            pltpu.VMEM((depth, tokens), BF16),
            pltpu.VMEM((depth, tokens), BF16),
            pltpu.VMEM((blocks, tokens, width), BF16),
            pltpu.VMEM((blocks, tokens, width), BF16),
            pltpu.VMEM((blocks, tokens, width), BF16),
            pltpu.VMEM((tokens, LANES), F32),
            pltpu.VMEM((tokens, LANES), F32),
            pltpu.VMEM((tokens, depth), F32),
            pltpu.VMEM(padded, BF16),
            pltpu.VMEM(padded, BF16),
            pltpu.VMEM((tokens, width), BF16),
            pltpu.VMEM((tokens, width), BF16),
            pltpu.VMEM((taps, SEG, LANES), F32),
        ],
        compiler_params=pltpu.CompilerParams(vmem_limit_bytes=60 * 2**20),
    )(length, dcg, x, gain, res, w, zr, zg, conv, gate, mean, rstd, g_gain, g_conv)


def merge_forward_kernel(taps, x_ref, att_ref, cg_ref, w_ref, m_conv_ref, out_ref, merged_ref, padded):
    c = pl.program_id(0)
    tokens = x_ref.shape[0]
    rows = tokens // SEG
    half = pl.num_programs(0) // 2
    width = merged_ref.shape[1]
    for l in range(width // LANES):
        cols = pl.ds(l * LANES, LANES)

        @pl.when(c < half)
        def _():
            fill_padded(padded, att_ref[:, cols].reshape(rows, SEG, LANES), taps)

        @pl.when(c >= half)
        def _():
            fill_padded(padded, cg_ref[:, cols].reshape(rows, SEG, LANES), taps)

        def taps_of(k):
            return low(jnp.broadcast_to(m_conv_ref[k : k + 1, cols], (SEG, LANES)))[None]

        def emit(start, value):
            block = value.shape[0]
            here = pl.ds(pl.multiple_of(start * SEG, block * SEG), block * SEG)
            value = value + padded[pl.ds(start + (taps - 1) // 2, block)].astype(F32)
            merged_ref[here, cols] = low(value.reshape(block * SEG, LANES))

        convolve(padded, taps_of, taps, rows, 16, emit)
    w = jnp.concatenate([w_ref[m] for m in range(w_ref.shape[0])], axis=1)
    part = dot(merged_ref[...], w)

    @pl.when(c == 0)
    def _():
        out_ref[...] = x_ref[...] + part

    @pl.when(c != 0)
    def _():
        out_ref[...] += part


def merge_forward(x, att, cg, w, m_conv):
    tokens, depth = x.shape
    blocks, both, cols = w.shape
    taps = m_conv.shape[0]
    width = 256
    steps = both // width
    half = steps // 2
    full = pl.BlockSpec((tokens, depth), lambda i: (0, 0))
    return pl.pallas_call(
        functools.partial(merge_forward_kernel, taps),
        grid=(steps,),
        in_specs=[
            full,
            pl.BlockSpec((tokens, width), lambda i: (0, jnp.minimum(i, half - 1))),
            pl.BlockSpec((tokens, width), lambda i: (0, jnp.maximum(i - half, 0))),
            pl.BlockSpec((blocks, width, cols), lambda i: (0, i, 0)),
            pl.BlockSpec((taps, width), lambda i: (0, i)),
        ],
        out_specs=[full, pl.BlockSpec((tokens, width), lambda i: (0, i))],
        out_shape=[jax.ShapeDtypeStruct(x.shape, F32), jax.ShapeDtypeStruct((tokens, both), BF16)],
        scratch_shapes=[pltpu.VMEM((tokens // SEG + taps - 1, SEG, LANES), BF16)],
        compiler_params=pltpu.CompilerParams(vmem_limit_bytes=56 * 2**20),
    )(x, att, cg, w, m_conv)


def merge_backward_kernel(taps, len_ref, g_ref, att_ref, cg_ref, merged_ref, w_ref, m_conv_ref, datt_ref, dcg_ref, dw_ref, dconv_ref, g_rows, padded, j_padded, out, sums):
    c = pl.program_id(0)
    tokens = g_ref.shape[0]
    rows = tokens // SEG
    half = pl.num_programs(0) // 2
    blocks, width, narrow = w_ref.shape
    length = len_ref[0]

    @pl.when(c == 0)
    def _():
        g_rows[...] = low(g_ref[...])

    w = jnp.concatenate([w_ref[m] for m in range(blocks)], axis=1)
    dmerged = low(dot_nt(g_rows[...], w))
    dw = dot(merged_ref[...].T, g_rows[...])
    for m in range(blocks):
        dw_ref[m] = low(dw[:, m * narrow : (m + 1) * narrow])
    for l in range(width // LANES):
        cols = pl.ds(l * LANES, LANES)

        @pl.when(c < half)
        def _():
            fill_padded(j_padded, att_ref[:, cols].reshape(rows, SEG, LANES), taps)

        @pl.when(c >= half)
        def _():
            fill_padded(j_padded, cg_ref[:, cols].reshape(rows, SEG, LANES), taps)

        fill_padded(padded, dmerged[:, l * LANES : (l + 1) * LANES].reshape(rows, SEG, LANES), taps)
        tap_grads(j_padded, padded.at[pl.ds((taps - 1) // 2, rows)], sums, taps, rows, 8)
        dconv_ref[:, cols] = jnp.sum(sums[...], axis=1)

        def taps_of(k):
            return low(jnp.broadcast_to(m_conv_ref[taps - 1 - k : taps - k, cols], (SEG, LANES)))[None]

        def emit(start, value):
            block = value.shape[0]
            here = pl.ds(pl.multiple_of(start * SEG, block * SEG), block * SEG)
            value = value + padded[pl.ds(start + (taps - 1) // 2, block)].astype(F32)
            out[here, cols] = low(value.reshape(block * SEG, LANES) * rows_keep(start * SEG, block * SEG, tokens, length))

        convolve(padded, taps_of, taps, rows, 16, emit)

    @pl.when(c < half)
    def _():
        datt_ref[...] = out[...]

    @pl.when(c >= half)
    def _():
        dcg_ref[...] = out[...]


def merge_backward(length, g, att, cg, merged, w, m_conv):
    tokens, depth = g.shape
    blocks, both, cols = w.shape
    taps = m_conv.shape[0]
    width = 256
    steps = both // width
    half = steps // 2
    full = pl.BlockSpec((tokens, depth), lambda i: (0, 0))
    early = pl.BlockSpec((tokens, width), lambda i: (0, jnp.minimum(i, half - 1)))
    late = pl.BlockSpec((tokens, width), lambda i: (0, jnp.maximum(i - half, 0)))
    wide = pl.BlockSpec((tokens, width), lambda i: (0, i))
    w_spec = pl.BlockSpec((blocks, width, cols), lambda i: (0, i, 0))
    conv_spec = pl.BlockSpec((taps, width), lambda i: (0, i))
    padded = (tokens // SEG + taps - 1, SEG, LANES)
    return pl.pallas_call(
        functools.partial(merge_backward_kernel, taps),
        grid=(steps,),
        in_specs=[pl.BlockSpec(memory_space=pltpu.SMEM), full, early, late, wide, w_spec, conv_spec],
        out_specs=[early, late, w_spec, conv_spec],
        out_shape=[
            jax.ShapeDtypeStruct((tokens, depth), BF16),
            jax.ShapeDtypeStruct((tokens, depth), BF16),
            jax.ShapeDtypeStruct(w.shape, BF16),
            jax.ShapeDtypeStruct(m_conv.shape, F32),
        ],
        scratch_shapes=[
            pltpu.VMEM((tokens, depth), BF16),
            pltpu.VMEM(padded, BF16),
            pltpu.VMEM(padded, BF16),
            pltpu.VMEM((tokens, width), BF16),
            pltpu.VMEM((taps, SEG, LANES), F32),
        ],
        compiler_params=pltpu.CompilerParams(vmem_limit_bytes=56 * 2**20),
    )(length, g, att, cg, merged, w, m_conv)


def layer_forward(x, length, weights, small):
    g1, g2, g3, g4, g5 = weights
    gains, table, g_gain, g_conv, m_conv = small
    taps = m_conv.shape[0]
    x1, h1 = ffn_forward(x, gains[0:1], g1)
    att, q, k, v, o = attention_forward(length, x1, gains[1:2], g2, table)
    cg, zr, zg, mean, rstd, conv, gate = gate_forward(length, x1, gains[2:3], g3, g_gain, g_conv, taps)
    x2, merged = merge_forward(x1, att, cg, g4, m_conv)
    x3, h2, y = ffn_forward(x2, gains[3:4], g5, gains[4:5])
    saved = (x, x1, h1, att, q, k, v, o, cg, zr, zg, mean, rstd, conv, gate, x2, merged, x3, h2)
    return y, saved


def layer_backward(g, length, saved, weights, small):
    g1, g2, g3, g4, g5 = weights
    gains, table, g_gain, g_conv, m_conv = small
    taps = m_conv.shape[0]
    x, x1, h1, att, q, k, v, o, cg, zr, zg, mean, rstd, conv, gate, x2, merged, x3, h2 = saved
    dx2, dg5, dgain3, dgain4 = ffn_backward(g, x2, gains[3:4], h2, g5, gains[4:5], x3)
    datt, dcg, dg4, dm_conv = merge_backward(length, dx2, att, cg, merged, g4, m_conv)
    dx1, dwr, dwg, dwo, dgain2, dg_gain, dg_conv = gate_backward(
        length, dcg, x1, gains[2:3], dx2, g3, zr, zg, conv, gate, mean, rstd, g_gain, g_conv, taps
    )
    dx1, dg2, dgain1, dtable = attention_backward(datt, x1, gains[1:2], dx1, g2, table[:, :, ::-1], q, k, v, o)
    dx, dg1, dgain0 = ffn_backward(dx1, x, gains[0:1], h1, g1)
    dg3 = jnp.concatenate([dwr, dwg, dwo], axis=2)
    dgains = jnp.concatenate([dgain0, dgain1, dgain2, dgain3, dgain4], axis=0)
    return dx, (dg1, dg2, dg3, dg4, dg5), (dgains, dtable[:, :, ::-1], dg_gain, dg_conv, dm_conv)


def to_segments(values):
    tokens, depth = values.shape
    return values.reshape(SEG, tokens // SEG, depth).transpose(1, 0, 2).reshape(tokens, depth)


def from_segments(values):
    tokens, depth = values.shape
    return values.reshape(tokens // SEG, SEG, depth).transpose(1, 0, 2).reshape(tokens, depth)


MESH = pl.DeviceIdType.MESH


class Links:
    def __init__(self, mp, bits, send, recv, local):
        self.mp = mp
        self.bits = bits
        self.me = lax.axis_index("mp")
        self.dp = lax.axis_index("dp")
        self.bit = [lax.rem(self.dp // (1 << i), 2) for i in range(bits)]
        self.send, self.recv, self.local = send, recv, local
        self.used = 0
        self.used_local = 0

    def other(self, i):
        return {"dp": self.dp + (1 - 2 * self.bit[i]) * (1 << i)}

    def along(self, offset):
        return {"mp": lax.rem(self.me + offset, self.mp)}

    def before(self, offset):
        return lax.rem(self.me + self.mp - offset, self.mp)

    def barrier(self, own_bits=None, line=True):
        peers = [self.other(i) for i in (range(self.bits) if own_bits is None else own_bits)]
        if line:
            peers += [self.along(offset) for offset in range(1, self.mp)]
        semaphore = pltpu.get_barrier_semaphore()
        for peer in peers:
            pl.semaphore_signal(semaphore, inc=1, device_id=peer, device_id_type=MESH)
        pl.semaphore_wait(semaphore, len(peers))

    def copy(self, source, target, arrives, device):
        at = self.used
        self.used += 1

        def make(where):
            return pltpu.make_async_remote_copy(
                src_ref=source, dst_ref=where, send_sem=self.send.at[at], recv_sem=self.recv.at[at], device_id=device, device_id_type=MESH
            )

        return make(target), make(arrives)

    def here(self, source, target):
        at = self.used_local
        self.used_local += 1
        return pltpu.make_async_copy(source, target, self.local.at[at])

    def orders(self):
        rest = list(range(1, self.bits))
        return rest + [0], rest[::-1] + [0]

    def halves(self):
        half = self.mp // 2
        return (pl.ds(0, half), pl.ds(half, half))


def start(pairs):
    for out, _ in pairs:
        out.start()


def wait_recv(pairs):
    for _, arriving in pairs:
        arriving.wait_recv()


def wait_send(pairs):
    for out, _ in pairs:
        out.wait_send()


class Gather:
    def __init__(self, links, shard, buffer, line_only=False):
        self.links, self.shard, self.buffer = links, shard, buffer
        self.stages = 1 if line_only else 1 + links.bits
        self.line_only = line_only
        self.own = links.here(shard, self.at(links.me, {}))
        self.pairs = {}

    def at(self, m, free, flip=None):
        if self.line_only:
            return self.buffer.at[m]
        index = [m]
        for i in reversed(range(self.links.bits)):
            if i in free:
                index.append(pl.ds(0, 2))
            elif i == flip:
                index.append(1 - self.links.bit[i])
            else:
                index.append(self.links.bit[i])
        return self.buffer.at[tuple(index)]

    def stage(self, s):
        links = self.links
        if s in self.pairs:
            return self.pairs[s]
        made = []
        if s == 0:
            for offset in range(1, links.mp):
                made.append(links.copy(self.shard, self.at(links.me, {}), self.at(links.before(offset), {}), links.along(offset)))
        elif s == links.bits:
            free = set(range(1, links.bits))
            everything = pl.ds(0, links.mp)
            made.append(links.copy(self.at(everything, free), self.at(everything, free), self.at(everything, free, 0), links.other(0)))
        else:
            for half, order in zip(links.halves(), links.orders()):
                free = set(order[: s - 1])
                now = order[s - 1]
                made.append(links.copy(self.at(half, free), self.at(half, free), self.at(half, free, now), links.other(now)))
        self.pairs[s] = made
        return made


def gather_copies(bits, mp):
    return mp - 1 + 2 * (bits - 1) + 1


def gather_kernel(mp, bits, groups, line_groups, *refs):
    count = groups + line_groups
    shards = refs[:count]
    buffers = refs[count : 2 * count]
    send, recv, local = refs[2 * count :]
    links = Links(mp, bits, send, recv, local)
    links.barrier()
    all_of = [Gather(links, shards[i], buffers[i], i >= groups) for i in range(count)]
    order = all_of[groups:] + all_of[:groups]
    for g in order:
        g.own.start()
    last = max(i + g.stages for i, g in enumerate(order))
    for g in order:
        g.own.wait()
    for round_ in range(last):
        for i, g in enumerate(order):
            s = round_ - i
            if 0 <= s < g.stages:
                if s > 0:
                    wait_recv(g.stage(s - 1))
                start(g.stage(s))
    for g in order:
        wait_recv(g.stage(g.stages - 1))
        for s in range(g.stages):
            wait_send(g.stage(s))


def gather_all(shards, line_shards, mp, bits, collective_id):
    copies = len(shards) * gather_copies(bits, mp) + len(line_shards) * (mp - 1)
    everything = list(shards) + list(line_shards)
    out_shape = [jax.ShapeDtypeStruct((mp,) + (2,) * bits + s.shape, s.dtype) for s in shards]
    out_shape += [jax.ShapeDtypeStruct((mp,) + s.shape, s.dtype) for s in line_shards]
    anywhere = pl.BlockSpec(memory_space=pltpu.HBM)
    return pl.pallas_call(
        functools.partial(gather_kernel, mp, bits, len(shards), len(line_shards)),
        in_specs=[anywhere] * len(everything),
        out_specs=[anywhere] * len(everything),
        out_shape=out_shape,
        scratch_shapes=[pltpu.SemaphoreType.DMA((copies,)), pltpu.SemaphoreType.DMA((copies,)), pltpu.SemaphoreType.DMA((len(everything),))],
        compiler_params=pltpu.CompilerParams(collective_id=collective_id, has_side_effects=True),
    )(*everything)


class Scatter:
    def __init__(self, links, source, own, arrived):
        self.links, self.source, self.own, self.arrived = links, source, own, arrived
        self.stages = links.bits + 1
        self.pairs = {}
        self.load = links.here(self.pick(source, pl.ds(0, links.mp), list(range(links.bits))[::-1], 0, False), own)

    def pick(self, ref, m, bits, now, flip):
        index = [m]
        for i in bits:
            if i == now:
                index.append(1 - self.links.bit[i] if flip else self.links.bit[i])
            else:
                index.append(pl.ds(0, 2))
        return ref.at[tuple(index)]

    def left(self, order, s):
        return sorted(order[: len(order) - s], reverse=True)

    def held(self, s):
        return self.source if s == 0 else self.arrived[s - 1]

    def stage(self, s):
        links = self.links
        if s in self.pairs:
            return self.pairs[s]
        made = []
        if s == 0:
            everything = pl.ds(0, links.mp)
            bits = self.left(links.orders()[0], 0)
            made.append(links.copy(self.pick(self.source, everything, bits, 0, True), self.arrived[0], self.arrived[0], links.other(0)))
        elif s < links.bits:
            for half, order in zip(links.halves(), links.orders()):
                bits = self.left(order, s)
                now = order[len(order) - 1 - s]
                slot = self.arrived[s].at[half]
                made.append(links.copy(self.pick(self.held(s), half, bits, now, True), slot, slot, links.other(now)))
        else:
            for offset in range(1, links.mp):
                to = lax.rem(links.me + offset, links.mp)
                slot = self.arrived[s]
                made.append(links.copy(self.held(s).at[to], slot.at[links.me], slot.at[links.before(offset)], links.along(offset)))
        self.pairs[s] = made
        return made

    def add(self, s):
        links = self.links
        target = self.arrived[s]
        half = links.mp // 2

        def step(m, carry):
            for part, order in enumerate(links.orders()):
                at = m + part * half
                if s == 0:
                    target[at] += self.own[at]
                else:
                    bits = self.left(order, s)
                    now = order[len(order) - 1 - s]
                    target[at] += self.pick(self.held(s), at, bits, now, False)[...]
            return carry

        lax.fori_loop(0, half, step, 0)

    def finish(self, out):
        links = self.links
        held = self.held(links.bits)
        total = held[links.me].astype(F32)
        for offset in range(1, links.mp):
            total = total + self.arrived[links.bits][links.before(offset)].astype(F32)
        out[...] = total


def scatter_kernel(mp, bits, groups, *refs):
    sources = refs[:groups]
    outs = refs[groups : 2 * groups]
    rest = refs[2 * groups :]
    send, recv, local = rest[:3]
    rest = rest[3:]
    per = bits + 2
    links = Links(mp, bits, send, recv, local)
    all_of = []
    for g in range(groups):
        mine = rest[g * per : (g + 1) * per]
        all_of.append(Scatter(links, sources[g], mine[0], mine[1:]))
    links.barrier()
    for g in all_of:
        g.load.start()
    for round_ in range(groups + bits + 1):
        for i, g in enumerate(all_of):
            s = round_ - i
            if s < 0 or s > g.stages:
                continue
            if s > 0:
                wait_recv(g.stage(s - 1))
                if s == 1:
                    g.load.wait()
                if s < g.stages:
                    g.add(s - 1)
                else:
                    g.finish(outs[i])
            if s < g.stages:
                start(g.stage(s))
    for g in all_of:
        for s in range(g.stages):
            wait_send(g.stage(s))


def scatter_shapes(mp, bits, rows, cols):
    shapes = [(mp,) + (2,) * (bits - 1) + (rows, cols)]
    shapes += [(mp,) + (2,) * (bits - 1 - s) + (rows, cols) for s in range(bits)]
    shapes.append((mp, rows, cols))
    return [pltpu.VMEM(shape, BF16) for shape in shapes]


def scatter_all(grads, mp, bits, collective_id):
    copies = len(grads) * (1 + 2 * (bits - 1) + mp - 1)
    scratch = []
    for grad in grads:
        scratch += scatter_shapes(mp, bits, grad.shape[-2], grad.shape[-1])
    return pl.pallas_call(
        functools.partial(scatter_kernel, mp, bits, len(grads)),
        in_specs=[pl.BlockSpec(memory_space=pltpu.HBM)] * len(grads),
        out_specs=[pl.BlockSpec(memory_space=pltpu.VMEM)] * len(grads),
        out_shape=[jax.ShapeDtypeStruct(g.shape[-2:], F32) for g in grads],
        scratch_shapes=[pltpu.SemaphoreType.DMA((copies,)), pltpu.SemaphoreType.DMA((copies,)), pltpu.SemaphoreType.DMA((len(grads),))] + scratch,
        compiler_params=pltpu.CompilerParams(collective_id=collective_id, has_side_effects=True, vmem_limit_bytes=62 * 2**20),
    )(*grads)


def pack_layer(layer, ffn_in, ffn_out, attn_in, attn_out, cg_in, cg_out, merge_out, mp_index, mp_size):
    cols = merge_out.shape[2] // mp_size
    part = lax.dynamic_slice_in_dim(merge_out[layer], mp_index * cols, cols, axis=1)
    pieces = (
        jnp.concatenate([ffn_in[layer, 0], ffn_out[layer, 0].T], axis=1),
        jnp.concatenate([attn_in[layer, 0], attn_in[layer, 1], attn_in[layer, 2], attn_out[layer].T], axis=1),
        jnp.concatenate([cg_in[layer, 0], cg_in[layer, 1], cg_out[layer].T], axis=1),
        part,
        jnp.concatenate([ffn_in[layer, 1], ffn_out[layer, 1].T], axis=1),
    )
    return tuple(low(piece) for piece in pieces)


def body(frames, cotangent, lengths, norm_gains, ffn_in, ffn_out, attn_in, attn_out, rel_bias, cg_in, csgu_gain, csgu_conv, cg_out, merge_conv, merge_out):
    layers = norm_gains.shape[0]
    mp_size = lax.axis_size("mp")
    bits = lax.axis_size("dp").bit_length() - 1
    mp_index = lax.axis_index("mp")
    length = lax.dynamic_slice_in_dim(lengths, mp_index, 1)
    tokens, depth = frames.shape
    taps = merge_conv.shape[1]
    heads, span = rel_bias.shape[1:]
    channels = csgu_gain.shape[1]

    shards = []
    for layer in range(layers):
        shards += pack_layer(layer, ffn_in, ffn_out, attn_in, attn_out, cg_in, cg_out, merge_out, mp_index, mp_size)
    line = jnp.concatenate([rel_bias.reshape(layers, -1), csgu_gain, csgu_conv.reshape(layers, -1)], axis=1)
    line = line.reshape(-1, LANES)
    *gathered, line_all = gather_all(shards, [line], mp_size, bits, 1)
    line_all = line_all.reshape(mp_size, layers, -1)
    table = line_all[:, :, : heads * span].reshape(mp_size, layers, heads, span)
    g_gain = line_all[:, :, heads * span : heads * span + channels].reshape(mp_size, layers, 1, channels)
    g_conv = line_all[:, :, heads * span + channels :].reshape(mp_size, layers, taps, channels)
    groups = len(shards) // layers

    state = to_segments(frames).astype(F32)
    weights = []
    smalls = []
    saved = []
    for layer in range(layers):
        mine = gathered[layer * groups : (layer + 1) * groups]
        weights.append(tuple(w.reshape(mp_size, -1, w.shape[-1]) for w in mine))
        smalls.append((norm_gains[layer], table[:, layer], g_gain[:, layer], g_conv[:, layer], merge_conv[layer]))
        state, kept = layer_forward(state, length, weights[layer], smalls[layer])
        saved.append(kept)
    frame = lax.broadcasted_iota(jnp.int32, (tokens, 1), 0)
    keep = (frame < length).astype(F32)
    output_frames = from_segments(state) * keep
    incoming = to_segments(cotangent.astype(F32) * keep)
    big = []
    tiny = [None] * layers
    for layer in reversed(range(layers)):
        incoming, grads, small = layer_backward(incoming, length, saved[layer], weights[layer], smalls[layer])
        big = [g.reshape((mp_size,) + (2,) * bits + (-1, g.shape[-1])) for g in grads] + big
        tiny[layer] = small
    input_grad = from_segments(incoming)

    split = [jnp.concatenate([t[1].reshape(mp_size, -1), t[2].reshape(mp_size, -1), t[3].reshape(mp_size, -1)], axis=1) for t in tiny]
    split = jnp.concatenate(split, axis=1).reshape(mp_size, -1, LANES)
    shared = jnp.concatenate([jnp.stack([t[0] for t in tiny]).reshape(-1), jnp.stack([t[4] for t in tiny]).reshape(-1)]).reshape(mp_size, -1, LANES)
    split_rows = split.shape[1]
    shared_rows = shared.shape[1]
    unit = 16 << bits
    padding = -(split_rows + shared_rows) % unit
    packed = jnp.concatenate([split, shared, jnp.zeros((mp_size, padding, LANES), F32)], axis=1)
    packed = low(packed).reshape((mp_size,) + (2,) * bits + (-1, LANES))
    *big, packed = scatter_all(big + [packed], mp_size, bits, 2)
    merge_line = low(jnp.concatenate([big[layer * groups + 3] for layer in range(layers)], axis=0))
    packed, merge_all = gather_all([low(packed)], [merge_line], mp_size, bits, 3)
    packed = packed.reshape(mp_size, -1, LANES).astype(F32)
    split = lax.dynamic_index_in_dim(packed, mp_index, 0, keepdims=False)[:split_rows].reshape(layers, -1)
    grad_table = split[:, : heads * span].reshape(layers, heads, span)
    grad_g_gain = split[:, heads * span : heads * span + channels]
    grad_g_conv = split[:, heads * span + channels :].reshape(layers, taps, channels)
    shared = packed[:, split_rows : split_rows + shared_rows].reshape(-1)
    grad_gains = shared[: norm_gains.size].reshape(norm_gains.shape)
    grad_m_conv = shared[norm_gains.size :].reshape(merge_conv.shape)
    merge_all = merge_all.astype(F32).reshape(mp_size, layers, -1, merge_all.shape[-1])
    grad_merge = merge_all.transpose(1, 2, 0, 3).reshape(merge_out.shape)

    f = ffn_in.shape[3]
    h = attn_in.shape[3]
    c = cg_in.shape[3]
    one, two, three, _, five = [[big[layer * groups + g] for layer in range(layers)] for g in range(groups)]
    grad_ffn_in = jnp.stack([jnp.stack([a[:, :f], b[:, :f]]) for a, b in zip(one, five)])
    grad_ffn_out = jnp.stack([jnp.stack([a[:, f:].T, b[:, f:].T]) for a, b in zip(one, five)])
    grad_attn_in = jnp.stack([jnp.stack([a[:, :h], a[:, h : 2 * h], a[:, 2 * h : 3 * h]]) for a in two])
    grad_attn_out = jnp.stack([a[:, 3 * h :].T for a in two])
    grad_cg_in = jnp.stack([jnp.stack([a[:, :c], a[:, c : 2 * c]]) for a in three])
    grad_cg_out = jnp.stack([a[:, 2 * c :].T for a in three])
    return (
        output_frames,
        input_grad,
        grad_gains,
        grad_ffn_in,
        grad_ffn_out,
        grad_attn_in,
        grad_attn_out,
        grad_table,
        grad_cg_in,
        grad_g_gain,
        grad_g_conv,
        grad_cg_out,
        grad_m_conv,
        grad_merge,
    )


def solution(mesh):
    tokens = P(("dp", "mp"), None)
    columns = P(None, None, "dp", "mp")
    rows = P(None, "mp", "dp")
    ffn_rows = P(None, None, "mp", "dp")
    heads = P(None, "mp", None)
    taps = P(None, None, "mp")
    return jax.shard_map(
        body,
        mesh=mesh,
        in_specs=(tokens, tokens, P("dp"), P(), columns, ffn_rows, columns, rows, heads, columns, P(None, "mp"), taps, rows, P(), P(None, "dp", None)),
        out_specs=(tokens, tokens, P(), columns, ffn_rows, columns, rows, heads, columns, P(None, "mp"), taps, rows, P(), P(None, "dp", None)),
        check_vma=False,
    )
```

```python
import functools

import jax
import jax.numpy as jnp
from jax import lax
from jax.experimental import pallas as pl
from jax.experimental.pallas import tpu as pltpu
from jax.sharding import PartitionSpec as P

EPSILON = 1e-05
MASKED = -1000000000.0
F32 = jnp.float32
BF16 = jnp.bfloat16
SEG = 16
GELU_A = 0.7978845608028654
GELU_B = 0.044715


def dot(left, right):
    return lax.dot_general(left, right, (((1,), (0,)), ((), ())), preferred_element_type=F32)


def dot_nt(left, right):
    return lax.dot_general(left, right, (((1,), (1,)), ((), ())), preferred_element_type=F32)


def low(values):
    return values.astype(BF16)


def norm_parts(values):
    mean = jnp.mean(values, axis=-1, keepdims=True)
    centred = values - mean
    spread = jnp.mean(centred * centred, axis=-1, keepdims=True)
    rstd = lax.rsqrt(spread + EPSILON)
    return centred * rstd, rstd


def norm_back(normed, rstd, gain, grad):
    scaled = grad * gain
    first = jnp.mean(scaled, axis=-1, keepdims=True)
    second = jnp.mean(scaled * normed, axis=-1, keepdims=True)
    return rstd * (scaled - first - normed * second)


def gelu(values):
    half = 0.5 * values
    inner = values * (GELU_A + (GELU_A * GELU_B) * (values * values))
    return half + half * jnp.tanh(inner)


def gelu_and_slope(values):
    half = 0.5 * values
    square = values * values
    tanh = jnp.tanh(values * (GELU_A + (GELU_A * GELU_B) * square))
    value = half + half * tanh
    slope = 0.5 + 0.5 * tanh + (half - half * tanh * tanh) * (GELU_A + (3.0 * GELU_A * GELU_B) * square)
    return value, slope


def rows_keep(start, rows, frames, length):
    at = lax.broadcasted_iota(jnp.int32, (rows, 1), 0) + start
    frame = (at % SEG) * (frames // SEG) + at // SEG
    return (frame < length).astype(F32)


MESH = pl.DeviceIdType.MESH


class Links:
    def __init__(self, mp, bits, send, recv):
        self.mp = mp
        self.bits = bits
        self.me = lax.axis_index("mp")
        self.dp = lax.axis_index("dp")
        self.bit = [lax.rem(self.dp // (1 << i), 2) for i in range(bits)]
        self.send, self.recv = send, recv

    def other(self, i):
        return {"dp": self.dp + (1 - 2 * self.bit[i]) * (1 << i)}

    def along(self, offset):
        return {"mp": lax.rem(self.me + offset, self.mp)}

    def before(self, offset):
        return lax.rem(self.me + self.mp - offset, self.mp)

    def barrier(self):
        peers = [self.other(i) for i in range(self.bits)] + [self.along(offset) for offset in range(1, self.mp)]
        semaphore = pltpu.get_barrier_semaphore()
        for peer in peers:
            pl.semaphore_signal(semaphore, inc=1, device_id=peer, device_id_type=MESH)
        pl.semaphore_wait(semaphore, len(peers))

    def copy(self, at, source, target, arrives, device):
        def make(where):
            return pltpu.make_async_remote_copy(
                src_ref=source, dst_ref=where, send_sem=self.send.at[at], recv_sem=self.recv.at[at], device_id=device, device_id_type=MESH
            )

        return lambda: make(target), lambda: make(arrives)


def orders(bits):
    rest = list(range(1, bits))
    return rest + [0], rest[::-1] + [0]


def halves(mp):
    return (pl.ds(0, mp // 2), pl.ds(mp // 2, mp // 2))


class Gather:
    def __init__(self, mp, bits, line=False):
        self.mp, self.bits, self.line = mp, bits, line

    def copies(self, s):
        return self.mp - 1 if s == 0 else 1 if s == self.bits else 2

    def at(self, links, buffer, m, free, flip=None):
        index = [m]
        if not self.line:
            for i in reversed(range(self.bits)):
                index.append(pl.ds(0, 2) if i in free else 1 - links.bit[i] if i == flip else links.bit[i])
        return buffer.at[tuple(index)]

    def pairs(self, links, buffer, s, base):
        made = []

        def add(m, arriving, free, flip, device):
            mine = self.at(links, buffer, m, free)
            made.append(links.copy(base + len(made), mine, mine, self.at(links, buffer, arriving, free, flip), device))

        if s == 0:
            for offset in range(1, self.mp):
                add(links.me, links.before(offset), (), None, links.along(offset))
        elif s == self.bits:
            whole = pl.ds(0, self.mp)
            add(whole, whole, range(1, self.bits), 0, links.other(0))
        else:
            for half, order in zip(halves(self.mp), orders(self.bits)):
                add(half, half, order[: s - 1], order[s - 1], links.other(order[s - 1]))
        return made


class Scatter:
    def __init__(self, mp, bits, rows, cols):
        self.mp, self.bits, self.rows, self.cols = mp, bits, rows, cols

    def shape(self, s):
        return (self.mp,) + (2,) * (self.bits - s) + (self.rows, self.cols)

    def arrived(self, s):
        return self.shape(s + 1) if s < self.bits else self.shape(s)

    def own(self, s):
        return self.arrived(s) if s < self.bits else (self.rows, self.cols)

    def copies(self, s):
        return 1 if s == 0 else self.mp - 1 if s == self.bits else 2

    def loads(self, s):
        return 2 if 0 < s < self.bits else 1

    def parts(self, s):
        if s == 0:
            return [(pl.ds(0, self.mp), list(range(self.bits))[::-1], 0)]
        made = []
        for half, order in zip(halves(self.mp), orders(self.bits)):
            made.append((half, sorted(order[: self.bits - s], reverse=True), order[self.bits - 1 - s]))
        return made

    def pick(self, links, ref, m, left, now, flip):
        index = [m]
        for i in left:
            index.append(pl.ds(0, 2) if i != now else 1 - links.bit[i] if flip else links.bit[i])
        return ref.at[tuple(index)]

    def pairs(self, links, held, slots, s, base):
        made = []
        if s < self.bits:
            for m, left, now in self.parts(s):
                slot = slots.at[m]
                made.append(links.copy(base + len(made), self.pick(links, held, m, left, now, True), slot, slot, links.other(now)))
        else:
            for offset in range(1, self.mp):
                to = lax.rem(links.me + offset, self.mp)
                made.append(links.copy(base + len(made), held.at[to], slots.at[links.me], slots.at[links.before(offset)], links.along(offset)))
        return made

    def load_pairs(self, links, held, own, s):
        if s == self.bits:
            return [(held.at[links.me], own)]
        return [(self.pick(links, held, m, left, now, False), own.at[m]) for m, left, now in self.parts(s)]

    def add(self, links, slots, s, own, held):
        half = self.mp // 2

        def step(m, carry):
            for part, order in enumerate(orders(self.bits)):
                at = m + part * half
                if own is not None:
                    slots[at] += own[at]
                else:
                    left = sorted(order[: self.bits - s], reverse=True)
                    slots[at] += self.pick(links, held, at, left, order[self.bits - 1 - s], False)[...]
            return carry

        lax.fori_loop(0, half, step, 0)

    def total(self, links, slots, own, held):
        value = (own[...] if own is not None else held[links.me]).astype(F32)
        for offset in range(1, self.mp):
            value = value + slots[links.before(offset)].astype(F32)
        return value


HBM = pl.BlockSpec(memory_space=pltpu.HBM)


class Ride:
    def __init__(self, flow, mp, bits, collective_id, rounds):
        self.flow, self.mp, self.bits, self.collective_id = flow, mp, bits, collective_id
        self.rounds = rounds
        names = []
        self.base = {}
        self.count = 0
        self.stages = {}
        for _, tasks in rounds:
            for name, s in tasks:
                if name not in names:
                    names.append(name)
                    self.stages[name] = []
                self.stages[name].append(s)
                self.base[name, s] = self.count
                self.count += flow[name][0].copies(s)
        self.gathers = [n for n in names if isinstance(flow[n][0], Gather)]
        self.scatters = [n for n in names if isinstance(flow[n][0], Scatter)]
        self.local = {}
        self.local_count = 0
        self.scratch = []
        self.place = {}
        for n in self.scatters:
            kind = flow[n][0]
            first, last = self.stages[n][0], self.stages[n][-1]
            self.local[n] = self.local_count
            self.local_count += kind.loads(first) + 1
            self.place[n, "own"] = len(self.scratch)
            self.scratch.append(pltpu.VMEM(kind.own(first), BF16))
            for s in self.stages[n]:
                self.place[n, s] = len(self.scratch)
                self.scratch.append(pltpu.VMEM(kind.arrived(s), BF16))
        self.sems = [pltpu.SemaphoreType.DMA((max(1, k),)) for k in (self.count, self.count, self.local_count)]

    def inputs(self):
        return [self.flow[n][1] for n in self.gathers + self.scatters]

    def finals(self, n):
        return self.stages[n][-1] == self.bits

    def outputs(self):
        shapes = [jax.ShapeDtypeStruct(self.flow[n][1].shape, self.flow[n][1].dtype) for n in self.gathers]
        specs = [HBM] * len(shapes)
        for n in self.scatters:
            kind = self.flow[n][0]
            if self.finals(n):
                shapes.append(jax.ShapeDtypeStruct((kind.rows, kind.cols), F32))
                specs.append(pl.BlockSpec((kind.rows, kind.cols), lambda *_: (0, 0)))
            else:
                shapes.append(jax.ShapeDtypeStruct(kind.shape(self.stages[n][-1] + 1), BF16))
                specs.append(HBM)
        return shapes, specs

    def bind(self, ins, outs, scratch):
        names = self.gathers + self.scatters
        self.ins = dict(zip(names, ins))
        self.outs = dict(zip(names, outs))
        send, recv, self.local_sem = scratch[:3]
        self.buffers = scratch[3:]
        self.links = Links(self.mp, self.bits, send, recv)

    def held(self, n, s):
        return self.ins[n] if s == self.stages[n][0] else self.buffers[self.place[n, s - 1]]

    def pairs(self, task):
        n, s = task
        kind = self.flow[n][0]
        if n in self.gathers:
            return kind.pairs(self.links, self.outs[n], s, self.base[task])
        return kind.pairs(self.links, self.held(n, s), self.buffers[self.place[task]], s, self.base[task])

    def loads(self, n):
        first = self.stages[n][0]
        pairs = self.flow[n][0].load_pairs(self.links, self.ins[n], self.buffers[self.place[n, "own"]], first)
        return [pltpu.make_async_copy(a, b, self.local_sem.at[self.local[n] + i]) for i, (a, b) in enumerate(pairs)]

    def stores(self, n):
        last = self.stages[n][-1]
        at = self.local[n] + self.flow[n][0].loads(self.stages[n][0])
        return pltpu.make_async_copy(self.buffers[self.place[n, last]], self.outs[n], self.local_sem.at[at])

    def begin(self, number):
        if number == 0:
            self.links.barrier()
        else:
            self.finish(number - 1)
        for n, s in self.rounds[number][1]:
            if n in self.scatters and s == self.stages[n][0]:
                for load in self.loads(n):
                    load.start()
        for task in self.rounds[number][1]:
            for out, _ in self.pairs(task):
                out().start()

    def finish(self, number):
        for task in self.rounds[number][1]:
            n, s = task
            for _, arriving in self.pairs(task):
                arriving().wait_recv()
            if n in self.scatters:
                kind = self.flow[n][0]
                own = None
                if s == self.stages[n][0]:
                    own = self.buffers[self.place[n, "own"]]
                    for load in self.loads(n):
                        load.wait()
                slots = self.buffers[self.place[task]]
                if s < self.bits:
                    kind.add(self.links, slots, s, own, self.held(n, s))
                    if s == self.stages[n][-1]:
                        self.stores(n).start()
                else:
                    self.outs[n][...] = kind.total(self.links, slots, own, self.held(n, s))

    def end(self):
        self.finish(len(self.rounds) - 1)
        for _, tasks in self.rounds:
            for task in tasks:
                for out, _ in self.pairs(task):
                    out().wait_send()
        for n in self.scatters:
            if not self.finals(n):
                self.stores(n).wait()

    def done(self, arrays):
        for n, array in zip(self.gathers + self.scatters, arrays):
            self.flow[n] = (self.flow[n][0], array)


def launch(kernel, grid, in_specs, out_specs, out_shape, scratch_shapes=(), vmem=56, ride=None, args=()):
    scratch_shapes = list(scratch_shapes)
    if ride is None:
        return pl.pallas_call(
            kernel,
            grid=grid,
            in_specs=in_specs,
            out_specs=out_specs,
            out_shape=out_shape,
            scratch_shapes=scratch_shapes,
            compiler_params=pltpu.CompilerParams(vmem_limit_bytes=vmem * 2**20),
        )(*args)
    extra_in = ride.inputs()
    extra_shapes, extra_specs = ride.outputs()
    n_in, n_out, n_scratch = len(in_specs), len(out_specs), len(scratch_shapes)

    def riding(*refs):
        ins, refs = refs[:n_in], refs[n_in:]
        ride_ins, refs = refs[: len(extra_in)], refs[len(extra_in) :]
        outs, refs = refs[:n_out], refs[n_out:]
        ride_outs, refs = refs[: len(extra_shapes)], refs[len(extra_shapes) :]
        scratch, ride_scratch = refs[:n_scratch], refs[n_scratch:]
        ride.bind(ride_ins, ride_outs, ride_scratch)
        step = pl.program_id(0)
        for number, (at, _) in enumerate(ride.rounds):

            @pl.when(step == at)
            def _():
                ride.begin(number)

        if kernel is not None:
            kernel(*ins, *outs, *scratch)

        @pl.when(step == pl.num_programs(0) - 1)
        def _():
            ride.end()

    made = pl.pallas_call(
        riding,
        grid=grid,
        in_specs=list(in_specs) + [HBM] * len(extra_in),
        out_specs=list(out_specs) + extra_specs,
        out_shape=list(out_shape) + extra_shapes,
        scratch_shapes=scratch_shapes + ride.sems + ride.scratch,
        input_output_aliases={n_in + i: n_out + i for i in range(len(ride.gathers))},
        compiler_params=pltpu.CompilerParams(collective_id=ride.collective_id, has_side_effects=True, vmem_limit_bytes=vmem * 2**20),
    )(*args, *extra_in)
    ride.done(made[n_out:])
    return made[:n_out]


def start_kernel(mp, bits, kinds, *refs):
    count = len(kinds)
    shards, buffers, local = refs[:count], refs[count : 2 * count], refs[2 * count]
    links = Links(mp, bits, None, None)
    copies = [pltpu.make_async_copy(shards[i], kinds[i].at(links, buffers[i], links.me, ()), local.at[i]) for i in range(count)]
    for copy in copies:
        copy.start()
    for copy in copies:
        copy.wait()


def start_buffers(shards, kinds, mp, bits):
    shapes = []
    for shard, kind in zip(shards, kinds):
        shapes.append(jax.ShapeDtypeStruct((mp,) + (() if kind.line else (2,) * bits) + shard.shape, shard.dtype))
    return pl.pallas_call(
        functools.partial(start_kernel, mp, bits, kinds),
        in_specs=[pl.BlockSpec(memory_space=pltpu.VMEM)] * len(shards),
        out_specs=[HBM] * len(shards),
        out_shape=shapes,
        scratch_shapes=[pltpu.SemaphoreType.DMA((len(shards),))],
    )(*shards)


def fill_padded(padded, values, taps):
    rows, _, lanes = values.shape
    half = (taps - 1) // 2
    padded[pl.ds(half, rows)] = values
    place = lax.broadcasted_iota(jnp.int32, (half, SEG, lanes), 1)
    before = pltpu.roll(values[rows - half :].astype(F32), 1, axis=1)
    padded[pl.ds(0, half)] = low(jnp.where(place == 0, 0.0, before))
    after = pltpu.roll(values[:half].astype(F32), SEG - 1, axis=1)
    padded[pl.ds(half + rows, half)] = low(jnp.where(place == SEG - 1, 0.0, after))


def convolve(padded, taps_of, taps, rows, block, emit):
    weights = [taps_of(k) for k in range(taps)]

    def step(index, carry):
        start = index * block
        total = None
        for first in range(0, taps, 8):
            part = None
            for k in range(first, min(taps, first + 8)):
                term = weights[k] * padded[pl.ds(start + k, block)]
                part = term if part is None else part + term
            part = part.astype(F32)
            total = part if total is None else total + part
        emit(start, total)
        return carry

    lax.fori_loop(0, rows // block, step, 0)


def tap_grads(padded, grads, sums, taps, rows, block):
    sums[...] = jnp.zeros_like(sums)

    def step(index, carry):
        start = index * block
        here = grads[pl.ds(start, block)]
        for k in range(taps):
            term = here * padded[pl.ds(start + k, block)]
            count = block
            while count > 1:
                count //= 2
                term = term[:count] + term[count:]
            sums[k] += term[0].astype(F32)
        return carry

    lax.fori_loop(0, rows // block, step, 0)


def ffn_forward_kernel(final, blocks, x_ref, gain_ref, w_ref, *rest):
    if final:
        last_ref, out_ref, h_ref, y_ref = rest
    else:
        out_ref, h_ref = rest
    width = h_ref.shape[2]
    x = x_ref[...]
    normed, _ = norm_parts(x)
    a = low(normed * gain_ref[...])
    total = None
    for m in range(blocks):
        h = dot(a, w_ref[m, :, :width])
        h_ref[m] = low(h)
        half = 0.5 * h
        s = low(half + half * jnp.tanh(half))
        part = dot_nt(s, w_ref[m, :, width:])
        total = part if total is None else total + part
    out = x + 0.5 * total
    out_ref[...] = out
    if final:
        normed, _ = norm_parts(out)
        y_ref[...] = normed * last_ref[...]


def ffn_forward(x, gain, w, last=None, ride=None):
    tokens, depth = x.shape
    blocks, _, width = w.shape
    width //= 2
    tile = min(256, tokens)
    row = pl.BlockSpec((tile, depth), lambda i: (i, 0))
    vec = pl.BlockSpec((1, depth), lambda i: (0, 0))
    out_shape = [jax.ShapeDtypeStruct(x.shape, F32), jax.ShapeDtypeStruct((blocks, tokens, width), BF16)]
    out_specs = [row, pl.BlockSpec((blocks, tile, width), lambda i: (0, i, 0))]
    in_specs = [row, vec, pl.BlockSpec(w.shape, lambda i: (0, 0, 0))]
    args = [x, gain, w]
    if last is not None:
        in_specs.append(vec)
        args.append(last)
        out_shape.append(jax.ShapeDtypeStruct(x.shape, F32))
        out_specs.append(row)
    return launch(
        functools.partial(ffn_forward_kernel, last is not None, blocks),
        grid=(tokens // tile,),
        in_specs=in_specs,
        out_specs=out_specs,
        out_shape=out_shape,
        vmem=56,
        ride=ride,
        args=args,
    )


def ffn_backward_kernel(final, tile, g_ref, x_ref, gain_ref, h_ref, w_ref, *rest):
    if final:
        last_ref, y_ref, dx_ref, dw_ref, dgain_ref, dlast_ref, grad, at, gt, a_rows, g_rows, s_rows, d_rows, da = rest
    else:
        dx_ref, dw_ref, dgain_ref, grad, at, gt, a_rows, g_rows, s_rows, d_rows, da = rest
    m = pl.program_id(0)
    tokens = x_ref.shape[0]
    width = h_ref.shape[2]
    chunks = tokens // tile

    @pl.when(m == 0)
    def _():
        if final:
            dlast_ref[...] = jnp.zeros_like(dlast_ref)
        for c in range(chunks):
            here = pl.ds(c * tile, tile)
            g = g_ref[here, :]
            if final:
                normed, rstd = norm_parts(y_ref[here, :])
                dlast_ref[...] += jnp.sum(g * normed, axis=0, keepdims=True)
                g = norm_back(normed, rstd, last_ref[...], g)
                grad[here, :] = g
            g_low = low(0.5 * g)
            g_rows[here, :] = g_low
            normed, _ = norm_parts(x_ref[here, :])
            a_rows[here, :] = low(normed * gain_ref[...])
        at[...] = a_rows[...].T
        gt[...] = g_rows[...].T

    w_in = w_ref[0, :, :width]
    w_out = w_ref[0, :, width:]
    for c in range(chunks):
        here = pl.ds(c * tile, tile)
        ds = dot(g_rows[here, :], w_out)
        h = h_ref[0, here, :].astype(F32)
        half = 0.5 * h
        tanh = jnp.tanh(half)
        s = half + half * tanh
        s_rows[here, :] = low(s)
        sig = 0.5 + 0.5 * tanh
        dh = low(ds * (sig + s * (1.0 - sig)))
        d_rows[here, :] = dh
        part = dot_nt(dh, w_in)

        @pl.when(m == 0)
        def _():
            da[here, :] = part

        @pl.when(m != 0)
        def _():
            da[here, :] += part

    dw_ref[0, :, :width] = low(dot(at[...], d_rows[...]))
    dw_ref[0, :, width:] = low(dot(gt[...], s_rows[...]))

    @pl.when(m == pl.num_programs(0) - 1)
    def _():
        dgain_ref[...] = jnp.zeros_like(dgain_ref)
        for c in range(chunks):
            here = pl.ds(c * tile, tile)
            normed, rstd = norm_parts(x_ref[here, :])
            d = da[here, :]
            dgain_ref[...] += jnp.sum(d * normed, axis=0, keepdims=True)
            base = grad[here, :] if final else g_ref[here, :]
            dx_ref[here, :] = base + norm_back(normed, rstd, gain_ref[...], d)


def ffn_backward(g, x, gain, h, w, last=None, final_in=None, ride=None):
    tokens, depth = x.shape
    blocks, _, width = w.shape
    width //= 2
    tile = min(256, tokens)
    full = pl.BlockSpec((tokens, depth), lambda i: (0, 0))
    vec = pl.BlockSpec((1, depth), lambda i: (0, 0))
    vec_shape = jax.ShapeDtypeStruct((1, depth), F32)
    in_specs = [full, full, vec, pl.BlockSpec((1, tokens, width), lambda i: (i, 0, 0)), pl.BlockSpec((1, depth, 2 * width), lambda i: (i, 0, 0))]
    args = [g, x, gain, h, w]
    out_specs = [full, pl.BlockSpec((1, depth, 2 * width), lambda i: (i, 0, 0)), vec]
    out_shape = [jax.ShapeDtypeStruct(x.shape, F32), jax.ShapeDtypeStruct(w.shape, BF16), vec_shape]
    if last is not None:
        in_specs += [vec, full]
        args += [last, final_in]
        out_specs.append(vec)
        out_shape.append(vec_shape)
    return launch(
        functools.partial(ffn_backward_kernel, last is not None, tile),
        grid=(blocks,),
        in_specs=in_specs,
        out_specs=out_specs,
        out_shape=out_shape,
        scratch_shapes=[
            pltpu.VMEM((tokens, depth) if last is not None else (8, 128), F32),
            pltpu.VMEM((depth, tokens), BF16),
            pltpu.VMEM((depth, tokens), BF16),
            pltpu.VMEM((tokens, depth), BF16),
            pltpu.VMEM((tokens, depth), BF16),
            pltpu.VMEM((tokens, width), BF16),
            pltpu.VMEM((tokens, width), BF16),
            pltpu.VMEM((tokens, depth), F32),
        ],
        vmem=56,
        ride=ride,
        args=args,
    )


HEAD = 64
PAIR = 2
LANES = 128


def split_lanes(lanes_ref, here, values):
    for l in range(values.shape[1] // LANES):
        lanes_ref[l, here, :] = values[:, l * LANES : (l + 1) * LANES]


def reorder(lanes_ref, stride, emit):
    blocks, tokens, _ = lanes_ref.shape
    count = tokens // stride
    for start in range(stride):
        for l in range(blocks):
            emit(start * count, l, lanes_ref[l, pl.ds(start, count, stride=stride), :])


def attention_forward_kernel(len_ref, x_ref, gain_ref, w_ref, table_ref, att_ref, q_ref, k_ref, v_ref, o_ref, lse_ref, b_rows, total, bias, flat):
    m = pl.program_id(0)
    tokens = x_ref.shape[0]
    rows = tokens // SEG
    length = len_ref[0]
    tile = 256

    @pl.when(m == 0)
    def _():
        for c in range(tokens // tile):
            here = pl.ds(c * tile, tile)
            normed, _ = norm_parts(x_ref[here, :])
            split_lanes(flat, here, normed * gain_ref[...])

        def emit(start, l, piece):
            b_rows[pl.ds(start, rows), pl.ds(l * LANES, LANES)] = low(piece)

        reorder(flat, SEG, emit)

    wide = PAIR * HEAD
    qkv = dot(b_rows[...], w_ref[0, :, : 3 * wide])
    lane = lax.broadcasted_iota(jnp.int32, (tokens, LANES), 1)
    at = lax.broadcasted_iota(jnp.int32, (tokens, LANES), 0)
    hidden = jnp.where(at < length, 0.0, MASKED)
    for head in range(PAIR):
        cols = pl.ds(head * LANES, LANES)

        def mine(piece):
            return piece if head == 0 else pltpu.roll(piece, HEAD, axis=1)

        q = low(mine(qkv[:, :wide])).astype(F32) * (HEAD**-0.5)
        k = mine(qkv[:, wide : 2 * wide])
        v = mine(qkv[:, 2 * wide :])
        q_ref[0, :, cols] = low(jnp.where(lane < HEAD, q, jnp.where(lane == HEAD, 1.0, 0.0)))
        k_ref[0, :, cols] = low(jnp.where(lane < HEAD, k, jnp.where(lane == HEAD, hidden, jnp.where(lane <= HEAD + 2, -1.0, 0.0))))
        v_ref[0, :, cols] = low(jnp.where(lane < HEAD, v, jnp.where(lane <= HEAD + 1, 1.0, 0.0)))
        span = table_ref.shape[2]
        line = jnp.broadcast_to(table_ref[0, head : head + 1, :], (LANES, span))
        bias[...] = pltpu.roll(line, span - LANES, axis=1, stride=1, stride_axis=0)
        for t in range(tokens // tile):
            here = pl.ds(t * tile, tile)
            scores = dot_nt(q_ref[0, here, cols], k_ref[0, :, cols])
            parts = []
            for sub in range(tile // LANES):
                first = tokens - LANES - t * tile - sub * LANES
                parts.append(scores[sub * LANES : (sub + 1) * LANES] + bias[:, pl.ds(first, tokens)])
            scores = jnp.concatenate(parts, axis=0)
            peak = jnp.max(scores, axis=-1, keepdims=True)
            expos = low(jnp.exp(scores - peak))
            out = dot(expos, v_ref[0, :, cols])
            denom = out[:, HEAD : HEAD + 1]
            out = out * (1.0 / denom)
            lse = peak + jnp.log(denom)
            if head == 0:
                o_ref[0, here, :] = low(out)
            else:
                lane_t = lax.broadcasted_iota(jnp.int32, (tile, LANES), 1)
                o_ref[0, here, :] = low(jnp.where(lane_t < HEAD, o_ref[0, here, :].astype(F32), pltpu.roll(out, HEAD, axis=1)))
            lse_ref[here, :] = jnp.broadcast_to(lse, (tile, LANES))
        lse = lse_ref[...]
        lse_high = low(lse).astype(F32)
        q_now = q_ref[0, :, cols].astype(F32)
        q_ref[0, :, cols] = low(jnp.where(lane == HEAD + 1, lse_high, jnp.where(lane == HEAD + 2, lse - lse_high, q_now)))
    part = dot_nt(o_ref[0], w_ref[0, :, 3 * wide :])

    @pl.when(m == 0)
    def _():
        total[...] = part

    @pl.when(m != 0)
    def _():
        total[...] += part

    @pl.when(m == pl.num_programs(0) - 1)
    def _():
        split_lanes(flat, pl.ds(0, tokens), total[...])

        def emit(start, l, piece):
            att_ref[pl.ds(start, SEG), pl.ds(l * LANES, LANES)] = low(piece * rows_keep(start, SEG, tokens, length))

        reorder(flat, rows, emit)


def attention_forward(length, x, gain, w, table, ride=None):
    tokens, depth = x.shape
    blocks = w.shape[0]
    full = pl.BlockSpec((tokens, depth), lambda i: (0, 0))
    heads = pl.BlockSpec((1, tokens, PAIR * LANES), lambda i: (i, 0, 0))
    pair = pl.BlockSpec((1, tokens, LANES), lambda i: (i, 0, 0))
    heads_shape = jax.ShapeDtypeStruct((blocks, tokens, PAIR * LANES), BF16)
    return launch(
        attention_forward_kernel,
        grid=(blocks,),
        in_specs=[
            pl.BlockSpec(memory_space=pltpu.SMEM),
            full,
            pl.BlockSpec((1, depth), lambda i: (0, 0)),
            pl.BlockSpec((1, depth, w.shape[2]), lambda i: (i, 0, 0)),
            pl.BlockSpec((1, PAIR, table.shape[2]), lambda i: (i, 0, 0)),
        ],
        out_specs=[full, heads, heads, heads, pair],
        out_shape=[
            jax.ShapeDtypeStruct((tokens, depth), BF16),
            heads_shape,
            heads_shape,
            heads_shape,
            jax.ShapeDtypeStruct((blocks, tokens, LANES), BF16),
        ],
        scratch_shapes=[
            pltpu.VMEM((tokens, LANES), F32),
            pltpu.VMEM((tokens, depth), BF16),
            pltpu.VMEM((tokens, depth), F32),
            pltpu.VMEM((LANES, table.shape[2]), F32),
            pltpu.VMEM((depth // LANES, tokens, LANES), F32),
        ],
        vmem=56,
        ride=ride,
        args=(length, x, gain, w, table,),
    )


def attention_backward_kernel(
    datt_ref, x_ref, gain_ref, res_ref, w_ref, table_ref, q_ref, k_ref, v_ref, o_ref,
    dx_ref, dw_ref, dgain_ref, dtable_ref,
    b_t, g_t, g_rows, flat, bias, dbias, do_aug, d_pair, dq_t, k_t, d_rows, db,
):
    m = pl.program_id(0)
    tokens = x_ref.shape[0]
    rows = tokens // SEG
    wide = PAIR * HEAD
    tile = 256
    span = table_ref.shape[2]
    stored = tokens // tile

    @pl.when(m == 0)
    def _():
        def emit(start, l, piece):
            g_rows[pl.ds(start, rows), pl.ds(l * LANES, LANES)] = low(piece)

        for c in range(tokens // tile):
            here = pl.ds(c * tile, tile)
            normed, _ = norm_parts(x_ref[here, :])
            split_lanes(flat, here, normed * gain_ref[...])
        reorder(flat, SEG, emit)
        b_t[...] = g_rows[...].T
        split_lanes(flat, pl.ds(0, tokens), datt_ref[...].astype(F32))
        reorder(flat, SEG, emit)
        g_t[...] = g_rows[...].T

    w_out = w_ref[0, :, 3 * wide :]
    do = low(dot(g_rows[...], w_out))
    dw_ref[0, :, 3 * wide :] = low(dot(g_t[...], o_ref[0]))
    lane = lax.broadcasted_iota(jnp.int32, (tokens, LANES), 1)
    do_full = do.astype(F32)
    product = do_full * o_ref[0].astype(F32)
    for head in range(PAIR):
        cols = pl.ds(head * LANES, LANES)
        inside = lane < HEAD if head == 0 else lane >= HEAD
        delta = jnp.sum(jnp.where(inside, product, 0.0), axis=-1, keepdims=True)
        delta_high = low(delta).astype(F32)
        mine = do_full if head == 0 else pltpu.roll(do_full, HEAD, axis=1)
        do_aug[...] = low(jnp.where(lane < HEAD, mine, jnp.where(lane == HEAD, -delta_high, jnp.where(lane == HEAD + 1, delta_high - delta, 0.0))))
        k_t[...] = k_ref[0, :, cols].T
        line = jnp.broadcast_to(table_ref[0, head : head + 1, :], (LANES, span))
        bias[...] = pltpu.roll(line, span - (LANES - 1), axis=1, stride=1, stride_axis=0)
        dbias[...] = jnp.zeros_like(dbias)
        for t in range(stored):
            here = pl.ds(t * tile, tile)
            scores = dot_nt(k_ref[0, here, cols], q_ref[0, :, cols])
            grads = dot_nt(v_ref[0, here, cols], do_aug[...])
            p_parts = []
            d_parts = []
            for sub in range(tile // LANES):
                first = tokens - LANES - t * tile - sub * LANES
                now = slice(sub * LANES, (sub + 1) * LANES)
                p = jnp.exp(scores[now] + bias[:, pl.ds(first, tokens)])
                ds = low(p * grads[now])
                dbias[:, pl.ds(first, tokens)] += ds.astype(F32)
                p_parts.append(low(p))
                d_parts.append(ds)
            p = jnp.concatenate(p_parts, axis=0)
            ds = jnp.concatenate(d_parts, axis=0)
            dv = dot(p, do_aug[...])
            dk = dot(ds, q_ref[0, :, cols])
            dq = dot(k_t[:, here], ds)
            if t == 0:
                dq_t[...] = dq
            else:
                dq_t[...] += dq
            if head == 0:
                d_pair[1, here, :] = dk
                d_pair[2, here, :] = dv
            else:
                lane_t = lax.broadcasted_iota(jnp.int32, (tile, LANES), 1)
                d_pair[1, here, :] = jnp.where(lane_t < HEAD, d_pair[1, here, :], pltpu.roll(dk, HEAD, axis=1))
                d_pair[2, here, :] = jnp.where(lane_t < HEAD, d_pair[2, here, :], pltpu.roll(dv, HEAD, axis=1))
        dq = dq_t[...].T * (HEAD**-0.5)
        if head == 0:
            d_pair[0] = dq
        else:
            d_pair[0] = jnp.where(lane < HEAD, d_pair[0], pltpu.roll(dq, HEAD, axis=1))
        folded = dbias[...]
        count = LANES
        while count > 1:
            count //= 2
            folded = folded[:count] + pltpu.roll(folded[count:], span - count, axis=1)
        dtable_ref[0, head : head + 1, :] = pltpu.roll(folded, LANES - 1, axis=1)
    for part in range(3):
        d_rows[:, pl.ds(part * wide, wide)] = low(d_pair[part])
    dw_ref[0, :, : 3 * wide] = low(dot(b_t[...], d_rows[...]))
    part = dot_nt(d_rows[...], w_ref[0, :, : 3 * wide])

    @pl.when(m == 0)
    def _():
        db[...] = part

    @pl.when(m != 0)
    def _():
        db[...] += part

    @pl.when(m == pl.num_programs(0) - 1)
    def _():
        dgain_ref[...] = jnp.zeros_like(dgain_ref)
        split_lanes(flat, pl.ds(0, tokens), db[...])

        def emit(start, l, piece):
            db[pl.ds(start, SEG), pl.ds(l * LANES, LANES)] = piece

        reorder(flat, rows, emit)
        for c in range(tokens // tile):
            here = pl.ds(c * tile, tile)
            normed, rstd = norm_parts(x_ref[here, :])
            d = db[here, :]
            dgain_ref[...] += jnp.sum(d * normed, axis=0, keepdims=True)
            dx_ref[here, :] = res_ref[here, :] + norm_back(normed, rstd, gain_ref[...], d)


def attention_backward(datt, x, gain, res, w, table_back, q, k, v, o, ride=None):
    tokens, depth = x.shape
    blocks = w.shape[0]
    span = table_back.shape[2]
    full = pl.BlockSpec((tokens, depth), lambda i: (0, 0))
    heads = pl.BlockSpec((1, tokens, PAIR * LANES), lambda i: (i, 0, 0))
    pair = pl.BlockSpec((1, tokens, LANES), lambda i: (i, 0, 0))
    vec = pl.BlockSpec((1, depth), lambda i: (0, 0))
    w_spec = pl.BlockSpec((1, depth, w.shape[2]), lambda i: (i, 0, 0))
    t_spec = pl.BlockSpec((1, PAIR, span), lambda i: (i, 0, 0))
    wide = PAIR * HEAD
    return launch(
        attention_backward_kernel,
        grid=(blocks,),
        in_specs=[full, full, vec, full, w_spec, t_spec, heads, heads, heads, pair],
        out_specs=[full, w_spec, vec, t_spec],
        out_shape=[
            jax.ShapeDtypeStruct((tokens, depth), F32),
            jax.ShapeDtypeStruct(w.shape, BF16),
            jax.ShapeDtypeStruct((1, depth), F32),
            jax.ShapeDtypeStruct(table_back.shape, F32),
        ],
        scratch_shapes=[
            pltpu.VMEM((depth, tokens), BF16),
            pltpu.VMEM((depth, tokens), BF16),
            pltpu.VMEM((tokens, depth), BF16),
            pltpu.VMEM((depth // LANES, tokens, LANES), F32),
            pltpu.VMEM((LANES, span), F32),
            pltpu.VMEM((LANES, span), F32),
            pltpu.VMEM((tokens, LANES), BF16),
            pltpu.VMEM((3, tokens, LANES), F32),
            pltpu.VMEM((LANES, tokens), F32),
            pltpu.VMEM((LANES, tokens), BF16),
            pltpu.VMEM((tokens, 3 * wide), BF16),
            pltpu.VMEM((tokens, depth), F32),
        ],
        vmem=56,
        ride=ride,
        args=(datt, x, gain, res, w, table_back, q, k, v, o,),
    )


def gate_forward_kernel(
    taps, len_ref, x_ref, gain_ref, w_in_ref, w_out_ref, g_gain_ref, g_conv_ref,
    cg_ref, zr_ref, zg_ref, mean_ref, rstd_ref, conv_ref, gate_ref,
    c_rows, ur_all, ug_all, first, second, total, padded,
):
    i = pl.program_id(0)
    blocks = pl.num_programs(0) // 2
    tokens = x_ref.shape[0]
    rows = tokens // SEG
    width = zr_ref.shape[2]
    tile = 256
    channels = width * blocks
    length = len_ref[0]

    @pl.when(i == 0)
    def _():
        for c in range(tokens // tile):
            here = pl.ds(c * tile, tile)
            normed, _ = norm_parts(x_ref[here, :])
            c_rows[here, :] = low(normed * gain_ref[...])
        first[...] = jnp.zeros_like(first)
        second[...] = jnp.zeros_like(second)

    @pl.when(i < blocks)
    def _():
        for c in range(tokens // tile):
            here = pl.ds(c * tile, tile)
            z = dot(c_rows[here, :], w_in_ref[0])
            zr = z[:, :width]
            zg = z[:, width:]
            zr_ref[0, here, :] = low(zr)
            zg_ref[0, here, :] = low(zg)
            ur_all[i, here, :] = low(gelu(zr))
            ug = gelu(zg)
            ug_all[i, here, :] = low(ug)
            square = ug * ug
            one = ug[:, :LANES]
            two = square[:, :LANES]
            for l in range(1, width // LANES):
                one = one + ug[:, l * LANES : (l + 1) * LANES]
                two = two + square[:, l * LANES : (l + 1) * LANES]
            first[here, :] += one
            second[here, :] += two

    @pl.when(i == blocks - 1)
    def _():
        for c in range(tokens // tile):
            here = pl.ds(c * tile, tile)
            mean = jnp.sum(first[here, :], axis=-1, keepdims=True) / channels
            spread = jnp.sum(second[here, :], axis=-1, keepdims=True) / channels - mean * mean
            mean_ref[here, :] = jnp.broadcast_to(mean, (tile, LANES))
            rstd_ref[here, :] = jnp.broadcast_to(lax.rsqrt(spread + EPSILON), (tile, LANES))

    @pl.when(i >= blocks)
    def _():
        m = i - blocks
        keep = rows_keep(0, tokens, tokens, length)
        scale = rstd_ref[...] * keep
        shift = mean_ref[...] * scale
        for l in range(width // LANES):
            cols = pl.ds(l * LANES, LANES)
            ug = ug_all[m, :, cols].astype(F32)
            n = low((ug * scale - shift) * g_gain_ref[0, :, cols])
            fill_padded(padded, n.reshape(rows, SEG, LANES), taps)

            def taps_of(k):
                return low(jnp.broadcast_to(g_conv_ref[0, k : k + 1, cols], (SEG, LANES)))[None]

            def emit(start, value):
                block = value.shape[0]
                here = pl.ds(pl.multiple_of(start * SEG, block * SEG), block * SEG)
                flat = value.reshape(block * SEG, LANES)
                conv_ref[0, here, cols] = low(flat)
                gate_ref[0, here, cols] = low(ur_all[m, here, cols].astype(F32) * flat)

            convolve(padded, taps_of, taps, rows, 16, emit)
        part = dot_nt(gate_ref[0], w_out_ref[0])

        @pl.when(m == 0)
        def _():
            total[...] = part

        @pl.when(m != 0)
        def _():
            total[...] += part

        @pl.when(m == blocks - 1)
        def _():
            cg_ref[...] = low(total[...] * keep)


def gate_forward(length, x, gain, w, g_gain, g_conv, taps, ride=None):
    tokens, depth = x.shape
    blocks = w.shape[0]
    width = w.shape[2] // 3
    full = pl.BlockSpec((tokens, depth), lambda i: (0, 0))
    lanes = pl.BlockSpec((tokens, LANES), lambda i: (0, 0))

    def early(i):
        return jnp.minimum(i, blocks - 1)

    def late(i):
        return jnp.maximum(i - blocks, 0)

    z_early = pl.BlockSpec((1, tokens, width), lambda i: (early(i), 0, 0))
    z_late = pl.BlockSpec((1, tokens, width), lambda i: (late(i), 0, 0))
    z_shape = jax.ShapeDtypeStruct((blocks, tokens, width), BF16)
    lane_shape = jax.ShapeDtypeStruct((tokens, LANES), F32)
    return launch(
        functools.partial(gate_forward_kernel, taps),
        grid=(2 * blocks,),
        in_specs=[
            pl.BlockSpec(memory_space=pltpu.SMEM),
            full,
            pl.BlockSpec((1, depth), lambda i: (0, 0)),
            pl.BlockSpec((1, depth, 2 * width), lambda i: (early(i), 0, 0)),
            pl.BlockSpec((1, depth, width), lambda i: (late(i), 0, 2)),
            pl.BlockSpec((1, 1, width), lambda i: (late(i), 0, 0)),
            pl.BlockSpec((1, taps, width), lambda i: (late(i), 0, 0)),
        ],
        out_specs=[full, z_early, z_early, lanes, lanes, z_late, z_late],
        out_shape=[jax.ShapeDtypeStruct((tokens, depth), BF16), z_shape, z_shape, lane_shape, lane_shape, z_shape, z_shape],
        scratch_shapes=[
            pltpu.VMEM((tokens, depth), BF16),
            pltpu.VMEM((blocks, tokens, width), BF16),
            pltpu.VMEM((blocks, tokens, width), BF16),
            pltpu.VMEM((tokens, LANES), F32),
            pltpu.VMEM((tokens, LANES), F32),
            pltpu.VMEM((tokens, depth), F32),
            pltpu.VMEM((tokens // SEG + taps - 1, SEG, LANES), BF16),
        ],
        vmem=60,
        ride=ride,
        args=(length, x, gain, w, w, g_gain, g_conv,),
    )


def gate_backward_kernel(
    taps, len_ref, dcg_ref, x_ref, gain_ref, res_ref, w_ref, zr_ref, zg_ref, conv_ref, gate_ref, mean_ref, rstd_ref, g_gain_ref, g_conv_ref,
    dx_ref, dw_ref, dgain_ref, dg_gain_ref, dg_conv_ref,
    c_rows, c_t, g_t, ug_all, slope_all, dn_all, first, second, dc, padded, n_padded, d_rows, dconv, sums,
):
    i = pl.program_id(0)
    blocks = pl.num_programs(0) // 2
    tokens = x_ref.shape[0]
    rows = tokens // SEG
    width = zr_ref.shape[2]
    tile = 256
    channels = width * blocks
    length = len_ref[0]
    chunks = tokens // tile

    @pl.when(i == 0)
    def _():
        for c in range(chunks):
            here = pl.ds(c * tile, tile)
            normed, _ = norm_parts(x_ref[here, :])
            c_rows[here, :] = low(normed * gain_ref[...])
        c_t[...] = c_rows[...].T
        g_t[...] = dcg_ref[...].T
        first[...] = jnp.zeros_like(first)
        second[...] = jnp.zeros_like(second)
        dc[...] = jnp.zeros_like(dc)

    @pl.when(i < blocks)
    def _():
        m = i
        for c in range(chunks):
            here = pl.ds(c * tile, tile)
            dgate = dot(dcg_ref[here, :], w_ref[0, :, 2 * width :])
            ur, slope = gelu_and_slope(zr_ref[0, here, :].astype(F32))
            dzr = low(dgate * conv_ref[0, here, :].astype(F32) * slope)
            d_rows[here, :] = dzr
            dconv[here, :] = low(dgate * ur)
            dc[here, :] += dot_nt(dzr, w_ref[0, :, :width])
            ug, slope = gelu_and_slope(zg_ref[0, here, :].astype(F32))
            ug_all[m, here, :] = low(ug)
            slope_all[m, here, :] = low(slope)
        dw_ref[m, :, :width] = low(dot(c_t[...], d_rows[...]))
        dw_ref[m, :, 2 * width :] = low(dot(g_t[...], gate_ref[0]))
        keep = rows_keep(0, tokens, tokens, length)
        rstd = rstd_ref[...]
        shift = mean_ref[...] * rstd
        for l in range(width // LANES):
            cols = pl.ds(l * LANES, LANES)
            ug = ug_all[m, :, cols].astype(F32)
            n = low((ug * rstd - shift) * (g_gain_ref[0, :, cols] * keep))
            fill_padded(n_padded, n.reshape(rows, SEG, LANES), taps)
            d = dconv[:, cols].reshape(rows, SEG, LANES)
            fill_padded(padded, d, taps)
            tap_grads(n_padded, padded.at[pl.ds((taps - 1) // 2, rows)], sums, taps, rows, 8)
            dg_conv_ref[0, :, cols] = jnp.sum(sums[...], axis=1)
            dg_gain_ref[0, :, cols] = jnp.zeros((1, LANES), F32)

            def taps_of(k):
                return low(jnp.broadcast_to(g_conv_ref[0, taps - 1 - k : taps - k, cols], (SEG, LANES)))[None]

            def emit(start, value):
                block = value.shape[0]
                here = pl.ds(pl.multiple_of(start * SEG, block * SEG), block * SEG)
                dn = value.reshape(block * SEG, LANES) * rows_keep(start * SEG, block * SEG, tokens, length)
                normed = ug_all[m, here, cols].astype(F32) * rstd_ref[here, :] - mean_ref[here, :] * rstd_ref[here, :]
                product = dn * normed
                dg_gain_ref[0, :, cols] += jnp.sum(product, axis=0, keepdims=True)
                scaled = dn * g_gain_ref[0, :, cols]
                dn_all[m, here, cols] = low(scaled)
                first[here, :] += scaled
                second[here, :] += product * g_gain_ref[0, :, cols]

            convolve(padded, taps_of, taps, rows, 16, emit)

    @pl.when(i == blocks - 1)
    def _():
        for c in range(chunks):
            here = pl.ds(c * tile, tile)
            one = jnp.sum(first[here, :], axis=-1, keepdims=True) / channels
            two = jnp.sum(second[here, :], axis=-1, keepdims=True) / channels
            first[here, :] = jnp.broadcast_to(one, (tile, LANES))
            second[here, :] = jnp.broadcast_to(two, (tile, LANES))

    @pl.when(i >= blocks)
    def _():
        m = i - blocks
        for c in range(chunks):
            here = pl.ds(c * tile, tile)
            rstd = rstd_ref[here, :]
            shift = mean_ref[here, :] * rstd
            one = first[here, :]
            two = second[here, :]
            for l in range(width // LANES):
                cols = pl.ds(l * LANES, LANES)
                normed = ug_all[m, here, cols].astype(F32) * rstd - shift
                dug = rstd * (dn_all[m, here, cols].astype(F32) - one - normed * two)
                d_rows[here, cols] = low(dug * slope_all[m, here, cols].astype(F32))
            dc[here, :] += dot_nt(d_rows[here, :], w_ref[0, :, width : 2 * width])
        dw_ref[m, :, width : 2 * width] = low(dot(c_t[...], d_rows[...]))

    @pl.when(i == 2 * blocks - 1)
    def _():
        dgain_ref[...] = jnp.zeros_like(dgain_ref)
        for c in range(chunks):
            here = pl.ds(c * tile, tile)
            normed, rstd = norm_parts(x_ref[here, :])
            d = dc[here, :]
            dgain_ref[...] += jnp.sum(d * normed, axis=0, keepdims=True)
            dx_ref[here, :] = res_ref[here, :] + norm_back(normed, rstd, gain_ref[...], d)


def gate_backward(length, dcg, x, gain, res, w, zr, zg, conv, gate, mean, rstd, g_gain, g_conv, taps, ride=None):
    tokens, depth = x.shape
    blocks = w.shape[0]
    width = w.shape[2] // 3
    full = pl.BlockSpec((tokens, depth), lambda i: (0, 0))
    lanes = pl.BlockSpec((tokens, LANES), lambda i: (0, 0))
    vec = pl.BlockSpec((1, depth), lambda i: (0, 0))

    def early(i):
        return jnp.minimum(i, blocks - 1)

    z_early = pl.BlockSpec((1, tokens, width), lambda i: (early(i), 0, 0))
    gain_spec = pl.BlockSpec((1, 1, width), lambda i: (early(i), 0, 0))
    conv_spec = pl.BlockSpec((1, taps, width), lambda i: (early(i), 0, 0))
    padded = (tokens // SEG + taps - 1, SEG, LANES)
    return launch(
        functools.partial(gate_backward_kernel, taps),
        grid=(2 * blocks,),
        in_specs=[
            pl.BlockSpec(memory_space=pltpu.SMEM),
            full,
            full,
            vec,
            full,
            pl.BlockSpec((1, depth, 3 * width), lambda i: (lax.rem(i, blocks), 0, 0)),
            z_early,
            z_early,
            z_early,
            z_early,
            lanes,
            lanes,
            gain_spec,
            conv_spec,
        ],
        out_specs=[full, pl.BlockSpec(w.shape, lambda i: (0, 0, 0)), vec, gain_spec, conv_spec],
        out_shape=[
            jax.ShapeDtypeStruct((tokens, depth), F32),
            jax.ShapeDtypeStruct(w.shape, BF16),
            jax.ShapeDtypeStruct((1, depth), F32),
            jax.ShapeDtypeStruct(g_gain.shape, F32),
            jax.ShapeDtypeStruct(g_conv.shape, F32),
        ],
        scratch_shapes=[
            pltpu.VMEM((tokens, depth), BF16),
            pltpu.VMEM((depth, tokens), BF16),
            pltpu.VMEM((depth, tokens), BF16),
            pltpu.VMEM((blocks, tokens, width), BF16),
            pltpu.VMEM((blocks, tokens, width), BF16),
            pltpu.VMEM((blocks, tokens, width), BF16),
            pltpu.VMEM((tokens, LANES), F32),
            pltpu.VMEM((tokens, LANES), F32),
            pltpu.VMEM((tokens, depth), F32),
            pltpu.VMEM(padded, BF16),
            pltpu.VMEM(padded, BF16),
            pltpu.VMEM((tokens, width), BF16),
            pltpu.VMEM((tokens, width), BF16),
            pltpu.VMEM((taps, SEG, LANES), F32),
        ],
        vmem=60,
        ride=ride,
        args=(length, dcg, x, gain, res, w, zr, zg, conv, gate, mean, rstd, g_gain, g_conv,),
    )


def merge_forward_kernel(taps, x_ref, att_ref, cg_ref, w_ref, m_conv_ref, out_ref, merged_ref, padded):
    c = pl.program_id(0)
    tokens = x_ref.shape[0]
    rows = tokens // SEG
    half = pl.num_programs(0) // 2
    width = merged_ref.shape[1]
    for l in range(width // LANES):
        cols = pl.ds(l * LANES, LANES)

        @pl.when(c < half)
        def _():
            fill_padded(padded, att_ref[:, cols].reshape(rows, SEG, LANES), taps)

        @pl.when(c >= half)
        def _():
            fill_padded(padded, cg_ref[:, cols].reshape(rows, SEG, LANES), taps)

        def taps_of(k):
            return low(jnp.broadcast_to(m_conv_ref[k : k + 1, cols], (SEG, LANES)))[None]

        def emit(start, value):
            block = value.shape[0]
            here = pl.ds(pl.multiple_of(start * SEG, block * SEG), block * SEG)
            value = value + padded[pl.ds(start + (taps - 1) // 2, block)].astype(F32)
            merged_ref[here, cols] = low(value.reshape(block * SEG, LANES))

        convolve(padded, taps_of, taps, rows, 16, emit)
    w = jnp.concatenate([w_ref[m] for m in range(w_ref.shape[0])], axis=1)
    part = dot(merged_ref[...], w)

    @pl.when(c == 0)
    def _():
        out_ref[...] = x_ref[...] + part

    @pl.when(c != 0)
    def _():
        out_ref[...] += part


def merge_forward(x, att, cg, w, m_conv, ride=None):
    tokens, depth = x.shape
    blocks, both, cols = w.shape
    taps = m_conv.shape[0]
    width = 256
    steps = both // width
    half = steps // 2
    full = pl.BlockSpec((tokens, depth), lambda i: (0, 0))
    return launch(
        functools.partial(merge_forward_kernel, taps),
        grid=(steps,),
        in_specs=[
            full,
            pl.BlockSpec((tokens, width), lambda i: (0, jnp.minimum(i, half - 1))),
            pl.BlockSpec((tokens, width), lambda i: (0, jnp.maximum(i - half, 0))),
            pl.BlockSpec((blocks, width, cols), lambda i: (0, i, 0)),
            pl.BlockSpec((taps, width), lambda i: (0, i)),
        ],
        out_specs=[full, pl.BlockSpec((tokens, width), lambda i: (0, i))],
        out_shape=[jax.ShapeDtypeStruct(x.shape, F32), jax.ShapeDtypeStruct((tokens, both), BF16)],
        scratch_shapes=[pltpu.VMEM((tokens // SEG + taps - 1, SEG, LANES), BF16)],
        vmem=56,
        ride=ride,
        args=(x, att, cg, w, m_conv,),
    )


def merge_backward_kernel(taps, len_ref, g_ref, att_ref, cg_ref, merged_ref, w_ref, m_conv_ref, datt_ref, dcg_ref, dw_ref, dconv_ref, g_rows, padded, j_padded, out, sums):
    c = pl.program_id(0)
    tokens = g_ref.shape[0]
    rows = tokens // SEG
    half = pl.num_programs(0) // 2
    blocks, width, narrow = w_ref.shape
    length = len_ref[0]

    @pl.when(c == 0)
    def _():
        g_rows[...] = low(g_ref[...])

    w = jnp.concatenate([w_ref[m] for m in range(blocks)], axis=1)
    dmerged = low(dot_nt(g_rows[...], w))
    dw = dot(merged_ref[...].T, g_rows[...])
    for m in range(blocks):
        dw_ref[m] = low(dw[:, m * narrow : (m + 1) * narrow])
    for l in range(width // LANES):
        cols = pl.ds(l * LANES, LANES)

        @pl.when(c < half)
        def _():
            fill_padded(j_padded, att_ref[:, cols].reshape(rows, SEG, LANES), taps)

        @pl.when(c >= half)
        def _():
            fill_padded(j_padded, cg_ref[:, cols].reshape(rows, SEG, LANES), taps)

        fill_padded(padded, dmerged[:, l * LANES : (l + 1) * LANES].reshape(rows, SEG, LANES), taps)
        tap_grads(j_padded, padded.at[pl.ds((taps - 1) // 2, rows)], sums, taps, rows, 8)
        dconv_ref[:, cols] = jnp.sum(sums[...], axis=1)

        def taps_of(k):
            return low(jnp.broadcast_to(m_conv_ref[taps - 1 - k : taps - k, cols], (SEG, LANES)))[None]

        def emit(start, value):
            block = value.shape[0]
            here = pl.ds(pl.multiple_of(start * SEG, block * SEG), block * SEG)
            value = value + padded[pl.ds(start + (taps - 1) // 2, block)].astype(F32)
            out[here, cols] = low(value.reshape(block * SEG, LANES) * rows_keep(start * SEG, block * SEG, tokens, length))

        convolve(padded, taps_of, taps, rows, 16, emit)

    @pl.when(c < half)
    def _():
        datt_ref[...] = out[...]

    @pl.when(c >= half)
    def _():
        dcg_ref[...] = out[...]


def merge_backward(length, g, att, cg, merged, w, m_conv, ride=None):
    tokens, depth = g.shape
    blocks, both, cols = w.shape
    taps = m_conv.shape[0]
    width = 256
    steps = both // width
    half = steps // 2
    full = pl.BlockSpec((tokens, depth), lambda i: (0, 0))
    early = pl.BlockSpec((tokens, width), lambda i: (0, jnp.minimum(i, half - 1)))
    late = pl.BlockSpec((tokens, width), lambda i: (0, jnp.maximum(i - half, 0)))
    wide = pl.BlockSpec((tokens, width), lambda i: (0, i))
    w_spec = pl.BlockSpec((blocks, width, cols), lambda i: (0, i, 0))
    conv_spec = pl.BlockSpec((taps, width), lambda i: (0, i))
    padded = (tokens // SEG + taps - 1, SEG, LANES)
    return launch(
        functools.partial(merge_backward_kernel, taps),
        grid=(steps,),
        in_specs=[pl.BlockSpec(memory_space=pltpu.SMEM), full, early, late, wide, w_spec, conv_spec],
        out_specs=[early, late, w_spec, conv_spec],
        out_shape=[
            jax.ShapeDtypeStruct((tokens, depth), BF16),
            jax.ShapeDtypeStruct((tokens, depth), BF16),
            jax.ShapeDtypeStruct(w.shape, BF16),
            jax.ShapeDtypeStruct(m_conv.shape, F32),
        ],
        scratch_shapes=[
            pltpu.VMEM((tokens, depth), BF16),
            pltpu.VMEM(padded, BF16),
            pltpu.VMEM(padded, BF16),
            pltpu.VMEM((tokens, width), BF16),
            pltpu.VMEM((taps, SEG, LANES), F32),
        ],
        vmem=56,
        ride=ride,
        args=(length, g, att, cg, merged, w, m_conv,),
    )


def no_ride(index):
    return None


def layer_forward(x, length, weights, small, ride=no_ride):
    gains, table, g_gain, g_conv, m_conv = small
    taps = m_conv.shape[0]
    x1, h1 = ffn_forward(x, gains[0:1], weights(0), ride=ride(0))
    att, q, k, v, o = attention_forward(length, x1, gains[1:2], weights(1), table, ride=ride(1))
    cg, zr, zg, mean, rstd, conv, gate = gate_forward(length, x1, gains[2:3], weights(2), g_gain, g_conv, taps, ride=ride(2))
    x2, merged = merge_forward(x1, att, cg, weights(3), m_conv, ride=ride(3))
    x3, h2, y = ffn_forward(x2, gains[3:4], weights(4), gains[4:5], ride=ride(4))
    saved = (x, x1, h1, att, q, k, v, o, cg, zr, zg, mean, rstd, conv, gate, x2, merged, x3, h2)
    return y, saved


def layer_backward(g, length, saved, weights, small, ride=no_ride, ready=lambda index, grad: None, before_last=lambda *_: None):
    gains, table, g_gain, g_conv, m_conv = small
    taps = m_conv.shape[0]
    x, x1, h1, att, q, k, v, o, cg, zr, zg, mean, rstd, conv, gate, x2, merged, x3, h2 = saved
    dx2, dg5, dgain3, dgain4 = ffn_backward(g, x2, gains[3:4], h2, weights(4), gains[4:5], x3, ride=ride(4))
    ready(4, dg5)
    datt, dcg, dg4, dm_conv = merge_backward(length, dx2, att, cg, merged, weights(3), m_conv, ride=ride(3))
    ready(3, dg4)
    dx1, dg3, dgain2, dg_gain, dg_conv = gate_backward(
        length, dcg, x1, gains[2:3], dx2, weights(2), zr, zg, conv, gate, mean, rstd, g_gain, g_conv, taps, ride=ride(2)
    )
    ready(2, dg3)
    dx1, dg2, dgain1, dtable = attention_backward(datt, x1, gains[1:2], dx1, weights(1), table[:, :, ::-1], q, k, v, o, ride=ride(1))
    ready(1, dg2)
    dgains = jnp.concatenate([dgain1, dgain2, dgain3, dgain4], axis=0)
    before_last(0, dgains, (dtable[:, :, ::-1], dg_gain, dg_conv, dm_conv))
    dx, dg1, dgain0 = ffn_backward(dx1, x, gains[0:1], h1, weights(0), ride=ride(0))
    ready(0, dg1)
    return dx, dgain0


def to_segments(values):
    tokens, depth = values.shape
    return values.reshape(SEG, tokens // SEG, depth).transpose(1, 0, 2).reshape(tokens, depth)


def from_segments(values):
    tokens, depth = values.shape
    return values.reshape(tokens // SEG, SEG, depth).transpose(1, 0, 2).reshape(tokens, depth)


def pack_layer(layer, ffn_in, ffn_out, attn_in, attn_out, cg_in, cg_out, merge_out, mp_index, mp_size):
    cols = merge_out.shape[2] // mp_size
    part = lax.dynamic_slice_in_dim(merge_out[layer], mp_index * cols, cols, axis=1)
    pieces = (
        jnp.concatenate([ffn_in[layer, 0], ffn_out[layer, 0].T], axis=1),
        jnp.concatenate([attn_in[layer, 0], attn_in[layer, 1], attn_in[layer, 2], attn_out[layer].T], axis=1),
        jnp.concatenate([cg_in[layer, 0], cg_in[layer, 1], cg_out[layer].T], axis=1),
        part,
        jnp.concatenate([ffn_in[layer, 1], ffn_out[layer, 1].T], axis=1),
    )
    return tuple(low(piece) for piece in pieces)


GROUPS = 5
OPENING = [(0, [("line", 0), (0, 0)]), (1, [(0, 1), (1, 0)]), (2, [(0, 2), (1, 1), (2, 0)]), (3, [(0, 3), (1, 2)])]
FORWARD = {
    0: [(0, [(1, 3), (2, 1), (3, 0)]), (2, [(4, 0)])],
    1: [(0, [(2, 2), (5, 0)]), (3, [(2, 3), (3, 1), (4, 1)])],
    2: [(0, [(4, 2), (3, 2), (6, 0)]), (4, [(4, 3), (3, 3), (5, 1), (7, 0)])],
    3: [(0, [(5, 2), (8, 0)]), (3, [(5, 3), (6, 1)])],
    4: [(0, [(6, 2), (7, 1)]), (2, [(6, 3), (9, 0)])],
    5: [(0, [(7, 2)])],
    6: [(0, [(7, 3), (8, 1), (9, 1)]), (2, [(8, 2), (9, 2)])],
    7: [(0, [(8, 3), (9, 3)])],
}
BACKWARD = {
    8: [(0, [(9, 0)]), (1, [(9, 1)])],
    7: [(0, [(9, 2), (8, 0)]), (1, [(9, 3), (8, 1)]), (2, [(8, 2)]), (3, [(8, 3)])],
    6: [(0, [(7, 0)]), (1, [(7, 1)]), (3, [(7, 2)])],
    5: [(0, [(7, 3), (6, 0)]), (2, [(6, 1)])],
    4: [(0, [(6, 2), (5, 0)]), (1, [(6, 3), (5, 1)])],
    3: [(0, [(5, 2), (4, 0)]), (1, [(5, 3), (4, 1)])],
    2: [(0, [(4, 2), (3, 0)]), (1, [(4, 3), (3, 1)]), (2, [(3, 2)]), (3, [(3, 3)])],
    1: [(0, [(2, 0)]), (1, [(2, 1)]), (3, [(2, 2)])],
    0: [(0, [(2, 3), (1, 0), ("small", 0)]), (1, [(1, 1), ("small", 1)]), (2, [("small", 2)]), (3, [("small", 3)])],
}
CLOSING = [
    (0, [(0, 0), (1, 2), ("all", 0), ("vector", 0), ("merge", 0)]),
    (1, [(0, 1), (1, 3), ("all", 1), ("vector", 1)]),
    (2, [(0, 2), ("all", 2), ("vector", 2)]),
    (3, [(0, 3), ("all", 3), ("vector", 3)]),
]


def plans(bits, groups):
    if bits == 3 and groups == 2 * GROUPS:
        return OPENING, FORWARD, BACKWARD, CLOSING
    count = groups + bits
    opening = [(r, [(g, r - g) for g in range(groups) if 0 <= r - g <= bits] + ([("line", 0)] if r == 0 else [])) for r in range(count)]
    small = [(r, [("small", r)]) for r in range(bits + 1)]
    closing = [(r, [(g, r - g) for g in range(groups) if 0 <= r - g <= bits]) for r in range(count)]
    for s in range(bits + 1):
        closing[s][1].extend([("all", s), ("vector", s)])
    closing.append((count, [("merge", 0)]))
    return opening, {}, {"small": small}, closing


def body(frames, cotangent, lengths, norm_gains, ffn_in, ffn_out, attn_in, attn_out, rel_bias, cg_in, csgu_gain, csgu_conv, cg_out, merge_conv, merge_out):
    layers = norm_gains.shape[0]
    mp_size = lax.axis_size("mp")
    bits = lax.axis_size("dp").bit_length() - 1
    mp_index = lax.axis_index("mp")
    length = lax.dynamic_slice_in_dim(lengths, mp_index, 1)
    tokens, depth = frames.shape
    taps = merge_conv.shape[1]
    heads, span = rel_bias.shape[1:]
    channels = csgu_gain.shape[1]

    flow = {}
    ids = iter(range(1, 100))

    def ride(plan):
        return Ride(flow, mp_size, bits, next(ids), plan)

    def alone(plan):
        launch(None, (len(plan),), [], [], [], vmem=62, ride=ride(plan))

    shards = []
    for layer in range(layers):
        shards += pack_layer(layer, ffn_in, ffn_out, attn_in, attn_out, cg_in, cg_out, merge_out, mp_index, mp_size)
    line = jnp.concatenate([rel_bias.reshape(layers, -1), csgu_gain, csgu_conv.reshape(layers, -1)], axis=1)
    line = line.reshape(-1, LANES)
    kinds = [Gather(mp_size, bits) for _ in shards] + [Gather(mp_size, bits, True)]
    names = list(range(len(shards))) + ["line"]
    for name, kind, buffer in zip(names, kinds, start_buffers(shards + [line], kinds, mp_size, bits)):
        flow[name] = (kind, buffer)
    opening, forward, backward, closing = plans(bits, len(shards))
    alone(opening)
    line_all = flow["line"][1].reshape(mp_size, layers, -1)
    table = line_all[:, :, : heads * span].reshape(mp_size, layers, heads, span)
    g_gain = line_all[:, :, heads * span : heads * span + channels].reshape(mp_size, layers, 1, channels)
    g_conv = line_all[:, :, heads * span + channels :].reshape(mp_size, layers, taps, channels)

    state = to_segments(frames).astype(F32)
    weights = {}
    smalls = []
    saved = []
    for layer in range(layers):

        def weight(index):
            at = layer * GROUPS + index
            if at not in weights:
                w = flow[at][1]
                weights[at] = w.reshape(mp_size, -1, w.shape[-1])
            return weights[at]

        def beside(index):
            at = layer * GROUPS + index
            return ride(forward[at]) if at in forward else None

        smalls.append((norm_gains[layer], table[:, layer], g_gain[:, layer], g_conv[:, layer], merge_conv[layer]))
        state, kept = layer_forward(state, length, weight, smalls[layer], beside)
        saved.append(kept)
    frame = lax.broadcasted_iota(jnp.int32, (tokens, 1), 0)
    keep = (frame < length).astype(F32)
    output_frames = from_segments(state) * keep
    incoming = to_segments(cotangent.astype(F32) * keep)
    tiny = [None] * layers
    counts = []

    def pack_small():
        split = [jnp.concatenate([t[1].reshape(mp_size, -1), t[2].reshape(mp_size, -1), t[3].reshape(mp_size, -1)], axis=1) for t in tiny]
        split = jnp.concatenate(split, axis=1).reshape(mp_size, -1, LANES)
        shared = jnp.concatenate([t[0].reshape(-1) for t in tiny] + [t[4].reshape(-1) for t in tiny])
        shared = jnp.pad(shared, (0, -shared.size % (mp_size * LANES))).reshape(mp_size, -1, LANES)
        counts.extend([split.shape[1], shared.shape[1]])
        padding = -sum(counts) % (16 << bits)
        packed = low(jnp.concatenate([split, shared, jnp.zeros((mp_size, padding, LANES), F32)], axis=1))
        packed = packed.reshape((mp_size,) + (2,) * bits + (-1, LANES))
        flow["small"] = (Scatter(mp_size, bits, *packed.shape[-2:]), packed)
        if "small" in backward:
            alone(backward["small"])

    for layer in reversed(range(layers)):

        def weight(index):
            return weights[layer * GROUPS + index]

        def beside(index):
            at = layer * GROUPS + index
            return ride(backward[at]) if at in backward else None

        def ready(index, grad):
            grad = grad.reshape((mp_size,) + (2,) * bits + (-1, grad.shape[-1]))
            flow[layer * GROUPS + index] = (Scatter(mp_size, bits, *grad.shape[-2:]), grad)

        def before_last(index, gains, small):
            tiny[layer] = (gains, *small)
            if layer == 0:
                pack_small()

        incoming, last_gain = layer_backward(incoming, length, saved[layer], weight, smalls[layer], beside, ready, before_last)
        if layer > 0:
            tiny[layer] = (jnp.concatenate([last_gain, tiny[layer][0]], axis=0), *tiny[layer][1:])
    vector = jnp.pad(last_gain.reshape(-1, LANES), ((0, -(depth // LANES) % 8), (0, 0)))
    kinds = [Gather(mp_size, bits), Gather(mp_size, bits)]
    flow["all"], flow["vector"] = zip(kinds, start_buffers([low(flow["small"][1]), vector], kinds, mp_size, bits))

    def start_merge():
        line = low(jnp.concatenate([flow[layer * GROUPS + 3][1] for layer in range(layers)], axis=0))
        kind = Gather(mp_size, bits, True)
        flow["merge"] = (kind, start_buffers([line], [kind], mp_size, bits)[0])

    if closing[-1][1] == [("merge", 0)]:
        alone(closing[:-1])
        start_merge()
        alone([(0, closing[-1][1])])
    else:
        start_merge()
        alone(closing)
    input_grad = from_segments(incoming)

    big = [flow[at][1] for at in range(layers * GROUPS)]
    packed = flow["all"][1].reshape(mp_size, -1, LANES).astype(F32)
    split_rows, shared_rows = counts
    split = lax.dynamic_index_in_dim(packed, mp_index, 0, keepdims=False)[:split_rows].reshape(layers, -1)
    grad_table = split[:, : heads * span].reshape(layers, heads, span)
    grad_g_gain = split[:, heads * span : heads * span + channels]
    grad_g_conv = split[:, heads * span + channels :].reshape(layers, taps, channels)
    shared = packed[:, split_rows : split_rows + shared_rows].reshape(-1)
    grad_gains = shared[: norm_gains.size - depth]
    vector = jnp.sum(flow["vector"][1].reshape(-1, flow["vector"][1].shape[-2] * LANES), axis=0)[:depth]
    grad_gains = jnp.concatenate([vector, grad_gains]).reshape(norm_gains.shape)
    grad_m_conv = shared[norm_gains.size - depth :][: merge_conv.size].reshape(merge_conv.shape)
    merge_all = flow["merge"][1].astype(F32).reshape(mp_size, layers, -1, LANES)
    grad_merge = merge_all.transpose(1, 2, 0, 3).reshape(merge_out.shape)

    f = ffn_in.shape[3]
    h = attn_in.shape[3]
    c = cg_in.shape[3]
    one, two, three, _, five = [[big[layer * GROUPS + g] for layer in range(layers)] for g in range(GROUPS)]
    grad_ffn_in = jnp.stack([jnp.stack([a[:, :f], b[:, :f]]) for a, b in zip(one, five)])
    grad_ffn_out = jnp.stack([jnp.stack([a[:, f:].T, b[:, f:].T]) for a, b in zip(one, five)])
    grad_attn_in = jnp.stack([jnp.stack([a[:, :h], a[:, h : 2 * h], a[:, 2 * h : 3 * h]]) for a in two])
    grad_attn_out = jnp.stack([a[:, 3 * h :].T for a in two])
    grad_cg_in = jnp.stack([jnp.stack([a[:, :c], a[:, c : 2 * c]]) for a in three])
    grad_cg_out = jnp.stack([a[:, 2 * c :].T for a in three])
    return (
        output_frames,
        input_grad,
        grad_gains,
        grad_ffn_in,
        grad_ffn_out,
        grad_attn_in,
        grad_attn_out,
        grad_table,
        grad_cg_in,
        grad_g_gain,
        grad_g_conv,
        grad_cg_out,
        grad_m_conv,
        grad_merge,
    )


def solution(mesh):
    tokens = P(("dp", "mp"), None)
    columns = P(None, None, "dp", "mp")
    rows = P(None, "mp", "dp")
    ffn_rows = P(None, None, "mp", "dp")
    heads = P(None, "mp", None)
    taps = P(None, None, "mp")
    return jax.shard_map(
        body,
        mesh=mesh,
        in_specs=(tokens, tokens, P("dp"), P(), columns, ffn_rows, columns, rows, heads, columns, P(None, "mp"), taps, rows, P(), P(None, "dp", None)),
        out_specs=(tokens, tokens, P(), columns, ffn_rows, columns, rows, heads, columns, P(None, "mp"), taps, rows, P(), P(None, "dp", None)),
        check_vma=False,
    )
```

```python
import functools

import jax
import jax.numpy as jnp
from jax import lax
from jax.experimental import pallas as pl
from jax.experimental.pallas import tpu as pltpu
from jax.sharding import PartitionSpec as P

EPSILON = 1e-05
MASKED = -1000000000.0
F32 = jnp.float32
BF16 = jnp.bfloat16
SEG = 16
GELU_A = 0.7978845608028654
GELU_B = 0.044715
HEAD = 64
PAIR = 2
LANES = 128


def dot(left, right):
    return lax.dot_general(left, right, (((1,), (0,)), ((), ())), preferred_element_type=F32)


def dot_nt(left, right):
    return lax.dot_general(left, right, (((1,), (1,)), ((), ())), preferred_element_type=F32)


def low(values):
    return values.astype(BF16)


def norm_parts(values):
    mean = jnp.mean(values, axis=-1, keepdims=True)
    centred = values - mean
    spread = jnp.mean(centred * centred, axis=-1, keepdims=True)
    rstd = lax.rsqrt(spread + EPSILON)
    return centred * rstd, rstd


def norm_back(normed, rstd, gain, grad):
    scaled = grad * gain
    first = jnp.mean(scaled, axis=-1, keepdims=True)
    second = jnp.mean(scaled * normed, axis=-1, keepdims=True)
    return rstd * (scaled - first - normed * second)


def gelu(values):
    half = 0.5 * values
    inner = values * (GELU_A + (GELU_A * GELU_B) * (values * values))
    return half + half * jnp.tanh(inner)


def gelu_and_slope(values):
    half = 0.5 * values
    square = values * values
    tanh = jnp.tanh(values * (GELU_A + (GELU_A * GELU_B) * square))
    value = half + half * tanh
    slope = 0.5 + 0.5 * tanh + (half - half * tanh * tanh) * (GELU_A + (3.0 * GELU_A * GELU_B) * square)
    return value, slope


def keep_lanes(length, tokens):
    at = lax.broadcasted_iota(jnp.int32, (tokens, LANES), 0)
    frame = (at % SEG) * (tokens // SEG) + at // SEG
    return (frame < length).astype(F32)


MESH = pl.DeviceIdType.MESH


class Links:
    def __init__(self, mp, bits, send, recv):
        self.mp = mp
        self.bits = bits
        self.me = lax.axis_index("mp")
        self.dp = lax.axis_index("dp")
        self.bit = [lax.rem(self.dp // (1 << i), 2) for i in range(bits)]
        self.send, self.recv = send, recv

    def other(self, i):
        return {"dp": self.dp + (1 - 2 * self.bit[i]) * (1 << i)}

    def along(self, offset):
        return {"mp": lax.rem(self.me + offset, self.mp)}

    def before(self, offset):
        return lax.rem(self.me + self.mp - offset, self.mp)

    def barrier(self):
        peers = [self.other(i) for i in range(self.bits)] + [self.along(offset) for offset in range(1, self.mp)]
        semaphore = pltpu.get_barrier_semaphore()
        for peer in peers:
            pl.semaphore_signal(semaphore, inc=1, device_id=peer, device_id_type=MESH)
        pl.semaphore_wait(semaphore, len(peers))

    def copy(self, at, source, target, arrives, device):
        def make(where):
            return pltpu.make_async_remote_copy(
                src_ref=source, dst_ref=where, send_sem=self.send.at[at], recv_sem=self.recv.at[at], device_id=device, device_id_type=MESH
            )

        return lambda: make(target), lambda: make(arrives)


def orders(bits):
    rest = list(range(1, bits))
    return rest + [0], rest[::-1] + [0]


def halves(mp):
    return (pl.ds(0, mp // 2), pl.ds(mp // 2, mp // 2))


class Gather:
    def __init__(self, mp, bits, line=False):
        self.mp, self.bits, self.line = mp, bits, line

    def copies(self, s):
        return self.mp - 1 if s == 0 else 1 if s == self.bits else 2

    def at(self, links, buffer, m, free, flip=None):
        index = [m]
        if not self.line:
            for i in reversed(range(self.bits)):
                index.append(pl.ds(0, 2) if i in free else 1 - links.bit[i] if i == flip else links.bit[i])
        return buffer.at[tuple(index)]

    def pairs(self, links, buffer, s, base):
        made = []

        def add(m, arriving, free, flip, device):
            mine = self.at(links, buffer, m, free)
            made.append(links.copy(base + len(made), mine, mine, self.at(links, buffer, arriving, free, flip), device))

        if s == 0:
            for offset in range(1, self.mp):
                add(links.me, links.before(offset), (), None, links.along(offset))
        elif s == self.bits:
            whole = pl.ds(0, self.mp)
            add(whole, whole, range(1, self.bits), 0, links.other(0))
        else:
            for half, order in zip(halves(self.mp), orders(self.bits)):
                add(half, half, order[: s - 1], order[s - 1], links.other(order[s - 1]))
        return made


class Scatter:
    def __init__(self, mp, bits, rows, cols):
        self.mp, self.bits, self.rows, self.cols = mp, bits, rows, cols

    def shape(self, s):
        return (self.mp,) + (2,) * (self.bits - s) + (self.rows, self.cols)

    def arrived(self, s):
        return self.shape(s + 1) if s < self.bits else self.shape(s)

    def own(self, s):
        return self.arrived(s) if s < self.bits else (self.rows, self.cols)

    def copies(self, s):
        return 1 if s == 0 else self.mp - 1 if s == self.bits else 2

    def loads(self, s):
        return 2 if 0 < s < self.bits else 1

    def parts(self, s):
        if s == 0:
            return [(pl.ds(0, self.mp), list(range(self.bits))[::-1], 0)]
        made = []
        for half, order in zip(halves(self.mp), orders(self.bits)):
            made.append((half, sorted(order[: self.bits - s], reverse=True), order[self.bits - 1 - s]))
        return made

    def pick(self, links, ref, m, left, now, flip):
        index = [m]
        for i in left:
            index.append(pl.ds(0, 2) if i != now else 1 - links.bit[i] if flip else links.bit[i])
        return ref.at[tuple(index)]

    def pairs(self, links, held, slots, s, base):
        made = []
        if s < self.bits:
            for m, left, now in self.parts(s):
                slot = slots.at[m]
                made.append(links.copy(base + len(made), self.pick(links, held, m, left, now, True), slot, slot, links.other(now)))
        else:
            for offset in range(1, self.mp):
                to = lax.rem(links.me + offset, self.mp)
                made.append(links.copy(base + len(made), held.at[to], slots.at[links.me], slots.at[links.before(offset)], links.along(offset)))
        return made

    def load_pairs(self, links, held, own, s):
        if s == self.bits:
            return [(held.at[links.me], own)]
        return [(self.pick(links, held, m, left, now, False), own.at[m]) for m, left, now in self.parts(s)]

    def add(self, links, slots, s, own, held):
        half = self.mp // 2

        def step(m, carry):
            for part, order in enumerate(orders(self.bits)):
                at = m + part * half
                if own is not None:
                    slots[at] += own[at]
                else:
                    left = sorted(order[: self.bits - s], reverse=True)
                    slots[at] += self.pick(links, held, at, left, order[self.bits - 1 - s], False)[...]
            return carry

        lax.fori_loop(0, half, step, 0)

    def total(self, links, slots, own, held):
        value = (own[...] if own is not None else held[links.me]).astype(F32)
        for offset in range(1, self.mp):
            value = value + slots[links.before(offset)].astype(F32)
        return value


HBM = pl.BlockSpec(memory_space=pltpu.HBM)


class Ride:
    def __init__(self, flow, mp, bits, collective_id, rounds):
        self.flow, self.mp, self.bits, self.collective_id = flow, mp, bits, collective_id
        self.rounds = rounds
        names = []
        self.base = {}
        self.count = 0
        self.stages = {}
        for _, tasks in rounds:
            for name, s in tasks:
                if name not in names:
                    names.append(name)
                    self.stages[name] = []
                self.stages[name].append(s)
                self.base[name, s] = self.count
                self.count += flow[name][0].copies(s)
        self.gathers = [n for n in names if isinstance(flow[n][0], Gather)]
        self.scatters = [n for n in names if isinstance(flow[n][0], Scatter)]
        self.local = {}
        self.local_count = 0
        self.scratch = []
        self.place = {}
        for n in self.scatters:
            kind = flow[n][0]
            first, last = self.stages[n][0], self.stages[n][-1]
            self.local[n] = self.local_count
            self.local_count += kind.loads(first) + 1
            self.place[n, "own"] = len(self.scratch)
            self.scratch.append(pltpu.VMEM(kind.own(first), BF16))
            for s in self.stages[n]:
                self.place[n, s] = len(self.scratch)
                self.scratch.append(pltpu.VMEM(kind.arrived(s), BF16))
        self.sems = [pltpu.SemaphoreType.DMA((max(1, k),)) for k in (self.count, self.count, self.local_count)]

    def inputs(self):
        return [self.flow[n][1] for n in self.gathers + self.scatters]

    def finals(self, n):
        return self.stages[n][-1] == self.bits

    def outputs(self):
        shapes = [jax.ShapeDtypeStruct(self.flow[n][1].shape, self.flow[n][1].dtype) for n in self.gathers]
        specs = [HBM] * len(shapes)
        for n in self.scatters:
            kind = self.flow[n][0]
            if self.finals(n):
                shapes.append(jax.ShapeDtypeStruct((kind.rows, kind.cols), F32))
                specs.append(pl.BlockSpec((kind.rows, kind.cols), lambda *_: (0, 0)))
            else:
                shapes.append(jax.ShapeDtypeStruct(kind.shape(self.stages[n][-1] + 1), BF16))
                specs.append(HBM)
        return shapes, specs

    def bind(self, ins, outs, scratch):
        names = self.gathers + self.scatters
        self.ins = dict(zip(names, ins))
        self.outs = dict(zip(names, outs))
        send, recv, self.local_sem = scratch[:3]
        self.buffers = scratch[3:]
        self.links = Links(self.mp, self.bits, send, recv)

    def held(self, n, s):
        return self.ins[n] if s == self.stages[n][0] else self.buffers[self.place[n, s - 1]]

    def pairs(self, task):
        n, s = task
        kind = self.flow[n][0]
        if n in self.gathers:
            return kind.pairs(self.links, self.outs[n], s, self.base[task])
        return kind.pairs(self.links, self.held(n, s), self.buffers[self.place[task]], s, self.base[task])

    def loads(self, n):
        first = self.stages[n][0]
        pairs = self.flow[n][0].load_pairs(self.links, self.ins[n], self.buffers[self.place[n, "own"]], first)
        return [functools.partial(pltpu.make_async_copy, a, b, self.local_sem.at[self.local[n] + i]) for i, (a, b) in enumerate(pairs)]

    def stores(self, n):
        last = self.stages[n][-1]
        at = self.local[n] + self.flow[n][0].loads(self.stages[n][0])
        return pltpu.make_async_copy(self.buffers[self.place[n, last]], self.outs[n], self.local_sem.at[at])

    def begin(self, number):
        tasks = self.rounds[number][1]
        if number == 0:
            self.links.barrier()
            self.finished = set()
        for n, s in tasks:
            if s > self.stages[n][0]:
                self.finish((n, s - 1))
            elif n in self.scatters:
                for load in self.loads(n):
                    load().start()
            for out, _ in self.pairs((n, s)):
                out().start()

    def finish(self, task):
        if task in self.finished:
            return
        self.finished.add(task)
        n, s = task
        for _, arriving in self.pairs(task):
            arriving().wait_recv()
        if n in self.scatters:
            kind = self.flow[n][0]
            own = None
            if s == self.stages[n][0]:
                own = self.buffers[self.place[n, "own"]]
                for load in self.loads(n):
                    load().wait()
            slots = self.buffers[self.place[task]]
            if s < self.bits:
                kind.add(self.links, slots, s, own, self.held(n, s))
                if s == self.stages[n][-1]:
                    self.stores(n).start()
            else:
                self.outs[n][...] = kind.total(self.links, slots, own, self.held(n, s))

    def end(self):
        for _, tasks in self.rounds:
            for task in tasks:
                self.finish(task)
        for _, tasks in self.rounds:
            for task in tasks:
                for out, _ in self.pairs(task):
                    out().wait_send()
        for n in self.scatters:
            if not self.finals(n):
                self.stores(n).wait()

    def done(self, arrays):
        for n, array in zip(self.gathers + self.scatters, arrays):
            self.flow[n] = (self.flow[n][0], array)


def launch(kernel, grid, in_specs, out_specs, out_shape, scratch_shapes=(), vmem=56, ride=None, args=()):
    scratch_shapes = list(scratch_shapes)
    if ride is None:
        return pl.pallas_call(
            kernel,
            grid=grid,
            in_specs=in_specs,
            out_specs=out_specs,
            out_shape=out_shape,
            scratch_shapes=scratch_shapes,
            compiler_params=pltpu.CompilerParams(vmem_limit_bytes=vmem * 2**20),
        )(*args)
    extra_in = ride.inputs()
    extra_shapes, extra_specs = ride.outputs()
    n_in, n_out, n_scratch = len(in_specs), len(out_specs), len(scratch_shapes)

    def riding(*refs):
        ins, refs = refs[:n_in], refs[n_in:]
        ride_ins, refs = refs[: len(extra_in)], refs[len(extra_in) :]
        outs, refs = refs[:n_out], refs[n_out:]
        ride_outs, refs = refs[: len(extra_shapes)], refs[len(extra_shapes) :]
        scratch, ride_scratch = refs[:n_scratch], refs[n_scratch:]
        ride.bind(ride_ins, ride_outs, ride_scratch)
        step = pl.program_id(0)
        for number, (at, _) in enumerate(ride.rounds):

            @pl.when(step == at)
            def _():
                ride.begin(number)

        if kernel is not None:
            kernel(*ins, *outs, *scratch)

        @pl.when(step == pl.num_programs(0) - 1)
        def _():
            ride.end()

    made = pl.pallas_call(
        riding,
        grid=grid,
        in_specs=list(in_specs) + [HBM] * len(extra_in),
        out_specs=list(out_specs) + extra_specs,
        out_shape=list(out_shape) + extra_shapes,
        scratch_shapes=scratch_shapes + ride.sems + ride.scratch,
        input_output_aliases={n_in + i: n_out + i for i in range(len(ride.gathers))},
        compiler_params=pltpu.CompilerParams(collective_id=ride.collective_id, has_side_effects=True, vmem_limit_bytes=vmem * 2**20),
    )(*args, *extra_in)
    ride.done(made[n_out:])
    return made[:n_out]


def start_kernel(mp, bits, kinds, *refs):
    count = len(kinds)
    shards, buffers, local = refs[:count], refs[count : 2 * count], refs[2 * count]
    links = Links(mp, bits, None, None)
    copies = [pltpu.make_async_copy(shards[i], kinds[i].at(links, buffers[i], links.me, ()), local.at[i]) for i in range(count)]
    for copy in copies:
        copy.start()
    for copy in copies:
        copy.wait()


def start_buffers(shards, kinds, mp, bits):
    shapes = []
    for shard, kind in zip(shards, kinds):
        shapes.append(jax.ShapeDtypeStruct((mp,) + (() if kind.line else (2,) * bits) + shard.shape, shard.dtype))
    return pl.pallas_call(
        functools.partial(start_kernel, mp, bits, kinds),
        in_specs=[pl.BlockSpec(memory_space=pltpu.VMEM)] * len(shards),
        out_specs=[HBM] * len(shards),
        out_shape=shapes,
        scratch_shapes=[pltpu.SemaphoreType.DMA((len(shards),))],
    )(*shards)


def fill_padded(padded, values, taps):
    rows, _, lanes = values.shape
    half = (taps - 1) // 2
    padded[pl.ds(half, rows)] = values
    place = lax.broadcasted_iota(jnp.int32, (half, SEG, lanes), 1)
    before = pltpu.roll(values[rows - half :].astype(F32), 1, axis=1)
    padded[pl.ds(0, half)] = low(jnp.where(place == 0, 0.0, before))
    after = pltpu.roll(values[:half].astype(F32), SEG - 1, axis=1)
    padded[pl.ds(half + rows, half)] = low(jnp.where(place == SEG - 1, 0.0, after))


def convolve(padded, taps_of, taps, rows, block, emit):
    weights = [taps_of(k) for k in range(taps)]

    def step(index, carry):
        start = index * block
        total = None
        for first in range(0, taps, 8):
            part = None
            for k in range(first, min(taps, first + 8)):
                term = weights[k] * padded[pl.ds(start + k, block)]
                part = term if part is None else part + term
            part = part.astype(F32)
            total = part if total is None else total + part
        emit(start, total)
        return carry

    lax.fori_loop(0, rows // block, step, 0)


def tap_grads(padded, grads, sums, pick, taps, rows, block):
    group = 8
    count = sums.shape[0] // SEG
    for first in range(0, taps, group):
        ks = range(first, min(taps, first + group))

        def step(index, totals):
            start = index * block
            here = grads[pl.ds(start, block)]
            made = []
            for k, total in zip(ks, totals):
                term = here * padded[pl.ds(start + k, block)]
                size = block
                while size > 1:
                    size //= 2
                    term = term[:size] + term[size:]
                made.append(total + term[0].astype(F32))
            return tuple(made)

        zero = jnp.zeros((SEG, LANES), F32)
        totals = lax.fori_loop(0, rows // block, step, (zero,) * len(ks), unroll=True)
        for k, total in zip(ks, totals):
            sums[pl.ds(k * SEG, SEG), :] = total
    for k in range(taps, count):
        sums[pl.ds(k * SEG, SEG), :] = jnp.zeros((SEG, LANES), F32)
    high = low(sums[...])
    rest = low(sums[...] - high.astype(F32))
    return (dot(pick[...], high) + dot(pick[...], rest))[:taps]


def tap_pick(shape):
    row = lax.broadcasted_iota(jnp.int32, shape, 0)
    col = lax.broadcasted_iota(jnp.int32, shape, 1)
    return low(((col >= row * SEG) & (col < row * SEG + SEG)).astype(F32))


def tap_scratch(taps):
    count = -(-taps // 16) * 16
    return [pltpu.VMEM((count * SEG, LANES), F32), pltpu.VMEM((count, count * SEG), BF16)]


def ffn_forward_kernel(final, blocks, x_ref, gain_ref, w_ref, *rest):
    if final:
        last_ref, out_ref, h_ref, y_ref = rest
    else:
        out_ref, h_ref = rest
    width = h_ref.shape[2]
    x = x_ref[...]
    normed, _ = norm_parts(x)
    a = low(normed * gain_ref[...])
    total = None
    for m in range(blocks):
        h = dot(a, w_ref[m, :, :width])
        h_ref[m] = low(h)
        half = 0.5 * h
        s = low(half + half * jnp.tanh(half))
        part = dot_nt(s, w_ref[m, :, width:])
        total = part if total is None else total + part
    out = x + 0.5 * total
    out_ref[...] = out
    if final:
        normed, _ = norm_parts(out)
        y_ref[...] = normed * last_ref[...]


def ffn_forward(x, gain, w, last=None, ride=None):
    tokens, depth = x.shape
    blocks, _, width = w.shape
    width //= 2
    tile = min(256, tokens)
    row = pl.BlockSpec((tile, depth), lambda i: (i, 0))
    vec = pl.BlockSpec((1, depth), lambda i: (0, 0))
    out_shape = [jax.ShapeDtypeStruct(x.shape, F32), jax.ShapeDtypeStruct((blocks, tokens, width), BF16)]
    out_specs = [row, pl.BlockSpec((blocks, tile, width), lambda i: (0, i, 0))]
    in_specs = [row, vec, pl.BlockSpec(w.shape, lambda i: (0, 0, 0))]
    args = [x, gain, w]
    if last is not None:
        in_specs.append(vec)
        args.append(last)
        out_shape.append(jax.ShapeDtypeStruct(x.shape, F32))
        out_specs.append(row)
    return launch(
        functools.partial(ffn_forward_kernel, last is not None, blocks),
        grid=(tokens // tile,),
        in_specs=in_specs,
        out_specs=out_specs,
        out_shape=out_shape,
        vmem=56,
        ride=ride,
        args=args,
    )


def ffn_backward_kernel(final, tile, g_ref, x_ref, gain_ref, h_ref, w_ref, *rest):
    if final:
        last_ref, y_ref, dx_ref, dw_ref, dgain_ref, dlast_ref, grad, at, gt, a_rows, g_rows, s_rows, d_rows, da = rest
    else:
        dx_ref, dw_ref, dgain_ref, grad, at, gt, a_rows, g_rows, s_rows, d_rows, da = rest
    m = pl.program_id(0)
    tokens = x_ref.shape[0]
    width = h_ref.shape[2]
    chunks = tokens // tile

    @pl.when(m == 0)
    def _():
        if final:
            dlast_ref[...] = jnp.zeros_like(dlast_ref)
        for c in range(chunks):
            here = pl.ds(c * tile, tile)
            g = g_ref[here, :]
            if final:
                normed, rstd = norm_parts(y_ref[here, :])
                dlast_ref[...] += jnp.sum(g * normed, axis=0, keepdims=True)
                g = norm_back(normed, rstd, last_ref[...], g)
                grad[here, :] = g
            g_low = low(0.5 * g)
            g_rows[here, :] = g_low
            normed, _ = norm_parts(x_ref[here, :])
            a_rows[here, :] = low(normed * gain_ref[...])
        at[...] = a_rows[...].T
        gt[...] = g_rows[...].T

    w_in = w_ref[0, :, :width]
    w_out = w_ref[0, :, width:]
    for c in range(chunks):
        here = pl.ds(c * tile, tile)
        ds = dot(g_rows[here, :], w_out)
        h = h_ref[0, here, :].astype(F32)
        half = 0.5 * h
        tanh = jnp.tanh(half)
        s = half + half * tanh
        s_rows[here, :] = low(s)
        sig = 0.5 + 0.5 * tanh
        dh = low(ds * (sig + s * (1.0 - sig)))
        d_rows[here, :] = dh
        part = dot_nt(dh, w_in)

        @pl.when(m == 0)
        def _():
            da[here, :] = part

        @pl.when(m != 0)
        def _():
            da[here, :] += part

    dw_ref[0, :, :width] = low(dot(at[...], d_rows[...]))
    dw_ref[0, :, width:] = low(dot(gt[...], s_rows[...]))

    @pl.when(m == pl.num_programs(0) - 1)
    def _():
        dgain_ref[...] = jnp.zeros_like(dgain_ref)
        for c in range(chunks):
            here = pl.ds(c * tile, tile)
            normed, rstd = norm_parts(x_ref[here, :])
            d = da[here, :]
            dgain_ref[...] += jnp.sum(d * normed, axis=0, keepdims=True)
            base = grad[here, :] if final else g_ref[here, :]
            dx_ref[here, :] = base + norm_back(normed, rstd, gain_ref[...], d)


def ffn_backward(g, x, gain, h, w, last=None, final_in=None, ride=None):
    tokens, depth = x.shape
    blocks, _, width = w.shape
    width //= 2
    tile = tokens
    full = pl.BlockSpec((tokens, depth), lambda i: (0, 0))
    vec = pl.BlockSpec((1, depth), lambda i: (0, 0))
    vec_shape = jax.ShapeDtypeStruct((1, depth), F32)
    in_specs = [full, full, vec, pl.BlockSpec((1, tokens, width), lambda i: (i, 0, 0)), pl.BlockSpec((1, depth, 2 * width), lambda i: (i, 0, 0))]
    args = [g, x, gain, h, w]
    out_specs = [full, pl.BlockSpec((1, depth, 2 * width), lambda i: (i, 0, 0)), vec]
    out_shape = [jax.ShapeDtypeStruct(x.shape, F32), jax.ShapeDtypeStruct(w.shape, BF16), vec_shape]
    if last is not None:
        in_specs += [vec, full]
        args += [last, final_in]
        out_specs.append(vec)
        out_shape.append(vec_shape)
    return launch(
        functools.partial(ffn_backward_kernel, last is not None, tile),
        grid=(blocks,),
        in_specs=in_specs,
        out_specs=out_specs,
        out_shape=out_shape,
        scratch_shapes=[
            pltpu.VMEM((tokens, depth) if last is not None else (8, 128), F32),
            pltpu.VMEM((depth, tokens), BF16),
            pltpu.VMEM((depth, tokens), BF16),
            pltpu.VMEM((tokens, depth), BF16),
            pltpu.VMEM((tokens, depth), BF16),
            pltpu.VMEM((tokens, width), BF16),
            pltpu.VMEM((tokens, width), BF16),
            pltpu.VMEM((tokens, depth), F32),
        ],
        vmem=56,
        ride=ride,
        args=args,
    )


def split_lanes(lanes_ref, here, values):
    for l in range(values.shape[1] // LANES):
        lanes_ref[l, here, :] = values[:, l * LANES : (l + 1) * LANES]


def reorder(lanes_ref, stride, emit):
    blocks, tokens, _ = lanes_ref.shape
    count = tokens // stride
    for start in range(stride):
        for l in range(blocks):
            emit(start * count, l, lanes_ref[l, pl.ds(start, count, stride=stride), :])


def attention_forward_kernel(len_ref, keep_ref, x_ref, gain_ref, w_ref, table_ref, att_ref, q_ref, k_ref, v_ref, o_ref, lse_ref, b_rows, total, bias, flat):
    m = pl.program_id(0)
    tokens = x_ref.shape[0]
    rows = tokens // SEG
    length = len_ref[0]
    tile = 256

    @pl.when(m == 0)
    def _():
        for c in range(tokens // tile):
            here = pl.ds(c * tile, tile)
            normed, _ = norm_parts(x_ref[here, :])
            split_lanes(flat, here, normed * gain_ref[...])

        def emit(start, l, piece):
            b_rows[pl.ds(start, rows), pl.ds(l * LANES, LANES)] = low(piece)

        reorder(flat, SEG, emit)

    wide = PAIR * HEAD
    qkv = dot(b_rows[...], w_ref[0, :, : 3 * wide])
    lane = lax.broadcasted_iota(jnp.int32, (tokens, LANES), 1)
    at = lax.broadcasted_iota(jnp.int32, (tokens, LANES), 0)
    hidden = jnp.where(at < length, 0.0, MASKED)
    for head in range(PAIR):
        cols = pl.ds(head * LANES, LANES)

        def mine(piece):
            return piece if head == 0 else pltpu.roll(piece, HEAD, axis=1)

        q = low(mine(qkv[:, :wide])).astype(F32) * (HEAD**-0.5)
        k = mine(qkv[:, wide : 2 * wide])
        v = mine(qkv[:, 2 * wide :])
        q_ref[0, :, cols] = low(jnp.where(lane < HEAD, q, jnp.where(lane == HEAD, 1.0, 0.0)))
        k_ref[0, :, cols] = low(jnp.where(lane < HEAD, k, jnp.where(lane == HEAD, hidden, jnp.where(lane <= HEAD + 2, -1.0, 0.0))))
        v_ref[0, :, cols] = low(jnp.where(lane < HEAD, v, jnp.where(lane <= HEAD + 1, 1.0, 0.0)))
        span = table_ref.shape[2]
        line = jnp.broadcast_to(table_ref[0, head : head + 1, :], (LANES, span))
        bias[...] = pltpu.roll(line, span - LANES, axis=1, stride=1, stride_axis=0)
        for t in range(tokens // tile):
            here = pl.ds(t * tile, tile)
            scores = dot_nt(q_ref[0, here, cols], k_ref[0, :, cols])
            parts = []
            for sub in range(tile // LANES):
                first = tokens - LANES - t * tile - sub * LANES
                parts.append(scores[sub * LANES : (sub + 1) * LANES] + bias[:, pl.ds(first, tokens)])
            scores = jnp.concatenate(parts, axis=0)
            peak = jnp.max(scores, axis=-1, keepdims=True)
            expos = low(jnp.exp(scores - peak))
            out = dot(expos, v_ref[0, :, cols])
            denom = out[:, HEAD : HEAD + 1]
            out = out * (1.0 / denom)
            lse = peak + jnp.log(denom)
            if head == 0:
                o_ref[0, here, :] = low(out)
            else:
                lane_t = lax.broadcasted_iota(jnp.int32, (tile, LANES), 1)
                o_ref[0, here, :] = low(jnp.where(lane_t < HEAD, o_ref[0, here, :].astype(F32), pltpu.roll(out, HEAD, axis=1)))
            lse_ref[here, :] = jnp.broadcast_to(lse, (tile, LANES))
        lse = lse_ref[...]
        lse_high = low(lse).astype(F32)
        q_now = q_ref[0, :, cols].astype(F32)
        q_ref[0, :, cols] = low(jnp.where(lane == HEAD + 1, lse_high, jnp.where(lane == HEAD + 2, lse - lse_high, q_now)))
    part = dot_nt(o_ref[0], w_ref[0, :, 3 * wide :])

    @pl.when(m == 0)
    def _():
        total[...] = part

    @pl.when(m != 0)
    def _():
        total[...] += part

    @pl.when(m == pl.num_programs(0) - 1)
    def _():
        split_lanes(flat, pl.ds(0, tokens), total[...])

        def emit(start, l, piece):
            att_ref[pl.ds(start, SEG), pl.ds(l * LANES, LANES)] = low(piece * keep_ref[pl.ds(start, SEG), :])

        reorder(flat, rows, emit)


def attention_forward(length, keep, x, gain, w, table, ride=None):
    tokens, depth = x.shape
    blocks = w.shape[0]
    full = pl.BlockSpec((tokens, depth), lambda i: (0, 0))
    heads = pl.BlockSpec((1, tokens, PAIR * LANES), lambda i: (i, 0, 0))
    pair = pl.BlockSpec((1, tokens, LANES), lambda i: (i, 0, 0))
    heads_shape = jax.ShapeDtypeStruct((blocks, tokens, PAIR * LANES), BF16)
    return launch(
        attention_forward_kernel,
        grid=(blocks,),
        in_specs=[
            pl.BlockSpec(memory_space=pltpu.SMEM),
            pl.BlockSpec(keep.shape, lambda i: (0, 0)),
            full,
            pl.BlockSpec((1, depth), lambda i: (0, 0)),
            pl.BlockSpec((1, depth, w.shape[2]), lambda i: (i, 0, 0)),
            pl.BlockSpec((1, PAIR, table.shape[2]), lambda i: (i, 0, 0)),
        ],
        out_specs=[full, heads, heads, heads, pair],
        out_shape=[
            jax.ShapeDtypeStruct((tokens, depth), BF16),
            heads_shape,
            heads_shape,
            heads_shape,
            jax.ShapeDtypeStruct((blocks, tokens, LANES), BF16),
        ],
        scratch_shapes=[
            pltpu.VMEM((tokens, LANES), F32),
            pltpu.VMEM((tokens, depth), BF16),
            pltpu.VMEM((tokens, depth), F32),
            pltpu.VMEM((LANES, table.shape[2]), F32),
            pltpu.VMEM((depth // LANES, tokens, LANES), F32),
        ],
        vmem=56,
        ride=ride,
        args=(length, keep, x, gain, w, table,),
    )


def attention_backward_kernel(
    datt_ref, x_ref, gain_ref, res_ref, w_ref, table_ref, q_ref, k_ref, v_ref, o_ref,
    dx_ref, dw_ref, dgain_ref, dtable_ref,
    b_t, g_t, g_rows, flat, bias, dbias, do_aug, d_pair, dq_t, k_t, d_rows, db,
):
    m = pl.program_id(0)
    tokens = x_ref.shape[0]
    rows = tokens // SEG
    wide = PAIR * HEAD
    tile = 256
    span = table_ref.shape[2]
    stored = tokens // tile

    @pl.when(m == 0)
    def _():
        def emit(start, l, piece):
            g_rows[pl.ds(start, rows), pl.ds(l * LANES, LANES)] = low(piece)

        for c in range(tokens // tile):
            here = pl.ds(c * tile, tile)
            normed, _ = norm_parts(x_ref[here, :])
            split_lanes(flat, here, normed * gain_ref[...])
        reorder(flat, SEG, emit)
        b_t[...] = g_rows[...].T
        split_lanes(flat, pl.ds(0, tokens), datt_ref[...].astype(F32))
        reorder(flat, SEG, emit)
        g_t[...] = g_rows[...].T

    w_out = w_ref[0, :, 3 * wide :]
    do = low(dot(g_rows[...], w_out))
    dw_ref[0, :, 3 * wide :] = low(dot(g_t[...], o_ref[0]))
    lane = lax.broadcasted_iota(jnp.int32, (tokens, LANES), 1)
    do_full = do.astype(F32)
    product = do_full * o_ref[0].astype(F32)
    for head in range(PAIR):
        cols = pl.ds(head * LANES, LANES)
        inside = lane < HEAD if head == 0 else lane >= HEAD
        delta = jnp.sum(jnp.where(inside, product, 0.0), axis=-1, keepdims=True)
        delta_high = low(delta).astype(F32)
        mine = do_full if head == 0 else pltpu.roll(do_full, HEAD, axis=1)
        do_aug[...] = low(jnp.where(lane < HEAD, mine, jnp.where(lane == HEAD, -delta_high, jnp.where(lane == HEAD + 1, delta_high - delta, 0.0))))
        k_t[...] = k_ref[0, :, cols].T
        line = jnp.broadcast_to(table_ref[0, head : head + 1, :], (LANES, span))
        bias[...] = pltpu.roll(line, span - (LANES - 1), axis=1, stride=1, stride_axis=0)
        dbias[...] = jnp.zeros_like(dbias)
        for t in range(stored):
            here = pl.ds(t * tile, tile)
            scores = dot_nt(k_ref[0, here, cols], q_ref[0, :, cols])
            grads = dot_nt(v_ref[0, here, cols], do_aug[...])
            p_parts = []
            d_parts = []
            for sub in range(tile // LANES):
                first = tokens - LANES - t * tile - sub * LANES
                now = slice(sub * LANES, (sub + 1) * LANES)
                p = jnp.exp(scores[now] + bias[:, pl.ds(first, tokens)])
                ds = low(p * grads[now])
                dbias[:, pl.ds(first, tokens)] += ds.astype(F32)
                p_parts.append(low(p))
                d_parts.append(ds)
            p = jnp.concatenate(p_parts, axis=0)
            ds = jnp.concatenate(d_parts, axis=0)
            dv = dot(p, do_aug[...])
            dk = dot(ds, q_ref[0, :, cols])
            dq = dot(k_t[:, here], ds)
            if t == 0:
                dq_t[...] = dq
            else:
                dq_t[...] += dq
            if head == 0:
                d_pair[1, here, :] = dk
                d_pair[2, here, :] = dv
            else:
                lane_t = lax.broadcasted_iota(jnp.int32, (tile, LANES), 1)
                d_pair[1, here, :] = jnp.where(lane_t < HEAD, d_pair[1, here, :], pltpu.roll(dk, HEAD, axis=1))
                d_pair[2, here, :] = jnp.where(lane_t < HEAD, d_pair[2, here, :], pltpu.roll(dv, HEAD, axis=1))
        dq = dq_t[...].T * (HEAD**-0.5)
        if head == 0:
            d_pair[0] = dq
        else:
            d_pair[0] = jnp.where(lane < HEAD, d_pair[0], pltpu.roll(dq, HEAD, axis=1))
        folded = dbias[...]
        count = LANES
        while count > 1:
            count //= 2
            folded = folded[:count] + pltpu.roll(folded[count:], span - count, axis=1)
        dtable_ref[0, head : head + 1, :] = pltpu.roll(folded, LANES - 1, axis=1)
    for part in range(3):
        d_rows[:, pl.ds(part * wide, wide)] = low(d_pair[part])
    dw_ref[0, :, : 3 * wide] = low(dot(b_t[...], d_rows[...]))
    part = dot_nt(d_rows[...], w_ref[0, :, : 3 * wide])

    @pl.when(m == 0)
    def _():
        db[...] = part

    @pl.when(m != 0)
    def _():
        db[...] += part

    @pl.when(m == pl.num_programs(0) - 1)
    def _():
        dgain_ref[...] = jnp.zeros_like(dgain_ref)
        split_lanes(flat, pl.ds(0, tokens), db[...])

        def emit(start, l, piece):
            db[pl.ds(start, SEG), pl.ds(l * LANES, LANES)] = piece

        reorder(flat, rows, emit)
        for c in range(tokens // tile):
            here = pl.ds(c * tile, tile)
            normed, rstd = norm_parts(x_ref[here, :])
            d = db[here, :]
            dgain_ref[...] += jnp.sum(d * normed, axis=0, keepdims=True)
            dx_ref[here, :] = res_ref[here, :] + norm_back(normed, rstd, gain_ref[...], d)


def attention_backward(datt, x, gain, res, w, table_back, q, k, v, o, ride=None):
    tokens, depth = x.shape
    blocks = w.shape[0]
    span = table_back.shape[2]
    full = pl.BlockSpec((tokens, depth), lambda i: (0, 0))
    heads = pl.BlockSpec((1, tokens, PAIR * LANES), lambda i: (i, 0, 0))
    pair = pl.BlockSpec((1, tokens, LANES), lambda i: (i, 0, 0))
    vec = pl.BlockSpec((1, depth), lambda i: (0, 0))
    w_spec = pl.BlockSpec((1, depth, w.shape[2]), lambda i: (i, 0, 0))
    t_spec = pl.BlockSpec((1, PAIR, span), lambda i: (i, 0, 0))
    wide = PAIR * HEAD
    return launch(
        attention_backward_kernel,
        grid=(blocks,),
        in_specs=[full, full, vec, full, w_spec, t_spec, heads, heads, heads, pair],
        out_specs=[full, w_spec, vec, t_spec],
        out_shape=[
            jax.ShapeDtypeStruct((tokens, depth), F32),
            jax.ShapeDtypeStruct(w.shape, BF16),
            jax.ShapeDtypeStruct((1, depth), F32),
            jax.ShapeDtypeStruct(table_back.shape, F32),
        ],
        scratch_shapes=[
            pltpu.VMEM((depth, tokens), BF16),
            pltpu.VMEM((depth, tokens), BF16),
            pltpu.VMEM((tokens, depth), BF16),
            pltpu.VMEM((depth // LANES, tokens, LANES), F32),
            pltpu.VMEM((LANES, span), F32),
            pltpu.VMEM((LANES, span), F32),
            pltpu.VMEM((tokens, LANES), BF16),
            pltpu.VMEM((3, tokens, LANES), F32),
            pltpu.VMEM((LANES, tokens), F32),
            pltpu.VMEM((LANES, tokens), BF16),
            pltpu.VMEM((tokens, 3 * wide), BF16),
            pltpu.VMEM((tokens, depth), F32),
        ],
        vmem=56,
        ride=ride,
        args=(datt, x, gain, res, w, table_back, q, k, v, o,),
    )


def gate_forward_kernel(
    taps, keep_ref, x_ref, gain_ref, w_in_ref, w_out_ref, g_gain_ref, g_conv_ref,
    cg_ref, ur_ref, sr_ref, ug_ref, sg_ref, mean_ref, rstd_ref, conv_ref, gate_ref,
    c_rows, ur_all, ug_all, first, second, total, padded,
):
    i = pl.program_id(0)
    blocks = pl.num_programs(0) // 2
    tokens = x_ref.shape[0]
    rows = tokens // SEG
    width = ur_ref.shape[2]
    tile = 256
    channels = width * blocks

    @pl.when(i == 0)
    def _():
        for c in range(tokens // tile):
            here = pl.ds(c * tile, tile)
            normed, _ = norm_parts(x_ref[here, :])
            c_rows[here, :] = low(normed * gain_ref[...])
        first[...] = jnp.zeros_like(first)
        second[...] = jnp.zeros_like(second)

    @pl.when(i < blocks)
    def _():
        for c in range(tokens // tile):
            here = pl.ds(c * tile, tile)
            z = dot(c_rows[here, :], w_in_ref[0])
            zr = z[:, :width]
            zg = z[:, width:]
            ur, slope = gelu_and_slope(zr)
            ur = low(ur)
            ur_ref[0, here, :] = ur
            ur_all[i, here, :] = ur
            sr_ref[0, here, :] = low(slope)
            ug, slope = gelu_and_slope(zg)
            ug_low = low(ug)
            ug_ref[0, here, :] = ug_low
            ug_all[i, here, :] = ug_low
            sg_ref[0, here, :] = low(slope)
            square = ug * ug
            one = ug[:, :LANES]
            two = square[:, :LANES]
            for l in range(1, width // LANES):
                one = one + ug[:, l * LANES : (l + 1) * LANES]
                two = two + square[:, l * LANES : (l + 1) * LANES]
            first[here, :] += one
            second[here, :] += two

    @pl.when(i == blocks - 1)
    def _():
        for c in range(tokens // tile):
            here = pl.ds(c * tile, tile)
            mean = jnp.sum(first[here, :], axis=-1, keepdims=True) / channels
            spread = jnp.sum(second[here, :], axis=-1, keepdims=True) / channels - mean * mean
            mean_ref[here, :] = jnp.broadcast_to(mean, (tile, LANES))
            rstd_ref[here, :] = jnp.broadcast_to(lax.rsqrt(spread + EPSILON), (tile, LANES))

    @pl.when(i >= blocks)
    def _():
        m = i - blocks
        scale = rstd_ref[...] * keep_ref[...]
        shift = mean_ref[...] * scale
        for l in range(width // LANES):
            cols = pl.ds(l * LANES, LANES)
            ug = ug_all[m, :, cols].astype(F32)
            n = low((ug * scale - shift) * g_gain_ref[0, :, cols])
            fill_padded(padded, n.reshape(rows, SEG, LANES), taps)

            def taps_of(k):
                return low(jnp.broadcast_to(g_conv_ref[0, k : k + 1, cols], (SEG, LANES)))[None]

            def emit(start, value):
                block = value.shape[0]
                here = pl.ds(pl.multiple_of(start * SEG, block * SEG), block * SEG)
                flat = value.reshape(block * SEG, LANES)
                conv_ref[0, here, cols] = low(flat)
                gate_ref[0, here, cols] = low(ur_all[m, here, cols].astype(F32) * flat)

            convolve(padded, taps_of, taps, rows, 16, emit)
        part = dot_nt(gate_ref[0], w_out_ref[0])

        @pl.when(m == 0)
        def _():
            total[...] = part

        @pl.when(m != 0)
        def _():
            total[...] += part

        @pl.when(m == blocks - 1)
        def _():
            for l in range(total.shape[1] // LANES):
                cols = pl.ds(l * LANES, LANES)
                cg_ref[:, cols] = low(total[:, cols] * keep_ref[...])


def gate_forward(keep, x, gain, w, g_gain, g_conv, taps, ride=None):
    tokens, depth = x.shape
    blocks = w.shape[0]
    width = w.shape[2] // 3
    full = pl.BlockSpec((tokens, depth), lambda i: (0, 0))
    lanes = pl.BlockSpec((tokens, LANES), lambda i: (0, 0))

    def early(i):
        return jnp.minimum(i, blocks - 1)

    def late(i):
        return jnp.maximum(i - blocks, 0)

    z_early = pl.BlockSpec((1, tokens, width), lambda i: (early(i), 0, 0))
    z_late = pl.BlockSpec((1, tokens, width), lambda i: (late(i), 0, 0))
    z_shape = jax.ShapeDtypeStruct((blocks, tokens, width), BF16)
    lane_shape = jax.ShapeDtypeStruct((tokens, LANES), F32)
    return launch(
        functools.partial(gate_forward_kernel, taps),
        grid=(2 * blocks,),
        in_specs=[
            lanes,
            full,
            pl.BlockSpec((1, depth), lambda i: (0, 0)),
            pl.BlockSpec((1, depth, 2 * width), lambda i: (early(i), 0, 0)),
            pl.BlockSpec((1, depth, width), lambda i: (late(i), 0, 2)),
            pl.BlockSpec((1, 1, width), lambda i: (late(i), 0, 0)),
            pl.BlockSpec((1, taps, width), lambda i: (late(i), 0, 0)),
        ],
        out_specs=[full, z_early, z_early, z_early, z_early, lanes, lanes, z_late, z_late],
        out_shape=[jax.ShapeDtypeStruct((tokens, depth), BF16), z_shape, z_shape, z_shape, z_shape, lane_shape, lane_shape, z_shape, z_shape],
        scratch_shapes=[
            pltpu.VMEM((tokens, depth), BF16),
            pltpu.VMEM((blocks, tokens, width), BF16),
            pltpu.VMEM((blocks, tokens, width), BF16),
            pltpu.VMEM((tokens, LANES), F32),
            pltpu.VMEM((tokens, LANES), F32),
            pltpu.VMEM((tokens, depth), F32),
            pltpu.VMEM((tokens // SEG + taps - 1, SEG, LANES), BF16),
        ],
        vmem=60,
        ride=ride,
        args=(keep, x, gain, w, w, g_gain, g_conv,),
    )


def gate_backward_kernel(
    taps, keep_ref, dcg_ref, x_ref, gain_ref, res_ref, w_ref, ur_ref, sr_ref, ug_ref, sg_ref, conv_ref, gate_ref, mean_ref, rstd_ref, g_gain_ref, g_conv_ref,
    dx_ref, dw_ref, dgain_ref, dg_gain_ref, dg_conv_ref,
    c_rows, c_t, g_t, dn_all, first, second, dc, padded, n_padded, d_rows, dconv, shift, sums, pick,
):
    i = pl.program_id(0)
    blocks = pl.num_programs(0) // 2
    tokens = x_ref.shape[0]
    rows = tokens // SEG
    width = ur_ref.shape[2]
    tile = 256
    channels = width * blocks
    chunks = tokens // tile

    @pl.when(i == 0)
    def _():
        for c in range(chunks):
            here = pl.ds(c * tile, tile)
            normed, _ = norm_parts(x_ref[here, :])
            c_rows[here, :] = low(normed * gain_ref[...])
        c_t[...] = c_rows[...].T
        g_t[...] = dcg_ref[...].T
        first[...] = jnp.zeros_like(first)
        second[...] = jnp.zeros_like(second)
        dc[...] = jnp.zeros_like(dc)
        shift[...] = mean_ref[...] * rstd_ref[...]
        pick[...] = tap_pick(pick.shape)

    @pl.when(i < blocks)
    def _():
        m = i
        for c in range(chunks):
            here = pl.ds(c * tile, tile)
            dgate = dot(dcg_ref[here, :], w_ref[0, :, 2 * width :])
            dzr = low(dgate * (conv_ref[0, here, :].astype(F32) * sr_ref[0, here, :].astype(F32)))
            d_rows[here, :] = dzr
            dconv[here, :] = low(dgate * ur_ref[0, here, :].astype(F32))
            dc[here, :] += dot_nt(dzr, w_ref[0, :, :width])
        dw_ref[m, :, :width] = low(dot(c_t[...], d_rows[...]))
        dw_ref[m, :, 2 * width :] = low(dot(g_t[...], gate_ref[0]))
        for l in range(width // LANES):
            cols = pl.ds(l * LANES, LANES)
            ug = ug_ref[0, :, cols].astype(F32)
            n = low((ug * rstd_ref[...] - shift[...]) * keep_ref[...] * g_gain_ref[0, :, cols])
            fill_padded(n_padded, n.reshape(rows, SEG, LANES), taps)
            d = dconv[:, cols].reshape(rows, SEG, LANES)
            fill_padded(padded, d, taps)
            dg_conv_ref[0, :, cols] = tap_grads(n_padded, padded.at[pl.ds((taps - 1) // 2, rows)], sums, pick, taps, rows, 8)
            dg_gain_ref[0, :, cols] = jnp.zeros((1, LANES), F32)

            def taps_of(k):
                return low(jnp.broadcast_to(g_conv_ref[0, taps - 1 - k : taps - k, cols], (SEG, LANES)))[None]

            def emit(start, value):
                block = value.shape[0]
                here = pl.ds(pl.multiple_of(start * SEG, block * SEG), block * SEG)
                dn = value.reshape(block * SEG, LANES) * keep_ref[here, :]
                normed = ug_ref[0, here, cols].astype(F32) * rstd_ref[here, :] - shift[here, :]
                product = dn * normed
                dg_gain_ref[0, :, cols] += jnp.sum(product, axis=0, keepdims=True)
                scaled = dn * g_gain_ref[0, :, cols]
                dn_all[m, here, cols] = low(scaled)
                first[here, :] += scaled
                second[here, :] += product * g_gain_ref[0, :, cols]

            convolve(padded, taps_of, taps, rows, 16, emit)

    @pl.when(i == blocks - 1)
    def _():
        for c in range(chunks):
            here = pl.ds(c * tile, tile)
            one = jnp.sum(first[here, :], axis=-1, keepdims=True) / channels
            two = jnp.sum(second[here, :], axis=-1, keepdims=True) / channels
            first[here, :] = jnp.broadcast_to(one, (tile, LANES))
            second[here, :] = jnp.broadcast_to(two, (tile, LANES))

    @pl.when(i >= blocks)
    def _():
        m = i - blocks
        for c in range(chunks):
            here = pl.ds(c * tile, tile)
            rstd = rstd_ref[here, :]
            one = first[here, :]
            two = second[here, :]
            for l in range(width // LANES):
                cols = pl.ds(l * LANES, LANES)
                normed = ug_ref[0, here, cols].astype(F32) * rstd - shift[here, :]
                dug = rstd * (dn_all[m, here, cols].astype(F32) - one - normed * two)
                d_rows[here, cols] = low(dug * sg_ref[0, here, cols].astype(F32))
            dc[here, :] += dot_nt(d_rows[here, :], w_ref[0, :, width : 2 * width])
        dw_ref[m, :, width : 2 * width] = low(dot(c_t[...], d_rows[...]))

    @pl.when(i == 2 * blocks - 1)
    def _():
        dgain_ref[...] = jnp.zeros_like(dgain_ref)
        for c in range(chunks):
            here = pl.ds(c * tile, tile)
            normed, rstd = norm_parts(x_ref[here, :])
            d = dc[here, :]
            dgain_ref[...] += jnp.sum(d * normed, axis=0, keepdims=True)
            dx_ref[here, :] = res_ref[here, :] + norm_back(normed, rstd, gain_ref[...], d)


def gate_backward(keep, dcg, x, gain, res, w, ur, sr, ug, sg, conv, gate, mean, rstd, g_gain, g_conv, taps, ride=None):
    tokens, depth = x.shape
    blocks = w.shape[0]
    width = w.shape[2] // 3
    full = pl.BlockSpec((tokens, depth), lambda i: (0, 0))
    lanes = pl.BlockSpec((tokens, LANES), lambda i: (0, 0))
    vec = pl.BlockSpec((1, depth), lambda i: (0, 0))

    def early(i):
        return jnp.minimum(i, blocks - 1)

    z_early = pl.BlockSpec((1, tokens, width), lambda i: (early(i), 0, 0))
    z_cycle = pl.BlockSpec((1, tokens, width), lambda i: (lax.rem(i, blocks), 0, 0))
    gain_spec = pl.BlockSpec((1, 1, width), lambda i: (early(i), 0, 0))
    conv_spec = pl.BlockSpec((1, taps, width), lambda i: (early(i), 0, 0))
    padded = (tokens // SEG + taps - 1, SEG, LANES)
    return launch(
        functools.partial(gate_backward_kernel, taps),
        grid=(2 * blocks,),
        in_specs=[
            lanes,
            full,
            full,
            vec,
            full,
            pl.BlockSpec((1, depth, 3 * width), lambda i: (lax.rem(i, blocks), 0, 0)),
            z_early,
            z_early,
            z_cycle,
            z_cycle,
            z_early,
            z_early,
            lanes,
            lanes,
            gain_spec,
            conv_spec,
        ],
        out_specs=[full, pl.BlockSpec(w.shape, lambda i: (0, 0, 0)), vec, gain_spec, conv_spec],
        out_shape=[
            jax.ShapeDtypeStruct((tokens, depth), F32),
            jax.ShapeDtypeStruct(w.shape, BF16),
            jax.ShapeDtypeStruct((1, depth), F32),
            jax.ShapeDtypeStruct(g_gain.shape, F32),
            jax.ShapeDtypeStruct(g_conv.shape, F32),
        ],
        scratch_shapes=[
            pltpu.VMEM((tokens, depth), BF16),
            pltpu.VMEM((depth, tokens), BF16),
            pltpu.VMEM((depth, tokens), BF16),
            pltpu.VMEM((blocks, tokens, width), BF16),
            pltpu.VMEM((tokens, LANES), F32),
            pltpu.VMEM((tokens, LANES), F32),
            pltpu.VMEM((tokens, depth), F32),
            pltpu.VMEM(padded, BF16),
            pltpu.VMEM(padded, BF16),
            pltpu.VMEM((tokens, width), BF16),
            pltpu.VMEM((tokens, width), BF16),
            pltpu.VMEM((tokens, LANES), F32),
            *tap_scratch(taps),
        ],
        vmem=60,
        ride=ride,
        args=(keep, dcg, x, gain, res, w, ur, sr, ug, sg, conv, gate, mean, rstd, g_gain, g_conv,),
    )


def merge_forward_kernel(taps, x_ref, att_ref, cg_ref, w_ref, m_conv_ref, out_ref, merged_ref, padded):
    c = pl.program_id(0)
    tokens = x_ref.shape[0]
    rows = tokens // SEG
    half = pl.num_programs(0) // 2
    width = merged_ref.shape[1]
    for l in range(width // LANES):
        cols = pl.ds(l * LANES, LANES)

        @pl.when(c < half)
        def _():
            fill_padded(padded, att_ref[:, cols].reshape(rows, SEG, LANES), taps)

        @pl.when(c >= half)
        def _():
            fill_padded(padded, cg_ref[:, cols].reshape(rows, SEG, LANES), taps)

        def taps_of(k):
            return low(jnp.broadcast_to(m_conv_ref[k : k + 1, cols], (SEG, LANES)))[None]

        def emit(start, value):
            block = value.shape[0]
            here = pl.ds(pl.multiple_of(start * SEG, block * SEG), block * SEG)
            value = value + padded[pl.ds(start + (taps - 1) // 2, block)].astype(F32)
            merged_ref[here, cols] = low(value.reshape(block * SEG, LANES))

        convolve(padded, taps_of, taps, rows, 16, emit)
    w = jnp.concatenate([w_ref[m] for m in range(w_ref.shape[0])], axis=1)
    part = dot(merged_ref[...], w)

    @pl.when(c == 0)
    def _():
        out_ref[...] = x_ref[...] + part

    @pl.when(c != 0)
    def _():
        out_ref[...] += part


def merge_forward(x, att, cg, w, m_conv, ride=None):
    tokens, depth = x.shape
    blocks, both, cols = w.shape
    taps = m_conv.shape[0]
    width = 256
    steps = both // width
    half = steps // 2
    full = pl.BlockSpec((tokens, depth), lambda i: (0, 0))
    return launch(
        functools.partial(merge_forward_kernel, taps),
        grid=(steps,),
        in_specs=[
            full,
            pl.BlockSpec((tokens, width), lambda i: (0, jnp.minimum(i, half - 1))),
            pl.BlockSpec((tokens, width), lambda i: (0, jnp.maximum(i - half, 0))),
            pl.BlockSpec((blocks, width, cols), lambda i: (0, i, 0)),
            pl.BlockSpec((taps, width), lambda i: (0, i)),
        ],
        out_specs=[full, pl.BlockSpec((tokens, width), lambda i: (0, i))],
        out_shape=[jax.ShapeDtypeStruct(x.shape, F32), jax.ShapeDtypeStruct((tokens, both), BF16)],
        scratch_shapes=[pltpu.VMEM((tokens // SEG + taps - 1, SEG, LANES), BF16)],
        vmem=56,
        ride=ride,
        args=(x, att, cg, w, m_conv,),
    )


def merge_backward_kernel(taps, keep_ref, g_ref, att_ref, cg_ref, merged_ref, w_ref, m_conv_ref, datt_ref, dcg_ref, dw_ref, dconv_ref, g_rows, padded, j_padded, out, sums, pick):
    c = pl.program_id(0)
    tokens = g_ref.shape[0]
    rows = tokens // SEG
    half = pl.num_programs(0) // 2
    blocks, width, narrow = w_ref.shape

    @pl.when(c == 0)
    def _():
        g_rows[...] = low(g_ref[...])
        pick[...] = tap_pick(pick.shape)

    w = jnp.concatenate([w_ref[m] for m in range(blocks)], axis=1)
    dmerged = low(dot_nt(g_rows[...], w))
    dw = dot(merged_ref[...].T, g_rows[...])
    for m in range(blocks):
        dw_ref[m] = low(dw[:, m * narrow : (m + 1) * narrow])
    for l in range(width // LANES):
        cols = pl.ds(l * LANES, LANES)

        @pl.when(c < half)
        def _():
            fill_padded(j_padded, att_ref[:, cols].reshape(rows, SEG, LANES), taps)

        @pl.when(c >= half)
        def _():
            fill_padded(j_padded, cg_ref[:, cols].reshape(rows, SEG, LANES), taps)

        fill_padded(padded, dmerged[:, l * LANES : (l + 1) * LANES].reshape(rows, SEG, LANES), taps)
        dconv_ref[:, cols] = tap_grads(j_padded, padded.at[pl.ds((taps - 1) // 2, rows)], sums, pick, taps, rows, 8)

        def taps_of(k):
            return low(jnp.broadcast_to(m_conv_ref[taps - 1 - k : taps - k, cols], (SEG, LANES)))[None]

        def emit(start, value):
            block = value.shape[0]
            here = pl.ds(pl.multiple_of(start * SEG, block * SEG), block * SEG)
            value = value + padded[pl.ds(start + (taps - 1) // 2, block)].astype(F32)
            out[here, cols] = low(value.reshape(block * SEG, LANES) * keep_ref[here, :])

        convolve(padded, taps_of, taps, rows, 16, emit)

    @pl.when(c < half)
    def _():
        datt_ref[...] = out[...]

    @pl.when(c >= half)
    def _():
        dcg_ref[...] = out[...]


def merge_backward(keep, g, att, cg, merged, w, m_conv, ride=None):
    tokens, depth = g.shape
    blocks, both, cols = w.shape
    taps = m_conv.shape[0]
    width = 256
    steps = both // width
    half = steps // 2
    full = pl.BlockSpec((tokens, depth), lambda i: (0, 0))
    early = pl.BlockSpec((tokens, width), lambda i: (0, jnp.minimum(i, half - 1)))
    late = pl.BlockSpec((tokens, width), lambda i: (0, jnp.maximum(i - half, 0)))
    wide = pl.BlockSpec((tokens, width), lambda i: (0, i))
    w_spec = pl.BlockSpec((blocks, width, cols), lambda i: (0, i, 0))
    conv_spec = pl.BlockSpec((taps, width), lambda i: (0, i))
    padded = (tokens // SEG + taps - 1, SEG, LANES)
    return launch(
        functools.partial(merge_backward_kernel, taps),
        grid=(steps,),
        in_specs=[pl.BlockSpec(keep.shape, lambda i: (0, 0)), full, early, late, wide, w_spec, conv_spec],
        out_specs=[early, late, w_spec, conv_spec],
        out_shape=[
            jax.ShapeDtypeStruct((tokens, depth), BF16),
            jax.ShapeDtypeStruct((tokens, depth), BF16),
            jax.ShapeDtypeStruct(w.shape, BF16),
            jax.ShapeDtypeStruct(m_conv.shape, F32),
        ],
        scratch_shapes=[
            pltpu.VMEM((tokens, depth), BF16),
            pltpu.VMEM(padded, BF16),
            pltpu.VMEM(padded, BF16),
            pltpu.VMEM((tokens, width), BF16),
            *tap_scratch(taps),
        ],
        vmem=56,
        ride=ride,
        args=(keep, g, att, cg, merged, w, m_conv,),
    )


def no_ride(index):
    return None


def layer_forward(x, length, keep, weights, small, ride=no_ride):
    gains, table, table_back, g_gain, g_conv, m_conv = small
    taps = m_conv.shape[0]
    x1, h1 = ffn_forward(x, gains[0:1], weights(0), ride=ride(0))
    att, q, k, v, o = attention_forward(length, keep, x1, gains[1:2], weights(1), table, ride=ride(1))
    cg, *inner = gate_forward(keep, x1, gains[2:3], weights(2), g_gain, g_conv, taps, ride=ride(2))
    x2, merged = merge_forward(x1, att, cg, weights(3), m_conv, ride=ride(3))
    x3, h2, y = ffn_forward(x2, gains[3:4], weights(4), gains[4:5], ride=ride(4))
    saved = (x, x1, h1, att, q, k, v, o, cg, inner, x2, merged, x3, h2)
    return y, saved


def layer_backward(g, keep, saved, weights, small, ride=no_ride, ready=lambda index, grad: None, before_last=lambda *_: None):
    gains, table, table_back, g_gain, g_conv, m_conv = small
    taps = m_conv.shape[0]
    x, x1, h1, att, q, k, v, o, cg, inner, x2, merged, x3, h2 = saved
    ur, sr, ug, sg, mean, rstd, conv, gate = inner
    dx2, dg5, dgain3, dgain4 = ffn_backward(g, x2, gains[3:4], h2, weights(4), gains[4:5], x3, ride=ride(4))
    ready(4, dg5)
    datt, dcg, dg4, dm_conv = merge_backward(keep, dx2, att, cg, merged, weights(3), m_conv, ride=ride(3))
    ready(3, dg4)
    dx1, dg3, dgain2, dg_gain, dg_conv = gate_backward(
        keep, dcg, x1, gains[2:3], dx2, weights(2), ur, sr, ug, sg, conv, gate, mean, rstd, g_gain, g_conv, taps, ride=ride(2)
    )
    ready(2, dg3)
    dx1, dg2, dgain1, dtable = attention_backward(datt, x1, gains[1:2], dx1, weights(1), table_back, q, k, v, o, ride=ride(1))
    ready(1, dg2)
    dgains = jnp.concatenate([dgain1, dgain2, dgain3, dgain4], axis=0)
    before_last(0, dgains, (dtable, dg_gain, dg_conv, dm_conv))
    dx, dg1, dgain0 = ffn_backward(dx1, x, gains[0:1], h1, weights(0), ride=ride(0))
    ready(0, dg1)
    return dx, dgain0


def to_segments(values):
    tokens, depth = values.shape
    return values.reshape(SEG, tokens // SEG, depth).transpose(1, 0, 2).reshape(tokens, depth)


def from_segments(values):
    tokens, depth = values.shape
    return values.reshape(tokens // SEG, SEG, depth).transpose(1, 0, 2).reshape(tokens, depth)


def pack_layer(layer, ffn_in, ffn_out, attn_in, attn_out, cg_in, cg_out, merge_out, mp_index, mp_size):
    cols = merge_out.shape[2] // mp_size
    part = lax.dynamic_slice_in_dim(merge_out[layer], mp_index * cols, cols, axis=1)
    pieces = (
        jnp.concatenate([ffn_in[layer, 0], ffn_out[layer, 0].T], axis=1),
        jnp.concatenate([attn_in[layer, 0], attn_in[layer, 1], attn_in[layer, 2], attn_out[layer].T], axis=1),
        jnp.concatenate([cg_in[layer, 0], cg_in[layer, 1], cg_out[layer].T], axis=1),
        part,
        jnp.concatenate([ffn_in[layer, 1], ffn_out[layer, 1].T], axis=1),
    )
    return tuple(low(piece) for piece in pieces)


GROUPS = 5
OPENING = [
    (0, [("line", 0), (0, 0)]),
    (1, [(0, 1), (1, 0)]),
    (2, [(0, 2), (2, 0)]),
    (3, [(0, 3), (1, 1)]),
]
FORWARD = {
    0: [(0, [(1, 2), (3, 0), (6, 0)]), (1, [(2, 1)]), (2, [(1, 3), (3, 1)])],
    1: [(0, [(2, 2), (4, 0)]), (1, [(5, 0)]), (2, [(4, 1)]), (3, [(2, 3), (3, 2)])],
    2: [(0, [(4, 2)]), (1, [(6, 1)]), (2, [(7, 0)]), (3, [(3, 3), (8, 0)]), (4, [(5, 1)]), (6, [(4, 3)])],
    3: [(0, [(5, 2), (9, 0)])],
    4: [(0, [(5, 3), (6, 2), (8, 1)])],
    5: [(0, [(6, 3), (7, 1)])],
    6: [(0, [(7, 2)]), (1, [(9, 1)]), (3, [(7, 3)])],
    7: [(0, [(9, 2)]), (2, [(8, 2)]), (6, [(9, 3)]), (7, [(8, 3)])],
}
BACKWARD = {
    8: [(0, [(9, 0)]), (1, [(9, 1)])],
    7: [(0, [(9, 2), (8, 0)]), (1, [(9, 3), (8, 1)]), (2, [(8, 2)]), (3, [(8, 3)])],
    6: [(0, [(7, 0)]), (1, [(7, 1)])],
    5: [(0, [(7, 2), (6, 0)]), (2, [(6, 1)])],
    4: [(0, [(7, 3), (6, 2), (5, 0)]), (1, [(5, 1)])],
    3: [(0, [(6, 3), (5, 2), (4, 0)]), (1, [(4, 1)])],
    2: [(0, [(5, 3), (4, 2), (3, 0)]), (1, [(4, 3), (3, 1)]), (2, [(3, 2)]), (3, [(3, 3)])],
    1: [(0, [(2, 0)]), (1, [(2, 1)])],
    0: [(0, [(2, 2), (1, 0), ("small", 0)]), (1, [("small", 1)]), (2, [(1, 1), ("small", 2)]), (3, [("small", 3)])],
}
CLOSING = [
    (0, [(0, 0), (1, 2), (2, 3), ("all", 0), ("vector", 0), ("merge", 0)]),
    (1, [(0, 1), ("all", 1), ("vector", 1)]),
    (2, [(0, 2), (1, 3), ("all", 2), ("vector", 2)]),
    (3, [(0, 3), ("all", 3), ("vector", 3)]),
]


def reverse(values):
    shape = values.shape
    turn = (lax.broadcasted_iota(jnp.int32, (LANES, LANES), 0) + lax.broadcasted_iota(jnp.int32, (LANES, LANES), 1) == LANES - 1).astype(F32)
    blocks = values.reshape(-1, LANES)
    turned = jnp.dot(blocks, turn, precision=lax.Precision.HIGHEST, preferred_element_type=F32)
    return turned.reshape(*shape[:-1], -1, LANES)[..., ::-1, :].reshape(shape)


def plans(bits, groups):
    if bits == 3 and groups == 2 * GROUPS:
        return OPENING, FORWARD, BACKWARD, CLOSING
    count = groups + bits
    opening = [(r, [(g, r - g) for g in range(groups) if 0 <= r - g <= bits] + ([("line", 0)] if r == 0 else [])) for r in range(count)]
    small = [(r, [("small", r)]) for r in range(bits + 1)]
    closing = [(r, [(g, r - g) for g in range(groups) if 0 <= r - g <= bits]) for r in range(count)]
    for s in range(bits + 1):
        closing[s][1].extend([("all", s), ("vector", s)])
    closing.append((count, [("merge", 0)]))
    return opening, {}, {"small": small}, closing


def body(frames, cotangent, lengths, norm_gains, ffn_in, ffn_out, attn_in, attn_out, rel_bias, cg_in, csgu_gain, csgu_conv, cg_out, merge_conv, merge_out):
    layers = norm_gains.shape[0]
    mp_size = lax.axis_size("mp")
    bits = lax.axis_size("dp").bit_length() - 1
    mp_index = lax.axis_index("mp")
    length = lax.dynamic_slice_in_dim(lengths, mp_index, 1)
    tokens, depth = frames.shape
    taps = merge_conv.shape[1]
    heads, span = rel_bias.shape[1:]
    channels = csgu_gain.shape[1]

    flow = {}
    ids = iter(range(1, 100))

    def ride(plan):
        return Ride(flow, mp_size, bits, next(ids), plan)

    def alone(plan):
        launch(None, (len(plan),), [], [], [], vmem=62, ride=ride(plan))

    shards = []
    for layer in range(layers):
        shards += pack_layer(layer, ffn_in, ffn_out, attn_in, attn_out, cg_in, cg_out, merge_out, mp_index, mp_size)
    line = jnp.concatenate([rel_bias.reshape(layers, -1), csgu_gain, csgu_conv.reshape(layers, -1)], axis=1)
    line = line.reshape(-1, LANES)
    kinds = [Gather(mp_size, bits) for _ in shards] + [Gather(mp_size, bits, True)]
    names = list(range(len(shards))) + ["line"]
    for name, kind, buffer in zip(names, kinds, start_buffers(shards + [line], kinds, mp_size, bits)):
        flow[name] = (kind, buffer)
    opening, forward, backward, closing = plans(bits, len(shards))
    alone(opening)
    line_all = flow["line"][1].reshape(mp_size, layers, -1)
    table = line_all[:, :, : heads * span].reshape(mp_size, layers, heads, span)
    g_gain = line_all[:, :, heads * span : heads * span + channels].reshape(mp_size, layers, 1, channels)
    g_conv = line_all[:, :, heads * span + channels :].reshape(mp_size, layers, taps, channels)

    table_back = reverse(table)
    keep_rows = keep_lanes(length, tokens)
    state = to_segments(frames).astype(F32)
    weights = {}
    smalls = []
    saved = []
    for layer in range(layers):

        def weight(index):
            at = layer * GROUPS + index
            if at not in weights:
                w = flow[at][1]
                weights[at] = w.reshape(mp_size, -1, w.shape[-1])
            return weights[at]

        def beside(index):
            at = layer * GROUPS + index
            return ride(forward[at]) if at in forward else None

        smalls.append((norm_gains[layer], table[:, layer], table_back[:, layer], g_gain[:, layer], g_conv[:, layer], merge_conv[layer]))
        state, kept = layer_forward(state, length, keep_rows, weight, smalls[layer], beside)
        saved.append(kept)
    frame = lax.broadcasted_iota(jnp.int32, (tokens, 1), 0)
    keep = (frame < length).astype(F32)
    output_frames = from_segments(state) * keep
    incoming = to_segments(cotangent.astype(F32) * keep)
    tiny = [None] * layers
    counts = []

    def pack_small():
        split = [jnp.concatenate([t[1].reshape(mp_size, -1), t[2].reshape(mp_size, -1), t[3].reshape(mp_size, -1)], axis=1) for t in tiny]
        split = jnp.concatenate(split, axis=1).reshape(mp_size, -1, LANES)
        shared = jnp.concatenate([t[0].reshape(-1) for t in tiny] + [t[4].reshape(-1) for t in tiny])
        shared = jnp.pad(shared, (0, -shared.size % (mp_size * LANES))).reshape(mp_size, -1, LANES)
        counts.extend([split.shape[1], shared.shape[1]])
        padding = -sum(counts) % (16 << bits)
        packed = low(jnp.concatenate([split, shared, jnp.zeros((mp_size, padding, LANES), F32)], axis=1))
        packed = packed.reshape((mp_size,) + (2,) * bits + (-1, LANES))
        flow["small"] = (Scatter(mp_size, bits, *packed.shape[-2:]), packed)
        if "small" in backward:
            alone(backward["small"])

    for layer in reversed(range(layers)):

        def weight(index):
            return weights[layer * GROUPS + index]

        def beside(index):
            at = layer * GROUPS + index
            return ride(backward[at]) if at in backward else None

        def ready(index, grad):
            grad = grad.reshape((mp_size,) + (2,) * bits + (-1, grad.shape[-1]))
            flow[layer * GROUPS + index] = (Scatter(mp_size, bits, *grad.shape[-2:]), grad)

        def before_last(index, gains, small):
            tiny[layer] = (gains, *small)
            if layer == 0:
                pack_small()

        incoming, last_gain = layer_backward(incoming, keep_rows, saved[layer], weight, smalls[layer], beside, ready, before_last)
        if layer > 0:
            tiny[layer] = (jnp.concatenate([last_gain, tiny[layer][0]], axis=0), *tiny[layer][1:])
    vector = jnp.pad(last_gain.reshape(-1, LANES), ((0, -(depth // LANES) % 8), (0, 0)))
    kinds = [Gather(mp_size, bits), Gather(mp_size, bits)]
    flow["all"], flow["vector"] = zip(kinds, start_buffers([low(flow["small"][1]), vector], kinds, mp_size, bits))

    def start_merge():
        line = low(jnp.concatenate([flow[layer * GROUPS + 3][1] for layer in range(layers)], axis=0))
        kind = Gather(mp_size, bits, True)
        flow["merge"] = (kind, start_buffers([line], [kind], mp_size, bits)[0])

    if closing[-1][1] == [("merge", 0)]:
        alone(closing[:-1])
        start_merge()
        alone([(0, closing[-1][1])])
    else:
        start_merge()
        alone(closing)
    input_grad = from_segments(incoming)

    big = [flow[at][1] for at in range(layers * GROUPS)]
    packed = flow["all"][1].reshape(mp_size, -1, LANES).astype(F32)
    split_rows, shared_rows = counts
    split = lax.dynamic_index_in_dim(packed, mp_index, 0, keepdims=False)[:split_rows].reshape(layers, -1)
    grad_table = reverse(split[:, : heads * span].reshape(layers, heads, span))
    grad_g_gain = split[:, heads * span : heads * span + channels]
    grad_g_conv = split[:, heads * span + channels :].reshape(layers, taps, channels)
    shared = packed[:, split_rows : split_rows + shared_rows].reshape(-1)
    grad_gains = shared[: norm_gains.size - depth]
    vector = jnp.sum(flow["vector"][1].reshape(-1, flow["vector"][1].shape[-2] * LANES), axis=0)[:depth]
    grad_gains = jnp.concatenate([vector, grad_gains]).reshape(norm_gains.shape)
    grad_m_conv = shared[norm_gains.size - depth :][: merge_conv.size].reshape(merge_conv.shape)
    merge_all = flow["merge"][1].astype(F32).reshape(mp_size, layers, -1, LANES)
    grad_merge = merge_all.transpose(1, 2, 0, 3).reshape(merge_out.shape)

    f = ffn_in.shape[3]
    h = attn_in.shape[3]
    c = cg_in.shape[3]
    one, two, three, _, five = [[big[layer * GROUPS + g] for layer in range(layers)] for g in range(GROUPS)]
    grad_ffn_in = jnp.stack([jnp.stack([a[:, :f], b[:, :f]]) for a, b in zip(one, five)])
    grad_ffn_out = jnp.stack([jnp.stack([a[:, f:].T, b[:, f:].T]) for a, b in zip(one, five)])
    grad_attn_in = jnp.stack([jnp.stack([a[:, :h], a[:, h : 2 * h], a[:, 2 * h : 3 * h]]) for a in two])
    grad_attn_out = jnp.stack([a[:, 3 * h :].T for a in two])
    grad_cg_in = jnp.stack([jnp.stack([a[:, :c], a[:, c : 2 * c]]) for a in three])
    grad_cg_out = jnp.stack([a[:, 2 * c :].T for a in three])
    return (
        output_frames,
        input_grad,
        grad_gains,
        grad_ffn_in,
        grad_ffn_out,
        grad_attn_in,
        grad_attn_out,
        grad_table,
        grad_cg_in,
        grad_g_gain,
        grad_g_conv,
        grad_cg_out,
        grad_m_conv,
        grad_merge,
    )


def solution(mesh):
    tokens = P(("dp", "mp"), None)
    columns = P(None, None, "dp", "mp")
    rows = P(None, "mp", "dp")
    ffn_rows = P(None, None, "mp", "dp")
    heads = P(None, "mp", None)
    taps = P(None, None, "mp")
    return jax.shard_map(
        body,
        mesh=mesh,
        in_specs=(tokens, tokens, P("dp"), P(), columns, ffn_rows, columns, rows, heads, columns, P(None, "mp"), taps, rows, P(), P(None, "dp", None)),
        out_specs=(tokens, tokens, P(), columns, ffn_rows, columns, rows, heads, columns, P(None, "mp"), taps, rows, P(), P(None, "dp", None)),
        check_vma=False,
    )
```

```python
import functools

import jax
import jax.numpy as jnp
from jax import lax
from jax.experimental import pallas as pl
from jax.experimental.pallas import tpu as pltpu
from jax.sharding import PartitionSpec as P

EPSILON = 1e-05
MASKED = -1000000000.0
F32 = jnp.float32
BF16 = jnp.bfloat16
SEG = 16
GELU_A = 0.7978845608028654
GELU_B = 0.044715
HEAD = 64
PAIR = 2
LANES = 128


def dot(left, right):
    return lax.dot_general(left, right, (((1,), (0,)), ((), ())), preferred_element_type=F32)


def dot_nt(left, right):
    return lax.dot_general(left, right, (((1,), (1,)), ((), ())), preferred_element_type=F32)


def low(values):
    return values.astype(BF16)


def norm_parts(values):
    mean = jnp.mean(values, axis=-1, keepdims=True)
    centred = values - mean
    spread = jnp.mean(centred * centred, axis=-1, keepdims=True)
    rstd = lax.rsqrt(spread + EPSILON)
    return centred * rstd, rstd


def norm_back(normed, rstd, gain, grad):
    scaled = grad * gain
    first = jnp.mean(scaled, axis=-1, keepdims=True)
    second = jnp.mean(scaled * normed, axis=-1, keepdims=True)
    return rstd * (scaled - first - normed * second)


def gelu(values):
    half = 0.5 * values
    inner = values * (GELU_A + (GELU_A * GELU_B) * (values * values))
    return half + half * jnp.tanh(inner)


def gelu_and_slope(values):
    half = 0.5 * values
    square = values * values
    tanh = jnp.tanh(values * (GELU_A + (GELU_A * GELU_B) * square))
    value = half + half * tanh
    slope = 0.5 + 0.5 * tanh + (half - half * tanh * tanh) * (GELU_A + (3.0 * GELU_A * GELU_B) * square)
    return value, slope


def keep_lanes(length, tokens):
    at = lax.broadcasted_iota(jnp.int32, (tokens, LANES), 0)
    frame = (at % SEG) * (tokens // SEG) + at // SEG
    return (frame < length).astype(F32)


def split_lanes(lanes_ref, here, values):
    for l in range(values.shape[1] // LANES):
        lanes_ref[l, here, :] = values[:, l * LANES : (l + 1) * LANES]


def reorder(lanes_ref, stride, emit):
    blocks, tokens, _ = lanes_ref.shape
    count = tokens // stride
    for start in range(stride):
        for l in range(blocks):
            emit(start * count, l, lanes_ref[l, pl.ds(start, count, stride=stride), :])


def to_frames(lanes_ref, out_ref):
    rows = lanes_ref.shape[1] // SEG

    def emit(start, l, piece):
        out_ref[pl.ds(start, rows), pl.ds(l * LANES, LANES)] = piece

    reorder(lanes_ref, SEG, emit)


MESH = pl.DeviceIdType.MESH


class Links:
    def __init__(self, mp, bits, send, recv):
        self.mp = mp
        self.bits = bits
        self.me = lax.axis_index("mp")
        self.dp = lax.axis_index("dp")
        self.bit = [lax.rem(self.dp // (1 << i), 2) for i in range(bits)]
        self.send, self.recv = send, recv

    def other(self, i):
        return {"dp": self.dp + (1 - 2 * self.bit[i]) * (1 << i)}

    def along(self, offset):
        return {"mp": lax.rem(self.me + offset, self.mp)}

    def before(self, offset):
        return lax.rem(self.me + self.mp - offset, self.mp)

    def barrier(self):
        peers = [self.other(i) for i in range(self.bits)] + [self.along(offset) for offset in range(1, self.mp)]
        semaphore = pltpu.get_barrier_semaphore()
        for peer in peers:
            pl.semaphore_signal(semaphore, inc=1, device_id=peer, device_id_type=MESH)
        pl.semaphore_wait(semaphore, len(peers))

    def copy(self, at, source, target, arrives, device):
        def make(where):
            return pltpu.make_async_remote_copy(
                src_ref=source, dst_ref=where, send_sem=self.send.at[at], recv_sem=self.recv.at[at], device_id=device, device_id_type=MESH
            )

        return lambda: make(target), lambda: make(arrives)


def orders(bits):
    rest = list(range(1, bits))
    return rest + [0], rest[::-1] + [0]


def halves(mp):
    return (pl.ds(0, mp // 2), pl.ds(mp // 2, mp // 2))


class Gather:
    def __init__(self, mp, bits, line=False):
        self.mp, self.bits, self.line = mp, bits, line

    def copies(self, s):
        return self.mp - 1 if s == 0 else 1 if s == self.bits else 2

    def at(self, links, buffer, m, free, flip=None):
        index = [m]
        if not self.line:
            for i in reversed(range(self.bits)):
                index.append(pl.ds(0, 2) if i in free else 1 - links.bit[i] if i == flip else links.bit[i])
        return buffer.at[tuple(index)]

    def pairs(self, links, buffer, s, base):
        made = []

        def add(m, arriving, free, flip, device):
            mine = self.at(links, buffer, m, free)
            made.append(links.copy(base + len(made), mine, mine, self.at(links, buffer, arriving, free, flip), device))

        if s == 0:
            for offset in range(1, self.mp):
                add(links.me, links.before(offset), (), None, links.along(offset))
        elif s == self.bits:
            whole = pl.ds(0, self.mp)
            add(whole, whole, range(1, self.bits), 0, links.other(0))
        else:
            for half, order in zip(halves(self.mp), orders(self.bits)):
                add(half, half, order[: s - 1], order[s - 1], links.other(order[s - 1]))
        return made


class Scatter:
    def __init__(self, mp, bits, rows, cols):
        self.mp, self.bits, self.rows, self.cols = mp, bits, rows, cols

    def shape(self, s):
        return (self.mp,) + (2,) * (self.bits - s) + (self.rows, self.cols)

    def arrived(self, s):
        return self.shape(s + 1) if s < self.bits else self.shape(s)

    def own(self, s):
        return self.arrived(s) if s < self.bits else (self.rows, self.cols)

    def copies(self, s):
        return 1 if s == 0 else self.mp - 1 if s == self.bits else 2

    def loads(self, s):
        return 2 if 0 < s < self.bits else 1

    def parts(self, s):
        if s == 0:
            return [(pl.ds(0, self.mp), list(range(self.bits))[::-1], 0)]
        made = []
        for half, order in zip(halves(self.mp), orders(self.bits)):
            made.append((half, sorted(order[: self.bits - s], reverse=True), order[self.bits - 1 - s]))
        return made

    def pick(self, links, ref, m, left, now, flip):
        index = [m]
        for i in left:
            index.append(pl.ds(0, 2) if i != now else 1 - links.bit[i] if flip else links.bit[i])
        return ref.at[tuple(index)]

    def pairs(self, links, held, slots, s, base):
        made = []
        if s < self.bits:
            for m, left, now in self.parts(s):
                slot = slots.at[m]
                made.append(links.copy(base + len(made), self.pick(links, held, m, left, now, True), slot, slot, links.other(now)))
        else:
            for offset in range(1, self.mp):
                to = lax.rem(links.me + offset, self.mp)
                made.append(links.copy(base + len(made), held.at[to], slots.at[links.me], slots.at[links.before(offset)], links.along(offset)))
        return made

    def load_pairs(self, links, held, own, s):
        if s == self.bits:
            return [(held.at[links.me], own)]
        return [(self.pick(links, held, m, left, now, False), own.at[m]) for m, left, now in self.parts(s)]

    def add(self, links, slots, s, own, held):
        half = self.mp // 2

        def step(m, carry):
            for part, order in enumerate(orders(self.bits)):
                at = m + part * half
                if own is not None:
                    slots[at] += own[at]
                else:
                    left = sorted(order[: self.bits - s], reverse=True)
                    slots[at] += self.pick(links, held, at, left, order[self.bits - 1 - s], False)[...]
            return carry

        lax.fori_loop(0, half, step, 0)

    def total(self, links, slots, own, held):
        value = (own[...] if own is not None else held[links.me]).astype(F32)
        for offset in range(1, self.mp):
            value = value + slots[links.before(offset)].astype(F32)
        return value


HBM = pl.BlockSpec(memory_space=pltpu.HBM)


class Ride:
    def __init__(self, flow, mp, bits, collective_id, rounds):
        self.flow, self.mp, self.bits, self.collective_id = flow, mp, bits, collective_id
        self.rounds = rounds
        names = []
        self.base = {}
        self.count = 0
        self.stages = {}
        for _, tasks in rounds:
            for name, s in tasks:
                if name not in names:
                    names.append(name)
                    self.stages[name] = []
                self.stages[name].append(s)
                self.base[name, s] = self.count
                self.count += flow[name][0].copies(s)
        self.gathers = [n for n in names if isinstance(flow[n][0], Gather)]
        self.scatters = [n for n in names if isinstance(flow[n][0], Scatter)]
        self.local = {}
        self.local_count = 0
        self.scratch = []
        self.place = {}
        for n in self.scatters:
            kind = flow[n][0]
            first, last = self.stages[n][0], self.stages[n][-1]
            self.local[n] = self.local_count
            self.local_count += kind.loads(first) + 1
            self.place[n, "own"] = len(self.scratch)
            self.scratch.append(pltpu.VMEM(kind.own(first), BF16))
            for s in self.stages[n]:
                self.place[n, s] = len(self.scratch)
                self.scratch.append(pltpu.VMEM(kind.arrived(s), BF16))
        self.sems = [pltpu.SemaphoreType.DMA((max(1, k),)) for k in (self.count, self.count, self.local_count)]

    def inputs(self):
        return [self.flow[n][1] for n in self.gathers + self.scatters]

    def finals(self, n):
        return self.stages[n][-1] == self.bits

    def outputs(self):
        shapes = [jax.ShapeDtypeStruct(self.flow[n][1].shape, self.flow[n][1].dtype) for n in self.gathers]
        specs = [HBM] * len(shapes)
        for n in self.scatters:
            kind = self.flow[n][0]
            if self.finals(n):
                shapes.append(jax.ShapeDtypeStruct((kind.rows, kind.cols), F32))
                specs.append(pl.BlockSpec((kind.rows, kind.cols), lambda *_: (0, 0)))
            else:
                shapes.append(jax.ShapeDtypeStruct(kind.shape(self.stages[n][-1] + 1), BF16))
                specs.append(HBM)
        return shapes, specs

    def bind(self, ins, outs, scratch):
        names = self.gathers + self.scatters
        self.ins = dict(zip(names, ins))
        self.outs = dict(zip(names, outs))
        send, recv, self.local_sem = scratch[:3]
        self.buffers = scratch[3:]
        self.links = Links(self.mp, self.bits, send, recv)

    def held(self, n, s):
        return self.ins[n] if s == self.stages[n][0] else self.buffers[self.place[n, s - 1]]

    def pairs(self, task):
        n, s = task
        kind = self.flow[n][0]
        if n in self.gathers:
            return kind.pairs(self.links, self.outs[n], s, self.base[task])
        return kind.pairs(self.links, self.held(n, s), self.buffers[self.place[task]], s, self.base[task])

    def loads(self, n):
        first = self.stages[n][0]
        pairs = self.flow[n][0].load_pairs(self.links, self.ins[n], self.buffers[self.place[n, "own"]], first)
        return [functools.partial(pltpu.make_async_copy, a, b, self.local_sem.at[self.local[n] + i]) for i, (a, b) in enumerate(pairs)]

    def stores(self, n):
        last = self.stages[n][-1]
        at = self.local[n] + self.flow[n][0].loads(self.stages[n][0])
        return pltpu.make_async_copy(self.buffers[self.place[n, last]], self.outs[n], self.local_sem.at[at])

    def begin(self, number):
        tasks = self.rounds[number][1]
        if number == 0:
            self.links.barrier()
            self.finished = set()
        for n, s in tasks:
            if s > self.stages[n][0]:
                self.finish((n, s - 1))
            elif n in self.scatters:
                for load in self.loads(n):
                    load().start()
            for out, _ in self.pairs((n, s)):
                out().start()

    def finish(self, task):
        if task in self.finished:
            return
        self.finished.add(task)
        n, s = task
        for _, arriving in self.pairs(task):
            arriving().wait_recv()
        if n in self.scatters:
            kind = self.flow[n][0]
            own = None
            if s == self.stages[n][0]:
                own = self.buffers[self.place[n, "own"]]
                for load in self.loads(n):
                    load().wait()
            slots = self.buffers[self.place[task]]
            if s < self.bits:
                kind.add(self.links, slots, s, own, self.held(n, s))
                if s == self.stages[n][-1]:
                    self.stores(n).start()
            else:
                self.outs[n][...] = kind.total(self.links, slots, own, self.held(n, s))

    def end(self):
        for _, tasks in self.rounds:
            for task in tasks:
                self.finish(task)
        for _, tasks in self.rounds:
            for task in tasks:
                for out, _ in self.pairs(task):
                    out().wait_send()
        for n in self.scatters:
            if not self.finals(n):
                self.stores(n).wait()

    def done(self, arrays):
        for n, array in zip(self.gathers + self.scatters, arrays):
            self.flow[n] = (self.flow[n][0], array)


def launch(kernel, grid, in_specs, out_specs, out_shape, scratch_shapes=(), vmem=56, ride=None, args=()):
    scratch_shapes = list(scratch_shapes)
    if ride is None:
        return pl.pallas_call(
            kernel,
            grid=grid,
            in_specs=in_specs,
            out_specs=out_specs,
            out_shape=out_shape,
            scratch_shapes=scratch_shapes,
            compiler_params=pltpu.CompilerParams(vmem_limit_bytes=vmem * 2**20),
        )(*args)
    extra_in = ride.inputs()
    extra_shapes, extra_specs = ride.outputs()
    n_in, n_out, n_scratch = len(in_specs), len(out_specs), len(scratch_shapes)

    def riding(*refs):
        ins, refs = refs[:n_in], refs[n_in:]
        ride_ins, refs = refs[: len(extra_in)], refs[len(extra_in) :]
        outs, refs = refs[:n_out], refs[n_out:]
        ride_outs, refs = refs[: len(extra_shapes)], refs[len(extra_shapes) :]
        scratch, ride_scratch = refs[:n_scratch], refs[n_scratch:]
        ride.bind(ride_ins, ride_outs, ride_scratch)
        step = pl.program_id(0)
        for number, (at, _) in enumerate(ride.rounds):

            @pl.when(step == at)
            def _():
                ride.begin(number)

        if kernel is not None:
            kernel(*ins, *outs, *scratch)

        @pl.when(step == pl.num_programs(0) - 1)
        def _():
            ride.end()

    made = pl.pallas_call(
        riding,
        grid=grid,
        in_specs=list(in_specs) + [HBM] * len(extra_in),
        out_specs=list(out_specs) + extra_specs,
        out_shape=list(out_shape) + extra_shapes,
        scratch_shapes=scratch_shapes + ride.sems + ride.scratch,
        input_output_aliases={n_in + i: n_out + i for i in range(len(ride.gathers))},
        compiler_params=pltpu.CompilerParams(collective_id=ride.collective_id, has_side_effects=True, vmem_limit_bytes=vmem * 2**20),
    )(*args, *extra_in)
    ride.done(made[n_out:])
    return made[:n_out]


def start_kernel(mp, bits, kinds, *refs):
    count = len(kinds)
    shards, buffers, local = refs[:count], refs[count : 2 * count], refs[2 * count]
    links = Links(mp, bits, None, None)
    copies = [pltpu.make_async_copy(shards[i], kinds[i].at(links, buffers[i], links.me, ()), local.at[i]) for i in range(count)]
    for copy in copies:
        copy.start()
    for copy in copies:
        copy.wait()


def start_buffers(shards, kinds, mp, bits):
    shapes = []
    for shard, kind in zip(shards, kinds):
        shapes.append(jax.ShapeDtypeStruct((mp,) + (() if kind.line else (2,) * bits) + shard.shape, shard.dtype))
    return pl.pallas_call(
        functools.partial(start_kernel, mp, bits, kinds),
        in_specs=[pl.BlockSpec(memory_space=pltpu.VMEM)] * len(shards),
        out_specs=[HBM] * len(shards),
        out_shape=shapes,
        scratch_shapes=[pltpu.SemaphoreType.DMA((len(shards),))],
    )(*shards)


def fill_padded(padded, values, taps):
    rows, _, lanes = values.shape
    half = (taps - 1) // 2
    padded[pl.ds(half, rows)] = values
    place = lax.broadcasted_iota(jnp.int32, (half, SEG, lanes), 1)
    before = pltpu.roll(values[rows - half :].astype(F32), 1, axis=1)
    padded[pl.ds(0, half)] = low(jnp.where(place == 0, 0.0, before))
    after = pltpu.roll(values[:half].astype(F32), SEG - 1, axis=1)
    padded[pl.ds(half + rows, half)] = low(jnp.where(place == SEG - 1, 0.0, after))


def convolve(padded, taps_of, taps, rows, block, emit):
    weights = [taps_of(k) for k in range(taps)]

    def step(index, carry):
        start = index * block
        total = None
        for first in range(0, taps, 8):
            part = None
            for k in range(first, min(taps, first + 8)):
                term = weights[k] * padded[pl.ds(start + k, block)]
                part = term if part is None else part + term
            part = part.astype(F32)
            total = part if total is None else total + part
        emit(start, total)
        return carry

    lax.fori_loop(0, rows // block, step, 0)


def tap_grads(padded, grads, sums, pick, taps, rows, block):
    group = 8
    count = sums.shape[0] // SEG
    for first in range(0, taps, group):
        ks = range(first, min(taps, first + group))

        def step(index, totals):
            start = index * block
            here = grads[pl.ds(start, block)]
            made = []
            for k, total in zip(ks, totals):
                term = here * padded[pl.ds(start + k, block)]
                size = block
                while size > 1:
                    size //= 2
                    term = term[:size] + term[size:]
                made.append(total + term[0].astype(F32))
            return tuple(made)

        zero = jnp.zeros((SEG, LANES), F32)
        totals = lax.fori_loop(0, rows // block, step, (zero,) * len(ks), unroll=True)
        for k, total in zip(ks, totals):
            sums[pl.ds(k * SEG, SEG), :] = total
    for k in range(taps, count):
        sums[pl.ds(k * SEG, SEG), :] = jnp.zeros((SEG, LANES), F32)
    high = low(sums[...])
    rest = low(sums[...] - high.astype(F32))
    return (dot(pick[...], high) + dot(pick[...], rest))[:taps]


def tap_pick(shape):
    row = lax.broadcasted_iota(jnp.int32, shape, 0)
    col = lax.broadcasted_iota(jnp.int32, shape, 1)
    return low(((col >= row * SEG) & (col < row * SEG + SEG)).astype(F32))


def tap_scratch(taps):
    count = -(-taps // 16) * 16
    return [pltpu.VMEM((count * SEG, LANES), F32), pltpu.VMEM((count, count * SEG), BF16)]


def ffn_forward_kernel(final, ending, blocks, x_ref, gain_ref, w_in_ref, w_out_ref, *rest):
    if ending:
        last_ref, keep_ref, out_ref, h_ref, y_ref, flat = rest
    elif final:
        last_ref, out_ref, h_ref, y_ref = rest
    else:
        out_ref, h_ref = rest
    width = h_ref.shape[2]
    x = x_ref[...]
    normed, _ = norm_parts(x)
    a = low(normed * gain_ref[...])
    total = None
    for m in range(blocks):
        h = dot(a, w_in_ref[m])
        h_ref[m] = low(h)
        half = 0.5 * h
        s = low(half + half * jnp.tanh(half))
        part = dot_nt(s, w_out_ref[m])
        total = part if total is None else total + part
    out = x + 0.5 * total
    out_ref[...] = out
    if final:
        normed, _ = norm_parts(out)
        y = normed * last_ref[...]
        if ending:
            i = pl.program_id(0)
            tile = y.shape[0]
            here = pl.ds(pl.multiple_of(i * tile, tile), tile)
            for l in range(flat.shape[0]):
                flat[l, here, :] = y[:, l * LANES : (l + 1) * LANES] * keep_ref[here, :]

            @pl.when(i == pl.num_programs(0) - 1)
            def _():
                to_frames(flat, y_ref)
        else:
            y_ref[...] = y


def weight_parts(w):
    if isinstance(w, tuple):
        return w, (0, 0), w[0].shape
    return (w, w), (0, 1), w.shape[:2] + (w.shape[2] // 2,)


def ffn_forward(x, gain, w, last=None, keep=None, ride=None):
    tokens, depth = x.shape
    w, place, (blocks, _, width) = weight_parts(w)
    tile = min(256, tokens)
    row = pl.BlockSpec((tile, depth), lambda i: (i, 0))
    vec = pl.BlockSpec((1, depth), lambda i: (0, 0))
    out_shape = [jax.ShapeDtypeStruct(x.shape, F32), jax.ShapeDtypeStruct((blocks, tokens, width), BF16)]
    out_specs = [row, pl.BlockSpec((blocks, tile, width), lambda i: (0, i, 0))]
    in_specs = [row, vec] + [pl.BlockSpec((blocks, depth, width), lambda i, p=p: (0, 0, p)) for p in place]
    args = [x, gain, *w]
    scratch = []
    if last is not None:
        in_specs.append(vec)
        args.append(last)
        out_shape.append(jax.ShapeDtypeStruct(x.shape, F32))
        out_specs.append(row)
    if keep is not None:
        in_specs.append(pl.BlockSpec(keep.shape, lambda i: (0, 0)))
        args.append(keep)
        out_specs[-1] = pl.BlockSpec((tokens, depth), lambda i: (0, 0))
        scratch.append(pltpu.VMEM((depth // LANES, tokens, LANES), F32))
    return launch(
        functools.partial(ffn_forward_kernel, last is not None, keep is not None, blocks),
        grid=(tokens // tile,),
        in_specs=in_specs,
        out_specs=out_specs,
        out_shape=out_shape,
        scratch_shapes=scratch,
        vmem=56,
        ride=ride,
        args=args,
    )


def ffn_backward_kernel(final, ending, tile, g_ref, x_ref, gain_ref, h_ref, w_in_ref, w_out_ref, *rest):
    if final:
        last_ref, y_ref, dx_ref, dw_ref, dgain_ref, dlast_ref, grad, at, gt, a_rows, g_rows, s_rows, d_rows, da, flat = rest
    elif ending:
        dx_ref, dw_ref, dgain_ref, grad, at, gt, a_rows, g_rows, s_rows, d_rows, da, flat = rest
    else:
        dx_ref, dw_ref, dgain_ref, grad, at, gt, a_rows, g_rows, s_rows, d_rows, da, flat = rest
    m = pl.program_id(0)
    tokens = x_ref.shape[0]
    width = h_ref.shape[2]
    chunks = tokens // tile

    @pl.when(m == 0)
    def _():
        if final:
            dlast_ref[...] = jnp.zeros_like(dlast_ref)
        for c in range(chunks):
            here = pl.ds(c * tile, tile)
            g = g_ref[here, :]
            if final:
                normed, rstd = norm_parts(y_ref[here, :])
                dlast_ref[...] += jnp.sum(g * normed, axis=0, keepdims=True)
                g = norm_back(normed, rstd, last_ref[...], g)
                grad[here, :] = g
            g_low = low(0.5 * g)
            g_rows[here, :] = g_low
            normed, _ = norm_parts(x_ref[here, :])
            a_rows[here, :] = low(normed * gain_ref[...])
        at[...] = a_rows[...].T
        if not ending:
            gt[...] = g_rows[...].T

    w_in = w_in_ref[0]
    w_out = w_out_ref[0]
    for c in range(chunks):
        here = pl.ds(c * tile, tile)
        ds = dot(g_rows[here, :], w_out)
        h = h_ref[0, here, :].astype(F32)
        half = 0.5 * h
        tanh = jnp.tanh(half)
        s = half + half * tanh
        if not ending:
            s_rows[here, :] = low(s)
        sig = 0.5 + 0.5 * tanh
        dh = low(ds * (sig + s * (1.0 - sig)))
        d_rows[here, :] = dh
        part = dot_nt(dh, w_in)

        @pl.when(m == 0)
        def _():
            da[here, :] = part

        @pl.when(m != 0)
        def _():
            da[here, :] += part

    dw_ref[0, :, :width] = low(dot(at[...], d_rows[...]))
    if not ending:
        dw_ref[0, :, width:] = low(dot(gt[...], s_rows[...]))

    @pl.when(m == pl.num_programs(0) - 1)
    def _():
        dgain_ref[...] = jnp.zeros_like(dgain_ref)
        for c in range(chunks):
            here = pl.ds(c * tile, tile)
            normed, rstd = norm_parts(x_ref[here, :])
            d = da[here, :]
            dgain_ref[...] += jnp.sum(d * normed, axis=0, keepdims=True)
            base = grad[here, :] if final else g_ref[here, :]
            dx = base + norm_back(normed, rstd, gain_ref[...], d)
            if ending:
                split_lanes(flat, here, dx)
            else:
                dx_ref[here, :] = dx
        if ending:
            to_frames(flat, dx_ref)


def ffn_backward(g, x, gain, h, w, last=None, final_in=None, ending=False, ride=None):
    tokens, depth = x.shape
    w, place, (blocks, _, width) = weight_parts(w)
    tile = tokens
    full = pl.BlockSpec((tokens, depth), lambda i: (0, 0))
    vec = pl.BlockSpec((1, depth), lambda i: (0, 0))
    vec_shape = jax.ShapeDtypeStruct((1, depth), F32)
    in_specs = [full, full, vec, pl.BlockSpec((1, tokens, width), lambda i: (i, 0, 0))]
    in_specs += [pl.BlockSpec((1, depth, width), lambda i, p=p: (i, 0, p)) for p in place]
    args = [g, x, gain, h, *w]
    dw_width = width if ending else 2 * width
    out_specs = [full] + [pl.BlockSpec((1, depth, dw_width), lambda i: (i, 0, 0)), vec]
    out_shape = [jax.ShapeDtypeStruct(x.shape, F32)] + [jax.ShapeDtypeStruct((blocks, depth, dw_width), BF16), vec_shape]
    if last is not None:
        in_specs += [vec, full]
        args += [last, final_in]
        out_specs.append(vec)
        out_shape.append(vec_shape)
    return launch(
        functools.partial(ffn_backward_kernel, last is not None, ending, tile),
        grid=(blocks,),
        in_specs=in_specs,
        out_specs=out_specs,
        out_shape=out_shape,
        scratch_shapes=[
            pltpu.VMEM((tokens, depth) if last is not None else (8, 128), F32),
            pltpu.VMEM((depth, tokens), BF16),
            pltpu.VMEM((depth, tokens), BF16),
            pltpu.VMEM((tokens, depth), BF16),
            pltpu.VMEM((tokens, depth), BF16),
            pltpu.VMEM((tokens, width), BF16),
            pltpu.VMEM((tokens, width), BF16),
            pltpu.VMEM((tokens, depth), F32),
            pltpu.VMEM((depth // LANES, tokens if ending else 8, LANES), F32),
        ],
        vmem=56,
        ride=ride,
        args=args,
    )


def ffn_out_grad_kernel(g_ref, h_ref, dw_ref, gt):
    @pl.when(pl.program_id(0) == 0)
    def _():
        gt[...] = low(0.5 * g_ref[...]).T

    half = 0.5 * h_ref[0].astype(F32)
    dw_ref[0] = low(dot(gt[...], low(half + half * jnp.tanh(half))))


def ffn_out_grad(g, h, ride=None):
    tokens, depth = g.shape
    blocks, _, width = h.shape
    return launch(
        ffn_out_grad_kernel,
        grid=(blocks,),
        in_specs=[pl.BlockSpec((tokens, depth), lambda i: (0, 0)), pl.BlockSpec((1, tokens, width), lambda i: (i, 0, 0))],
        out_specs=[pl.BlockSpec((1, depth, width), lambda i: (i, 0, 0))],
        out_shape=[jax.ShapeDtypeStruct((blocks, depth, width), BF16)],
        scratch_shapes=[pltpu.VMEM((depth, tokens), BF16)],
        vmem=56,
        ride=ride,
        args=(g, h),
    )


def attention_forward_kernel(len_ref, keep_ref, x_ref, gain_ref, w_ref, table_ref, att_ref, q_ref, k_ref, v_ref, o_ref, lse_ref, b_rows, total, bias, flat):
    m = pl.program_id(0)
    tokens = x_ref.shape[0]
    rows = tokens // SEG
    length = len_ref[0]
    tile = 384

    @pl.when(m == 0)
    def _():
        for c in range(tokens // tile):
            here = pl.ds(c * tile, tile)
            normed, _ = norm_parts(x_ref[here, :])
            split_lanes(flat, here, normed * gain_ref[...])

        def emit(start, l, piece):
            b_rows[pl.ds(start, rows), pl.ds(l * LANES, LANES)] = low(piece)

        reorder(flat, SEG, emit)

    wide = PAIR * HEAD
    qkv = dot(b_rows[...], w_ref[0, :, : 3 * wide])
    lane = lax.broadcasted_iota(jnp.int32, (tokens, LANES), 1)
    at = lax.broadcasted_iota(jnp.int32, (tokens, LANES), 0)
    hidden = jnp.where(at < length, 0.0, MASKED)
    for head in range(PAIR):
        cols = pl.ds(head * LANES, LANES)

        def mine(piece):
            return piece if head == 0 else pltpu.roll(piece, HEAD, axis=1)

        q = low(mine(qkv[:, :wide])).astype(F32) * (HEAD**-0.5)
        k = mine(qkv[:, wide : 2 * wide])
        v = mine(qkv[:, 2 * wide :])
        q_ref[0, :, cols] = low(jnp.where(lane < HEAD, q, jnp.where(lane == HEAD, 1.0, 0.0)))
        k_ref[0, :, cols] = low(jnp.where(lane < HEAD, k, jnp.where(lane == HEAD, hidden, jnp.where(lane <= HEAD + 2, -1.0, 0.0))))
        v_ref[0, :, cols] = low(jnp.where(lane < HEAD, v, jnp.where(lane <= HEAD + 1, 1.0, 0.0)))
        span = table_ref.shape[2]
        line = jnp.broadcast_to(table_ref[0, head : head + 1, :], (LANES, span))
        bias[...] = pltpu.roll(line, span - LANES, axis=1, stride=1, stride_axis=0)
        for t in range(tokens // tile):
            here = pl.ds(t * tile, tile)
            scores = dot_nt(q_ref[0, here, cols], k_ref[0, :, cols])
            parts = []
            for sub in range(tile // LANES):
                first = tokens - LANES - t * tile - sub * LANES
                parts.append(scores[sub * LANES : (sub + 1) * LANES] + bias[:, pl.ds(first, tokens)])
            scores = jnp.concatenate(parts, axis=0)
            peak = jnp.max(scores, axis=-1, keepdims=True)
            expos = low(jnp.exp(scores - peak))
            out = dot(expos, v_ref[0, :, cols])
            denom = out[:, HEAD : HEAD + 1]
            out = out * (1.0 / denom)
            lse = peak + jnp.log(denom)
            if head == 0:
                o_ref[0, here, :] = low(out)
            else:
                lane_t = lax.broadcasted_iota(jnp.int32, (tile, LANES), 1)
                o_ref[0, here, :] = low(jnp.where(lane_t < HEAD, o_ref[0, here, :].astype(F32), pltpu.roll(out, HEAD, axis=1)))
            lse_ref[here, :] = jnp.broadcast_to(lse, (tile, LANES))
        lse = lse_ref[...]
        lse_high = low(lse).astype(F32)
        q_now = q_ref[0, :, cols].astype(F32)
        q_ref[0, :, cols] = low(jnp.where(lane == HEAD + 1, lse_high, jnp.where(lane == HEAD + 2, lse - lse_high, q_now)))
    part = dot_nt(o_ref[0], w_ref[0, :, 3 * wide :])

    @pl.when(m == 0)
    def _():
        total[...] = part

    @pl.when(m != 0)
    def _():
        total[...] += part

    @pl.when(m == pl.num_programs(0) - 1)
    def _():
        split_lanes(flat, pl.ds(0, tokens), total[...])

        def emit(start, l, piece):
            att_ref[pl.ds(start, SEG), pl.ds(l * LANES, LANES)] = low(piece * keep_ref[pl.ds(start, SEG), :])

        reorder(flat, rows, emit)


def attention_forward(length, keep, x, gain, w, table, ride=None):
    tokens, depth = x.shape
    blocks = w.shape[0]
    full = pl.BlockSpec((tokens, depth), lambda i: (0, 0))
    heads = pl.BlockSpec((1, tokens, PAIR * LANES), lambda i: (i, 0, 0))
    pair = pl.BlockSpec((1, tokens, LANES), lambda i: (i, 0, 0))
    heads_shape = jax.ShapeDtypeStruct((blocks, tokens, PAIR * LANES), BF16)
    return launch(
        attention_forward_kernel,
        grid=(blocks,),
        in_specs=[
            pl.BlockSpec(memory_space=pltpu.SMEM),
            pl.BlockSpec(keep.shape, lambda i: (0, 0)),
            full,
            pl.BlockSpec((1, depth), lambda i: (0, 0)),
            pl.BlockSpec((1, depth, w.shape[2]), lambda i: (i, 0, 0)),
            pl.BlockSpec((1, PAIR, table.shape[2]), lambda i: (i, 0, 0)),
        ],
        out_specs=[full, heads, heads, heads, pair],
        out_shape=[
            jax.ShapeDtypeStruct((tokens, depth), BF16),
            heads_shape,
            heads_shape,
            heads_shape,
            jax.ShapeDtypeStruct((blocks, tokens, LANES), BF16),
        ],
        scratch_shapes=[
            pltpu.VMEM((tokens, LANES), F32),
            pltpu.VMEM((tokens, depth), BF16),
            pltpu.VMEM((tokens, depth), F32),
            pltpu.VMEM((LANES, table.shape[2]), F32),
            pltpu.VMEM((depth // LANES, tokens, LANES), F32),
        ],
        vmem=56,
        ride=ride,
        args=(length, keep, x, gain, w, table,),
    )


def attention_backward_kernel(
    datt_ref, x_ref, gain_ref, res_ref, w_ref, table_ref, q_ref, k_ref, v_ref, o_ref,
    dx_ref, dw_ref, dgain_ref, dtable_ref,
    b_t, g_t, g_rows, flat, bias, dbias, do_aug, d_pair, dq_t, k_t, d_rows, db,
):
    m = pl.program_id(0)
    tokens = x_ref.shape[0]
    rows = tokens // SEG
    wide = PAIR * HEAD
    tile = 256
    span = table_ref.shape[2]
    stored = tokens // tile

    @pl.when(m == 0)
    def _():
        def emit(start, l, piece):
            g_rows[pl.ds(start, rows), pl.ds(l * LANES, LANES)] = low(piece)

        for c in range(tokens // tile):
            here = pl.ds(c * tile, tile)
            normed, _ = norm_parts(x_ref[here, :])
            split_lanes(flat, here, normed * gain_ref[...])
        reorder(flat, SEG, emit)
        b_t[...] = g_rows[...].T
        split_lanes(flat, pl.ds(0, tokens), datt_ref[...].astype(F32))
        reorder(flat, SEG, emit)
        g_t[...] = g_rows[...].T

    w_out = w_ref[0, :, 3 * wide :]
    do = low(dot(g_rows[...], w_out))
    dw_ref[0, :, 3 * wide :] = low(dot(g_t[...], o_ref[0]))
    lane = lax.broadcasted_iota(jnp.int32, (tokens, LANES), 1)
    do_full = do.astype(F32)
    product = do_full * o_ref[0].astype(F32)
    for head in range(PAIR):
        cols = pl.ds(head * LANES, LANES)
        inside = lane < HEAD if head == 0 else lane >= HEAD
        delta = jnp.sum(jnp.where(inside, product, 0.0), axis=-1, keepdims=True)
        delta_high = low(delta).astype(F32)
        mine = do_full if head == 0 else pltpu.roll(do_full, HEAD, axis=1)
        do_aug[...] = low(jnp.where(lane < HEAD, mine, jnp.where(lane == HEAD, -delta_high, jnp.where(lane == HEAD + 1, delta_high - delta, 0.0))))
        k_t[...] = k_ref[0, :, cols].T
        line = jnp.broadcast_to(table_ref[0, head : head + 1, :], (LANES, span))
        bias[...] = pltpu.roll(line, span - (LANES - 1), axis=1, stride=1, stride_axis=0)
        dbias[...] = jnp.zeros_like(dbias)
        for t in range(stored):
            here = pl.ds(t * tile, tile)
            scores = dot_nt(k_ref[0, here, cols], q_ref[0, :, cols])
            grads = dot_nt(v_ref[0, here, cols], do_aug[...])
            p_parts = []
            d_parts = []
            for sub in range(tile // LANES):
                first = tokens - LANES - t * tile - sub * LANES
                now = slice(sub * LANES, (sub + 1) * LANES)
                p = jnp.exp(scores[now] + bias[:, pl.ds(first, tokens)])
                ds = low(p * grads[now])
                dbias[:, pl.ds(first, tokens)] += ds.astype(F32)
                p_parts.append(low(p))
                d_parts.append(ds)
            p = jnp.concatenate(p_parts, axis=0)
            ds = jnp.concatenate(d_parts, axis=0)
            dv = dot(p, do_aug[...])
            dk = dot(ds, q_ref[0, :, cols])
            dq = dot(k_t[:, here], ds)
            if t == 0:
                dq_t[...] = dq
            else:
                dq_t[...] += dq
            if head == 0:
                d_pair[1, here, :] = dk
                d_pair[2, here, :] = dv
            else:
                lane_t = lax.broadcasted_iota(jnp.int32, (tile, LANES), 1)
                d_pair[1, here, :] = jnp.where(lane_t < HEAD, d_pair[1, here, :], pltpu.roll(dk, HEAD, axis=1))
                d_pair[2, here, :] = jnp.where(lane_t < HEAD, d_pair[2, here, :], pltpu.roll(dv, HEAD, axis=1))
        dq = dq_t[...].T * (HEAD**-0.5)
        if head == 0:
            d_pair[0] = dq
        else:
            d_pair[0] = jnp.where(lane < HEAD, d_pair[0], pltpu.roll(dq, HEAD, axis=1))
        folded = dbias[...]
        count = LANES
        while count > 1:
            count //= 2
            folded = folded[:count] + pltpu.roll(folded[count:], span - count, axis=1)
        dtable_ref[0, head : head + 1, :] = pltpu.roll(folded, LANES - 1, axis=1)
    for part in range(3):
        d_rows[:, pl.ds(part * wide, wide)] = low(d_pair[part])
    dw_ref[0, :, : 3 * wide] = low(dot(b_t[...], d_rows[...]))
    part = dot_nt(d_rows[...], w_ref[0, :, : 3 * wide])

    @pl.when(m == 0)
    def _():
        db[...] = part

    @pl.when(m != 0)
    def _():
        db[...] += part

    @pl.when(m == pl.num_programs(0) - 1)
    def _():
        dgain_ref[...] = jnp.zeros_like(dgain_ref)
        split_lanes(flat, pl.ds(0, tokens), db[...])

        def emit(start, l, piece):
            db[pl.ds(start, SEG), pl.ds(l * LANES, LANES)] = piece

        reorder(flat, rows, emit)
        for c in range(tokens // tile):
            here = pl.ds(c * tile, tile)
            normed, rstd = norm_parts(x_ref[here, :])
            d = db[here, :]
            dgain_ref[...] += jnp.sum(d * normed, axis=0, keepdims=True)
            dx_ref[here, :] = res_ref[here, :] + norm_back(normed, rstd, gain_ref[...], d)


def attention_backward(datt, x, gain, res, w, table_back, q, k, v, o, ride=None):
    tokens, depth = x.shape
    blocks = w.shape[0]
    span = table_back.shape[2]
    full = pl.BlockSpec((tokens, depth), lambda i: (0, 0))
    heads = pl.BlockSpec((1, tokens, PAIR * LANES), lambda i: (i, 0, 0))
    pair = pl.BlockSpec((1, tokens, LANES), lambda i: (i, 0, 0))
    vec = pl.BlockSpec((1, depth), lambda i: (0, 0))
    w_spec = pl.BlockSpec((1, depth, w.shape[2]), lambda i: (i, 0, 0))
    t_spec = pl.BlockSpec((1, PAIR, span), lambda i: (i, 0, 0))
    wide = PAIR * HEAD
    return launch(
        attention_backward_kernel,
        grid=(blocks,),
        in_specs=[full, full, vec, full, w_spec, t_spec, heads, heads, heads, pair],
        out_specs=[full, w_spec, vec, t_spec],
        out_shape=[
            jax.ShapeDtypeStruct((tokens, depth), F32),
            jax.ShapeDtypeStruct(w.shape, BF16),
            jax.ShapeDtypeStruct((1, depth), F32),
            jax.ShapeDtypeStruct(table_back.shape, F32),
        ],
        scratch_shapes=[
            pltpu.VMEM((depth, tokens), BF16),
            pltpu.VMEM((depth, tokens), BF16),
            pltpu.VMEM((tokens, depth), BF16),
            pltpu.VMEM((depth // LANES, tokens, LANES), F32),
            pltpu.VMEM((LANES, span), F32),
            pltpu.VMEM((LANES, span), F32),
            pltpu.VMEM((tokens, LANES), BF16),
            pltpu.VMEM((3, tokens, LANES), F32),
            pltpu.VMEM((LANES, tokens), F32),
            pltpu.VMEM((LANES, tokens), BF16),
            pltpu.VMEM((tokens, 3 * wide), BF16),
            pltpu.VMEM((tokens, depth), F32),
        ],
        vmem=56,
        ride=ride,
        args=(datt, x, gain, res, w, table_back, q, k, v, o,),
    )


def gate_forward_kernel(
    taps, keep_ref, x_ref, gain_ref, w_in_ref, w_out_ref, g_gain_ref, g_conv_ref,
    cg_ref, ur_ref, sr_ref, ug_ref, sg_ref, mean_ref, rstd_ref, conv_ref, gate_ref,
    c_rows, ur_all, ug_all, first, second, total, padded,
):
    i = pl.program_id(0)
    blocks = pl.num_programs(0) // 2
    tokens = x_ref.shape[0]
    rows = tokens // SEG
    width = ur_ref.shape[2]
    tile = 256
    channels = width * blocks

    @pl.when(i == 0)
    def _():
        for c in range(tokens // tile):
            here = pl.ds(c * tile, tile)
            normed, _ = norm_parts(x_ref[here, :])
            c_rows[here, :] = low(normed * gain_ref[...])
        first[...] = jnp.zeros_like(first)
        second[...] = jnp.zeros_like(second)

    @pl.when(i < blocks)
    def _():
        for c in range(tokens // tile):
            here = pl.ds(c * tile, tile)
            z = dot(c_rows[here, :], w_in_ref[0])
            zr = z[:, :width]
            zg = z[:, width:]
            ur, slope = gelu_and_slope(zr)
            ur = low(ur)
            ur_ref[0, here, :] = ur
            ur_all[i, here, :] = ur
            sr_ref[0, here, :] = low(slope)
            ug, slope = gelu_and_slope(zg)
            ug_low = low(ug)
            ug_ref[0, here, :] = ug_low
            ug_all[i, here, :] = ug_low
            sg_ref[0, here, :] = low(slope)
            square = ug * ug
            one = ug[:, :LANES]
            two = square[:, :LANES]
            for l in range(1, width // LANES):
                one = one + ug[:, l * LANES : (l + 1) * LANES]
                two = two + square[:, l * LANES : (l + 1) * LANES]
            first[here, :] += one
            second[here, :] += two

    @pl.when(i == blocks - 1)
    def _():
        for c in range(tokens // tile):
            here = pl.ds(c * tile, tile)
            mean = jnp.sum(first[here, :], axis=-1, keepdims=True) / channels
            spread = jnp.sum(second[here, :], axis=-1, keepdims=True) / channels - mean * mean
            mean_ref[here, :] = jnp.broadcast_to(mean, (tile, LANES))
            rstd_ref[here, :] = jnp.broadcast_to(lax.rsqrt(spread + EPSILON), (tile, LANES))

    @pl.when(i >= blocks)
    def _():
        m = i - blocks
        scale = rstd_ref[...] * keep_ref[...]
        shift = mean_ref[...] * scale
        for l in range(width // LANES):
            cols = pl.ds(l * LANES, LANES)
            ug = ug_all[m, :, cols].astype(F32)
            n = low((ug * scale - shift) * g_gain_ref[0, :, cols])
            fill_padded(padded, n.reshape(rows, SEG, LANES), taps)

            def taps_of(k):
                return low(jnp.broadcast_to(g_conv_ref[0, k : k + 1, cols], (SEG, LANES)))[None]

            def emit(start, value):
                block = value.shape[0]
                here = pl.ds(pl.multiple_of(start * SEG, block * SEG), block * SEG)
                flat = value.reshape(block * SEG, LANES)
                conv_ref[0, here, cols] = low(flat)
                gate_ref[0, here, cols] = low(ur_all[m, here, cols].astype(F32) * flat)

            convolve(padded, taps_of, taps, rows, 16, emit)
        part = dot_nt(gate_ref[0], w_out_ref[0])

        @pl.when(m == 0)
        def _():
            total[...] = part

        @pl.when(m != 0)
        def _():
            total[...] += part

        @pl.when(m == blocks - 1)
        def _():
            for l in range(total.shape[1] // LANES):
                cols = pl.ds(l * LANES, LANES)
                cg_ref[:, cols] = low(total[:, cols] * keep_ref[...])


def gate_forward(keep, x, gain, w, g_gain, g_conv, taps, ride=None):
    tokens, depth = x.shape
    blocks = w.shape[0]
    width = w.shape[2] // 3
    full = pl.BlockSpec((tokens, depth), lambda i: (0, 0))
    lanes = pl.BlockSpec((tokens, LANES), lambda i: (0, 0))

    def early(i):
        return jnp.minimum(i, blocks - 1)

    def late(i):
        return jnp.maximum(i - blocks, 0)

    z_early = pl.BlockSpec((1, tokens, width), lambda i: (early(i), 0, 0))
    z_late = pl.BlockSpec((1, tokens, width), lambda i: (late(i), 0, 0))
    z_shape = jax.ShapeDtypeStruct((blocks, tokens, width), BF16)
    lane_shape = jax.ShapeDtypeStruct((tokens, LANES), F32)
    return launch(
        functools.partial(gate_forward_kernel, taps),
        grid=(2 * blocks,),
        in_specs=[
            lanes,
            full,
            pl.BlockSpec((1, depth), lambda i: (0, 0)),
            pl.BlockSpec((1, depth, 2 * width), lambda i: (early(i), 0, 0)),
            pl.BlockSpec((1, depth, width), lambda i: (late(i), 0, 2)),
            pl.BlockSpec((1, 1, width), lambda i: (late(i), 0, 0)),
            pl.BlockSpec((1, taps, width), lambda i: (late(i), 0, 0)),
        ],
        out_specs=[full, z_early, z_early, z_early, z_early, lanes, lanes, z_late, z_late],
        out_shape=[jax.ShapeDtypeStruct((tokens, depth), BF16), z_shape, z_shape, z_shape, z_shape, lane_shape, lane_shape, z_shape, z_shape],
        scratch_shapes=[
            pltpu.VMEM((tokens, depth), BF16),
            pltpu.VMEM((blocks, tokens, width), BF16),
            pltpu.VMEM((blocks, tokens, width), BF16),
            pltpu.VMEM((tokens, LANES), F32),
            pltpu.VMEM((tokens, LANES), F32),
            pltpu.VMEM((tokens, depth), F32),
            pltpu.VMEM((tokens // SEG + taps - 1, SEG, LANES), BF16),
        ],
        vmem=60,
        ride=ride,
        args=(keep, x, gain, w, w, g_gain, g_conv,),
    )


def gate_backward_kernel(
    taps, keep_ref, dcg_ref, x_ref, gain_ref, res_ref, w_ref, ur_ref, sr_ref, ug_ref, sg_ref, conv_ref, gate_ref, mean_ref, rstd_ref, g_gain_ref, g_conv_ref,
    dx_ref, dw_ref, dgain_ref, dg_gain_ref, dg_conv_ref,
    c_rows, c_t, g_t, dn_all, first, second, dc, padded, n_padded, d_rows, dconv, shift, sums, pick,
):
    i = pl.program_id(0)
    blocks = pl.num_programs(0) // 2
    tokens = x_ref.shape[0]
    rows = tokens // SEG
    width = ur_ref.shape[2]
    tile = 256
    channels = width * blocks
    chunks = tokens // tile

    @pl.when(i == 0)
    def _():
        for c in range(chunks):
            here = pl.ds(c * tile, tile)
            normed, _ = norm_parts(x_ref[here, :])
            c_rows[here, :] = low(normed * gain_ref[...])
        c_t[...] = c_rows[...].T
        g_t[...] = dcg_ref[...].T
        first[...] = jnp.zeros_like(first)
        second[...] = jnp.zeros_like(second)
        dc[...] = jnp.zeros_like(dc)
        shift[...] = mean_ref[...] * rstd_ref[...]
        pick[...] = tap_pick(pick.shape)

    @pl.when(i < blocks)
    def _():
        m = i
        for c in range(chunks):
            here = pl.ds(c * tile, tile)
            dgate = dot(dcg_ref[here, :], w_ref[0, :, 2 * width :])
            dzr = low(dgate * (conv_ref[0, here, :].astype(F32) * sr_ref[0, here, :].astype(F32)))
            d_rows[here, :] = dzr
            dconv[here, :] = low(dgate * ur_ref[0, here, :].astype(F32))
            dc[here, :] += dot_nt(dzr, w_ref[0, :, :width])
        dw_ref[m, :, :width] = low(dot(c_t[...], d_rows[...]))
        dw_ref[m, :, 2 * width :] = low(dot(g_t[...], gate_ref[0]))
        for l in range(width // LANES):
            cols = pl.ds(l * LANES, LANES)
            ug = ug_ref[0, :, cols].astype(F32)
            n = low((ug * rstd_ref[...] - shift[...]) * keep_ref[...] * g_gain_ref[0, :, cols])
            fill_padded(n_padded, n.reshape(rows, SEG, LANES), taps)
            d = dconv[:, cols].reshape(rows, SEG, LANES)
            fill_padded(padded, d, taps)
            dg_conv_ref[0, :, cols] = tap_grads(n_padded, padded.at[pl.ds((taps - 1) // 2, rows)], sums, pick, taps, rows, 8)
            dg_gain_ref[0, :, cols] = jnp.zeros((1, LANES), F32)

            def taps_of(k):
                return low(jnp.broadcast_to(g_conv_ref[0, taps - 1 - k : taps - k, cols], (SEG, LANES)))[None]

            def emit(start, value):
                block = value.shape[0]
                here = pl.ds(pl.multiple_of(start * SEG, block * SEG), block * SEG)
                dn = value.reshape(block * SEG, LANES) * keep_ref[here, :]
                normed = ug_ref[0, here, cols].astype(F32) * rstd_ref[here, :] - shift[here, :]
                product = dn * normed
                dg_gain_ref[0, :, cols] += jnp.sum(product, axis=0, keepdims=True)
                scaled = dn * g_gain_ref[0, :, cols]
                dn_all[m, here, cols] = low(scaled)
                first[here, :] += scaled
                second[here, :] += product * g_gain_ref[0, :, cols]

            convolve(padded, taps_of, taps, rows, 16, emit)

    @pl.when(i == blocks - 1)
    def _():
        for c in range(chunks):
            here = pl.ds(c * tile, tile)
            one = jnp.sum(first[here, :], axis=-1, keepdims=True) / channels
            two = jnp.sum(second[here, :], axis=-1, keepdims=True) / channels
            first[here, :] = jnp.broadcast_to(one, (tile, LANES))
            second[here, :] = jnp.broadcast_to(two, (tile, LANES))

    @pl.when(i >= blocks)
    def _():
        m = i - blocks
        for c in range(chunks):
            here = pl.ds(c * tile, tile)
            rstd = rstd_ref[here, :]
            one = first[here, :]
            two = second[here, :]
            for l in range(width // LANES):
                cols = pl.ds(l * LANES, LANES)
                normed = ug_ref[0, here, cols].astype(F32) * rstd - shift[here, :]
                dug = rstd * (dn_all[m, here, cols].astype(F32) - one - normed * two)
                d_rows[here, cols] = low(dug * sg_ref[0, here, cols].astype(F32))
            dc[here, :] += dot_nt(d_rows[here, :], w_ref[0, :, width : 2 * width])
        dw_ref[m, :, width : 2 * width] = low(dot(c_t[...], d_rows[...]))

    @pl.when(i == 2 * blocks - 1)
    def _():
        dgain_ref[...] = jnp.zeros_like(dgain_ref)
        for c in range(chunks):
            here = pl.ds(c * tile, tile)
            normed, rstd = norm_parts(x_ref[here, :])
            d = dc[here, :]
            dgain_ref[...] += jnp.sum(d * normed, axis=0, keepdims=True)
            dx_ref[here, :] = res_ref[here, :] + norm_back(normed, rstd, gain_ref[...], d)


def gate_backward(keep, dcg, x, gain, res, w, ur, sr, ug, sg, conv, gate, mean, rstd, g_gain, g_conv, taps, ride=None):
    tokens, depth = x.shape
    blocks = w.shape[0]
    width = w.shape[2] // 3
    full = pl.BlockSpec((tokens, depth), lambda i: (0, 0))
    lanes = pl.BlockSpec((tokens, LANES), lambda i: (0, 0))
    vec = pl.BlockSpec((1, depth), lambda i: (0, 0))

    def early(i):
        return jnp.minimum(i, blocks - 1)

    z_early = pl.BlockSpec((1, tokens, width), lambda i: (early(i), 0, 0))
    z_cycle = pl.BlockSpec((1, tokens, width), lambda i: (lax.rem(i, blocks), 0, 0))
    gain_spec = pl.BlockSpec((1, 1, width), lambda i: (early(i), 0, 0))
    conv_spec = pl.BlockSpec((1, taps, width), lambda i: (early(i), 0, 0))
    padded = (tokens // SEG + taps - 1, SEG, LANES)
    return launch(
        functools.partial(gate_backward_kernel, taps),
        grid=(2 * blocks,),
        in_specs=[
            lanes,
            full,
            full,
            vec,
            full,
            pl.BlockSpec((1, depth, 3 * width), lambda i: (lax.rem(i, blocks), 0, 0)),
            z_early,
            z_early,
            z_cycle,
            z_cycle,
            z_early,
            z_early,
            lanes,
            lanes,
            gain_spec,
            conv_spec,
        ],
        out_specs=[full, pl.BlockSpec(w.shape, lambda i: (0, 0, 0)), vec, gain_spec, conv_spec],
        out_shape=[
            jax.ShapeDtypeStruct((tokens, depth), F32),
            jax.ShapeDtypeStruct(w.shape, BF16),
            jax.ShapeDtypeStruct((1, depth), F32),
            jax.ShapeDtypeStruct(g_gain.shape, F32),
            jax.ShapeDtypeStruct(g_conv.shape, F32),
        ],
        scratch_shapes=[
            pltpu.VMEM((tokens, depth), BF16),
            pltpu.VMEM((depth, tokens), BF16),
            pltpu.VMEM((depth, tokens), BF16),
            pltpu.VMEM((blocks, tokens, width), BF16),
            pltpu.VMEM((tokens, LANES), F32),
            pltpu.VMEM((tokens, LANES), F32),
            pltpu.VMEM((tokens, depth), F32),
            pltpu.VMEM(padded, BF16),
            pltpu.VMEM(padded, BF16),
            pltpu.VMEM((tokens, width), BF16),
            pltpu.VMEM((tokens, width), BF16),
            pltpu.VMEM((tokens, LANES), F32),
            *tap_scratch(taps),
        ],
        vmem=60,
        ride=ride,
        args=(keep, dcg, x, gain, res, w, ur, sr, ug, sg, conv, gate, mean, rstd, g_gain, g_conv,),
    )


def merge_forward_kernel(taps, x_ref, att_ref, cg_ref, w_ref, m_conv_ref, out_ref, merged_ref, padded):
    c = pl.program_id(0)
    tokens = x_ref.shape[0]
    rows = tokens // SEG
    half = pl.num_programs(0) // 2
    width = merged_ref.shape[1]
    for l in range(width // LANES):
        cols = pl.ds(l * LANES, LANES)

        @pl.when(c < half)
        def _():
            fill_padded(padded, att_ref[:, cols].reshape(rows, SEG, LANES), taps)

        @pl.when(c >= half)
        def _():
            fill_padded(padded, cg_ref[:, cols].reshape(rows, SEG, LANES), taps)

        def taps_of(k):
            return low(jnp.broadcast_to(m_conv_ref[k : k + 1, cols], (SEG, LANES)))[None]

        def emit(start, value):
            block = value.shape[0]
            here = pl.ds(pl.multiple_of(start * SEG, block * SEG), block * SEG)
            value = value + padded[pl.ds(start + (taps - 1) // 2, block)].astype(F32)
            merged_ref[here, cols] = low(value.reshape(block * SEG, LANES))

        convolve(padded, taps_of, taps, rows, 16, emit)
    w = jnp.concatenate([w_ref[m] for m in range(w_ref.shape[0])], axis=1)
    part = dot(merged_ref[...], w)

    @pl.when(c == 0)
    def _():
        out_ref[...] = x_ref[...] + part

    @pl.when(c != 0)
    def _():
        out_ref[...] += part


def merge_forward(x, att, cg, w, m_conv, ride=None):
    tokens, depth = x.shape
    blocks, both, cols = w.shape
    taps = m_conv.shape[0]
    width = 256
    steps = both // width
    half = steps // 2
    full = pl.BlockSpec((tokens, depth), lambda i: (0, 0))
    return launch(
        functools.partial(merge_forward_kernel, taps),
        grid=(steps,),
        in_specs=[
            full,
            pl.BlockSpec((tokens, width), lambda i: (0, jnp.minimum(i, half - 1))),
            pl.BlockSpec((tokens, width), lambda i: (0, jnp.maximum(i - half, 0))),
            pl.BlockSpec((blocks, width, cols), lambda i: (0, i, 0)),
            pl.BlockSpec((taps, width), lambda i: (0, i)),
        ],
        out_specs=[full, pl.BlockSpec((tokens, width), lambda i: (0, i))],
        out_shape=[jax.ShapeDtypeStruct(x.shape, F32), jax.ShapeDtypeStruct((tokens, both), BF16)],
        scratch_shapes=[pltpu.VMEM((tokens // SEG + taps - 1, SEG, LANES), BF16)],
        vmem=56,
        ride=ride,
        args=(x, att, cg, w, m_conv,),
    )


def merge_backward_kernel(taps, keep_ref, g_ref, att_ref, cg_ref, merged_ref, w_ref, m_conv_ref, datt_ref, dcg_ref, dw_ref, dconv_ref, g_rows, padded, j_padded, out, sums, pick):
    c = pl.program_id(0)
    tokens = g_ref.shape[0]
    rows = tokens // SEG
    half = pl.num_programs(0) // 2
    blocks, width, narrow = w_ref.shape

    @pl.when(c == 0)
    def _():
        g_rows[...] = low(g_ref[...])
        pick[...] = tap_pick(pick.shape)

    w = jnp.concatenate([w_ref[m] for m in range(blocks)], axis=1)
    dmerged = low(dot_nt(g_rows[...], w))
    dw = dot(merged_ref[...].T, g_rows[...])
    for m in range(blocks):
        dw_ref[m] = low(dw[:, m * narrow : (m + 1) * narrow])
    for l in range(width // LANES):
        cols = pl.ds(l * LANES, LANES)

        @pl.when(c < half)
        def _():
            fill_padded(j_padded, att_ref[:, cols].reshape(rows, SEG, LANES), taps)

        @pl.when(c >= half)
        def _():
            fill_padded(j_padded, cg_ref[:, cols].reshape(rows, SEG, LANES), taps)

        fill_padded(padded, dmerged[:, l * LANES : (l + 1) * LANES].reshape(rows, SEG, LANES), taps)
        dconv_ref[:, cols] = tap_grads(j_padded, padded.at[pl.ds((taps - 1) // 2, rows)], sums, pick, taps, rows, 8)

        def taps_of(k):
            return low(jnp.broadcast_to(m_conv_ref[taps - 1 - k : taps - k, cols], (SEG, LANES)))[None]

        def emit(start, value):
            block = value.shape[0]
            here = pl.ds(pl.multiple_of(start * SEG, block * SEG), block * SEG)
            value = value + padded[pl.ds(start + (taps - 1) // 2, block)].astype(F32)
            out[here, cols] = low(value.reshape(block * SEG, LANES) * keep_ref[here, :])

        convolve(padded, taps_of, taps, rows, 16, emit)

    @pl.when(c < half)
    def _():
        datt_ref[...] = out[...]

    @pl.when(c >= half)
    def _():
        dcg_ref[...] = out[...]


def merge_backward(keep, g, att, cg, merged, w, m_conv, ride=None):
    tokens, depth = g.shape
    blocks, both, cols = w.shape
    taps = m_conv.shape[0]
    width = 256
    steps = both // width
    half = steps // 2
    full = pl.BlockSpec((tokens, depth), lambda i: (0, 0))
    early = pl.BlockSpec((tokens, width), lambda i: (0, jnp.minimum(i, half - 1)))
    late = pl.BlockSpec((tokens, width), lambda i: (0, jnp.maximum(i - half, 0)))
    wide = pl.BlockSpec((tokens, width), lambda i: (0, i))
    w_spec = pl.BlockSpec((blocks, width, cols), lambda i: (0, i, 0))
    conv_spec = pl.BlockSpec((taps, width), lambda i: (0, i))
    padded = (tokens // SEG + taps - 1, SEG, LANES)
    return launch(
        functools.partial(merge_backward_kernel, taps),
        grid=(steps,),
        in_specs=[pl.BlockSpec(keep.shape, lambda i: (0, 0)), full, early, late, wide, w_spec, conv_spec],
        out_specs=[early, late, w_spec, conv_spec],
        out_shape=[
            jax.ShapeDtypeStruct((tokens, depth), BF16),
            jax.ShapeDtypeStruct((tokens, depth), BF16),
            jax.ShapeDtypeStruct(w.shape, BF16),
            jax.ShapeDtypeStruct(m_conv.shape, F32),
        ],
        scratch_shapes=[
            pltpu.VMEM((tokens, depth), BF16),
            pltpu.VMEM(padded, BF16),
            pltpu.VMEM(padded, BF16),
            pltpu.VMEM((tokens, width), BF16),
            *tap_scratch(taps),
        ],
        vmem=56,
        ride=ride,
        args=(keep, g, att, cg, merged, w, m_conv,),
    )


def no_ride(index):
    return None


def layer_forward(x, length, keep, weights, small, ride=no_ride, ending=False):
    gains, table, table_back, g_gain, g_conv, m_conv = small
    taps = m_conv.shape[0]
    x1, h1 = ffn_forward(x, gains[0:1], weights(0), ride=ride(0))
    att, q, k, v, o = attention_forward(length, keep, x1, gains[1:2], weights(1), table, ride=ride(1))
    cg, *inner = gate_forward(keep, x1, gains[2:3], weights(2), g_gain, g_conv, taps, ride=ride(2))
    x2, merged = merge_forward(x1, att, cg, weights(3), m_conv, ride=ride(3))
    x3, h2, y = ffn_forward(x2, gains[3:4], weights(4), gains[4:5], keep if ending else None, ride=ride(4))
    saved = (x, x1, h1, att, q, k, v, o, cg, inner, x2, merged, x3, h2)
    return y, saved


def layer_backward(g, keep, saved, weights, small, ride=no_ride, ready=lambda index, grad: None, before_last=lambda *_: None, ending=False):
    gains, table, table_back, g_gain, g_conv, m_conv = small
    taps = m_conv.shape[0]
    x, x1, h1, att, q, k, v, o, cg, inner, x2, merged, x3, h2 = saved
    ur, sr, ug, sg, mean, rstd, conv, gate = inner
    dx2, dg5, dgain3, dgain4 = ffn_backward(g, x2, gains[3:4], h2, weights(4), gains[4:5], x3, ride=ride(4))
    ready(4, dg5)
    datt, dcg, dg4, dm_conv = merge_backward(keep, dx2, att, cg, merged, weights(3), m_conv, ride=ride(3))
    ready(3, dg4)
    dx1, dg3, dgain2, dg_gain, dg_conv = gate_backward(
        keep, dcg, x1, gains[2:3], dx2, weights(2), ur, sr, ug, sg, conv, gate, mean, rstd, g_gain, g_conv, taps, ride=ride(2)
    )
    ready(2, dg3)
    dx1, dg2, dgain1, dtable = attention_backward(datt, x1, gains[1:2], dx1, weights(1), table_back, q, k, v, o, ride=ride(1))
    ready(1, dg2)
    dgains = jnp.concatenate([dgain1, dgain2, dgain3, dgain4], axis=0)
    before_last(0, dgains, (dtable, dg_gain, dg_conv, dm_conv))
    if ending:
        ready("out", *ffn_out_grad(dx1, h1, ride=ride("out")))
    dx, dg1, dgain0 = ffn_backward(dx1, x, gains[0:1], h1, weights(0), ending=ending, ride=ride(0))
    ready(0, dg1)
    return dx, dgain0


def to_segments(values):
    tokens, depth = values.shape
    return values.reshape(SEG, tokens // SEG, depth).transpose(1, 0, 2).reshape(tokens, depth)


def from_segments(values):
    tokens, depth = values.shape
    return values.reshape(tokens // SEG, SEG, depth).transpose(1, 0, 2).reshape(tokens, depth)


def pack_layer(layer, ffn_in, ffn_out, attn_in, attn_out, cg_in, cg_out, merge_out, mp_index, mp_size):
    cols = merge_out.shape[2] // mp_size
    part = lax.dynamic_slice_in_dim(merge_out[layer], mp_index * cols, cols, axis=1)
    pieces = (
        jnp.concatenate([ffn_in[layer, 0], ffn_out[layer, 0].T], axis=1),
        jnp.concatenate([attn_in[layer, 0], attn_in[layer, 1], attn_in[layer, 2], attn_out[layer].T], axis=1),
        jnp.concatenate([cg_in[layer, 0], cg_in[layer, 1], cg_out[layer].T], axis=1),
        part,
        jnp.concatenate([ffn_in[layer, 1], ffn_out[layer, 1].T], axis=1),
    )
    return tuple(low(piece) for piece in pieces)


GROUPS = 5
OPENING = [
    (0, [("line", 0), (0, 0)]),
    (1, [(0, 1), ("out", 0)]),
    (2, [(0, 2), ("out", 1), (1, 0)]),
    (3, [("out", 2), (0, 3), (2, 0)]),
    (4, [("out", 3), (1, 1)]),
]
FORWARD = {
    0: [(0, [(1, 2), (3, 0), (6, 0)]), (1, [(2, 1)]), (2, [(1, 3), (3, 1)])],
    1: [(0, [(2, 2), (4, 0)]), (1, [(5, 0)]), (2, [(4, 1)]), (3, [(2, 3), (3, 2)])],
    2: [(0, [(4, 2)]), (1, [(6, 1)]), (2, [(7, 0)]), (3, [(3, 3), (8, 0)]), (4, [(5, 1)]), (6, [(4, 3)])],
    3: [(0, [(5, 2), (9, 0)])],
    4: [(0, [(5, 3), (6, 2), (8, 1)])],
    5: [(0, [(6, 3), (7, 1)])],
    6: [(0, [(7, 2)]), (1, [(9, 1)]), (3, [(7, 3)])],
    7: [(0, [(9, 2)]), (2, [(8, 2)]), (6, [(9, 3)]), (7, [(8, 3)])],
}
BACKWARD = {
    8: [(0, [(9, 0)]), (1, [(9, 1)])],
    7: [(0, [(9, 2), (8, 0)]), (1, [(9, 3), (8, 1)]), (2, [(8, 2)]), (3, [(8, 3)])],
    6: [(0, [(7, 0)]), (1, [(7, 1)])],
    5: [(0, [(7, 2), (6, 0)]), (2, [(6, 1)])],
    4: [(0, [(7, 3), (6, 2), (5, 0)]), (1, [(5, 1)])],
    3: [(0, [(6, 3), (5, 2), (4, 0)]), (1, [(4, 1)])],
    2: [(0, [(5, 3), (4, 2), (3, 0)]), (1, [(4, 3), (3, 1)]), (2, [(3, 2)]), (3, [(3, 3)])],
    1: [(0, [(2, 0)]), (1, [(2, 1)])],
    "out": [(0, [(2, 2), (1, 0), ("small", 0)]), (2, [("small", 1)])],
    0: [(0, [("out", 0), (2, 3), (1, 1), ("small", 2)]), (1, [("out", 1), ("small", 3)])],
}
CLOSING = [
    (0, [(0, 0), ("out", 2), (1, 2), ("all", 0), ("vector", 0), ("merge", 0)]),
    (1, [(0, 1), ("out", 3), ("all", 1), ("vector", 1)]),
    (2, [(0, 2), (1, 3), ("all", 2), ("vector", 2)]),
    (3, [(0, 3), ("all", 3), ("vector", 3)]),
]


def reverse(values):
    shape = values.shape
    turn = (lax.broadcasted_iota(jnp.int32, (LANES, LANES), 0) + lax.broadcasted_iota(jnp.int32, (LANES, LANES), 1) == LANES - 1).astype(F32)
    blocks = values.reshape(-1, LANES)
    turned = jnp.dot(blocks, turn, precision=lax.Precision.HIGHEST, preferred_element_type=F32)
    return turned.reshape(*shape[:-1], -1, LANES)[..., ::-1, :].reshape(shape)


def plans(bits, names):
    groups = len(names)
    if bits == 3 and groups == 2 * GROUPS + 1:
        return OPENING, FORWARD, BACKWARD, CLOSING
    count = groups + bits
    opening = [(r, [(g, r - i) for i, g in enumerate(names) if 0 <= r - i <= bits] + ([("line", 0)] if r == 0 else [])) for r in range(count)]
    small = [(r, [("small", r)]) for r in range(bits + 1)]
    closing = [(r, [(g, r - i) for i, g in enumerate(names) if 0 <= r - i <= bits]) for r in range(count)]
    for s in range(bits + 1):
        closing[s][1].extend([("all", s), ("vector", s)])
    closing.append((count, [("merge", 0)]))
    return opening, {}, {"small": small}, closing


def body(frames, cotangent, lengths, norm_gains, ffn_in, ffn_out, attn_in, attn_out, rel_bias, cg_in, csgu_gain, csgu_conv, cg_out, merge_conv, merge_out):
    layers = norm_gains.shape[0]
    mp_size = lax.axis_size("mp")
    bits = lax.axis_size("dp").bit_length() - 1
    mp_index = lax.axis_index("mp")
    length = lax.dynamic_slice_in_dim(lengths, mp_index, 1)
    tokens, depth = frames.shape
    taps = merge_conv.shape[1]
    heads, span = rel_bias.shape[1:]
    channels = csgu_gain.shape[1]

    flow = {}
    ids = iter(range(1, 100))

    def ride(plan):
        return Ride(flow, mp_size, bits, next(ids), plan)

    def alone(plan):
        launch(None, (len(plan),), [], [], [], vmem=62, ride=ride(plan))

    shards = []
    for layer in range(layers):
        shards += pack_layer(layer, ffn_in, ffn_out, attn_in, attn_out, cg_in, cg_out, merge_out, mp_index, mp_size)
    f = ffn_in.shape[3]
    shards[:1] = [low(ffn_in[0, 0]), low(ffn_out[0, 0].T)]
    line = jnp.concatenate([rel_bias.reshape(layers, -1), csgu_gain, csgu_conv.reshape(layers, -1)], axis=1)
    line = line.reshape(-1, LANES)
    kinds = [Gather(mp_size, bits) for _ in shards] + [Gather(mp_size, bits, True)]
    names = [0, "out"] + list(range(1, layers * GROUPS))
    for name, kind, buffer in zip(names + ["line"], kinds, start_buffers(shards + [line], kinds, mp_size, bits)):
        flow[name] = (kind, buffer)
    opening, forward, backward, closing = plans(bits, names)
    alone(opening)
    line_all = flow["line"][1].reshape(mp_size, layers, -1)
    table = line_all[:, :, : heads * span].reshape(mp_size, layers, heads, span)
    g_gain = line_all[:, :, heads * span : heads * span + channels].reshape(mp_size, layers, 1, channels)
    g_conv = line_all[:, :, heads * span + channels :].reshape(mp_size, layers, taps, channels)

    table_back = reverse(table)
    keep_rows = keep_lanes(length, tokens)
    state = to_segments(frames).astype(F32)
    weights = {}
    smalls = []
    saved = []
    for layer in range(layers):

        def weight(index):
            at = layer * GROUPS + index
            if at not in weights:
                made = [flow[name][1] for name in ([0, "out"] if at == 0 else [at])]
                made = tuple(w.reshape(mp_size, -1, w.shape[-1]) for w in made)
                weights[at] = made if at == 0 else made[0]
            return weights[at]

        def beside(index):
            at = layer * GROUPS + index
            return ride(forward[at]) if at in forward else None

        smalls.append((norm_gains[layer], table[:, layer], table_back[:, layer], g_gain[:, layer], g_conv[:, layer], merge_conv[layer]))
        state, kept = layer_forward(state, length, keep_rows, weight, smalls[layer], beside, layer == layers - 1)
        saved.append(kept)
    frame = lax.broadcasted_iota(jnp.int32, (tokens, 1), 0)
    keep = (frame < length).astype(F32)
    output_frames = state
    incoming = to_segments(cotangent.astype(F32) * keep)
    tiny = [None] * layers
    counts = []

    def pack_small():
        split = [jnp.concatenate([t[1].reshape(mp_size, -1), t[2].reshape(mp_size, -1), t[3].reshape(mp_size, -1)], axis=1) for t in tiny]
        split = jnp.concatenate(split, axis=1).reshape(mp_size, -1, LANES)
        shared = jnp.concatenate([t[0].reshape(-1) for t in tiny] + [t[4].reshape(-1) for t in tiny])
        shared = jnp.pad(shared, (0, -shared.size % (mp_size * LANES))).reshape(mp_size, -1, LANES)
        counts.extend([split.shape[1], shared.shape[1]])
        padding = -sum(counts) % (16 << bits)
        packed = low(jnp.concatenate([split, shared, jnp.zeros((mp_size, padding, LANES), F32)], axis=1))
        packed = packed.reshape((mp_size,) + (2,) * bits + (-1, LANES))
        flow["small"] = (Scatter(mp_size, bits, *packed.shape[-2:]), packed)
        if "small" in backward:
            alone(backward["small"])

    for layer in reversed(range(layers)):

        def weight(index):
            return weights[layer * GROUPS + index]

        def beside(index):
            at = index if index == "out" else layer * GROUPS + index
            return ride(backward[at]) if at in backward else None

        def ready(index, grad):
            grad = grad.reshape((mp_size,) + (2,) * bits + (-1, grad.shape[-1]))
            flow[index if index == "out" else layer * GROUPS + index] = (Scatter(mp_size, bits, *grad.shape[-2:]), grad)

        def before_last(index, gains, small):
            tiny[layer] = (gains, *small)
            if layer == 0:
                pack_small()

        incoming, last_gain = layer_backward(incoming, keep_rows, saved[layer], weight, smalls[layer], beside, ready, before_last, layer == 0)
        if layer > 0:
            tiny[layer] = (jnp.concatenate([last_gain, tiny[layer][0]], axis=0), *tiny[layer][1:])
    vector = jnp.pad(last_gain.reshape(-1, LANES), ((0, -(depth // LANES) % 8), (0, 0)))
    kinds = [Gather(mp_size, bits), Gather(mp_size, bits)]
    flow["all"], flow["vector"] = zip(kinds, start_buffers([low(flow["small"][1]), vector], kinds, mp_size, bits))

    def start_merge():
        line = low(jnp.concatenate([flow[layer * GROUPS + 3][1] for layer in range(layers)], axis=0))
        kind = Gather(mp_size, bits, True)
        flow["merge"] = (kind, start_buffers([line], [kind], mp_size, bits)[0])

    if closing[-1][1] == [("merge", 0)]:
        alone(closing[:-1])
        start_merge()
        alone([(0, closing[-1][1])])
    else:
        start_merge()
        alone(closing)
    input_grad = incoming

    big = [flow[at][1] for at in range(layers * GROUPS)]
    packed = flow["all"][1].reshape(mp_size, -1, LANES).astype(F32)
    split_rows, shared_rows = counts
    split = lax.dynamic_index_in_dim(packed, mp_index, 0, keepdims=False)[:split_rows].reshape(layers, -1)
    grad_table = reverse(split[:, : heads * span].reshape(layers, heads, span))
    grad_g_gain = split[:, heads * span : heads * span + channels]
    grad_g_conv = split[:, heads * span + channels :].reshape(layers, taps, channels)
    shared = packed[:, split_rows : split_rows + shared_rows].reshape(-1)
    grad_gains = shared[: norm_gains.size - depth]
    vector = jnp.sum(flow["vector"][1].reshape(-1, flow["vector"][1].shape[-2] * LANES), axis=0)[:depth]
    grad_gains = jnp.concatenate([vector, grad_gains]).reshape(norm_gains.shape)
    grad_m_conv = shared[norm_gains.size - depth :][: merge_conv.size].reshape(merge_conv.shape)
    merge_all = flow["merge"][1].astype(F32).reshape(mp_size, layers, -1, LANES)
    grad_merge = merge_all.transpose(1, 2, 0, 3).reshape(merge_out.shape)

    h = attn_in.shape[3]
    c = cg_in.shape[3]
    one, two, three, _, five = [[big[layer * GROUPS + g] for layer in range(layers)] for g in range(GROUPS)]
    one[0] = jnp.concatenate([one[0], flow["out"][1]], axis=1)
    grad_ffn_in = jnp.stack([jnp.stack([a[:, :f], b[:, :f]]) for a, b in zip(one, five)])
    grad_ffn_out = jnp.stack([jnp.stack([a[:, f:].T, b[:, f:].T]) for a, b in zip(one, five)])
    grad_attn_in = jnp.stack([jnp.stack([a[:, :h], a[:, h : 2 * h], a[:, 2 * h : 3 * h]]) for a in two])
    grad_attn_out = jnp.stack([a[:, 3 * h :].T for a in two])
    grad_cg_in = jnp.stack([jnp.stack([a[:, :c], a[:, c : 2 * c]]) for a in three])
    grad_cg_out = jnp.stack([a[:, 2 * c :].T for a in three])
    return (
        output_frames,
        input_grad,
        grad_gains,
        grad_ffn_in,
        grad_ffn_out,
        grad_attn_in,
        grad_attn_out,
        grad_table,
        grad_cg_in,
        grad_g_gain,
        grad_g_conv,
        grad_cg_out,
        grad_m_conv,
        grad_merge,
    )


def solution(mesh):
    tokens = P(("dp", "mp"), None)
    columns = P(None, None, "dp", "mp")
    rows = P(None, "mp", "dp")
    ffn_rows = P(None, None, "mp", "dp")
    heads = P(None, "mp", None)
    taps = P(None, None, "mp")
    return jax.shard_map(
        body,
        mesh=mesh,
        in_specs=(tokens, tokens, P("dp"), P(), columns, ffn_rows, columns, rows, heads, columns, P(None, "mp"), taps, rows, P(), P(None, "dp", None)),
        out_specs=(tokens, tokens, P(), columns, ffn_rows, columns, rows, heads, columns, P(None, "mp"), taps, rows, P(), P(None, "dp", None)),
        check_vma=False,
    )
```

```python
import functools

import jax
import jax.numpy as jnp
from jax import lax
from jax.experimental import pallas as pl
from jax.experimental.pallas import tpu as pltpu
from jax.sharding import PartitionSpec as P

EPSILON = 1e-05
MASKED = -1000000000.0
F32 = jnp.float32
BF16 = jnp.bfloat16
SEG = 16
GELU_A = 0.7978845608028654
GELU_B = 0.044715
HEAD = 64
PAIR = 2
LANES = 128


def dot(left, right):
    return lax.dot_general(left, right, (((1,), (0,)), ((), ())), preferred_element_type=F32)


def dot_nt(left, right):
    return lax.dot_general(left, right, (((1,), (1,)), ((), ())), preferred_element_type=F32)


def low(values):
    return values.astype(BF16)


def norm_parts(values):
    mean = jnp.mean(values, axis=-1, keepdims=True)
    centred = values - mean
    spread = jnp.mean(centred * centred, axis=-1, keepdims=True)
    rstd = lax.rsqrt(spread + EPSILON)
    return centred * rstd, rstd


def norm_back(normed, rstd, gain, grad):
    scaled = grad * gain
    first = jnp.mean(scaled, axis=-1, keepdims=True)
    second = jnp.mean(scaled * normed, axis=-1, keepdims=True)
    return rstd * (scaled - first - normed * second)


def gelu(values):
    half = 0.5 * values
    inner = values * (GELU_A + (GELU_A * GELU_B) * (values * values))
    return half + half * jnp.tanh(inner)


def gelu_and_slope(values):
    half = 0.5 * values
    square = values * values
    tanh = jnp.tanh(values * (GELU_A + (GELU_A * GELU_B) * square))
    value = half + half * tanh
    slope = 0.5 + 0.5 * tanh + (half - half * tanh * tanh) * (GELU_A + (3.0 * GELU_A * GELU_B) * square)
    return value, slope


def keep_lanes(length, tokens):
    at = lax.broadcasted_iota(jnp.int32, (tokens, LANES), 0)
    frame = (at % SEG) * (tokens // SEG) + at // SEG
    return (frame < length).astype(F32)


def split_lanes(lanes_ref, here, values):
    for l in range(values.shape[1] // LANES):
        lanes_ref[l, here, :] = values[:, l * LANES : (l + 1) * LANES]


def reorder(lanes_ref, stride, emit):
    blocks, tokens, _ = lanes_ref.shape
    count = tokens // stride
    for start in range(stride):
        for l in range(blocks):
            emit(start * count, l, lanes_ref[l, pl.ds(start, count, stride=stride), :])


def to_frames(lanes_ref, out_ref):
    rows = lanes_ref.shape[1] // SEG

    def emit(start, l, piece):
        out_ref[pl.ds(start, rows), pl.ds(l * LANES, LANES)] = piece

    reorder(lanes_ref, SEG, emit)


MESH = pl.DeviceIdType.MESH


class Links:
    def __init__(self, mp, bits, send, recv):
        self.mp = mp
        self.bits = bits
        self.me = lax.axis_index("mp")
        self.dp = lax.axis_index("dp")
        self.bit = [lax.rem(self.dp // (1 << i), 2) for i in range(bits)]
        self.send, self.recv = send, recv

    def other(self, i):
        return {"dp": self.dp + (1 - 2 * self.bit[i]) * (1 << i)}

    def along(self, offset):
        return {"mp": lax.rem(self.me + offset, self.mp)}

    def before(self, offset):
        return lax.rem(self.me + self.mp - offset, self.mp)

    def barrier(self):
        peers = [self.other(i) for i in range(self.bits)] + [self.along(offset) for offset in range(1, self.mp)]
        semaphore = pltpu.get_barrier_semaphore()
        for peer in peers:
            pl.semaphore_signal(semaphore, inc=1, device_id=peer, device_id_type=MESH)
        pl.semaphore_wait(semaphore, len(peers))

    def copy(self, at, source, target, arrives, device):
        def make(where):
            return pltpu.make_async_remote_copy(
                src_ref=source, dst_ref=where, send_sem=self.send.at[at], recv_sem=self.recv.at[at], device_id=device, device_id_type=MESH
            )

        return lambda: make(target), lambda: make(arrives)


def orders(bits):
    rest = list(range(1, bits))
    return rest + [0], rest[::-1] + [0]


def halves(mp):
    return (pl.ds(0, mp // 2), pl.ds(mp // 2, mp // 2))


class Gather:
    def __init__(self, mp, bits, line=False):
        self.mp, self.bits, self.line = mp, bits, line

    def copies(self, s):
        return self.mp - 1 if s == 0 else 1 if s == self.bits else 2

    def at(self, links, buffer, m, free, flip=None):
        index = [m]
        if not self.line:
            for i in reversed(range(self.bits)):
                index.append(pl.ds(0, 2) if i in free else 1 - links.bit[i] if i == flip else links.bit[i])
        return buffer.at[tuple(index)]

    def pairs(self, links, buffer, s, base):
        made = []

        def add(m, arriving, free, flip, device):
            mine = self.at(links, buffer, m, free)
            made.append(links.copy(base + len(made), mine, mine, self.at(links, buffer, arriving, free, flip), device))

        if s == 0:
            for offset in range(1, self.mp):
                add(links.me, links.before(offset), (), None, links.along(offset))
        elif s == self.bits:
            whole = pl.ds(0, self.mp)
            add(whole, whole, range(1, self.bits), 0, links.other(0))
        else:
            for half, order in zip(halves(self.mp), orders(self.bits)):
                add(half, half, order[: s - 1], order[s - 1], links.other(order[s - 1]))
        return made


class Scatter:
    def __init__(self, mp, bits, rows, cols):
        self.mp, self.bits, self.rows, self.cols = mp, bits, rows, cols

    def shape(self, s):
        return (self.mp,) + (2,) * (self.bits - s) + (self.rows, self.cols)

    def arrived(self, s):
        return self.shape(s + 1) if s < self.bits else self.shape(s)

    def own(self, s):
        return self.arrived(s) if s < self.bits else (self.rows, self.cols)

    def copies(self, s):
        return 1 if s == 0 else self.mp - 1 if s == self.bits else 2

    def loads(self, s):
        return 2 if 0 < s < self.bits else 1

    def parts(self, s):
        if s == 0:
            return [(pl.ds(0, self.mp), list(range(self.bits))[::-1], 0)]
        made = []
        for half, order in zip(halves(self.mp), orders(self.bits)):
            made.append((half, sorted(order[: self.bits - s], reverse=True), order[self.bits - 1 - s]))
        return made

    def pick(self, links, ref, m, left, now, flip):
        index = [m]
        for i in left:
            index.append(pl.ds(0, 2) if i != now else 1 - links.bit[i] if flip else links.bit[i])
        return ref.at[tuple(index)]

    def pairs(self, links, held, slots, s, base):
        made = []
        if s < self.bits:
            for m, left, now in self.parts(s):
                slot = slots.at[m]
                made.append(links.copy(base + len(made), self.pick(links, held, m, left, now, True), slot, slot, links.other(now)))
        else:
            for offset in range(1, self.mp):
                to = lax.rem(links.me + offset, self.mp)
                made.append(links.copy(base + len(made), held.at[to], slots.at[links.me], slots.at[links.before(offset)], links.along(offset)))
        return made

    def load_pairs(self, links, held, own, s):
        if s == self.bits:
            return [(held.at[links.me], own)]
        return [(self.pick(links, held, m, left, now, False), own.at[m]) for m, left, now in self.parts(s)]

    def add(self, links, slots, s, own, held):
        half = self.mp // 2

        def step(m, carry):
            for part, order in enumerate(orders(self.bits)):
                at = m + part * half
                if own is not None:
                    slots[at] += own[at]
                else:
                    left = sorted(order[: self.bits - s], reverse=True)
                    slots[at] += self.pick(links, held, at, left, order[self.bits - 1 - s], False)[...]
            return carry

        lax.fori_loop(0, half, step, 0)

    def total(self, links, slots, own, held):
        value = (own[...] if own is not None else held[links.me]).astype(F32)
        for offset in range(1, self.mp):
            value = value + slots[links.before(offset)].astype(F32)
        return value


HBM = pl.BlockSpec(memory_space=pltpu.HBM)


class Ride:
    def __init__(self, flow, mp, bits, collective_id, rounds):
        self.flow, self.mp, self.bits, self.collective_id = flow, mp, bits, collective_id
        self.rounds = rounds
        names = []
        self.base = {}
        self.count = 0
        self.stages = {}
        for _, tasks in rounds:
            for name, s in tasks:
                if name not in names:
                    names.append(name)
                    self.stages[name] = []
                self.stages[name].append(s)
                self.base[name, s] = self.count
                self.count += flow[name][0].copies(s)
        self.gathers = [n for n in names if isinstance(flow[n][0], Gather)]
        self.scatters = [n for n in names if isinstance(flow[n][0], Scatter)]
        self.local = {}
        self.local_count = 0
        self.scratch = []
        self.place = {}
        for n in self.scatters:
            kind = flow[n][0]
            first, last = self.stages[n][0], self.stages[n][-1]
            self.local[n] = self.local_count
            self.local_count += kind.loads(first) + 1
            self.place[n, "own"] = len(self.scratch)
            self.scratch.append(pltpu.VMEM(kind.own(first), BF16))
            for s in self.stages[n]:
                self.place[n, s] = len(self.scratch)
                self.scratch.append(pltpu.VMEM(kind.arrived(s), BF16))
        self.sems = [pltpu.SemaphoreType.DMA((max(1, k),)) for k in (self.count, self.count, self.local_count)]

    def inputs(self):
        return [self.flow[n][1] for n in self.gathers + self.scatters]

    def finals(self, n):
        return self.stages[n][-1] == self.bits

    def outputs(self):
        shapes = [jax.ShapeDtypeStruct(self.flow[n][1].shape, self.flow[n][1].dtype) for n in self.gathers]
        specs = [HBM] * len(shapes)
        for n in self.scatters:
            kind = self.flow[n][0]
            if self.finals(n):
                shapes.append(jax.ShapeDtypeStruct((kind.rows, kind.cols), F32))
                specs.append(pl.BlockSpec((kind.rows, kind.cols), lambda *_: (0, 0)))
            else:
                shapes.append(jax.ShapeDtypeStruct(kind.shape(self.stages[n][-1] + 1), BF16))
                specs.append(HBM)
        return shapes, specs

    def bind(self, ins, outs, scratch):
        names = self.gathers + self.scatters
        self.ins = dict(zip(names, ins))
        self.outs = dict(zip(names, outs))
        send, recv, self.local_sem = scratch[:3]
        self.buffers = scratch[3:]
        self.links = Links(self.mp, self.bits, send, recv)

    def held(self, n, s):
        return self.ins[n] if s == self.stages[n][0] else self.buffers[self.place[n, s - 1]]

    def pairs(self, task):
        n, s = task
        kind = self.flow[n][0]
        if n in self.gathers:
            return kind.pairs(self.links, self.outs[n], s, self.base[task])
        return kind.pairs(self.links, self.held(n, s), self.buffers[self.place[task]], s, self.base[task])

    def loads(self, n):
        first = self.stages[n][0]
        pairs = self.flow[n][0].load_pairs(self.links, self.ins[n], self.buffers[self.place[n, "own"]], first)
        return [functools.partial(pltpu.make_async_copy, a, b, self.local_sem.at[self.local[n] + i]) for i, (a, b) in enumerate(pairs)]

    def stores(self, n):
        last = self.stages[n][-1]
        at = self.local[n] + self.flow[n][0].loads(self.stages[n][0])
        return pltpu.make_async_copy(self.buffers[self.place[n, last]], self.outs[n], self.local_sem.at[at])

    def begin(self, number):
        tasks = self.rounds[number][1]
        if number == 0:
            self.links.barrier()
            self.finished = set()
        for n, s in tasks:
            if s > self.stages[n][0]:
                self.finish((n, s - 1))
            elif n in self.scatters:
                for load in self.loads(n):
                    load().start()
            for out, _ in self.pairs((n, s)):
                out().start()

    def finish(self, task):
        if task in self.finished:
            return
        self.finished.add(task)
        n, s = task
        for _, arriving in self.pairs(task):
            arriving().wait_recv()
        if n in self.scatters:
            kind = self.flow[n][0]
            own = None
            if s == self.stages[n][0]:
                own = self.buffers[self.place[n, "own"]]
                for load in self.loads(n):
                    load().wait()
            slots = self.buffers[self.place[task]]
            if s < self.bits:
                kind.add(self.links, slots, s, own, self.held(n, s))
                if s == self.stages[n][-1]:
                    self.stores(n).start()
            else:
                self.outs[n][...] = kind.total(self.links, slots, own, self.held(n, s))

    def end(self):
        for _, tasks in self.rounds:
            for task in tasks:
                self.finish(task)
        for _, tasks in self.rounds:
            for task in tasks:
                for out, _ in self.pairs(task):
                    out().wait_send()
        for n in self.scatters:
            if not self.finals(n):
                self.stores(n).wait()

    def done(self, arrays):
        for n, array in zip(self.gathers + self.scatters, arrays):
            self.flow[n] = (self.flow[n][0], array)


def launch(kernel, grid, in_specs, out_specs, out_shape, scratch_shapes=(), vmem=56, ride=None, args=()):
    scratch_shapes = list(scratch_shapes)
    if ride is None:
        return pl.pallas_call(
            kernel,
            grid=grid,
            in_specs=in_specs,
            out_specs=out_specs,
            out_shape=out_shape,
            scratch_shapes=scratch_shapes,
            compiler_params=pltpu.CompilerParams(vmem_limit_bytes=vmem * 2**20),
        )(*args)
    extra_in = ride.inputs()
    extra_shapes, extra_specs = ride.outputs()
    n_in, n_out, n_scratch = len(in_specs), len(out_specs), len(scratch_shapes)

    def riding(*refs):
        ins, refs = refs[:n_in], refs[n_in:]
        ride_ins, refs = refs[: len(extra_in)], refs[len(extra_in) :]
        outs, refs = refs[:n_out], refs[n_out:]
        ride_outs, refs = refs[: len(extra_shapes)], refs[len(extra_shapes) :]
        scratch, ride_scratch = refs[:n_scratch], refs[n_scratch:]
        ride.bind(ride_ins, ride_outs, ride_scratch)
        step = pl.program_id(0)
        for number, (at, _) in enumerate(ride.rounds):

            @pl.when(step == at)
            def _():
                ride.begin(number)

        if kernel is not None:
            kernel(*ins, *outs, *scratch)

        @pl.when(step == pl.num_programs(0) - 1)
        def _():
            ride.end()

    made = pl.pallas_call(
        riding,
        grid=grid,
        in_specs=list(in_specs) + [HBM] * len(extra_in),
        out_specs=list(out_specs) + extra_specs,
        out_shape=list(out_shape) + extra_shapes,
        scratch_shapes=scratch_shapes + ride.sems + ride.scratch,
        input_output_aliases={n_in + i: n_out + i for i in range(len(ride.gathers))},
        compiler_params=pltpu.CompilerParams(collective_id=ride.collective_id, has_side_effects=True, vmem_limit_bytes=vmem * 2**20),
    )(*args, *extra_in)
    ride.done(made[n_out:])
    return made[:n_out]


def start_kernel(mp, bits, kinds, *refs):
    count = len(kinds)
    shards, buffers, local = refs[:count], refs[count : 2 * count], refs[2 * count]
    links = Links(mp, bits, None, None)
    copies = [pltpu.make_async_copy(shards[i], kinds[i].at(links, buffers[i], links.me, ()), local.at[i]) for i in range(count)]
    for copy in copies:
        copy.start()
    for copy in copies:
        copy.wait()


def start_buffers(shards, kinds, mp, bits):
    shapes = []
    for shard, kind in zip(shards, kinds):
        shapes.append(jax.ShapeDtypeStruct((mp,) + (() if kind.line else (2,) * bits) + shard.shape, shard.dtype))
    return pl.pallas_call(
        functools.partial(start_kernel, mp, bits, kinds),
        in_specs=[pl.BlockSpec(memory_space=pltpu.VMEM)] * len(shards),
        out_specs=[HBM] * len(shards),
        out_shape=shapes,
        scratch_shapes=[pltpu.SemaphoreType.DMA((len(shards),))],
    )(*shards)


def fill_padded(padded, values, taps):
    rows, _, lanes = values.shape
    half = (taps - 1) // 2
    padded[pl.ds(half, rows)] = values
    place = lax.broadcasted_iota(jnp.int32, (half, SEG, lanes), 1)
    before = pltpu.roll(values[rows - half :].astype(F32), 1, axis=1)
    padded[pl.ds(0, half)] = low(jnp.where(place == 0, 0.0, before))
    after = pltpu.roll(values[:half].astype(F32), SEG - 1, axis=1)
    padded[pl.ds(half + rows, half)] = low(jnp.where(place == SEG - 1, 0.0, after))


def convolve(padded, taps_of, taps, rows, block, emit):
    weights = [taps_of(k) for k in range(taps)]

    def step(index, carry):
        start = index * block
        total = None
        for first in range(0, taps, 8):
            part = None
            for k in range(first, min(taps, first + 8)):
                term = weights[k] * padded[pl.ds(start + k, block)]
                part = term if part is None else part + term
            part = part.astype(F32)
            total = part if total is None else total + part
        emit(start, total)
        return carry

    lax.fori_loop(0, rows // block, step, 0)


def tap_grads(padded, grads, sums, pick, taps, rows, block):
    group = 8
    count = sums.shape[0] // SEG
    for first in range(0, taps, group):
        ks = range(first, min(taps, first + group))

        def step(index, totals):
            start = index * block
            here = grads[pl.ds(start, block)]
            made = []
            for k, total in zip(ks, totals):
                term = here * padded[pl.ds(start + k, block)]
                size = block
                while size > 1:
                    size //= 2
                    term = term[:size] + term[size:]
                made.append(total + term[0].astype(F32))
            return tuple(made)

        zero = jnp.zeros((SEG, LANES), F32)
        totals = lax.fori_loop(0, rows // block, step, (zero,) * len(ks), unroll=True)
        for k, total in zip(ks, totals):
            sums[pl.ds(k * SEG, SEG), :] = total
    for k in range(taps, count):
        sums[pl.ds(k * SEG, SEG), :] = jnp.zeros((SEG, LANES), F32)
    high = low(sums[...])
    rest = low(sums[...] - high.astype(F32))
    return (dot(pick[...], high) + dot(pick[...], rest))[:taps]


def tap_pick(shape):
    row = lax.broadcasted_iota(jnp.int32, shape, 0)
    col = lax.broadcasted_iota(jnp.int32, shape, 1)
    return low(((col >= row * SEG) & (col < row * SEG + SEG)).astype(F32))


def tap_scratch(taps):
    count = -(-taps // 16) * 16
    return [pltpu.VMEM((count * SEG, LANES), F32), pltpu.VMEM((count, count * SEG), BF16)]


def ffn_forward_kernel(final, ending, blocks, x_ref, gain_ref, w_in_ref, w_out_ref, *rest):
    if ending:
        last_ref, keep_ref, out_ref, h_ref, y_ref, flat = rest
    elif final:
        last_ref, out_ref, h_ref, y_ref = rest
    else:
        out_ref, h_ref = rest
    width = h_ref.shape[2]
    x = x_ref[...]
    normed, _ = norm_parts(x)
    a = low(normed * gain_ref[...])
    total = None
    for m in range(blocks):
        h = dot(a, w_in_ref[m])
        h_ref[m] = low(h)
        half = 0.5 * h
        s = low(half + half * jnp.tanh(half))
        part = dot_nt(s, w_out_ref[m])
        total = part if total is None else total + part
    out = x + 0.5 * total
    out_ref[...] = out
    if final:
        normed, _ = norm_parts(out)
        y = normed * last_ref[...]
        if ending:
            i = pl.program_id(0)
            tile = y.shape[0]
            here = pl.ds(pl.multiple_of(i * tile, tile), tile)
            for l in range(flat.shape[0]):
                flat[l, here, :] = y[:, l * LANES : (l + 1) * LANES] * keep_ref[here, :]

            @pl.when(i == pl.num_programs(0) - 1)
            def _():
                to_frames(flat, y_ref)
        else:
            y_ref[...] = y


def weight_parts(w):
    if isinstance(w, tuple):
        return w, (0, 0), w[0].shape
    return (w, w), (0, 1), w.shape[:2] + (w.shape[2] // 2,)


def ffn_forward(x, gain, w, last=None, keep=None, ride=None):
    tokens, depth = x.shape
    w, place, (blocks, _, width) = weight_parts(w)
    tile = min(256, tokens)
    row = pl.BlockSpec((tile, depth), lambda i: (i, 0))
    vec = pl.BlockSpec((1, depth), lambda i: (0, 0))
    out_shape = [jax.ShapeDtypeStruct(x.shape, F32), jax.ShapeDtypeStruct((blocks, tokens, width), BF16)]
    out_specs = [row, pl.BlockSpec((blocks, tile, width), lambda i: (0, i, 0))]
    in_specs = [row, vec] + [pl.BlockSpec((blocks, depth, width), lambda i, p=p: (0, 0, p)) for p in place]
    args = [x, gain, *w]
    scratch = []
    if last is not None:
        in_specs.append(vec)
        args.append(last)
        out_shape.append(jax.ShapeDtypeStruct(x.shape, F32))
        out_specs.append(row)
    if keep is not None:
        in_specs.append(pl.BlockSpec(keep.shape, lambda i: (0, 0)))
        args.append(keep)
        out_specs[-1] = pl.BlockSpec((tokens, depth), lambda i: (0, 0))
        scratch.append(pltpu.VMEM((depth // LANES, tokens, LANES), F32))
    return launch(
        functools.partial(ffn_forward_kernel, last is not None, keep is not None, blocks),
        grid=(tokens // tile,),
        in_specs=in_specs,
        out_specs=out_specs,
        out_shape=out_shape,
        scratch_shapes=scratch,
        vmem=56,
        ride=ride,
        args=args,
    )


def ffn_backward_kernel(final, ending, tile, g_ref, x_ref, gain_ref, h_ref, w_in_ref, w_out_ref, *rest):
    if final:
        last_ref, y_ref, dx_ref, dw_ref, dgain_ref, dlast_ref, grad, at, gt, a_rows, g_rows, s_rows, d_rows, da, flat = rest
    elif ending:
        dx_ref, dw_ref, dgain_ref, grad, at, gt, a_rows, g_rows, s_rows, d_rows, da, flat = rest
    else:
        dx_ref, dw_ref, dgain_ref, grad, at, gt, a_rows, g_rows, s_rows, d_rows, da, flat = rest
    m = pl.program_id(0)
    tokens = x_ref.shape[0]
    width = h_ref.shape[2]
    chunks = tokens // tile

    @pl.when(m == 0)
    def _():
        if final:
            dlast_ref[...] = jnp.zeros_like(dlast_ref)
        for c in range(chunks):
            here = pl.ds(c * tile, tile)
            g = g_ref[here, :]
            if final:
                normed, rstd = norm_parts(y_ref[here, :])
                dlast_ref[...] += jnp.sum(g * normed, axis=0, keepdims=True)
                g = norm_back(normed, rstd, last_ref[...], g)
                grad[here, :] = g
            g_low = low(0.5 * g)
            g_rows[here, :] = g_low
            normed, _ = norm_parts(x_ref[here, :])
            a_rows[here, :] = low(normed * gain_ref[...])
        at[...] = a_rows[...].T
        if not ending:
            gt[...] = g_rows[...].T

    w_in = w_in_ref[0]
    w_out = w_out_ref[0]
    for c in range(chunks):
        here = pl.ds(c * tile, tile)
        ds = dot(g_rows[here, :], w_out)
        h = h_ref[0, here, :].astype(F32)
        half = 0.5 * h
        tanh = jnp.tanh(half)
        s = half + half * tanh
        if not ending:
            s_rows[here, :] = low(s)
        sig = 0.5 + 0.5 * tanh
        dh = low(ds * (sig + s * (1.0 - sig)))
        d_rows[here, :] = dh
        part = dot_nt(dh, w_in)

        @pl.when(m == 0)
        def _():
            da[here, :] = part

        @pl.when(m != 0)
        def _():
            da[here, :] += part

    dw_ref[0, :, :width] = low(dot(at[...], d_rows[...]))
    if not ending:
        dw_ref[0, :, width:] = low(dot(gt[...], s_rows[...]))

    @pl.when(m == pl.num_programs(0) - 1)
    def _():
        dgain_ref[...] = jnp.zeros_like(dgain_ref)
        for c in range(chunks):
            here = pl.ds(c * tile, tile)
            normed, rstd = norm_parts(x_ref[here, :])
            d = da[here, :]
            dgain_ref[...] += jnp.sum(d * normed, axis=0, keepdims=True)
            base = grad[here, :] if final else g_ref[here, :]
            dx = base + norm_back(normed, rstd, gain_ref[...], d)
            if ending:
                split_lanes(flat, here, dx)
            else:
                dx_ref[here, :] = dx
        if ending:
            to_frames(flat, dx_ref)


def ffn_backward(g, x, gain, h, w, last=None, final_in=None, ending=False, ride=None):
    tokens, depth = x.shape
    w, place, (blocks, _, width) = weight_parts(w)
    tile = tokens
    full = pl.BlockSpec((tokens, depth), lambda i: (0, 0))
    vec = pl.BlockSpec((1, depth), lambda i: (0, 0))
    vec_shape = jax.ShapeDtypeStruct((1, depth), F32)
    in_specs = [full, full, vec, pl.BlockSpec((1, tokens, width), lambda i: (i, 0, 0))]
    in_specs += [pl.BlockSpec((1, depth, width), lambda i, p=p: (i, 0, p)) for p in place]
    args = [g, x, gain, h, *w]
    dw_width = width if ending else 2 * width
    out_specs = [full] + [pl.BlockSpec((1, depth, dw_width), lambda i: (i, 0, 0)), vec]
    out_shape = [jax.ShapeDtypeStruct(x.shape, F32)] + [jax.ShapeDtypeStruct((blocks, depth, dw_width), BF16), vec_shape]
    if last is not None:
        in_specs += [vec, full]
        args += [last, final_in]
        out_specs.append(vec)
        out_shape.append(vec_shape)
    return launch(
        functools.partial(ffn_backward_kernel, last is not None, ending, tile),
        grid=(blocks,),
        in_specs=in_specs,
        out_specs=out_specs,
        out_shape=out_shape,
        scratch_shapes=[
            pltpu.VMEM((tokens, depth) if last is not None else (8, 128), F32),
            pltpu.VMEM((depth, tokens), BF16),
            pltpu.VMEM((depth, tokens), BF16),
            pltpu.VMEM((tokens, depth), BF16),
            pltpu.VMEM((tokens, depth), BF16),
            pltpu.VMEM((tokens, width), BF16),
            pltpu.VMEM((tokens, width), BF16),
            pltpu.VMEM((tokens, depth), F32),
            pltpu.VMEM((depth // LANES, tokens if ending else 8, LANES), F32),
        ],
        vmem=56,
        ride=ride,
        args=args,
    )


def ffn_out_grad_kernel(g_ref, h_ref, dw_ref, gt):
    @pl.when(pl.program_id(0) == 0)
    def _():
        gt[...] = low(0.5 * g_ref[...]).T

    half = 0.5 * h_ref[0].astype(F32)
    dw_ref[0] = low(dot(gt[...], low(half + half * jnp.tanh(half))))


def ffn_out_grad(g, h, ride=None):
    tokens, depth = g.shape
    blocks, _, width = h.shape
    return launch(
        ffn_out_grad_kernel,
        grid=(blocks,),
        in_specs=[pl.BlockSpec((tokens, depth), lambda i: (0, 0)), pl.BlockSpec((1, tokens, width), lambda i: (i, 0, 0))],
        out_specs=[pl.BlockSpec((1, depth, width), lambda i: (i, 0, 0))],
        out_shape=[jax.ShapeDtypeStruct((blocks, depth, width), BF16)],
        scratch_shapes=[pltpu.VMEM((depth, tokens), BF16)],
        vmem=56,
        ride=ride,
        args=(g, h),
    )


def attention_forward_kernel(len_ref, keep_ref, x_ref, gain_ref, w_ref, table_ref, att_ref, q_ref, k_ref, v_ref, o_ref, lse_ref, b_rows, total, bias, flat):
    m = pl.program_id(0)
    tokens = x_ref.shape[0]
    rows = tokens // SEG
    length = len_ref[0]
    tile = 384

    @pl.when(m == 0)
    def _():
        for c in range(tokens // tile):
            here = pl.ds(c * tile, tile)
            normed, _ = norm_parts(x_ref[here, :])
            split_lanes(flat, here, normed * gain_ref[...])

        def emit(start, l, piece):
            b_rows[pl.ds(start, rows), pl.ds(l * LANES, LANES)] = low(piece)

        reorder(flat, SEG, emit)

    wide = PAIR * HEAD
    qkv = dot(b_rows[...], w_ref[0, :, : 3 * wide])
    lane = lax.broadcasted_iota(jnp.int32, (tokens, LANES), 1)
    at = lax.broadcasted_iota(jnp.int32, (tokens, LANES), 0)
    hidden = jnp.where(at < length, 0.0, MASKED)
    for head in range(PAIR):
        cols = pl.ds(head * LANES, LANES)

        def mine(piece):
            return piece if head == 0 else pltpu.roll(piece, HEAD, axis=1)

        q = low(mine(qkv[:, :wide])).astype(F32) * (HEAD**-0.5)
        k = mine(qkv[:, wide : 2 * wide])
        v = mine(qkv[:, 2 * wide :])
        q_ref[0, :, cols] = low(jnp.where(lane < HEAD, q, jnp.where(lane == HEAD, 1.0, 0.0)))
        k_ref[0, :, cols] = low(jnp.where(lane < HEAD, k, jnp.where(lane == HEAD, hidden, jnp.where(lane <= HEAD + 2, -1.0, 0.0))))
        v_ref[0, :, cols] = low(jnp.where(lane < HEAD, v, jnp.where(lane <= HEAD + 1, 1.0, 0.0)))
        span = table_ref.shape[2]
        line = jnp.broadcast_to(table_ref[0, head : head + 1, :], (LANES, span))
        bias[...] = pltpu.roll(line, span - LANES, axis=1, stride=1, stride_axis=0)
        for t in range(tokens // tile):
            here = pl.ds(t * tile, tile)
            scores = dot_nt(q_ref[0, here, cols], k_ref[0, :, cols])
            parts = []
            for sub in range(tile // LANES):
                first = tokens - LANES - t * tile - sub * LANES
                parts.append(scores[sub * LANES : (sub + 1) * LANES] + bias[:, pl.ds(first, tokens)])
            scores = jnp.concatenate(parts, axis=0)
            peak = jnp.max(scores, axis=-1, keepdims=True)
            expos = low(jnp.exp(scores - peak))
            out = dot(expos, v_ref[0, :, cols])
            denom = out[:, HEAD : HEAD + 1]
            out = out * (1.0 / denom)
            lse = peak + jnp.log(denom)
            if head == 0:
                o_ref[0, here, :] = low(out)
            else:
                lane_t = lax.broadcasted_iota(jnp.int32, (tile, LANES), 1)
                o_ref[0, here, :] = low(jnp.where(lane_t < HEAD, o_ref[0, here, :].astype(F32), pltpu.roll(out, HEAD, axis=1)))
            lse_ref[here, :] = jnp.broadcast_to(lse, (tile, LANES))
        lse = lse_ref[...]
        lse_high = low(lse).astype(F32)
        q_now = q_ref[0, :, cols].astype(F32)
        q_ref[0, :, cols] = low(jnp.where(lane == HEAD + 1, lse_high, jnp.where(lane == HEAD + 2, lse - lse_high, q_now)))
    part = dot_nt(o_ref[0], w_ref[0, :, 3 * wide :])

    @pl.when(m == 0)
    def _():
        total[...] = part

    @pl.when(m != 0)
    def _():
        total[...] += part

    @pl.when(m == pl.num_programs(0) - 1)
    def _():
        split_lanes(flat, pl.ds(0, tokens), total[...])

        def emit(start, l, piece):
            att_ref[pl.ds(start, SEG), pl.ds(l * LANES, LANES)] = low(piece * keep_ref[pl.ds(start, SEG), :])

        reorder(flat, rows, emit)


def attention_forward(length, keep, x, gain, w, table, ride=None):
    tokens, depth = x.shape
    blocks = w.shape[0]
    full = pl.BlockSpec((tokens, depth), lambda i: (0, 0))
    heads = pl.BlockSpec((1, tokens, PAIR * LANES), lambda i: (i, 0, 0))
    pair = pl.BlockSpec((1, tokens, LANES), lambda i: (i, 0, 0))
    heads_shape = jax.ShapeDtypeStruct((blocks, tokens, PAIR * LANES), BF16)
    return launch(
        attention_forward_kernel,
        grid=(blocks,),
        in_specs=[
            pl.BlockSpec(memory_space=pltpu.SMEM),
            pl.BlockSpec(keep.shape, lambda i: (0, 0)),
            full,
            pl.BlockSpec((1, depth), lambda i: (0, 0)),
            pl.BlockSpec((1, depth, w.shape[2]), lambda i: (i, 0, 0)),
            pl.BlockSpec((1, PAIR, table.shape[2]), lambda i: (i, 0, 0)),
        ],
        out_specs=[full, heads, heads, heads, pair],
        out_shape=[
            jax.ShapeDtypeStruct((tokens, depth), BF16),
            heads_shape,
            heads_shape,
            heads_shape,
            jax.ShapeDtypeStruct((blocks, tokens, LANES), BF16),
        ],
        scratch_shapes=[
            pltpu.VMEM((tokens, LANES), F32),
            pltpu.VMEM((tokens, depth), BF16),
            pltpu.VMEM((tokens, depth), F32),
            pltpu.VMEM((LANES, table.shape[2]), F32),
            pltpu.VMEM((depth // LANES, tokens, LANES), F32),
        ],
        vmem=56,
        ride=ride,
        args=(length, keep, x, gain, w, table,),
    )


def attention_backward_kernel(
    datt_ref, x_ref, gain_ref, res_ref, w_ref, table_ref, q_ref, k_ref, v_ref, o_ref,
    dx_ref, dw_ref, dgain_ref, dtable_ref,
    b_t, g_t, g_rows, flat, bias, dbias, do_aug, d_pair, dq_t, k_t, d_rows, db,
):
    m = pl.program_id(0)
    tokens = x_ref.shape[0]
    rows = tokens // SEG
    wide = PAIR * HEAD
    tile = 256
    span = table_ref.shape[2]
    stored = tokens // tile

    @pl.when(m == 0)
    def _():
        def emit(start, l, piece):
            g_rows[pl.ds(start, rows), pl.ds(l * LANES, LANES)] = low(piece)

        for c in range(tokens // tile):
            here = pl.ds(c * tile, tile)
            normed, _ = norm_parts(x_ref[here, :])
            split_lanes(flat, here, normed * gain_ref[...])
        reorder(flat, SEG, emit)
        b_t[...] = g_rows[...].T
        split_lanes(flat, pl.ds(0, tokens), datt_ref[...].astype(F32))
        reorder(flat, SEG, emit)
        g_t[...] = g_rows[...].T

    w_out = w_ref[0, :, 3 * wide :]
    do = low(dot(g_rows[...], w_out))
    dw_ref[0, :, 3 * wide :] = low(dot(g_t[...], o_ref[0]))
    lane = lax.broadcasted_iota(jnp.int32, (tokens, LANES), 1)
    do_full = do.astype(F32)
    product = do_full * o_ref[0].astype(F32)
    for head in range(PAIR):
        cols = pl.ds(head * LANES, LANES)
        inside = lane < HEAD if head == 0 else lane >= HEAD
        delta = jnp.sum(jnp.where(inside, product, 0.0), axis=-1, keepdims=True)
        delta_high = low(delta).astype(F32)
        mine = do_full if head == 0 else pltpu.roll(do_full, HEAD, axis=1)
        do_aug[...] = low(jnp.where(lane < HEAD, mine, jnp.where(lane == HEAD, -delta_high, jnp.where(lane == HEAD + 1, delta_high - delta, 0.0))))
        k_t[...] = k_ref[0, :, cols].T
        line = jnp.broadcast_to(table_ref[0, head : head + 1, :], (LANES, span))
        bias[...] = pltpu.roll(line, span - (LANES - 1), axis=1, stride=1, stride_axis=0)
        dbias[...] = jnp.zeros_like(dbias)
        for t in range(stored):
            here = pl.ds(t * tile, tile)
            scores = dot_nt(k_ref[0, here, cols], q_ref[0, :, cols])
            grads = dot_nt(v_ref[0, here, cols], do_aug[...])
            p_parts = []
            d_parts = []
            for sub in range(tile // LANES):
                first = tokens - LANES - t * tile - sub * LANES
                now = slice(sub * LANES, (sub + 1) * LANES)
                p = jnp.exp(scores[now] + bias[:, pl.ds(first, tokens)])
                ds = low(p * grads[now])
                dbias[:, pl.ds(first, tokens)] += ds.astype(F32)
                p_parts.append(low(p))
                d_parts.append(ds)
            p = jnp.concatenate(p_parts, axis=0)
            ds = jnp.concatenate(d_parts, axis=0)
            dv = dot(p, do_aug[...])
            dk = dot(ds, q_ref[0, :, cols])
            dq = dot(k_t[:, here], ds)
            if t == 0:
                dq_t[...] = dq
            else:
                dq_t[...] += dq
            if head == 0:
                d_pair[1, here, :] = dk
                d_pair[2, here, :] = dv
            else:
                lane_t = lax.broadcasted_iota(jnp.int32, (tile, LANES), 1)
                d_pair[1, here, :] = jnp.where(lane_t < HEAD, d_pair[1, here, :], pltpu.roll(dk, HEAD, axis=1))
                d_pair[2, here, :] = jnp.where(lane_t < HEAD, d_pair[2, here, :], pltpu.roll(dv, HEAD, axis=1))
        dq = dq_t[...].T * (HEAD**-0.5)
        if head == 0:
            d_pair[0] = dq
        else:
            d_pair[0] = jnp.where(lane < HEAD, d_pair[0], pltpu.roll(dq, HEAD, axis=1))
        folded = dbias[...]
        count = LANES
        while count > 1:
            count //= 2
            folded = folded[:count] + pltpu.roll(folded[count:], span - count, axis=1)
        dtable_ref[0, head : head + 1, :] = pltpu.roll(folded, LANES - 1, axis=1)
    for part in range(3):
        d_rows[:, pl.ds(part * wide, wide)] = low(d_pair[part])
    dw_ref[0, :, : 3 * wide] = low(dot(b_t[...], d_rows[...]))
    part = dot_nt(d_rows[...], w_ref[0, :, : 3 * wide])

    @pl.when(m == 0)
    def _():
        db[...] = part

    @pl.when(m != 0)
    def _():
        db[...] += part

    @pl.when(m == pl.num_programs(0) - 1)
    def _():
        dgain_ref[...] = jnp.zeros_like(dgain_ref)
        split_lanes(flat, pl.ds(0, tokens), db[...])

        def emit(start, l, piece):
            db[pl.ds(start, SEG), pl.ds(l * LANES, LANES)] = piece

        reorder(flat, rows, emit)
        for c in range(tokens // tile):
            here = pl.ds(c * tile, tile)
            normed, rstd = norm_parts(x_ref[here, :])
            d = db[here, :]
            dgain_ref[...] += jnp.sum(d * normed, axis=0, keepdims=True)
            dx_ref[here, :] = res_ref[here, :] + norm_back(normed, rstd, gain_ref[...], d)


def attention_backward(datt, x, gain, res, w, table_back, q, k, v, o, ride=None):
    tokens, depth = x.shape
    blocks = w.shape[0]
    span = table_back.shape[2]
    full = pl.BlockSpec((tokens, depth), lambda i: (0, 0))
    heads = pl.BlockSpec((1, tokens, PAIR * LANES), lambda i: (i, 0, 0))
    pair = pl.BlockSpec((1, tokens, LANES), lambda i: (i, 0, 0))
    vec = pl.BlockSpec((1, depth), lambda i: (0, 0))
    w_spec = pl.BlockSpec((1, depth, w.shape[2]), lambda i: (i, 0, 0))
    t_spec = pl.BlockSpec((1, PAIR, span), lambda i: (i, 0, 0))
    wide = PAIR * HEAD
    return launch(
        attention_backward_kernel,
        grid=(blocks,),
        in_specs=[full, full, vec, full, w_spec, t_spec, heads, heads, heads, pair],
        out_specs=[full, w_spec, vec, t_spec],
        out_shape=[
            jax.ShapeDtypeStruct((tokens, depth), F32),
            jax.ShapeDtypeStruct(w.shape, BF16),
            jax.ShapeDtypeStruct((1, depth), F32),
            jax.ShapeDtypeStruct(table_back.shape, F32),
        ],
        scratch_shapes=[
            pltpu.VMEM((depth, tokens), BF16),
            pltpu.VMEM((depth, tokens), BF16),
            pltpu.VMEM((tokens, depth), BF16),
            pltpu.VMEM((depth // LANES, tokens, LANES), F32),
            pltpu.VMEM((LANES, span), F32),
            pltpu.VMEM((LANES, span), F32),
            pltpu.VMEM((tokens, LANES), BF16),
            pltpu.VMEM((3, tokens, LANES), F32),
            pltpu.VMEM((LANES, tokens), F32),
            pltpu.VMEM((LANES, tokens), BF16),
            pltpu.VMEM((tokens, 3 * wide), BF16),
            pltpu.VMEM((tokens, depth), F32),
        ],
        vmem=56,
        ride=ride,
        args=(datt, x, gain, res, w, table_back, q, k, v, o,),
    )


def gate_forward_kernel(
    taps, keep_ref, x_ref, gain_ref, w_in_ref, w_out_ref, g_gain_ref, g_conv_ref,
    cg_ref, ur_ref, sr_ref, ug_ref, sg_ref, mean_ref, rstd_ref, conv_ref, gate_ref,
    c_rows, ur_all, ug_all, first, second, total, padded,
):
    i = pl.program_id(0)
    blocks = pl.num_programs(0) // 2
    tokens = x_ref.shape[0]
    rows = tokens // SEG
    width = ur_ref.shape[2]
    tile = 256
    channels = width * blocks

    @pl.when(i == 0)
    def _():
        for c in range(tokens // tile):
            here = pl.ds(c * tile, tile)
            normed, _ = norm_parts(x_ref[here, :])
            c_rows[here, :] = low(normed * gain_ref[...])
        first[...] = jnp.zeros_like(first)
        second[...] = jnp.zeros_like(second)

    @pl.when(i < blocks)
    def _():
        for c in range(tokens // tile):
            here = pl.ds(c * tile, tile)
            z = dot(c_rows[here, :], w_in_ref[0])
            zr = z[:, :width]
            zg = z[:, width:]
            ur, slope = gelu_and_slope(zr)
            ur = low(ur)
            ur_ref[0, here, :] = ur
            ur_all[i, here, :] = ur
            sr_ref[0, here, :] = low(slope)
            ug, slope = gelu_and_slope(zg)
            ug_low = low(ug)
            ug_ref[0, here, :] = ug_low
            ug_all[i, here, :] = ug_low
            sg_ref[0, here, :] = low(slope)
            square = ug * ug
            one = ug[:, :LANES]
            two = square[:, :LANES]
            for l in range(1, width // LANES):
                one = one + ug[:, l * LANES : (l + 1) * LANES]
                two = two + square[:, l * LANES : (l + 1) * LANES]
            first[here, :] += one
            second[here, :] += two

    @pl.when(i == blocks - 1)
    def _():
        for c in range(tokens // tile):
            here = pl.ds(c * tile, tile)
            mean = jnp.sum(first[here, :], axis=-1, keepdims=True) / channels
            spread = jnp.sum(second[here, :], axis=-1, keepdims=True) / channels - mean * mean
            mean_ref[here, :] = jnp.broadcast_to(mean, (tile, LANES))
            rstd_ref[here, :] = jnp.broadcast_to(lax.rsqrt(spread + EPSILON), (tile, LANES))

    @pl.when(i >= blocks)
    def _():
        m = i - blocks
        scale = rstd_ref[...] * keep_ref[...]
        shift = mean_ref[...] * scale
        for l in range(width // LANES):
            cols = pl.ds(l * LANES, LANES)
            ug = ug_all[m, :, cols].astype(F32)
            n = low((ug * scale - shift) * g_gain_ref[0, :, cols])
            fill_padded(padded, n.reshape(rows, SEG, LANES), taps)

            def taps_of(k):
                return low(jnp.broadcast_to(g_conv_ref[0, k : k + 1, cols], (SEG, LANES)))[None]

            def emit(start, value):
                block = value.shape[0]
                here = pl.ds(pl.multiple_of(start * SEG, block * SEG), block * SEG)
                flat = value.reshape(block * SEG, LANES)
                conv_ref[0, here, cols] = low(flat)
                gate_ref[0, here, cols] = low(ur_all[m, here, cols].astype(F32) * flat)

            convolve(padded, taps_of, taps, rows, 16, emit)
        part = dot_nt(gate_ref[0], w_out_ref[0])

        @pl.when(m == 0)
        def _():
            total[...] = part

        @pl.when(m != 0)
        def _():
            total[...] += part

        @pl.when(m == blocks - 1)
        def _():
            for l in range(total.shape[1] // LANES):
                cols = pl.ds(l * LANES, LANES)
                cg_ref[:, cols] = low(total[:, cols] * keep_ref[...])


def gate_forward(keep, x, gain, w, g_gain, g_conv, taps, ride=None):
    tokens, depth = x.shape
    blocks = w.shape[0]
    width = w.shape[2] // 3
    full = pl.BlockSpec((tokens, depth), lambda i: (0, 0))
    lanes = pl.BlockSpec((tokens, LANES), lambda i: (0, 0))

    def early(i):
        return jnp.minimum(i, blocks - 1)

    def late(i):
        return jnp.maximum(i - blocks, 0)

    z_early = pl.BlockSpec((1, tokens, width), lambda i: (early(i), 0, 0))
    z_late = pl.BlockSpec((1, tokens, width), lambda i: (late(i), 0, 0))
    z_shape = jax.ShapeDtypeStruct((blocks, tokens, width), BF16)
    lane_shape = jax.ShapeDtypeStruct((tokens, LANES), F32)
    return launch(
        functools.partial(gate_forward_kernel, taps),
        grid=(2 * blocks,),
        in_specs=[
            lanes,
            full,
            pl.BlockSpec((1, depth), lambda i: (0, 0)),
            pl.BlockSpec((1, depth, 2 * width), lambda i: (early(i), 0, 0)),
            pl.BlockSpec((1, depth, width), lambda i: (late(i), 0, 2)),
            pl.BlockSpec((1, 1, width), lambda i: (late(i), 0, 0)),
            pl.BlockSpec((1, taps, width), lambda i: (late(i), 0, 0)),
        ],
        out_specs=[full, z_early, z_early, z_early, z_early, lanes, lanes, z_late, z_late],
        out_shape=[jax.ShapeDtypeStruct((tokens, depth), BF16), z_shape, z_shape, z_shape, z_shape, lane_shape, lane_shape, z_shape, z_shape],
        scratch_shapes=[
            pltpu.VMEM((tokens, depth), BF16),
            pltpu.VMEM((blocks, tokens, width), BF16),
            pltpu.VMEM((blocks, tokens, width), BF16),
            pltpu.VMEM((tokens, LANES), F32),
            pltpu.VMEM((tokens, LANES), F32),
            pltpu.VMEM((tokens, depth), F32),
            pltpu.VMEM((tokens // SEG + taps - 1, SEG, LANES), BF16),
        ],
        vmem=60,
        ride=ride,
        args=(keep, x, gain, w, w, g_gain, g_conv,),
    )


def gate_backward_kernel(
    taps, keep_ref, dcg_ref, x_ref, gain_ref, res_ref, w_ref, ur_ref, sr_ref, ug_ref, sg_ref, conv_ref, gate_ref, mean_ref, rstd_ref, g_gain_ref, g_conv_ref,
    dx_ref, dw_ref, dgain_ref, dg_gain_ref, dg_conv_ref,
    c_rows, c_t, g_t, dn_all, first, second, dc, padded, n_padded, d_rows, dconv, shift, sums, pick,
):
    i = pl.program_id(0)
    blocks = pl.num_programs(0) // 2
    tokens = x_ref.shape[0]
    rows = tokens // SEG
    width = ur_ref.shape[2]
    tile = 256
    channels = width * blocks
    chunks = tokens // tile

    @pl.when(i == 0)
    def _():
        for c in range(chunks):
            here = pl.ds(c * tile, tile)
            normed, _ = norm_parts(x_ref[here, :])
            c_rows[here, :] = low(normed * gain_ref[...])
        c_t[...] = c_rows[...].T
        g_t[...] = dcg_ref[...].T
        first[...] = jnp.zeros_like(first)
        second[...] = jnp.zeros_like(second)
        dc[...] = jnp.zeros_like(dc)
        shift[...] = mean_ref[...] * rstd_ref[...]
        pick[...] = tap_pick(pick.shape)

    @pl.when(i < blocks)
    def _():
        m = i
        for c in range(chunks):
            here = pl.ds(c * tile, tile)
            dgate = dot(dcg_ref[here, :], w_ref[0, :, 2 * width :])
            dzr = low(dgate * (conv_ref[0, here, :].astype(F32) * sr_ref[0, here, :].astype(F32)))
            d_rows[here, :] = dzr
            dconv[here, :] = low(dgate * ur_ref[0, here, :].astype(F32))
            dc[here, :] += dot_nt(dzr, w_ref[0, :, :width])
        dw_ref[m, :, :width] = low(dot(c_t[...], d_rows[...]))
        dw_ref[m, :, 2 * width :] = low(dot(g_t[...], gate_ref[0]))
        for l in range(width // LANES):
            cols = pl.ds(l * LANES, LANES)
            ug = ug_ref[0, :, cols].astype(F32)
            n = low((ug * rstd_ref[...] - shift[...]) * keep_ref[...] * g_gain_ref[0, :, cols])
            fill_padded(n_padded, n.reshape(rows, SEG, LANES), taps)
            d = dconv[:, cols].reshape(rows, SEG, LANES)
            fill_padded(padded, d, taps)
            dg_conv_ref[0, :, cols] = tap_grads(n_padded, padded.at[pl.ds((taps - 1) // 2, rows)], sums, pick, taps, rows, 8)
            dg_gain_ref[0, :, cols] = jnp.zeros((1, LANES), F32)

            def taps_of(k):
                return low(jnp.broadcast_to(g_conv_ref[0, taps - 1 - k : taps - k, cols], (SEG, LANES)))[None]

            def emit(start, value):
                block = value.shape[0]
                here = pl.ds(pl.multiple_of(start * SEG, block * SEG), block * SEG)
                dn = value.reshape(block * SEG, LANES) * keep_ref[here, :]
                normed = ug_ref[0, here, cols].astype(F32) * rstd_ref[here, :] - shift[here, :]
                product = dn * normed
                dg_gain_ref[0, :, cols] += jnp.sum(product, axis=0, keepdims=True)
                scaled = dn * g_gain_ref[0, :, cols]
                dn_all[m, here, cols] = low(scaled)
                first[here, :] += scaled
                second[here, :] += product * g_gain_ref[0, :, cols]

            convolve(padded, taps_of, taps, rows, 16, emit)

    @pl.when(i == blocks - 1)
    def _():
        for c in range(chunks):
            here = pl.ds(c * tile, tile)
            one = jnp.sum(first[here, :], axis=-1, keepdims=True) / channels
            two = jnp.sum(second[here, :], axis=-1, keepdims=True) / channels
            first[here, :] = jnp.broadcast_to(one, (tile, LANES))
            second[here, :] = jnp.broadcast_to(two, (tile, LANES))

    @pl.when(i >= blocks)
    def _():
        m = i - blocks
        for c in range(chunks):
            here = pl.ds(c * tile, tile)
            rstd = rstd_ref[here, :]
            one = first[here, :]
            two = second[here, :]
            for l in range(width // LANES):
                cols = pl.ds(l * LANES, LANES)
                normed = ug_ref[0, here, cols].astype(F32) * rstd - shift[here, :]
                dug = rstd * (dn_all[m, here, cols].astype(F32) - one - normed * two)
                d_rows[here, cols] = low(dug * sg_ref[0, here, cols].astype(F32))
            dc[here, :] += dot_nt(d_rows[here, :], w_ref[0, :, width : 2 * width])
        dw_ref[m, :, width : 2 * width] = low(dot(c_t[...], d_rows[...]))

    @pl.when(i == 2 * blocks - 1)
    def _():
        dgain_ref[...] = jnp.zeros_like(dgain_ref)
        for c in range(chunks):
            here = pl.ds(c * tile, tile)
            normed, rstd = norm_parts(x_ref[here, :])
            d = dc[here, :]
            dgain_ref[...] += jnp.sum(d * normed, axis=0, keepdims=True)
            dx_ref[here, :] = res_ref[here, :] + norm_back(normed, rstd, gain_ref[...], d)


def gate_backward(keep, dcg, x, gain, res, w, ur, sr, ug, sg, conv, gate, mean, rstd, g_gain, g_conv, taps, ride=None):
    tokens, depth = x.shape
    blocks = w.shape[0]
    width = w.shape[2] // 3
    full = pl.BlockSpec((tokens, depth), lambda i: (0, 0))
    lanes = pl.BlockSpec((tokens, LANES), lambda i: (0, 0))
    vec = pl.BlockSpec((1, depth), lambda i: (0, 0))

    def early(i):
        return jnp.minimum(i, blocks - 1)

    z_early = pl.BlockSpec((1, tokens, width), lambda i: (early(i), 0, 0))
    z_cycle = pl.BlockSpec((1, tokens, width), lambda i: (lax.rem(i, blocks), 0, 0))
    gain_spec = pl.BlockSpec((1, 1, width), lambda i: (early(i), 0, 0))
    conv_spec = pl.BlockSpec((1, taps, width), lambda i: (early(i), 0, 0))
    padded = (tokens // SEG + taps - 1, SEG, LANES)
    return launch(
        functools.partial(gate_backward_kernel, taps),
        grid=(2 * blocks,),
        in_specs=[
            lanes,
            full,
            full,
            vec,
            full,
            pl.BlockSpec((1, depth, 3 * width), lambda i: (lax.rem(i, blocks), 0, 0)),
            z_early,
            z_early,
            z_cycle,
            z_cycle,
            z_early,
            z_early,
            lanes,
            lanes,
            gain_spec,
            conv_spec,
        ],
        out_specs=[full, pl.BlockSpec(w.shape, lambda i: (0, 0, 0)), vec, gain_spec, conv_spec],
        out_shape=[
            jax.ShapeDtypeStruct((tokens, depth), F32),
            jax.ShapeDtypeStruct(w.shape, BF16),
            jax.ShapeDtypeStruct((1, depth), F32),
            jax.ShapeDtypeStruct(g_gain.shape, F32),
            jax.ShapeDtypeStruct(g_conv.shape, F32),
        ],
        scratch_shapes=[
            pltpu.VMEM((tokens, depth), BF16),
            pltpu.VMEM((depth, tokens), BF16),
            pltpu.VMEM((depth, tokens), BF16),
            pltpu.VMEM((blocks, tokens, width), BF16),
            pltpu.VMEM((tokens, LANES), F32),
            pltpu.VMEM((tokens, LANES), F32),
            pltpu.VMEM((tokens, depth), F32),
            pltpu.VMEM(padded, BF16),
            pltpu.VMEM(padded, BF16),
            pltpu.VMEM((tokens, width), BF16),
            pltpu.VMEM((tokens, width), BF16),
            pltpu.VMEM((tokens, LANES), F32),
            *tap_scratch(taps),
        ],
        vmem=60,
        ride=ride,
        args=(keep, dcg, x, gain, res, w, ur, sr, ug, sg, conv, gate, mean, rstd, g_gain, g_conv,),
    )


def merge_forward_kernel(taps, x_ref, att_ref, cg_ref, w_ref, m_conv_ref, out_ref, merged_ref, padded):
    c = pl.program_id(0)
    tokens = x_ref.shape[0]
    rows = tokens // SEG
    half = pl.num_programs(0) // 2
    width = merged_ref.shape[1]
    for l in range(width // LANES):
        cols = pl.ds(l * LANES, LANES)

        @pl.when(c < half)
        def _():
            fill_padded(padded, att_ref[:, cols].reshape(rows, SEG, LANES), taps)

        @pl.when(c >= half)
        def _():
            fill_padded(padded, cg_ref[:, cols].reshape(rows, SEG, LANES), taps)

        def taps_of(k):
            return low(jnp.broadcast_to(m_conv_ref[k : k + 1, cols], (SEG, LANES)))[None]

        def emit(start, value):
            block = value.shape[0]
            here = pl.ds(pl.multiple_of(start * SEG, block * SEG), block * SEG)
            value = value + padded[pl.ds(start + (taps - 1) // 2, block)].astype(F32)
            merged_ref[here, cols] = low(value.reshape(block * SEG, LANES))

        convolve(padded, taps_of, taps, rows, 16, emit)
    w = jnp.concatenate([w_ref[m] for m in range(w_ref.shape[0])], axis=1)
    part = dot(merged_ref[...], w)

    @pl.when(c == 0)
    def _():
        out_ref[...] = x_ref[...] + part

    @pl.when(c != 0)
    def _():
        out_ref[...] += part


def merge_forward(x, att, cg, w, m_conv, ride=None):
    tokens, depth = x.shape
    blocks, both, cols = w.shape
    taps = m_conv.shape[0]
    width = 256
    steps = both // width
    half = steps // 2
    full = pl.BlockSpec((tokens, depth), lambda i: (0, 0))
    return launch(
        functools.partial(merge_forward_kernel, taps),
        grid=(steps,),
        in_specs=[
            full,
            pl.BlockSpec((tokens, width), lambda i: (0, jnp.minimum(i, half - 1))),
            pl.BlockSpec((tokens, width), lambda i: (0, jnp.maximum(i - half, 0))),
            pl.BlockSpec((blocks, width, cols), lambda i: (0, i, 0)),
            pl.BlockSpec((taps, width), lambda i: (0, i)),
        ],
        out_specs=[full, pl.BlockSpec((tokens, width), lambda i: (0, i))],
        out_shape=[jax.ShapeDtypeStruct(x.shape, F32), jax.ShapeDtypeStruct((tokens, both), BF16)],
        scratch_shapes=[pltpu.VMEM((tokens // SEG + taps - 1, SEG, LANES), BF16)],
        vmem=56,
        ride=ride,
        args=(x, att, cg, w, m_conv,),
    )


def merge_backward_kernel(taps, keep_ref, g_ref, att_ref, cg_ref, merged_ref, w_ref, m_conv_ref, datt_ref, dcg_ref, dw_ref, dconv_ref, g_rows, padded, j_padded, out, sums, pick):
    c = pl.program_id(0)
    tokens = g_ref.shape[0]
    rows = tokens // SEG
    half = pl.num_programs(0) // 2
    blocks, width, narrow = w_ref.shape

    @pl.when(c == 0)
    def _():
        g_rows[...] = low(g_ref[...])
        pick[...] = tap_pick(pick.shape)

    w = jnp.concatenate([w_ref[m] for m in range(blocks)], axis=1)
    dmerged = low(dot_nt(g_rows[...], w))
    dw = dot(merged_ref[...].T, g_rows[...])
    for m in range(blocks):
        dw_ref[m] = low(dw[:, m * narrow : (m + 1) * narrow])
    for l in range(width // LANES):
        cols = pl.ds(l * LANES, LANES)

        @pl.when(c < half)
        def _():
            fill_padded(j_padded, att_ref[:, cols].reshape(rows, SEG, LANES), taps)

        @pl.when(c >= half)
        def _():
            fill_padded(j_padded, cg_ref[:, cols].reshape(rows, SEG, LANES), taps)

        fill_padded(padded, dmerged[:, l * LANES : (l + 1) * LANES].reshape(rows, SEG, LANES), taps)
        dconv_ref[:, cols] = tap_grads(j_padded, padded.at[pl.ds((taps - 1) // 2, rows)], sums, pick, taps, rows, 8)

        def taps_of(k):
            return low(jnp.broadcast_to(m_conv_ref[taps - 1 - k : taps - k, cols], (SEG, LANES)))[None]

        def emit(start, value):
            block = value.shape[0]
            here = pl.ds(pl.multiple_of(start * SEG, block * SEG), block * SEG)
            value = value + padded[pl.ds(start + (taps - 1) // 2, block)].astype(F32)
            out[here, cols] = low(value.reshape(block * SEG, LANES) * keep_ref[here, :])

        convolve(padded, taps_of, taps, rows, 16, emit)

    @pl.when(c < half)
    def _():
        datt_ref[...] = out[...]

    @pl.when(c >= half)
    def _():
        dcg_ref[...] = out[...]


def merge_backward(keep, g, att, cg, merged, w, m_conv, ride=None):
    tokens, depth = g.shape
    blocks, both, cols = w.shape
    taps = m_conv.shape[0]
    width = 256
    steps = both // width
    half = steps // 2
    full = pl.BlockSpec((tokens, depth), lambda i: (0, 0))
    early = pl.BlockSpec((tokens, width), lambda i: (0, jnp.minimum(i, half - 1)))
    late = pl.BlockSpec((tokens, width), lambda i: (0, jnp.maximum(i - half, 0)))
    wide = pl.BlockSpec((tokens, width), lambda i: (0, i))
    w_spec = pl.BlockSpec((blocks, width, cols), lambda i: (0, i, 0))
    conv_spec = pl.BlockSpec((taps, width), lambda i: (0, i))
    padded = (tokens // SEG + taps - 1, SEG, LANES)
    return launch(
        functools.partial(merge_backward_kernel, taps),
        grid=(steps,),
        in_specs=[pl.BlockSpec(keep.shape, lambda i: (0, 0)), full, early, late, wide, w_spec, conv_spec],
        out_specs=[early, late, w_spec, conv_spec],
        out_shape=[
            jax.ShapeDtypeStruct((tokens, depth), BF16),
            jax.ShapeDtypeStruct((tokens, depth), BF16),
            jax.ShapeDtypeStruct(w.shape, BF16),
            jax.ShapeDtypeStruct(m_conv.shape, F32),
        ],
        scratch_shapes=[
            pltpu.VMEM((tokens, depth), BF16),
            pltpu.VMEM(padded, BF16),
            pltpu.VMEM(padded, BF16),
            pltpu.VMEM((tokens, width), BF16),
            *tap_scratch(taps),
        ],
        vmem=56,
        ride=ride,
        args=(keep, g, att, cg, merged, w, m_conv,),
    )


def no_ride(index):
    return None


def layer_forward(x, length, keep, weights, small, ride=no_ride, ending=False):
    gains, table, table_back, g_gain, g_conv, m_conv = small
    taps = m_conv.shape[0]
    x1, h1 = ffn_forward(x, gains[0:1], weights(0), ride=ride(0))
    att, q, k, v, o = attention_forward(length, keep, x1, gains[1:2], weights(1), table, ride=ride(1))
    cg, *inner = gate_forward(keep, x1, gains[2:3], weights(2), g_gain, g_conv, taps, ride=ride(2))
    x2, merged = merge_forward(x1, att, cg, weights(3), m_conv, ride=ride(3))
    x3, h2, y = ffn_forward(x2, gains[3:4], weights(4), gains[4:5], keep if ending else None, ride=ride(4))
    saved = (x, x1, h1, att, q, k, v, o, cg, inner, x2, merged, x3, h2)
    return y, saved


def layer_backward(g, keep, saved, weights, small, ride=no_ride, ready=lambda index, grad: None, before_last=lambda *_: None, ending=False):
    gains, table, table_back, g_gain, g_conv, m_conv = small
    taps = m_conv.shape[0]
    x, x1, h1, att, q, k, v, o, cg, inner, x2, merged, x3, h2 = saved
    ur, sr, ug, sg, mean, rstd, conv, gate = inner
    dx2, dg5, dgain3, dgain4 = ffn_backward(g, x2, gains[3:4], h2, weights(4), gains[4:5], x3, ride=ride(4))
    ready(4, dg5)
    datt, dcg, dg4, dm_conv = merge_backward(keep, dx2, att, cg, merged, weights(3), m_conv, ride=ride(3))
    ready(3, dg4)
    dx1, dg3, dgain2, dg_gain, dg_conv = gate_backward(
        keep, dcg, x1, gains[2:3], dx2, weights(2), ur, sr, ug, sg, conv, gate, mean, rstd, g_gain, g_conv, taps, ride=ride(2)
    )
    ready(2, dg3)
    dx1, dg2, dgain1, dtable = attention_backward(datt, x1, gains[1:2], dx1, weights(1), table_back, q, k, v, o, ride=ride(1))
    ready(1, dg2)
    dgains = jnp.concatenate([dgain1, dgain2, dgain3, dgain4], axis=0)
    before_last(0, dgains, (dtable, dg_gain, dg_conv, dm_conv))
    if ending:
        ready("out", *ffn_out_grad(dx1, h1, ride=ride("out")))
    dx, dg1, dgain0 = ffn_backward(dx1, x, gains[0:1], h1, weights(0), ending=ending, ride=ride(0))
    ready(0, dg1)
    return dx, dgain0


def to_segments(values):
    tokens, depth = values.shape
    return values.reshape(SEG, tokens // SEG, depth).transpose(1, 0, 2).reshape(tokens, depth)


def from_segments(values):
    tokens, depth = values.shape
    return values.reshape(tokens // SEG, SEG, depth).transpose(1, 0, 2).reshape(tokens, depth)


def pack_layer(layer, ffn_in, ffn_out, attn_in, attn_out, cg_in, cg_out, merge_out, mp_index, mp_size):
    cols = merge_out.shape[2] // mp_size
    part = lax.dynamic_slice_in_dim(merge_out[layer], mp_index * cols, cols, axis=1)
    pieces = (
        jnp.concatenate([ffn_in[layer, 0], ffn_out[layer, 0].T], axis=1),
        jnp.concatenate([attn_in[layer, 0], attn_in[layer, 1], attn_in[layer, 2], attn_out[layer].T], axis=1),
        jnp.concatenate([cg_in[layer, 0], cg_in[layer, 1], cg_out[layer].T], axis=1),
        part,
        jnp.concatenate([ffn_in[layer, 1], ffn_out[layer, 1].T], axis=1),
    )
    return tuple(low(piece) for piece in pieces)


GROUPS = 5
OPENING = [
    (0, [("line", 0), (0, 0)]),
    (1, [(0, 1), ("out", 0)]),
    (2, [(0, 2), ("out", 1), (1, 0)]),
    (3, [("out", 2), (0, 3), (2, 0)]),
    (4, [("out", 3), (1, 1)]),
]
FORWARD = {
    0: [(0, [(1, 2), (3, 0), (6, 0)]), (1, [(2, 1)]), (2, [(1, 3), (3, 1)])],
    1: [(0, [(2, 2), (4, 0)]), (1, [(5, 0)]), (2, [(4, 1)]), (3, [(2, 3), (3, 2)])],
    2: [(0, [(4, 2)]), (1, [(6, 1)]), (2, [(7, 0)]), (3, [(3, 3), (8, 0)]), (4, [(5, 1)])],
    3: [(0, [(4, 3), (5, 2), (9, 0)])],
    4: [(0, [(5, 3), (6, 2), (8, 1)])],
    5: [(0, [(6, 3), (7, 1)])],
    6: [(0, [(7, 2)]), (1, [(9, 1)]), (3, [(7, 3)])],
    7: [(0, [(9, 2)]), (2, [(8, 2)]), (6, [(9, 3)]), (7, [(8, 3)])],
}
BACKWARD = {
    8: [(0, [(9, 0)]), (1, [(9, 1)])],
    7: [(0, [(9, 2), (8, 0)]), (1, [(9, 3), (8, 1)]), (2, [(8, 2)]), (3, [(8, 3)])],
    6: [(0, [(7, 0)]), (1, [(7, 1)])],
    5: [(0, [(7, 2), (6, 0)]), (2, [(6, 1)])],
    4: [(0, [(7, 3), (6, 2), (5, 0)]), (1, [(5, 1)])],
    3: [(0, [(6, 3), (5, 2), (4, 0)]), (1, [(4, 1)])],
    2: [(0, [(5, 3), (4, 2), (3, 0)]), (1, [(4, 3), (3, 1)]), (2, [(3, 2)]), (3, [(3, 3)])],
    1: [(0, [(2, 0)]), (1, [(2, 1)])],
    "out": [(0, [(2, 2), (1, 0), ("small", 0)]), (2, [("small", 1)])],
    0: [(0, [("out", 0), (2, 3), (1, 1), ("small", 2)]), (1, [("out", 1), ("small", 3)])],
}
CLOSING = [
    (0, [(0, 0), ("out", 2), (1, 2), ("all", 0), ("vector", 0), ("merge", 0)]),
    (1, [(0, 1), ("out", 3), ("all", 1), ("vector", 1)]),
    (2, [(0, 2), (1, 3), ("all", 2), ("vector", 2)]),
    (3, [(0, 3), ("all", 3), ("vector", 3)]),
]


def reverse(values):
    shape = values.shape
    turn = (lax.broadcasted_iota(jnp.int32, (LANES, LANES), 0) + lax.broadcasted_iota(jnp.int32, (LANES, LANES), 1) == LANES - 1).astype(F32)
    blocks = values.reshape(-1, LANES)
    turned = jnp.dot(blocks, turn, precision=lax.Precision.HIGHEST, preferred_element_type=F32)
    return turned.reshape(*shape[:-1], -1, LANES)[..., ::-1, :].reshape(shape)


def plans(bits, names):
    groups = len(names)
    if bits == 3 and groups == 2 * GROUPS + 1:
        return OPENING, FORWARD, BACKWARD, CLOSING
    count = groups + bits
    opening = [(r, [(g, r - i) for i, g in enumerate(names) if 0 <= r - i <= bits] + ([("line", 0)] if r == 0 else [])) for r in range(count)]
    small = [(r, [("small", r)]) for r in range(bits + 1)]
    closing = [(r, [(g, r - i) for i, g in enumerate(names) if 0 <= r - i <= bits]) for r in range(count)]
    for s in range(bits + 1):
        closing[s][1].extend([("all", s), ("vector", s)])
    closing.append((count, [("merge", 0)]))
    return opening, {}, {"small": small}, closing


def body(frames, cotangent, lengths, norm_gains, ffn_in, ffn_out, attn_in, attn_out, rel_bias, cg_in, csgu_gain, csgu_conv, cg_out, merge_conv, merge_out):
    layers = norm_gains.shape[0]
    mp_size = lax.axis_size("mp")
    bits = lax.axis_size("dp").bit_length() - 1
    mp_index = lax.axis_index("mp")
    length = lax.dynamic_slice_in_dim(lengths, mp_index, 1)
    tokens, depth = frames.shape
    taps = merge_conv.shape[1]
    heads, span = rel_bias.shape[1:]
    channels = csgu_gain.shape[1]

    flow = {}
    ids = iter(range(1, 100))

    def ride(plan):
        return Ride(flow, mp_size, bits, next(ids), plan)

    def alone(plan):
        launch(None, (len(plan),), [], [], [], vmem=62, ride=ride(plan))

    shards = []
    for layer in range(layers):
        shards += pack_layer(layer, ffn_in, ffn_out, attn_in, attn_out, cg_in, cg_out, merge_out, mp_index, mp_size)
    f = ffn_in.shape[3]
    shards[:1] = [low(ffn_in[0, 0]), low(ffn_out[0, 0].T)]
    line = jnp.concatenate([rel_bias.reshape(layers, -1), csgu_gain, csgu_conv.reshape(layers, -1)], axis=1)
    line = line.reshape(-1, LANES)
    kinds = [Gather(mp_size, bits) for _ in shards] + [Gather(mp_size, bits, True)]
    names = [0, "out"] + list(range(1, layers * GROUPS))
    for name, kind, buffer in zip(names + ["line"], kinds, start_buffers(shards + [line], kinds, mp_size, bits)):
        flow[name] = (kind, buffer)
    opening, forward, backward, closing = plans(bits, names)
    alone(opening)
    line_all = flow["line"][1].reshape(mp_size, layers, -1)
    table = line_all[:, :, : heads * span].reshape(mp_size, layers, heads, span)
    g_gain = line_all[:, :, heads * span : heads * span + channels].reshape(mp_size, layers, 1, channels)
    g_conv = line_all[:, :, heads * span + channels :].reshape(mp_size, layers, taps, channels)

    table_back = reverse(table)
    keep_rows = keep_lanes(length, tokens)
    state = to_segments(frames).astype(F32)
    weights = {}
    smalls = []
    saved = []
    for layer in range(layers):

        def weight(index):
            at = layer * GROUPS + index
            if at not in weights:
                made = [flow[name][1] for name in ([0, "out"] if at == 0 else [at])]
                made = tuple(w.reshape(mp_size, -1, w.shape[-1]) for w in made)
                weights[at] = made if at == 0 else made[0]
            return weights[at]

        def beside(index):
            at = layer * GROUPS + index
            return ride(forward[at]) if at in forward else None

        smalls.append((norm_gains[layer], table[:, layer], table_back[:, layer], g_gain[:, layer], g_conv[:, layer], merge_conv[layer]))
        state, kept = layer_forward(state, length, keep_rows, weight, smalls[layer], beside, layer == layers - 1)
        saved.append(kept)
    frame = lax.broadcasted_iota(jnp.int32, (tokens, 1), 0)
    keep = (frame < length).astype(F32)
    output_frames = state
    incoming = to_segments(cotangent.astype(F32) * keep)
    tiny = [None] * layers
    counts = []

    def pack_small():
        split = [jnp.concatenate([t[1].reshape(mp_size, -1), t[2].reshape(mp_size, -1), t[3].reshape(mp_size, -1)], axis=1) for t in tiny]
        split = jnp.concatenate(split, axis=1).reshape(mp_size, -1, LANES)
        shared = jnp.concatenate([t[0].reshape(-1) for t in tiny] + [t[4].reshape(-1) for t in tiny])
        shared = jnp.pad(shared, (0, -shared.size % (mp_size * LANES))).reshape(mp_size, -1, LANES)
        counts.extend([split.shape[1], shared.shape[1]])
        padding = -sum(counts) % (16 << bits)
        packed = low(jnp.concatenate([split, shared, jnp.zeros((mp_size, padding, LANES), F32)], axis=1))
        packed = packed.reshape((mp_size,) + (2,) * bits + (-1, LANES))
        flow["small"] = (Scatter(mp_size, bits, *packed.shape[-2:]), packed)
        if "small" in backward:
            alone(backward["small"])

    for layer in reversed(range(layers)):

        def weight(index):
            return weights[layer * GROUPS + index]

        def beside(index):
            at = index if index == "out" else layer * GROUPS + index
            return ride(backward[at]) if at in backward else None

        def ready(index, grad):
            grad = grad.reshape((mp_size,) + (2,) * bits + (-1, grad.shape[-1]))
            flow[index if index == "out" else layer * GROUPS + index] = (Scatter(mp_size, bits, *grad.shape[-2:]), grad)

        def before_last(index, gains, small):
            tiny[layer] = (gains, *small)
            if layer == 0:
                pack_small()

        incoming, last_gain = layer_backward(incoming, keep_rows, saved[layer], weight, smalls[layer], beside, ready, before_last, layer == 0)
        if layer > 0:
            tiny[layer] = (jnp.concatenate([last_gain, tiny[layer][0]], axis=0), *tiny[layer][1:])
    vector = jnp.pad(last_gain.reshape(-1, LANES), ((0, -(depth // LANES) % 8), (0, 0)))
    kinds = [Gather(mp_size, bits), Gather(mp_size, bits)]
    flow["all"], flow["vector"] = zip(kinds, start_buffers([low(flow["small"][1]), vector], kinds, mp_size, bits))

    def start_merge():
        line = low(jnp.concatenate([flow[layer * GROUPS + 3][1] for layer in range(layers)], axis=0))
        kind = Gather(mp_size, bits, True)
        flow["merge"] = (kind, start_buffers([line], [kind], mp_size, bits)[0])

    if closing[-1][1] == [("merge", 0)]:
        alone(closing[:-1])
        start_merge()
        alone([(0, closing[-1][1])])
    else:
        start_merge()
        alone(closing)
    input_grad = incoming

    big = [flow[at][1] for at in range(layers * GROUPS)]
    packed = flow["all"][1].reshape(mp_size, -1, LANES).astype(F32)
    split_rows, shared_rows = counts
    split = lax.dynamic_index_in_dim(packed, mp_index, 0, keepdims=False)[:split_rows].reshape(layers, -1)
    grad_table = reverse(split[:, : heads * span].reshape(layers, heads, span))
    grad_g_gain = split[:, heads * span : heads * span + channels]
    grad_g_conv = split[:, heads * span + channels :].reshape(layers, taps, channels)
    shared = packed[:, split_rows : split_rows + shared_rows].reshape(-1)
    grad_gains = shared[: norm_gains.size - depth]
    vector = jnp.sum(flow["vector"][1].reshape(-1, flow["vector"][1].shape[-2] * LANES), axis=0)[:depth]
    grad_gains = jnp.concatenate([vector, grad_gains]).reshape(norm_gains.shape)
    grad_m_conv = shared[norm_gains.size - depth :][: merge_conv.size].reshape(merge_conv.shape)
    merge_all = flow["merge"][1].astype(F32).reshape(mp_size, layers, -1, LANES)
    grad_merge = merge_all.transpose(1, 2, 0, 3).reshape(merge_out.shape)

    h = attn_in.shape[3]
    c = cg_in.shape[3]
    one, two, three, _, five = [[big[layer * GROUPS + g] for layer in range(layers)] for g in range(GROUPS)]
    one[0] = jnp.concatenate([one[0], flow["out"][1]], axis=1)
    grad_ffn_in = jnp.stack([jnp.stack([a[:, :f], b[:, :f]]) for a, b in zip(one, five)])
    grad_ffn_out = jnp.stack([jnp.stack([a[:, f:].T, b[:, f:].T]) for a, b in zip(one, five)])
    grad_attn_in = jnp.stack([jnp.stack([a[:, :h], a[:, h : 2 * h], a[:, 2 * h : 3 * h]]) for a in two])
    grad_attn_out = jnp.stack([a[:, 3 * h :].T for a in two])
    grad_cg_in = jnp.stack([jnp.stack([a[:, :c], a[:, c : 2 * c]]) for a in three])
    grad_cg_out = jnp.stack([a[:, 2 * c :].T for a in three])
    return (
        output_frames,
        input_grad,
        grad_gains,
        grad_ffn_in,
        grad_ffn_out,
        grad_attn_in,
        grad_attn_out,
        grad_table,
        grad_cg_in,
        grad_g_gain,
        grad_g_conv,
        grad_cg_out,
        grad_m_conv,
        grad_merge,
    )


def solution(mesh):
    tokens = P(("dp", "mp"), None)
    columns = P(None, None, "dp", "mp")
    rows = P(None, "mp", "dp")
    ffn_rows = P(None, None, "mp", "dp")
    heads = P(None, "mp", None)
    taps = P(None, None, "mp")
    return jax.shard_map(
        body,
        mesh=mesh,
        in_specs=(tokens, tokens, P("dp"), P(), columns, ffn_rows, columns, rows, heads, columns, P(None, "mp"), taps, rows, P(), P(None, "dp", None)),
        out_specs=(tokens, tokens, P(), columns, ffn_rows, columns, rows, heads, columns, P(None, "mp"), taps, rows, P(), P(None, "dp", None)),
        check_vma=False,
    )
```
